32 devices in a mesh: dp: 8 (over y, x, core), chan: 4 (over z).
Axes of the slice: x: 2, y: 2, z: 4, core: 2. Of those that a mesh axis runs over, the one named last changes fastest.
Arguments:
- images: bfloat16 [128, 256, 192], P('dp'), may hold values from -6 to 6
- pixel_mask: int32 [128, 256], P('dp'), may hold values from 0 to 1, as said below
- counts: int32 [128], P('dp'), may hold values from 0 to 256, as said below
- labels: int32 [128], P('dp'), may hold values from 0 to 999
- block_w: float32 [537, 9216], P(None, 'chan')
- chan_side: float32 [101, 1152], P(None, 'chan')
- head_w: float32 [320, 10240], P(None, 'chan'), may hold values from -0.3125 to 0.3125
- head_side: float32 [1280, 1002], P('chan')
- shared: float32 [5784], replicated
- block_mom: float32 [537, 9216], P(None, 'chan')
- side_mom: float32 [101, 1152], P(None, 'chan')
- head_mom: float32 [320, 10240], P(None, 'chan'), may hold values from -0.3125 to 0.3125
- hside_mom: float32 [1280, 1002], P('chan')
- shared_mom: float32 [5784], replicated
- block_ema: float32 [537, 9216], P(None, 'chan')
- side_ema: float32 [101, 1152], P(None, 'chan')
- head_ema: float32 [320, 10240], P(None, 'chan'), may hold values from -0.3125 to 0.3125
- hside_ema: float32 [1280, 1002], P('chan')
- shared_ema: float32 [5784], replicated
- chan_stats: float32 [4, 1152], P(None, 'chan')
- head_stats: float32 [2, 1280], P(None, 'chan')
- proj_stats: float32 [2, 320], P(None, 'chan')
Outputs:
- loss: float32 [], replicated
- new_block: float32 [537, 9216], P(None, 'chan')
- new_side: float32 [101, 1152], P(None, 'chan')
- new_head: float32 [320, 10240], P(None, 'chan')
- new_hside: float32 [1280, 1002], P('chan')
- new_shared: float32 [5784], replicated
- mom_block: float32 [537, 9216], P(None, 'chan')
- mom_side: float32 [101, 1152], P(None, 'chan')
- mom_head: float32 [320, 10240], P(None, 'chan')
- mom_hside: float32 [1280, 1002], P('chan')
- mom_shared: float32 [5784], replicated
- ema_block: float32 [537, 9216], P(None, 'chan')
- ema_side: float32 [101, 1152], P(None, 'chan')
- ema_head: float32 [320, 10240], P(None, 'chan')
- ema_hside: float32 [1280, 1002], P('chan')
- ema_shared: float32 [5784], replicated
- new_chan_stats: float32 [4, 1152], P(None, 'chan')
- new_head_stats: float32 [2, 1280], P(None, 'chan')
- new_proj_stats: float32 [2, 320], P(None, 'chan')
The draws below stay inside these ranges and needn't reach their ends.
Inputs may be any that keep to these rules, and one draw needn't show every extreme that they name: `pixel_mask`: an image's ones form a rectangle of 4 to 16 rows and columns in the map's top-left corner, or the image has none; image 0 is full and image 1 empty. `counts`: the number of ones in the image's row of pixel_mask.
All inputs are finite; a program needn't handle non-finite values.
Results may differ from the reference program's by a relative error of at most 0.018.
Values may be sent and summed in bfloat16 or wider, within the bound.
A program may use at most 384 MiB of HBM per device.

```python
import jax
import jax.numpy as jnp
from jax import lax

WIDTH_IN = 192
EXPANDED = 1152
WIDTH_OUT = 320
HEAD_WIDTH = 1280
SQUEEZE = 48
CLASSES = 1000
EXPERTS = 8
KERNEL = 5
MAP_SIDE = 16
IMAGES = 128
BLOCK_ROWS = 537


def stacked(key, salt, lead, segments, columns, moment):
    keyed = jax.random.fold_in(key, salt)
    center = jnp.concatenate([jnp.full((count,), middle, jnp.float32) for count, middle, scale in segments])
    spread = jnp.concatenate([jnp.full((count,), scale, jnp.float32) for count, middle, scale in segments])
    if moment:
        spread = spread + jnp.abs(center)
        center = 0.0 * center
    noise = jax.random.normal(keyed, lead + (center.shape[0], columns), jnp.float32)
    return center[:, None] + spread[:, None] * noise


def block_rows():
    return [(WIDTH_IN, 0.0, WIDTH_IN ** (-0.5)), (KERNEL * KERNEL, 0.0, 0.2), (WIDTH_OUT, 0.0, EXPANDED ** (-0.5))]


def side_rows():
    return [(SQUEEZE, 0.0, EXPANDED ** (-0.5)), (SQUEEZE, 0.0, 2.0 * SQUEEZE ** (-0.5)), (1, 1.0, 0.1), (1, 0.0, 0.2), (1, 1.0, 0.1), (1, 0.0, 0.2), (1, 0.0, 0.5)]


def hside_rows():
    return [(1, 1.0, 0.1), (1, 0.0, 0.2), (CLASSES, 0.0, 4.0 * HEAD_WIDTH ** (-0.5))]


def shared_rows():
    return [(WIDTH_IN * EXPERTS, 0.0, 0.5), (WIDTH_OUT * EXPERTS, 0.0, 0.3), (WIDTH_OUT, 1.0, 0.1), (WIDTH_OUT, 0.0, 0.2), (SQUEEZE, 0.0, 0.5), (CLASSES, 0.0, 0.5)]


def stat_rows(pairs):
    rows = []
    for index_pair in range(pairs):
        rows = rows + [(1, 0.0, 0.1), (1, 0.3, 0.05)]
    return rows


def rectangles(key):
    keyed = jax.random.fold_in(key, 101)
    key_rows, key_cols, key_empty = jax.random.split(keyed, 3)
    height = jax.random.randint(key_rows, (IMAGES,), 4, MAP_SIDE + 1)
    width = jax.random.randint(key_cols, (IMAGES,), 4, MAP_SIDE + 1)
    empty = jax.random.randint(key_empty, (IMAGES,), 0, 8) == 0
    image_ids = jnp.arange(IMAGES)
    height = jnp.where(image_ids == 0, MAP_SIDE, jnp.where(empty | (image_ids == 1), 0, height))
    width = jnp.where(image_ids == 0, MAP_SIDE, width)
    return (height, width)


def draw_pixel_mask(key, part):
    height, width = rectangles(key)
    places = jnp.arange(MAP_SIDE * MAP_SIDE)
    inside = ((places // MAP_SIDE)[None, :] < height[:, None]) & ((places % MAP_SIDE)[None, :] < width[:, None])
    return inside.astype(jnp.int32)


def draw_counts(key, part):
    height, width = rectangles(key)
    return (height * width).astype(jnp.int32)


def draw_block_w(key, part):
    return stacked(key, 1, (), block_rows(), EXPANDED * EXPERTS, False)


def draw_block_mom(key, part):
    return stacked(key, 2, (), block_rows(), EXPANDED * EXPERTS, True)


def draw_block_ema(key, part):
    return stacked(key, 3, (), block_rows(), EXPANDED * EXPERTS, False)


def draw_chan_side(key, part):
    return stacked(key, 4, (), side_rows(), EXPANDED, False)


def draw_side_mom(key, part):
    return stacked(key, 5, (), side_rows(), EXPANDED, True)


def draw_side_ema(key, part):
    return stacked(key, 6, (), side_rows(), EXPANDED, False)


def draw_head_side(key, part):
    return stacked(key, 7, (), hside_rows(), HEAD_WIDTH, False).T


def draw_hside_mom(key, part):
    return stacked(key, 8, (), hside_rows(), HEAD_WIDTH, True).T


def draw_hside_ema(key, part):
    return stacked(key, 9, (), hside_rows(), HEAD_WIDTH, False).T


def draw_shared(key, part):
    return stacked(key, 10, (), shared_rows(), 1, False).reshape(-1)


def draw_shared_mom(key, part):
    return stacked(key, 11, (), shared_rows(), 1, True).reshape(-1)


def draw_shared_ema(key, part):
    return stacked(key, 12, (), shared_rows(), 1, False).reshape(-1)


def draw_chan_stats(key, part):
    return stacked(key, 13, (), stat_rows(2), EXPANDED, False)


def draw_head_stats(key, part):
    return stacked(key, 14, (), stat_rows(1), HEAD_WIDTH, False)


def draw_proj_stats(key, part):
    return stacked(key, 15, (), stat_rows(1), WIDTH_OUT, False)


def touch_ends(drawn, rng, low, high):
    spot = [jax.random.randint(jax.random.fold_in(rng, axis), (), 0, length) for axis, length in enumerate(drawn.shape)]
    main_axis = drawn.shape.index(max(drawn.shape))
    beside = spot[:main_axis] + [(spot[main_axis] + 1) % drawn.shape[main_axis]] + spot[main_axis + 1:]
    return drawn.at[tuple(spot)].set(low).at[tuple(beside)].set(high)


def block_levels(key, dims, pieces, least, top_value):
    def one(position, parts):
        heights = jax.random.uniform(jax.random.fold_in(jax.random.fold_in(key, 6), position), (parts,), jnp.float32, least / len(pieces), top_value / len(pieces))
        return jnp.repeat(jnp.exp(heights), dims[position] // parts).reshape((-1,) + (1,) * (len(dims) - position - 1))

    level = one(*pieces[0])
    for cut in pieces[1:]:
        level = level * one(*cut)
    return level


def scatter_about(key, extent, deviation, limit, pieces=(), dtype=jnp.bfloat16):
    values = jax.random.normal(key, extent, jnp.float32) * deviation
    if len(pieces) > 0:
        values = block_levels(key, extent, pieces, -0.22, 0.18) * values
    return jnp.clip(values, min=-limit, max=limit).astype(dtype)


def setup_inputs(seed: int = 0) -> dict:
    keys = jax.random.split(jax.random.key(seed), 23)
    return {
        "images": scatter_about(keys[0], (IMAGES, MAP_SIDE * MAP_SIDE, WIDTH_IN), 1.0, 6.0, ((0, 8),)),
        "pixel_mask": draw_pixel_mask(jax.random.fold_in(keys[22], 71), 0),
        "counts": draw_counts(jax.random.fold_in(keys[22], 71), 0),
        "labels": touch_ends(jax.random.randint(keys[3], (IMAGES,), 0, CLASSES), jax.random.fold_in(keys[3], 1), 0, CLASSES - 1).astype(jnp.int32),
        "block_w": draw_block_w(jax.random.fold_in(keys[22], 71), 0),
        "chan_side": draw_chan_side(jax.random.fold_in(keys[22], 71), 0),
        "head_w": scatter_about(keys[6], (WIDTH_OUT, HEAD_WIDTH * EXPERTS), WIDTH_OUT ** -0.5, 0.3125, ((1, 4),), jnp.float32),
        "head_side": draw_head_side(jax.random.fold_in(keys[22], 71), 0),
        "shared": draw_shared(jax.random.fold_in(keys[22], 71), 0),
        "block_mom": draw_block_mom(jax.random.fold_in(keys[22], 71), 0),
        "side_mom": draw_side_mom(jax.random.fold_in(keys[22], 71), 0),
        "head_mom": scatter_about(keys[11], (WIDTH_OUT, HEAD_WIDTH * EXPERTS), WIDTH_OUT ** -0.5, 0.3125, ((1, 4),), jnp.float32),
        "hside_mom": draw_hside_mom(jax.random.fold_in(keys[22], 71), 0),
        "shared_mom": draw_shared_mom(jax.random.fold_in(keys[22], 71), 0),
        "block_ema": draw_block_ema(jax.random.fold_in(keys[22], 71), 0),
        "side_ema": draw_side_ema(jax.random.fold_in(keys[22], 71), 0),
        "head_ema": scatter_about(keys[16], (WIDTH_OUT, HEAD_WIDTH * EXPERTS), WIDTH_OUT ** -0.5, 0.3125, ((1, 4),), jnp.float32),
        "hside_ema": draw_hside_ema(jax.random.fold_in(keys[22], 71), 0),
        "shared_ema": draw_shared_ema(jax.random.fold_in(keys[22], 71), 0),
        "chan_stats": draw_chan_stats(jax.random.fold_in(keys[22], 71), 0),
        "head_stats": draw_head_stats(jax.random.fold_in(keys[22], 71), 0),
        "proj_stats": draw_proj_stats(jax.random.fold_in(keys[22], 71), 0),
    }


@jax.custom_vjp
def low(v):
    return lax.optimization_barrier(v.astype(jnp.bfloat16)).astype(jnp.float32)

@jax.custom_vjp
def low_back(v):
    return v

def low_keep(v):
    return (low(v), None)

def low_pass(kept, grad):
    return (grad,)

def back_keep(v):
    return (v, None)

def back_low(kept, grad):
    return (low(grad),)
low.defvjp(low_keep, low_pass)
low_back.defvjp(back_keep, back_low)
eps_norm = 0.001
highest = lax.Precision.HIGHEST

def pooled(values, pix_mask, pool_div):
    return jnp.einsum('bp,bpc->bc', pix_mask, values, precision=highest) / pool_div[:, None]

def batch_norm(values, pix_mask, total, gain, bias):
    mask_cols = pix_mask[:, :, None]
    mean = lax.optimization_barrier(jnp.sum(mask_cols * values, axis=(0, 1))) / total
    variance = lax.optimization_barrier(jnp.sum(mask_cols * values * values, axis=(0, 1))) / total - mean * mean
    normed = (values - mean) * lax.rsqrt(variance + eps_norm) * gain + bias
    return (normed, mean, variance)

def depthwise(values, kernels):
    count, pixels, channels = values.shape
    grid = values.reshape(count, MAP_SIDE, MAP_SIDE, channels)
    reach = KERNEL // 2
    padded = jnp.pad(grid, ((0, 0), (reach, reach), (reach, reach), (0, 0)))
    result = jnp.zeros_like(grid)
    for tap_index in range(KERNEL * KERNEL):
        row_off = tap_index // KERNEL
        col_off = tap_index % KERNEL
        result = result + kernels[:, tap_index, None, None, :] * padded[:, row_off:row_off + MAP_SIDE, col_off:col_off + MAP_SIDE, :]
    return result.reshape(count, pixels, channels)

def split_shared(shared):
    end_route = WIDTH_IN * EXPERTS
    end_head = end_route + WIDTH_OUT * EXPERTS
    end_norm = end_head + 2 * WIDTH_OUT
    end_squeeze = end_norm + SQUEEZE
    return (shared[:end_route].reshape(WIDTH_IN, EXPERTS), shared[end_route:end_head].reshape(WIDTH_OUT, EXPERTS), shared[end_head:end_head + WIDTH_OUT], shared[end_head + WIDTH_OUT:end_norm], shared[end_norm:end_squeeze], shared[end_squeeze:])

def update(weight, grad, moment, average, grad_sq, weight_sq):
    scaled = grad * jnp.sqrt(weight_sq) * lax.rsqrt(grad_sq + 1e-12)
    moment_new = 0.5 * moment + scaled
    weight_new = weight - 0.2 * (scaled + 0.5 * moment_new)
    average_new = 0.5 * average + 0.5 * weight_new
    return (weight_new, moment_new, average_new)

def forward(params, image_vals, pix_mask, pool_div, total, valid, labels):
    block_flat, chan_side, head_flat, head_side, shared = params
    block_w = block_flat.reshape(BLOCK_ROWS, EXPANDED, EXPERTS)
    head_w = head_flat.reshape(WIDTH_OUT, HEAD_WIDTH, EXPERTS)
    route_in, route_head, gain_proj, bias_proj, squeeze_bias, class_bias = split_shared(shared)
    taps = KERNEL * KERNEL
    mask_cols = pix_mask[:, :, None]
    gates_in = jax.nn.sigmoid(jnp.dot(pooled(image_vals, pix_mask, pool_div), route_in, precision=highest))
    mixed_expand = low(jnp.einsum('be,ice->bic', gates_in, block_w[:WIDTH_IN], precision=highest))
    expand_pre = low_back(jnp.einsum('bpi,bic->bpc', image_vals, mixed_expand, precision=highest))
    normed, mean_one, var_one = batch_norm(expand_pre, pix_mask, total, chan_side[2 * SQUEEZE], chan_side[2 * SQUEEZE + 1])
    expand_act = jax.nn.silu(normed) * mask_cols
    kernels = jnp.einsum('be,tce->btc', gates_in, block_w[WIDTH_IN:WIDTH_IN + taps], precision=highest)
    depth_pre = depthwise(expand_act, kernels)
    normed, mean_two, var_two = batch_norm(depth_pre, pix_mask, total, chan_side[2 * SQUEEZE + 2], chan_side[2 * SQUEEZE + 3])
    depth_act = jax.nn.silu(normed) * mask_cols
    squeeze_act = jax.nn.silu(jnp.dot(pooled(depth_act, pix_mask, pool_div), chan_side[:SQUEEZE].T, precision=highest) + squeeze_bias)
    excite = jax.nn.sigmoid(jnp.dot(squeeze_act, chan_side[SQUEEZE:2 * SQUEEZE], precision=highest) + chan_side[2 * SQUEEZE + 4])
    excited = low(depth_act * excite[:, None, :])
    mixed_proj = low(jnp.einsum('be,oce->boc', gates_in, block_w[WIDTH_IN + taps:], precision=highest))
    proj_pre = low_back(jnp.einsum('bpc,boc->bpo', excited, mixed_proj, precision=highest))
    normed, mean_three, var_three = batch_norm(proj_pre, pix_mask, total, gain_proj, bias_proj)
    proj_low = low(normed * mask_cols)
    gates_head = jax.nn.sigmoid(jnp.dot(pooled(proj_low, pix_mask, pool_div), route_head, precision=highest))
    mixed_head = low(jnp.einsum('be,ice->bic', gates_head, head_w, precision=highest))
    head_pre = low_back(jnp.einsum('bpi,bic->bpc', proj_low, mixed_head, precision=highest))
    normed, mean_four, var_four = batch_norm(head_pre, pix_mask, total, head_side[:, 0], head_side[:, 1])
    features = pooled(jax.nn.silu(normed) * mask_cols, pix_mask, pool_div)
    logits = jnp.dot(features, head_side[:, 2:], precision=highest) + class_bias
    log_probs = jax.nn.log_softmax(logits, axis=1)
    picked = jnp.take_along_axis(log_probs, labels[:, None], axis=1)[:, 0]
    per_image = -(0.9 * picked + 0.1 * lax.optimization_barrier(jnp.mean(log_probs, axis=1)))
    loss = jnp.sum(per_image * valid) / jnp.sum(valid)
    return (loss, (mean_one, var_one, mean_two, var_two, mean_three, var_three, mean_four, var_four))

def reference(images, pixel_mask, counts, labels, block_w, chan_side, head_w, head_side, shared, block_mom, side_mom, head_mom, hside_mom, shared_mom, block_ema, side_ema, head_ema, hside_ema, shared_ema, chan_stats, head_stats, proj_stats):
    pix_mask = pixel_mask.astype(jnp.float32)
    pool_div = jnp.maximum(counts, 1).astype(jnp.float32)
    total = jnp.sum(counts).astype(jnp.float32)
    valid = (counts > 0).astype(jnp.float32)
    image_vals = images.astype(jnp.float32)
    params = (block_w, chan_side, head_w, head_side, shared)

    def objective(weights):
        return forward(weights, image_vals, pix_mask, pool_div, total, valid, labels)
    loss, pullback, stats = jax.vjp(objective, params, has_aux=True)
    grads = pullback(jnp.ones_like(loss))[0]
    moments = (block_mom, side_mom, head_mom, hside_mom, shared_mom)
    averages = (block_ema, side_ema, head_ema, hside_ema, shared_ema)
    results = [update(params[group], grads[group], moments[group], averages[group], jnp.sum(grads[group] * grads[group]), jnp.sum(params[group] * params[group])) for group in range(5)]
    unbias = total / (total - 1.0)
    mean_one, var_one, mean_two, var_two, mean_three, var_three, mean_four, var_four = stats
    new_chan = 0.5 * chan_stats + 0.5 * jnp.stack([mean_one, var_one * unbias, mean_two, var_two * unbias])
    new_head = 0.5 * head_stats + 0.5 * jnp.stack([mean_four, var_four * unbias])
    new_proj = 0.5 * proj_stats + 0.5 * jnp.stack([mean_three, var_three * unbias])
    return (loss, results[0][0], results[1][0], results[2][0], results[3][0], results[4][0], results[0][1], results[1][1], results[2][1], results[3][1], results[4][1], results[0][2], results[1][2], results[2][2], results[3][2], results[4][2], new_chan, new_head, new_proj)
```

```python
import functools

import jax
import jax.numpy as jnp
from jax import lax
from jax.experimental import pallas as pl
from jax.experimental.pallas import tpu as pltpu
from jax.sharding import PartitionSpec as P

WIDTH_IN = 192
WIDTH_OUT = 320
SQUEEZE = 48
CLASSES = 1000
EXPERTS = 8
KERNEL = 5
MAP_SIDE = 16
TAPS = KERNEL * KERNEL
PIXELS = MAP_SIDE * MAP_SIDE
LANES = 128
CLASS_PAD = 1024
eps_norm = 0.001
highest = lax.Precision.HIGHEST
MESH = pl.DeviceIdType.MESH
f32 = jnp.float32
bf16 = jnp.bfloat16
VMEM = pltpu.VMEM
VLIMIT = 60 * 1024 * 1024


def dot(a, b, dims=((1,), (0,)), precision=None):
    return lax.dot_general(a, b, (dims, ((), ())), precision=precision, preferred_element_type=f32)


NN = ((1,), (0,))
NT = ((1,), (1,))
TN = ((0,), (0,))


def sig(x):
    return 0.5 * jnp.tanh(0.5 * x) + 0.5


def dsilu(n):
    s = sig(n)
    return s * (1.0 + n * (1.0 - s))


def rsum(x):
    return jnp.sum(x, axis=0, keepdims=True)


def split(x):
    high = x.astype(bf16)
    return jnp.concatenate([high, (x - high.astype(f32)).astype(bf16)], axis=0)


def greet(peers):
    barrier = pltpu.get_barrier_semaphore()
    for peer in peers:
        pl.semaphore_signal(barrier, inc=1, device_id=peer, device_id_type=MESH)
    pl.semaphore_wait(barrier, len(peers))


def sum_kernel(nd, nz, x_ref, o_ref, plane, depth, s1, r1, s2, r2):
    d = lax.axis_index("dp")
    z = lax.axis_index("chan")
    in_plane = [(lax.rem(d + k, nd), z) for k in range(1, nd)]
    along = [(d, lax.rem(z + k, nz)) for k in range(1, nz)]
    greet(in_plane + along)
    first = []
    for k, peer in enumerate(in_plane):
        first.append(
            pltpu.make_async_remote_copy(
                src_ref=x_ref,
                dst_ref=plane.at[d],
                send_sem=s1.at[k],
                recv_sem=r1.at[k],
                device_id=peer,
                device_id_type=MESH,
            )
        )
        first[-1].start()
    plane[d] = x_ref[...]
    for copy in first:
        copy.wait_recv()
    total = plane[0]
    for k in range(1, nd):
        total = total + plane[k]
    depth[z] = total
    second = []
    for k, peer in enumerate(along):
        second.append(
            pltpu.make_async_remote_copy(
                src_ref=depth.at[z],
                dst_ref=depth.at[z],
                send_sem=s2.at[k],
                recv_sem=r2.at[k],
                device_id=peer,
                device_id_type=MESH,
            )
        )
        second[-1].start()
    for copy in second:
        copy.wait_recv()
    total = depth[0]
    for k in range(1, nz):
        total = total + depth[k]
    o_ref[...] = total
    for copy in first + second:
        copy.wait_send()


def all_sum(x, nd, nz, ident):
    return pl.pallas_call(
        functools.partial(sum_kernel, nd, nz),
        out_shape=jax.ShapeDtypeStruct(x.shape, x.dtype),
        in_specs=[pl.BlockSpec(memory_space=VMEM)],
        out_specs=pl.BlockSpec(memory_space=VMEM),
        scratch_shapes=[
            VMEM((nd,) + x.shape, x.dtype),
            VMEM((nz,) + x.shape, x.dtype),
            pltpu.SemaphoreType.DMA((nd,)),
            pltpu.SemaphoreType.DMA((nd,)),
            pltpu.SemaphoreType.DMA((nz,)),
            pltpu.SemaphoreType.DMA((nz,)),
        ],
        compiler_params=pltpu.CompilerParams(collective_id=ident, has_side_effects=True),
        name="all_sum",
    )(x)


def by_column(width):
    return (width // 2) % LANES == 0


def pad_rows(rows, width, nd):
    unit = 16 * (nd // 2 if by_column(width) else nd)
    return -(-rows // unit) * unit


def core_block(rows, width, core):
    if by_column(width):
        return 0, rows, pl.multiple_of(core * (width // 2), LANES), width // 2
    return pl.multiple_of(core * (rows // 2), 16), rows // 2, 0, width


def part(rows, width, nd, core, place):
    row, count, col, cols = core_block(rows, width, core)
    unit = count // (nd // 2)
    return pl.multiple_of(row + place * unit, 16), unit, col, cols


def gather_kernel(nd, nz, shapes, side_count, *refs):
    n = len(shapes)
    ins, sides = refs[:n], refs[n : n + side_count]
    outs = refs[n + side_count : 2 * n + side_count]
    side_outs = refs[2 * n + side_count : 2 * (n + side_count)]
    send, recv, local = refs[2 * (n + side_count) :]
    d = lax.axis_index("dp")
    z = lax.axis_index("chan")
    core = lax.rem(d, 2)
    place = d // 2
    nxy = nd // 2
    along = [(d, lax.rem(z + k, nz)) for k in range(1, nz)]
    others = [lax.rem(place + k, nxy) for k in range(1, nxy)]
    twin = 1 - core
    greet(along + [(2 * o + core, z) for o in others] + [(2 * place + twin, z)])
    count = [0]

    def remote(src, dst, peer):
        k = count[0]
        count[0] += 1
        copy = pltpu.make_async_remote_copy(
            src_ref=src,
            dst_ref=dst,
            send_sem=send.at[k],
            recv_sem=recv.at[k],
            device_id=peer,
            device_id_type=MESH,
        )
        copy.start()
        return copy

    waits = []
    stage = []
    for q, (rows, width) in enumerate(shapes):
        row, unit, col, cols = part(rows, width, nd, core, place)
        mine = pl.ds(pl.multiple_of(z * width + col, LANES), cols)
        stage.append(
            [
                remote(ins[q].at[pl.ds(row, unit), pl.ds(col, cols)], outs[q].at[pl.ds(row, unit), mine], peer)
                for peer in along
            ]
        )
    side = []
    for q in range(side_count):
        side += [remote(sides[q], side_outs[q].at[z], peer) for peer in along]
    own = []
    for q, (rows, width) in enumerate(shapes):
        own.append(
            pltpu.make_async_copy(
                ins[q], outs[q].at[:, pl.ds(pl.multiple_of(z * width, LANES), width)], local.at[q]
            )
        )
        own[-1].start()
    for q in range(side_count):
        own.append(pltpu.make_async_copy(sides[q], side_outs[q].at[z], local.at[n + q]))
        own[-1].start()
    later = []
    for q, (rows, width) in enumerate(shapes):
        row, unit, col, cols = part(rows, width, nd, core, place)
        for copy in stage[q]:
            copy.wait_recv()
        waits += stage[q]
        group = []
        for k in range(1, nz):
            zz = lax.rem(z + k, nz)
            where = pl.ds(pl.multiple_of(zz * width + col, LANES), cols)
            block = outs[q].at[pl.ds(row, unit), where]
            group += [remote(block, block, (2 * o + core, z)) for o in others]
        later.append(group)
    last = []
    for q, (rows, width) in enumerate(shapes):
        row, unit, col, cols = core_block(rows, width, core)
        for copy in later[q]:
            copy.wait_recv()
        waits += later[q]
        for k in range(1, nz):
            zz = lax.rem(z + k, nz)
            where = pl.ds(pl.multiple_of(zz * width + col, LANES), cols)
            block = outs[q].at[pl.ds(row, unit), where]
            last.append(remote(block, block, (2 * place + twin, z)))
    for copy in last + side:
        copy.wait_recv()
    for copy in waits + last + side:
        copy.wait_send()
    for copy in own:
        copy.wait()


def gather(arrays, sides, nd, nz, ident):
    shapes = tuple(a.shape for a in arrays)
    nxy = nd // 2
    copies = len(arrays) * ((nz - 1) * (1 + (nxy - 1) + 1)) + len(sides) * (nz - 1)
    total = len(arrays) + len(sides)
    return pl.pallas_call(
        functools.partial(gather_kernel, nd, nz, shapes, len(sides)),
        out_shape=[jax.ShapeDtypeStruct((a.shape[0], nz * a.shape[1]), a.dtype) for a in arrays]
        + [jax.ShapeDtypeStruct((nz,) + a.shape, a.dtype) for a in sides],
        in_specs=[pl.BlockSpec(memory_space=pltpu.HBM)] * total,
        out_specs=[pl.BlockSpec(memory_space=pltpu.HBM)] * total,
        scratch_shapes=[
            pltpu.SemaphoreType.DMA((copies,)),
            pltpu.SemaphoreType.DMA((copies,)),
            pltpu.SemaphoreType.DMA((total,)),
        ],
        compiler_params=pltpu.CompilerParams(collective_id=ident, has_side_effects=True),
        name="weight_gather",
    )(*arrays, *sides)


def reduce_kernel(nd, nz, rows, width, g_ref, o_ref, twin_buf, half, plane_buf, sums, depth_buf, piece, send, recv):
    d = lax.axis_index("dp")
    z = lax.axis_index("chan")
    core = lax.rem(d, 2)
    place = d // 2
    nxy = nd // 2
    along = [(d, lax.rem(z + k, nz)) for k in range(1, nz)]
    others = [lax.rem(place + k, nxy) for k in range(1, nxy)]
    twin = (2 * place + 1 - core, z)
    greet(along + [(2 * o + core, z) for o in others] + [twin])
    count = [0]

    def remote(src, dst, peer):
        k = count[0]
        count[0] += 1
        copy = pltpu.make_async_remote_copy(
            src_ref=src,
            dst_ref=dst,
            send_sem=send.at[k],
            recv_sem=recv.at[k],
            device_id=peer,
            device_id_type=MESH,
        )
        copy.start()
        return copy

    row, unit, col, cols = core_block(rows, width, 1 - core)
    first = [
        remote(
            g_ref.at[pl.ds(row, unit), pl.ds(pl.multiple_of(k * width + col, LANES), cols)],
            twin_buf.at[k],
            twin,
        )
        for k in range(nz)
    ]
    row, unit, col, cols = core_block(rows, width, core)
    for k in range(nz):
        first[k].wait_recv()

        @pl.loop(0, unit // 16)
        def _(i):
            at = pl.ds(pl.multiple_of(i * 16, 16), 16)
            mine = g_ref[
                pl.ds(pl.multiple_of(row + i * 16, 16), 16),
                pl.ds(pl.multiple_of(k * width + col, LANES), cols),
            ]
            half[k, at, :] = (mine.astype(f32) + twin_buf[k, at, :].astype(f32)).astype(bf16)

    size = unit // nxy
    second = [
        remote(
            half.at[:, pl.ds(pl.multiple_of(o * size, 16), size), :],
            plane_buf.at[k],
            (2 * o + core, z),
        )
        for k, o in enumerate(others)
    ]
    for copy in second:
        copy.wait_recv()
    for k in range(nz):

        @pl.loop(0, size // 16)
        def _(i):
            at = pl.ds(pl.multiple_of(i * 16, 16), 16)
            total = half[k, pl.ds(pl.multiple_of(place * size + i * 16, 16), 16), :].astype(f32)
            for q in range(nxy - 1):
                total = total + plane_buf[q, k, at, :].astype(f32)
            sums[k, at, :] = total.astype(bf16)

    third = [remote(sums.at[peer[1]], depth_buf.at[k], peer) for k, peer in enumerate(along)]
    for copy in third:
        copy.wait_recv()

    @pl.loop(0, size // 16)
    def _(i):
        at = pl.ds(pl.multiple_of(i * 16, 16), 16)
        total = sums[z, at, :].astype(f32)
        for q in range(nz - 1):
            total = total + depth_buf[q, at, :].astype(f32)
        piece[at, :] = total.astype(bf16)
        o_ref[
            pl.ds(pl.multiple_of(row + place * size + i * 16, 16), 16), pl.ds(col, cols)
        ] = total.astype(bf16)

    block = o_ref.at[pl.ds(pl.multiple_of(row + place * size, 16), size), pl.ds(col, cols)]
    fourth = [remote(piece, block, (2 * o + core, z)) for o in others]
    for copy in fourth:
        copy.wait_recv()
    block = o_ref.at[pl.ds(row, unit), pl.ds(col, cols)]
    fifth = remote(block, block, twin)
    fifth.wait_recv()
    for copy in first + second + third + fourth + [fifth]:
        copy.wait_send()


def reduce_grad(g, nd, nz, ident):
    rows, width = g.shape[0], g.shape[1] // nz
    nxy = nd // 2
    unit, cols = (rows, width // 2) if by_column(width) else (rows // 2, width)
    size = unit // nxy
    copies = nz + (nxy - 1) + (nz - 1) + (nxy - 1) + 1
    return pl.pallas_call(
        functools.partial(reduce_kernel, nd, nz, rows, width),
        out_shape=jax.ShapeDtypeStruct((rows, width), bf16),
        in_specs=[pl.BlockSpec(memory_space=VMEM)],
        out_specs=pl.BlockSpec(memory_space=VMEM),
        scratch_shapes=[
            VMEM((nz, unit, cols), bf16),
            VMEM((nz, unit, cols), bf16),
            VMEM((nxy - 1, nz, size, cols), bf16),
            VMEM((nz, size, cols), bf16),
            VMEM((nz - 1, size, cols), bf16),
            VMEM((size, cols), bf16),
            pltpu.SemaphoreType.DMA((copies,)),
            pltpu.SemaphoreType.DMA((copies,)),
        ],
        compiler_params=pltpu.CompilerParams(
            collective_id=ident, has_side_effects=True, vmem_limit_bytes=VLIMIT
        ),
        name="grad_reduce",
    )(g)


def build_mix(gates, nb):
    deep = LANES * EXPERTS
    row = lax.broadcasted_iota(jnp.int32, (deep, EXPERTS), 0)
    col = lax.broadcasted_iota(jnp.int32, (deep, EXPERTS), 1)
    pick = jnp.where((row & (EXPERTS - 1)) == col, 1.0, 0.0).astype(f32)
    row = lax.broadcasted_iota(jnp.int32, (deep, LANES), 0)
    col = lax.broadcasted_iota(jnp.int32, (deep, LANES), 1)
    same = (row >> 3) == col
    out = []
    for b in range(nb):
        spread = jnp.broadcast_to(gates[b : b + 1, :], (LANES, EXPERTS))
        out.append(jnp.where(same, dot(pick, spread, NT, highest), 0.0).astype(bf16))
    return out


def gate_sums(rows):
    deep = LANES * EXPERTS
    row = lax.broadcasted_iota(jnp.int32, (deep, EXPERTS), 0)
    col = lax.broadcasted_iota(jnp.int32, (deep, EXPERTS), 1)
    pick = jnp.where((row & (EXPERTS - 1)) == col, 1.0, 0.0).astype(f32)
    return dot(rows, pick, NN, highest)


def gate_rows(grad, kernel_block):
    both = dot(grad, kernel_block, TN)
    row = lax.broadcasted_iota(jnp.int32, both.shape, 0)
    col = lax.broadcasted_iota(jnp.int32, both.shape, 1)
    return rsum(jnp.where(row == (col >> 3), both, 0.0))


def norm_rows(stats, chunk, chunks, total):
    mean = stats[pl.ds(chunk, 1), :] / total
    var = stats[pl.ds(chunks + chunk, 1), :] / total - mean * mean
    return mean, lax.rsqrt(var + eps_norm)


def image(b):
    return pl.ds(pl.multiple_of(b * PIXELS, PIXELS), PIXELS)


def expand_kernel(nb, chunks, kern_ref, images, mask, mask_rows, counts, route, pre, taps, stats, mix, gates, pooled):
    j = pl.program_id(0)

    @pl.when(j == 0)
    def _():
        stats[...] = jnp.zeros_like(stats)
        stats[2 * chunks : 2 * chunks + 1, :] = rsum(counts[...])
        stats[2 * chunks + 1 : 2 * chunks + 2, :] = rsum(jnp.where(counts[...] > 0.0, 1.0, 0.0))
        pool = dot(mask_rows[...], images[...]) / jnp.maximum(counts[:, 0:1], 1.0)
        pooled[...] = pool
        gate = sig(dot(pool, route[...], NN, highest))
        gates[...] = gate
        for b, block in enumerate(build_mix(gate, nb)):
            mix[:, b * LANES : (b + 1) * LANES] = block

    mixed = dot(kern_ref[...], mix[...])
    one = jnp.zeros((1, LANES), f32)
    two = jnp.zeros((1, LANES), f32)
    for b in range(nb):
        at = slice(b * PIXELS, (b + 1) * PIXELS)
        lane = slice(b * LANES, (b + 1) * LANES)
        taps[b] = mixed[WIDTH_IN : WIDTH_IN + 32, lane]
        value = dot(images[at, :], mixed[:WIDTH_IN, lane].astype(bf16))
        pre[at, :] = value
        masked = mask[at, :] * value
        one = one + rsum(masked)
        two = two + rsum(masked * value)
    stats[pl.ds(j, 1), :] = one
    stats[pl.ds(chunks + j, 1), :] = two


def whole(shape):
    return pl.BlockSpec(shape, lambda *_: (0,) * len(shape))


def expand(kern, images, mask, mask_rows, counts, route, nb, width):
    chunks = width // LANES
    rows = nb * PIXELS
    deep = LANES * EXPERTS
    return pl.pallas_call(
        functools.partial(expand_kernel, nb, chunks),
        grid=(chunks,),
        out_shape=[
            jax.ShapeDtypeStruct((rows, width), f32),
            jax.ShapeDtypeStruct((nb, 32, width), f32),
            jax.ShapeDtypeStruct((24, LANES), f32),
            jax.ShapeDtypeStruct((deep, nb * LANES), bf16),
            jax.ShapeDtypeStruct((8, EXPERTS), f32),
            jax.ShapeDtypeStruct((8, WIDTH_IN), f32),
        ],
        in_specs=[
            pl.BlockSpec((kern.shape[0], deep), lambda j: (0, j)),
            whole(images.shape),
            whole(mask.shape),
            whole(mask_rows.shape),
            whole(counts.shape),
            whole(route.shape),
        ],
        out_specs=[
            pl.BlockSpec((rows, LANES), lambda j: (0, j)),
            pl.BlockSpec((nb, 32, LANES), lambda j: (0, 0, j)),
            whole((24, LANES)),
            whole((deep, nb * LANES)),
            whole((8, EXPERTS)),
            whole((8, WIDTH_IN)),
        ],
        compiler_params=pltpu.CompilerParams(vmem_limit_bytes=VLIMIT),
        name="expand",
    )(kern, images, mask, mask_rows, counts, route)


def shifted(value, step):
    if step == 0:
        return value
    col = lax.broadcasted_iota(jnp.int32, value.shape, 0) & (MAP_SIDE - 1)
    moved = pltpu.roll(value, (-step) % PIXELS, 0)
    keep = (col + step >= 0) & (col + step < MAP_SIDE)
    return jnp.where(keep, moved, 0.0)


def depth_kernel(nb, chunks, pre, taps, mask, side, stats, kern, mix, out, mixed_out, sums, buf, held):
    j = pl.program_id(0)

    @pl.when(j == 0)
    def _():
        sums[...] = jnp.zeros_like(sums)

    mixed = dot(kern[...], mix[...])
    for b in range(nb):
        mixed_out[b] = mixed[:, b * LANES : (b + 1) * LANES].astype(bf16)
    mean, rstd = norm_rows(stats, j, chunks, stats[2 * chunks : 2 * chunks + 1, :])
    scale = rstd * side[2 * SQUEEZE : 2 * SQUEEZE + 1, :]
    bias = side[2 * SQUEEZE + 1 : 2 * SQUEEZE + 2, :]
    held[...] = jnp.zeros_like(held)

    @pl.loop(0, nb)
    def _(b):
        at = image(b)
        normed = (pre[at, :] - mean) * scale + bias
        act = normed * sig(normed) * mask[at, :]
        for s in range(KERNEL):
            buf[s] = shifted(act, s - KERNEL // 2)
        taps_now = [jnp.broadcast_to(taps[b, t : t + 1, :], (MAP_SIDE, LANES)) for t in range(TAPS)]
        acc = [None] * MAP_SIDE
        for y in range(MAP_SIDE):
            for s in range(KERNEL):
                x = buf[s, y * MAP_SIDE : (y + 1) * MAP_SIDE, :]
                for r in range(KERNEL):
                    i = y - r + KERNEL // 2
                    if 0 <= i < MAP_SIDE:
                        term = taps_now[r * KERNEL + s] * x
                        acc[i] = term if acc[i] is None else acc[i] + term
            done = [y - 2] if y < MAP_SIDE - 1 else [y - 2, y - 1, y]
            for i in done:
                if i >= 0:
                    out[pl.ds(pl.multiple_of(b * PIXELS + i * MAP_SIDE, MAP_SIDE), MAP_SIDE), :] = acc[i]
        value = out[at, :]
        masked = mask[at, :] * value
        held[0:1, :] += rsum(masked)
        held[1:2, :] += rsum(masked * value)

    sums[pl.ds(j, 1), :] = held[0:1, :]
    sums[pl.ds(chunks + j, 1), :] = held[1:2, :]


def depthwise(pre, taps, mask, side, stats, kern, mix, nb):
    rows, width = pre.shape
    chunks = width // LANES
    deep = LANES * EXPERTS
    wide = lambda j: (0, j)
    return pl.pallas_call(
        functools.partial(depth_kernel, nb, chunks),
        grid=(chunks,),
        out_shape=[
            jax.ShapeDtypeStruct((rows, width), f32),
            jax.ShapeDtypeStruct((nb, WIDTH_OUT, width), bf16),
            jax.ShapeDtypeStruct((24, LANES), f32),
        ],
        in_specs=[
            pl.BlockSpec((rows, LANES), wide),
            pl.BlockSpec((nb, 32, LANES), lambda j: (0, 0, j)),
            whole(mask.shape),
            pl.BlockSpec((side.shape[0], LANES), wide),
            whole(stats.shape),
            pl.BlockSpec((WIDTH_OUT, deep), wide),
            whole(mix.shape),
        ],
        out_specs=[
            pl.BlockSpec((rows, LANES), wide),
            pl.BlockSpec((nb, WIDTH_OUT, LANES), lambda j: (0, 0, j)),
            whole((24, LANES)),
        ],
        scratch_shapes=[VMEM((KERNEL, PIXELS, LANES), f32), VMEM((8, LANES), f32)],
        compiler_params=pltpu.CompilerParams(vmem_limit_bytes=VLIMIT),
        name="depthwise",
    )(pre, taps, mask, side, stats, kern, mix)


def store_wide(ref, row, value):
    width = value.shape[1]
    for k in range(-(-width // LANES)):
        lanes = min(LANES, width - k * LANES)
        ref[row + k : row + k + 1, :lanes] = value[:, k * LANES : k * LANES + lanes]


def load_wide(ref, row, width):
    parts = []
    for k in range(-(-width // LANES)):
        lanes = min(LANES, width - k * LANES)
        parts.append(ref[row + k : row + k + 1, :lanes])
    return jnp.concatenate(parts, axis=1)


OUT_CHUNKS = -(-WIDTH_OUT // LANES)


def project_kernel(nb, chunks, dpre, mask, side, stats, totals, counts, sq_bias, mixed, excited, proj, pooled, gate_out, squeezed, sums, act, exc):
    phase = pl.program_id(0)
    j = pl.program_id(1)
    total = totals[2 * chunks : 2 * chunks + 1, :]

    @pl.when((phase == 0) & (j == 0))
    def _():
        squeezed[...] = jnp.zeros_like(squeezed)
        pooled[...] = jnp.zeros_like(pooled)
        sums[...] = jnp.zeros_like(sums)

    lane = pl.ds(pl.multiple_of(j * LANES, LANES), LANES)

    @pl.when(phase == 0)
    def _():
        mean, rstd = norm_rows(stats, j, chunks, total)
        scale = rstd * side[2 * SQUEEZE + 2 : 2 * SQUEEZE + 3, :]
        bias = side[2 * SQUEEZE + 3 : 2 * SQUEEZE + 4, :]
        for b in range(nb):
            at = slice(b * PIXELS, (b + 1) * PIXELS)
            normed = (dpre[at, :] - mean) * scale + bias
            value = normed * sig(normed) * mask[at, :]
            act[j, at, :] = value
            pooled[b : b + 1, lane] = rsum(value) / jnp.maximum(counts[b : b + 1, :], 1.0)
        squeezed[...] += dot(pooled[:, lane], side[0:SQUEEZE, :], NT, highest)

    @pl.when(phase == 1)
    def _():
        before = squeezed[...] + sq_bias[...]
        gate = sig(
            dot(before * sig(before), side[SQUEEZE : 2 * SQUEEZE, :], NN, highest)
            + side[2 * SQUEEZE + 4 : 2 * SQUEEZE + 5, :]
        )
        gate_out[:, lane] = gate
        for b in range(nb):
            at = slice(b * PIXELS, (b + 1) * PIXELS)
            value = (act[j, at, :] * gate[b : b + 1, :]).astype(bf16)
            excited[at, :] = value
            exc[at, lane] = value

    @pl.when((phase == 1) & (j == chunks - 1))
    def _():
        one = jnp.zeros((1, WIDTH_OUT), f32)
        two = jnp.zeros((1, WIDTH_OUT), f32)
        for b in range(nb):
            at = slice(b * PIXELS, (b + 1) * PIXELS)
            value = dot(exc[at, :], mixed[b], NT)
            proj[at, :] = value
            masked = mask[at, 0:1] * value
            one = one + rsum(masked)
            two = two + rsum(masked * value)
        store_wide(sums, 0, one)
        store_wide(sums, OUT_CHUNKS, two)


def project(dpre, mask, side, stats, totals, counts, sq_bias, mixed, nb):
    rows, width = dpre.shape
    chunks = width // LANES
    return pl.pallas_call(
        functools.partial(project_kernel, nb, chunks),
        grid=(2, chunks),
        out_shape=[
            jax.ShapeDtypeStruct((rows, width), bf16),
            jax.ShapeDtypeStruct((rows, WIDTH_OUT), f32),
            jax.ShapeDtypeStruct((8, width), f32),
            jax.ShapeDtypeStruct((8, width), f32),
            jax.ShapeDtypeStruct((8, SQUEEZE), f32),
            jax.ShapeDtypeStruct((8, LANES), f32),
        ],
        in_specs=[
            pl.BlockSpec((rows, LANES), lambda p, j: (0, jnp.where(p == 0, j, chunks - 1))),
            whole(mask.shape),
            pl.BlockSpec((side.shape[0], LANES), lambda p, j: (0, j)),
            whole(stats.shape),
            whole(totals.shape),
            whole(counts.shape),
            whole(sq_bias.shape),
            whole(mixed.shape),
        ],
        out_specs=[
            pl.BlockSpec((rows, LANES), lambda p, j: (0, jnp.where(p == 0, 0, j))),
            whole((rows, WIDTH_OUT)),
            whole((8, width)),
            whole((8, width)),
            whole((8, SQUEEZE)),
            whole((8, LANES)),
        ],
        scratch_shapes=[VMEM((chunks, rows, LANES), f32), VMEM((rows, width), bf16)],
        compiler_params=pltpu.CompilerParams(vmem_limit_bytes=VLIMIT),
        name="project",
    )(dpre, mask, side, stats, totals, counts, sq_bias, mixed)


def out_norm(sums, total):
    mean = load_wide(sums, 0, WIDTH_OUT) / total
    var = load_wide(sums, OUT_CHUNKS, WIDTH_OUT) / total - mean * mean
    return mean, lax.rsqrt(var + eps_norm)


def head_kernel(nb, chunks, kern, proj, mask, mask_rows, counts, gain, route, stats, totals, low, pre, mixed_out, sums, mix_out, gates, pooled):
    j = pl.program_id(0)

    @pl.when(j == 0)
    def _():
        sums[...] = jnp.zeros_like(sums)
        mean, rstd = out_norm(stats, totals[TOTAL_ROW : TOTAL_ROW + 1, 0:1])
        scale = rstd * gain[0:1, :]
        for b in range(nb):
            at = slice(b * PIXELS, (b + 1) * PIXELS)
            low[at, :] = (((proj[at, :] - mean) * scale + gain[1:2, :]) * mask[at, 0:1]).astype(bf16)
        pool = dot(mask_rows[...], low[...]) / jnp.maximum(counts[:, 0:1], 1.0)
        pooled[...] = pool
        gate = sig(dot(pool, route[...], NN, highest))
        gates[...] = gate
        for b, block in enumerate(build_mix(gate, nb)):
            mix_out[:, b * LANES : (b + 1) * LANES] = block

    mixed = dot(kern[...], mix_out[...])
    one = jnp.zeros((1, LANES), f32)
    two = jnp.zeros((1, LANES), f32)
    for b in range(nb):
        at = slice(b * PIXELS, (b + 1) * PIXELS)
        weight = mixed[:, b * LANES : (b + 1) * LANES].astype(bf16)
        mixed_out[b] = weight
        value = dot(low[at, :], weight)
        pre[at, :] = value
        masked = mask[at, :] * value
        one = one + rsum(masked)
        two = two + rsum(masked * value)
    sums[pl.ds(j, 1), :] = one
    sums[pl.ds(chunks + j, 1), :] = two


TOTAL_ROW = 18


def head(kern, proj, mask, mask_rows, counts, gain, route, stats, totals, nb):
    rows = proj.shape[0]
    width = kern.shape[1] // EXPERTS
    chunks = width // LANES
    deep = LANES * EXPERTS
    wide = lambda j: (0, j)
    return pl.pallas_call(
        functools.partial(head_kernel, nb, chunks),
        grid=(chunks,),
        out_shape=[
            jax.ShapeDtypeStruct((rows, WIDTH_OUT), bf16),
            jax.ShapeDtypeStruct((rows, width), f32),
            jax.ShapeDtypeStruct((nb, WIDTH_OUT, width), bf16),
            jax.ShapeDtypeStruct((24, LANES), f32),
            jax.ShapeDtypeStruct((deep, nb * LANES), bf16),
            jax.ShapeDtypeStruct((8, EXPERTS), f32),
            jax.ShapeDtypeStruct((8, WIDTH_OUT), f32),
        ],
        in_specs=[
            pl.BlockSpec((WIDTH_OUT, deep), wide),
            whole(proj.shape),
            whole(mask.shape),
            whole(mask_rows.shape),
            whole(counts.shape),
            whole(gain.shape),
            whole(route.shape),
            whole(stats.shape),
            whole(totals.shape),
        ],
        out_specs=[
            whole((rows, WIDTH_OUT)),
            pl.BlockSpec((rows, LANES), wide),
            pl.BlockSpec((nb, WIDTH_OUT, LANES), lambda j: (0, 0, j)),
            whole((24, LANES)),
            whole((deep, nb * LANES)),
            whole((8, EXPERTS)),
            whole((8, WIDTH_OUT)),
        ],
        compiler_params=pltpu.CompilerParams(vmem_limit_bytes=VLIMIT),
        name="head",
    )(kern, proj, mask, mask_rows, counts, gain, route, stats, totals)


def loss_kernel(nb, chunks, pre, mask, counts, labels, bias, cls, gain, stats, totals, features, grad_logits, grad_features, sums, logits):
    phase = pl.program_id(0)
    j = pl.program_id(1)
    lane = pl.ds(pl.multiple_of(j * LANES, LANES), LANES)

    @pl.when((phase == 0) & (j == 0))
    def _():
        sums[...] = jnp.zeros_like(sums)
        features[...] = jnp.zeros_like(features)
        logits[...] = jnp.zeros_like(logits)

    mean, rstd = norm_rows(stats, j, chunks, totals[TOTAL_ROW : TOTAL_ROW + 1, :])
    scale = rstd * gain[0:1, :]

    @pl.when(phase == 0)
    def _():
        for b in range(nb):
            at = slice(b * PIXELS, (b + 1) * PIXELS)
            normed = (pre[at, :] - mean) * scale + gain[1:2, :]
            features[b : b + 1, lane] = rsum(normed * sig(normed) * mask[at, :]) / jnp.maximum(
                counts[b : b + 1, :], 1.0
            )
        both = dot(split(features[:, lane]), cls[lane, :])
        logits[...] += both[:8] + both[8:]

    @pl.when((phase == 1) & (j == 0))
    def _():
        col = lax.broadcasted_iota(jnp.int32, (8, CLASS_PAD), 1)
        inside = col < CLASSES
        scores = jnp.where(inside, logits[...] + bias[...], -1e30)
        top = jnp.max(scores, axis=1, keepdims=True)
        spread = jnp.where(inside, jnp.exp(scores - top), 0.0)
        mass = jnp.sum(spread, axis=1, keepdims=True)
        hot = jnp.where(col == labels[:, 0:1], 1.0, 0.0)
        shifted_scores = jnp.where(inside, scores - top - jnp.log(mass), 0.0)
        per_image = -(
            0.9 * jnp.sum(shifted_scores * hot, axis=1, keepdims=True)
            + (0.1 / CLASSES) * jnp.sum(shifted_scores, axis=1, keepdims=True)
        )
        valid = jnp.where(counts[:, 0:1] > 0.0, 1.0, 0.0)
        sums[2 * chunks : 2 * chunks + 1, :] = jnp.broadcast_to(rsum(per_image * valid), (1, LANES))
        weight = valid / totals[TOTAL_ROW + 1 : TOTAL_ROW + 2, 0:1]
        grad_logits[...] = weight * jnp.where(inside, spread / mass - 0.9 * hot - 0.1 / CLASSES, 0.0)

    @pl.when(phase == 1)
    def _():
        both = dot(split(grad_logits[...]), cls[lane, :], NT)
        grads = (both[:8] + both[8:]) / jnp.maximum(counts[...], 1.0)
        grad_features[:, lane] = grads
        one = jnp.zeros((1, LANES), f32)
        two = jnp.zeros((1, LANES), f32)
        for b in range(nb):
            at = slice(b * PIXELS, (b + 1) * PIXELS)
            hat = (pre[at, :] - mean) * rstd
            grad = mask[at, :] * dsilu(hat * gain[0:1, :] + gain[1:2, :]) * grads[b : b + 1, :]
            one = one + rsum(grad)
            two = two + rsum(grad * hat)
        sums[pl.ds(j, 1), :] = one
        sums[pl.ds(chunks + j, 1), :] = two


def loss_stage(pre, mask, counts, labels, bias, cls, gain, stats, totals, nb):
    rows, width = pre.shape
    chunks = width // LANES
    return pl.pallas_call(
        functools.partial(loss_kernel, nb, chunks),
        grid=(2, chunks),
        out_shape=[
            jax.ShapeDtypeStruct((8, width), f32),
            jax.ShapeDtypeStruct((8, CLASS_PAD), f32),
            jax.ShapeDtypeStruct((8, width), f32),
            jax.ShapeDtypeStruct((24, LANES), f32),
        ],
        in_specs=[
            pl.BlockSpec((rows, LANES), lambda p, j: (0, j)),
            whole(mask.shape),
            whole(counts.shape),
            whole(labels.shape),
            whole(bias.shape),
            whole(cls.shape),
            pl.BlockSpec((2, LANES), lambda p, j: (0, j)),
            whole(stats.shape),
            whole(totals.shape),
        ],
        out_specs=[whole((8, width)), whole((8, CLASS_PAD)), whole((8, width)), whole((24, LANES))],
        scratch_shapes=[VMEM((8, CLASS_PAD), f32)],
        compiler_params=pltpu.CompilerParams(vmem_limit_bytes=VLIMIT),
        name="loss_stage",
    )(pre, mask, counts, labels, bias, cls, gain, stats, totals)


def head_back_kernel(nb, chunks, pre, grad_features, mask, counts, gain, stats, sums_in, totals, low, kern, mixed, mix, gates, route, proj, proj_stats, grad_kern, grad_out, sums, dz_out, held, grads, gate_acc):
    j = pl.program_id(0)
    lane = pl.ds(pl.multiple_of(j * LANES, LANES), LANES)
    total = totals[TOTAL_ROW : TOTAL_ROW + 1, :]

    @pl.when(j == 0)
    def _():
        gate_acc[...] = jnp.zeros_like(gate_acc)
        sums[...] = jnp.zeros_like(sums)

    mean, rstd = norm_rows(stats, j, chunks, total)
    scale = rstd * gain[0:1, :]
    one = sums_in[pl.ds(j, 1), :] / total
    two = sums_in[pl.ds(chunks + j, 1), :] / total
    for b in range(nb):
        at = slice(b * PIXELS, (b + 1) * PIXELS)
        hat = (pre[at, :] - mean) * rstd
        grad = dsilu(hat * gain[0:1, :] + gain[1:2, :]) * grad_features[b : b + 1, :]
        value = (scale * mask[at, :] * (grad - one - hat * two)).astype(bf16)
        held[at, lane] = value
        grad_mixed = dot(low[at, :], value, TN).astype(bf16)
        grads[:, b * LANES : (b + 1) * LANES] = grad_mixed
        gate_acc[b : b + 1, :] += gate_rows(grad_mixed, kern[...])
    grad_kern[...] = dot(grads[...], mix[...], NT).astype(bf16)

    @pl.when(j == chunks - 1)
    def _():
        dz = gate_sums(gate_acc[...]) * gates[...] * (1.0 - gates[...])
        dz_out[...] = dz
        pool_grad = dot(dz, route[...], NT, highest) / jnp.maximum(counts[:, 0:1], 1.0)
        mean, rstd = out_norm(proj_stats, total[:, 0:1])
        one = jnp.zeros((1, WIDTH_OUT), f32)
        two = jnp.zeros((1, WIDTH_OUT), f32)
        for b in range(nb):
            at = slice(b * PIXELS, (b + 1) * PIXELS)
            value = (dot(held[at, :], mixed[b], NT) + pool_grad[b : b + 1, :]) * mask[at, 0:1]
            grad_out[at, :] = value
            one = one + rsum(value)
            two = two + rsum(value * ((proj[at, :] - mean) * rstd))
        store_wide(sums, 0, one)
        store_wide(sums, OUT_CHUNKS, two)


def head_back(pre, grad_features, mask, counts, gain, stats, sums_in, totals, low, kern, mixed, mix, gates, route, proj, proj_stats, nb):
    rows, width = pre.shape
    chunks = width // LANES
    deep = LANES * EXPERTS
    wide = lambda j: (0, j)
    return pl.pallas_call(
        functools.partial(head_back_kernel, nb, chunks),
        grid=(chunks,),
        out_shape=[
            jax.ShapeDtypeStruct((kern.shape[0], width * EXPERTS), bf16),
            jax.ShapeDtypeStruct((rows, WIDTH_OUT), f32),
            jax.ShapeDtypeStruct((8, LANES), f32),
            jax.ShapeDtypeStruct((8, EXPERTS), f32),
        ],
        in_specs=[
            pl.BlockSpec((rows, LANES), wide),
            pl.BlockSpec((8, LANES), wide),
            whole(mask.shape),
            whole(counts.shape),
            pl.BlockSpec((2, LANES), wide),
            whole(stats.shape),
            whole(sums_in.shape),
            whole(totals.shape),
            whole(low.shape),
            pl.BlockSpec((WIDTH_OUT, deep), wide),
            whole(mixed.shape),
            whole(mix.shape),
            whole(gates.shape),
            whole(route.shape),
            whole(proj.shape),
            whole(proj_stats.shape),
        ],
        out_specs=[
            pl.BlockSpec((WIDTH_OUT, deep), wide),
            whole((rows, WIDTH_OUT)),
            whole((8, LANES)),
            whole((8, EXPERTS)),
        ],
        scratch_shapes=[
            VMEM((rows, width), bf16),
            VMEM((WIDTH_OUT, nb * LANES), bf16),
            VMEM((8, deep), f32),
        ],
        compiler_params=pltpu.CompilerParams(vmem_limit_bytes=VLIMIT),
        name="head_back",
    )(pre, grad_features, mask, counts, gain, stats, sums_in, totals, low, kern, mixed, mix, gates, route, proj, proj_stats)


def project_back_kernel(nb, chunks, grad_in, proj, proj_stats, proj_sums, gain, mask, counts, totals, stats, side, dpre, excited, mixed, kern, mix, gate, pooled, squeezed, sq_bias, grad_kern, grad_norm, sums, grad_squeeze, gate_grad, dz_gate, low, held, grads, gate_acc):
    phase = pl.program_id(0)
    j = pl.program_id(1)
    lane = pl.ds(pl.multiple_of(j * LANES, LANES), LANES)
    total = totals[TOTAL_ROW : TOTAL_ROW + 1, :]

    @pl.when((phase == 0) & (j == 0))
    def _():
        gate_acc[...] = jnp.zeros_like(gate_acc)
        sums[...] = jnp.zeros_like(sums)
        grad_squeeze[...] = jnp.zeros_like(grad_squeeze)
        dz_gate[...] = jnp.zeros_like(dz_gate)
        mean, rstd = out_norm(proj_stats, total[:, 0:1])
        scale = rstd * gain[0:1, :]
        one = load_wide(proj_sums, 0, WIDTH_OUT) / total[:, 0:1]
        two = load_wide(proj_sums, OUT_CHUNKS, WIDTH_OUT) / total[:, 0:1]
        for b in range(nb):
            at = slice(b * PIXELS, (b + 1) * PIXELS)
            hat = (proj[at, :] - mean) * rstd
            low[at, :] = (scale * (grad_in[at, :] - mask[at, 0:1] * (one + hat * two))).astype(bf16)

    mean, rstd = norm_rows(stats, j, chunks, total)
    gain_now = side[2 * SQUEEZE + 2 : 2 * SQUEEZE + 3, :]
    bias_now = side[2 * SQUEEZE + 3 : 2 * SQUEEZE + 4, :]

    @pl.when(phase == 0)
    def _():
        for b in range(nb):
            at = slice(b * PIXELS, (b + 1) * PIXELS)
            grad_mixed = dot(low[at, :], excited[at, :], TN).astype(bf16)
            grads[:, b * LANES : (b + 1) * LANES] = grad_mixed
            gate_acc[b : b + 1, :] += gate_rows(grad_mixed, kern[...])
            value = dot(low[at, :], mixed[b])
            held[j, at, :] = value
            normed = (dpre[at, :] - mean) * (rstd * gain_now) + bias_now
            act = normed * sig(normed) * mask[at, :]
            now = gate[b : b + 1, :]
            dz_gate[b : b + 1, lane] = rsum(value * act) * now * (1.0 - now)
        grad_kern[...] = dot(grads[...], mix[...], NT).astype(bf16)
        grad_squeeze[...] += dot(dz_gate[:, lane], side[SQUEEZE : 2 * SQUEEZE, :], NT, highest)

    @pl.when((phase == 1) & (j == 0))
    def _():
        grad_squeeze[...] = grad_squeeze[...] * dsilu(squeezed[...] + sq_bias[...])
        gate_grad[...] = gate_sums(gate_acc[...])

    @pl.when(phase == 1)
    def _():
        pool_grad = dot(grad_squeeze[...], side[0:SQUEEZE, :], NN, highest) / jnp.maximum(counts[...], 1.0)
        one = jnp.zeros((1, LANES), f32)
        two = jnp.zeros((1, LANES), f32)
        for b in range(nb):
            at = slice(b * PIXELS, (b + 1) * PIXELS)
            hat = (dpre[at, :] - mean) * rstd
            grad = held[j, at, :] * gate[b : b + 1, :] + pool_grad[b : b + 1, :]
            value = mask[at, :] * grad * dsilu(hat * gain_now + bias_now)
            grad_norm[at, :] = value
            one = one + rsum(value)
            two = two + rsum(value * hat)
        sums[pl.ds(j, 1), :] = one
        sums[pl.ds(chunks + j, 1), :] = two


def project_back(grad_in, proj, proj_stats, proj_sums, gain, mask, counts, totals, stats, side, dpre, excited, mixed, kern, mix, gate, pooled, squeezed, sq_bias, nb):
    rows, width = dpre.shape
    chunks = width // LANES
    deep = LANES * EXPERTS
    wide = lambda p, j: (0, j)
    early = lambda p, j: (0, jnp.where(p == 0, j, chunks - 1))
    late = lambda p, j: (0, jnp.where(p == 0, 0, j))
    return pl.pallas_call(
        functools.partial(project_back_kernel, nb, chunks),
        grid=(2, chunks),
        out_shape=[
            jax.ShapeDtypeStruct((kern.shape[0], width * EXPERTS), bf16),
            jax.ShapeDtypeStruct((rows, width), f32),
            jax.ShapeDtypeStruct((24, LANES), f32),
            jax.ShapeDtypeStruct((8, SQUEEZE), f32),
            jax.ShapeDtypeStruct((8, EXPERTS), f32),
            jax.ShapeDtypeStruct((8, width), f32),
        ],
        in_specs=[
            whole(grad_in.shape),
            whole(proj.shape),
            whole(proj_stats.shape),
            whole(proj_sums.shape),
            whole(gain.shape),
            whole(mask.shape),
            whole(counts.shape),
            whole(totals.shape),
            whole(stats.shape),
            pl.BlockSpec((side.shape[0], LANES), wide),
            pl.BlockSpec((rows, LANES), wide),
            pl.BlockSpec((rows, LANES), early),
            pl.BlockSpec((nb, WIDTH_OUT, LANES), lambda p, j: (0, 0, jnp.where(p == 0, j, chunks - 1))),
            pl.BlockSpec((WIDTH_OUT, deep), early),
            whole(mix.shape),
            pl.BlockSpec((8, LANES), wide),
            pl.BlockSpec((8, LANES), wide),
            whole(squeezed.shape),
            whole(sq_bias.shape),
        ],
        out_specs=[
            pl.BlockSpec((WIDTH_OUT, deep), early),
            pl.BlockSpec((rows, LANES), late),
            whole((24, LANES)),
            whole((8, SQUEEZE)),
            whole((8, EXPERTS)),
            whole((8, width)),
        ],
        scratch_shapes=[
            VMEM((rows, WIDTH_OUT), bf16),
            VMEM((chunks, rows, LANES), f32),
            VMEM((WIDTH_OUT, nb * LANES), bf16),
            VMEM((8, deep), f32),
        ],
        compiler_params=pltpu.CompilerParams(vmem_limit_bytes=VLIMIT),
        name="project_back",
    )(grad_in, proj, proj_stats, proj_sums, gain, mask, counts, totals, stats, side, dpre, excited, mixed, kern, mix, gate, pooled, squeezed, sq_bias)


def depth_back_kernel(nb, chunks, grad_in, dpre, pre, taps, mask, side, stats_one, stats_two, sums_two, totals, grad_out, tap_grads, sums, buf, acts, held):
    j = pl.program_id(0)
    total = totals[TOTAL_ROW : TOTAL_ROW + 1, :]

    @pl.when(j == 0)
    def _():
        sums[...] = jnp.zeros_like(sums)

    mean_two, rstd_two = norm_rows(stats_two, j, chunks, total)
    scale_two = rstd_two * side[2 * SQUEEZE + 2 : 2 * SQUEEZE + 3, :]
    one_two = sums_two[pl.ds(j, 1), :] / total
    two_two = sums_two[pl.ds(chunks + j, 1), :] / total
    mean, rstd = norm_rows(stats_one, j, chunks, total)
    gain = side[2 * SQUEEZE : 2 * SQUEEZE + 1, :]
    bias = side[2 * SQUEEZE + 1 : 2 * SQUEEZE + 2, :]
    held[...] = jnp.zeros_like(held)
    reach = KERNEL // 2

    @pl.loop(0, nb)
    def _(b):
        at = image(b)
        hat = (dpre[at, :] - mean_two) * rstd_two
        grad = scale_two * (grad_in[at, :] - mask[at, :] * (one_two + hat * two_two))
        for s in range(KERNEL):
            buf[s] = shifted(grad, reach - s)
        hat = (pre[at, :] - mean) * rstd
        normed = hat * gain + bias
        acts[...] = normed * sig(normed) * mask[at, :]
        taps_now = [jnp.broadcast_to(taps[b, t : t + 1, :], (MAP_SIDE, LANES)) for t in range(TAPS)]
        acc = [None] * MAP_SIDE
        for q in range(MAP_SIDE):
            for s in range(KERNEL):
                x = buf[s, q * MAP_SIDE : (q + 1) * MAP_SIDE, :]
                for r in range(KERNEL):
                    y = q + r - reach
                    if 0 <= y < MAP_SIDE:
                        term = taps_now[r * KERNEL + s] * x
                        acc[y] = term if acc[y] is None else acc[y] + term
            done = [q - 2] if q < MAP_SIDE - 1 else [q - 2, q - 1, q]
            for i in done:
                if i >= 0:
                    grad_out[pl.ds(pl.multiple_of(b * PIXELS + i * MAP_SIDE, MAP_SIDE), MAP_SIDE), :] = acc[i]
        tap_acc = [None] * TAPS
        for q in range(MAP_SIDE):
            for s in range(KERNEL):
                x = buf[s, q * MAP_SIDE : (q + 1) * MAP_SIDE, :]
                for r in range(KERNEL):
                    y = q + r - reach
                    if 0 <= y < MAP_SIDE:
                        both = acts[y * MAP_SIDE : (y + 1) * MAP_SIDE, :] * x
                        term = both[:8] + both[8:]
                        t = r * KERNEL + s
                        tap_acc[t] = term if tap_acc[t] is None else tap_acc[t] + term
        tap_grads[b] = jnp.zeros((32, LANES), f32)
        for t in range(TAPS):
            tap_grads[b, t : t + 1, :] = rsum(tap_acc[t])
        hat = (pre[at, :] - mean) * rstd
        value = grad_out[at, :] * mask[at, :] * dsilu(hat * gain + bias)
        grad_out[at, :] = value
        held[0:1, :] += rsum(value)
        held[1:2, :] += rsum(value * hat)

    sums[pl.ds(j, 1), :] = held[0:1, :]
    sums[pl.ds(chunks + j, 1), :] = held[1:2, :]


def depth_back(grad_in, dpre, pre, taps, mask, side, stats_one, stats_two, sums_two, totals, nb):
    rows, width = pre.shape
    chunks = width // LANES
    wide = lambda j: (0, j)
    tall = pl.BlockSpec((rows, LANES), wide)
    return pl.pallas_call(
        functools.partial(depth_back_kernel, nb, chunks),
        grid=(chunks,),
        out_shape=[
            jax.ShapeDtypeStruct((rows, width), f32),
            jax.ShapeDtypeStruct((nb, 32, width), f32),
            jax.ShapeDtypeStruct((24, LANES), f32),
        ],
        in_specs=[
            tall,
            tall,
            tall,
            pl.BlockSpec((nb, 32, LANES), lambda j: (0, 0, j)),
            whole(mask.shape),
            pl.BlockSpec((side.shape[0], LANES), wide),
            whole(stats_one.shape),
            whole(stats_two.shape),
            whole(sums_two.shape),
            whole(totals.shape),
        ],
        out_specs=[tall, pl.BlockSpec((nb, 32, LANES), lambda j: (0, 0, j)), whole((24, LANES))],
        scratch_shapes=[
            VMEM((KERNEL, PIXELS, LANES), f32),
            VMEM((PIXELS, LANES), f32),
            VMEM((8, LANES), f32),
        ],
        compiler_params=pltpu.CompilerParams(vmem_limit_bytes=VLIMIT),
        name="depth_back",
    )(grad_in, dpre, pre, taps, mask, side, stats_one, stats_two, sums_two, totals)


def expand_back_kernel(nb, chunks, grad_in, pre, images, tap_grads, mask, side, stats, sums_in, totals, kern, mix, gates, gate_grad, grad_kern, dz_out, grads, gate_acc):
    j = pl.program_id(0)
    total = totals[TOTAL_ROW : TOTAL_ROW + 1, :]

    @pl.when(j == 0)
    def _():
        gate_acc[...] = jnp.zeros_like(gate_acc)
        grads[...] = jnp.zeros_like(grads)

    mean, rstd = norm_rows(stats, j, chunks, total)
    scale = rstd * side[2 * SQUEEZE : 2 * SQUEEZE + 1, :]
    one = sums_in[pl.ds(j, 1), :] / total
    two = sums_in[pl.ds(chunks + j, 1), :] / total
    for b in range(nb):
        at = slice(b * PIXELS, (b + 1) * PIXELS)
        lane = slice(b * LANES, (b + 1) * LANES)
        hat = (pre[at, :] - mean) * rstd
        value = (scale * (grad_in[at, :] - mask[at, :] * (one + hat * two))).astype(bf16)
        grads[0:WIDTH_IN, lane] = dot(images[at, :], value, TN).astype(bf16)
        grads[WIDTH_IN : WIDTH_IN + 32, lane] = tap_grads[b].astype(bf16)
        gate_acc[b : b + 1, :] += gate_rows(grads[:, lane], kern[...])
    grad_kern[...] = dot(grads[...], mix[...], NT).astype(bf16)

    @pl.when(j == chunks - 1)
    def _():
        dz_out[...] = (gate_sums(gate_acc[...]) + gate_grad[...]) * gates[...] * (1.0 - gates[...])


def expand_back(grad_in, pre, images, tap_grads, mask, side, stats, sums_in, totals, kern, mix, gates, gate_grad, nb):
    rows, width = pre.shape
    chunks = width // LANES
    deep = LANES * EXPERTS
    wide = lambda j: (0, j)
    tall = pl.BlockSpec((rows, LANES), wide)
    return pl.pallas_call(
        functools.partial(expand_back_kernel, nb, chunks),
        grid=(chunks,),
        out_shape=[
            jax.ShapeDtypeStruct(kern.shape, bf16),
            jax.ShapeDtypeStruct((8, EXPERTS), f32),
        ],
        in_specs=[
            tall,
            tall,
            whole(images.shape),
            pl.BlockSpec((nb, 32, LANES), lambda j: (0, 0, j)),
            whole(mask.shape),
            pl.BlockSpec((side.shape[0], LANES), wide),
            whole(stats.shape),
            whole(sums_in.shape),
            whole(totals.shape),
            pl.BlockSpec((kern.shape[0], deep), wide),
            whole(mix.shape),
            whole(gates.shape),
            whole(gate_grad.shape),
        ],
        out_specs=[pl.BlockSpec((kern.shape[0], deep), wide), whole((8, EXPERTS))],
        scratch_shapes=[VMEM((kern.shape[0], nb * LANES), bf16), VMEM((8, deep), f32)],
        compiler_params=pltpu.CompilerParams(vmem_limit_bytes=VLIMIT),
        name="expand_back",
    )(grad_in, pre, images, tap_grads, mask, side, stats, sums_in, totals, kern, mix, gates, gate_grad)


def update(weight, grad, moment, average, factor):
    scaled = grad * factor
    moment_new = 0.5 * moment + scaled
    weight_new = weight - 0.2 * (scaled + 0.5 * moment_new)
    average_new = 0.5 * average + 0.5 * weight_new
    return (weight_new, moment_new, average_new)


def grow(array, rows, cols=None):
    cols = array.shape[1] if cols is None else cols
    return jnp.pad(array, ((0, rows - array.shape[0]), (0, cols - array.shape[1])))


def square_sum(x):
    x = x.astype(f32)
    return jnp.sum(x * x)


def body(
    nd,
    nz,
    images,
    pixel_mask,
    counts,
    labels,
    block_w,
    chan_side,
    head_w,
    head_side,
    shared,
    block_mom,
    side_mom,
    head_mom,
    hside_mom,
    shared_mom,
    block_ema,
    side_ema,
    head_ema,
    hside_ema,
    shared_ema,
    chan_stats,
    head_stats,
    proj_stats,
):
    z = lax.axis_index("chan")
    nb = images.shape[0] // nz
    own = chan_side.shape[1]
    own_head = head_side.shape[0]
    width = own * nz
    head_width = own_head * nz
    end_route = WIDTH_IN * EXPERTS
    end_head = end_route + WIDTH_OUT * EXPERTS
    end_norm = end_head + 2 * WIDTH_OUT
    end_squeeze = end_norm + SQUEEZE
    route_in = shared[:end_route].reshape(WIDTH_IN, EXPERTS)
    route_head = shared[end_route:end_head].reshape(WIDTH_OUT, EXPERTS)
    gain_out = shared[end_head:end_norm].reshape(2, WIDTH_OUT)
    sq_bias = shared[None, end_norm:end_squeeze]
    class_bias = jnp.pad(shared[end_squeeze:], (0, CLASS_PAD - CLASSES))[None, :]

    def mine(x):
        return lax.dynamic_slice_in_dim(x, z * nb, nb, 0)

    image_rows = mine(images).reshape(nb * PIXELS, WIDTH_IN)
    mask_now = mine(pixel_mask).astype(f32)
    mask = jnp.broadcast_to(mask_now.reshape(-1, 1), (nb * PIXELS, LANES))
    mask_rows = jnp.pad(
        (jnp.eye(nb, dtype=f32)[:, :, None] * mask_now[None]).reshape(nb, nb * PIXELS).astype(bf16),
        ((0, 8 - nb), (0, 0)),
    )
    count_rows = jnp.broadcast_to(jnp.pad(mine(counts).astype(f32), (0, 8 - nb))[:, None], (8, LANES))
    label_rows = jnp.broadcast_to(jnp.pad(mine(labels), (0, 8 - nb))[:, None], (8, LANES))

    block_width = block_w.shape[1]
    first_rows = WIDTH_IN + TAPS
    rows_a = pad_rows(first_rows, block_width, nd)
    kern_a = grow(block_w[:first_rows].astype(bf16), rows_a)
    kern_b = grow(block_w[first_rows:].astype(bf16), pad_rows(WIDTH_OUT, block_width, nd))
    kern_h = grow(head_w.astype(bf16), pad_rows(WIDTH_OUT, head_w.shape[1], nd))
    cls = head_side[:, 2:].astype(bf16)
    cls_t = grow(cls, pad_rows(own_head, CLASS_PAD, nd), CLASS_PAD)
    head_gain = head_side[:, :2].T
    full_a, full_side = gather([kern_a], [chan_side], nd, nz, 1)
    full_b, full_h, full_c, full_gain = gather([kern_b, kern_h, cls_t], [head_gain], nd, nz, 2)
    side = full_side.transpose(1, 0, 2).reshape(chan_side.shape[0], width)
    gain_head = full_gain.transpose(1, 0, 2).reshape(2, head_width)
    cls_full = (
        full_c.reshape(full_c.shape[0], nz, CLASS_PAD)[:own_head].transpose(1, 0, 2).reshape(head_width, CLASS_PAD)
    )

    pre, taps, stats_one, mix, gates, pooled_in = expand(
        full_a, image_rows, mask, mask_rows, count_rows, route_in, nb, width
    )
    stats_one = all_sum(stats_one, nd, nz, 3)
    totals = stats_one
    dpre, mixed_proj, stats_two = depthwise(pre, taps, mask, side, stats_one, full_b, mix, nb)
    stats_two = all_sum(stats_two, nd, nz, 4)
    excited, proj, pooled, gate, squeezed, stats_three = project(
        dpre, mask, side, stats_two, totals, count_rows, sq_bias, mixed_proj, nb
    )
    stats_three = all_sum(stats_three, nd, nz, 5)
    low, head_pre, mixed_head, stats_four, mix_head, gates_head, head_pool = head(
        full_h, proj, mask, mask_rows, count_rows, gain_out, route_head, stats_three, totals, nb
    )
    stats_four = all_sum(stats_four, nd, nz, 6)
    features, grad_logits, grad_features, sums_four = loss_stage(
        head_pre, mask, count_rows, label_rows, class_bias, cls_full, gain_head, stats_four, totals, nb
    )
    sums_four = all_sum(sums_four, nd, nz, 7)
    grad_h, grad_proj, sums_three, dz_head = head_back(
        head_pre,
        grad_features,
        mask,
        count_rows,
        gain_head,
        stats_four,
        sums_four,
        totals,
        low,
        full_h,
        mixed_head,
        mix_head,
        gates_head,
        route_head,
        proj,
        stats_three,
        nb,
    )
    sums_three = all_sum(sums_three, nd, nz, 8)
    grad_b, grad_norm, sums_two, grad_squeeze, gate_grad, dz_gate = project_back(
        grad_proj,
        proj,
        stats_three,
        sums_three,
        gain_out,
        mask,
        count_rows,
        totals,
        stats_two,
        side,
        dpre,
        excited,
        mixed_proj,
        full_b,
        mix,
        gate,
        pooled,
        squeezed,
        sq_bias,
        nb,
    )
    before = squeezed + sq_bias
    rows = jnp.concatenate(
        [
            features,
            grad_logits,
            pooled,
            dz_gate,
            head_pool,
            pooled_in,
            grad_squeeze,
            before * sig(before),
            dz_head,
        ],
        axis=1,
    )[:nb]
    every = lax.all_gather(rows, ("dp", "chan"), tiled=True)
    sums_two = all_sum(sums_two, nd, nz, 9)
    grad_pre, tap_grads, sums_one = depth_back(
        grad_norm, dpre, pre, taps, mask, side, stats_one, stats_two, sums_two, totals, nb
    )
    sums_one = all_sum(sums_one, nd, nz, 10)
    grad_a, dz_in = expand_back(
        grad_pre,
        pre,
        image_rows,
        tap_grads,
        mask,
        side,
        stats_one,
        sums_one,
        totals,
        full_a,
        mix,
        gates,
        gate_grad,
        nb,
    )
    grad_h = reduce_grad(grad_h, nd, nz, 11)
    grad_b = reduce_grad(grad_b, nd, nz, 12)
    grad_a = reduce_grad(grad_a, nd, nz, 13)

    cuts = [0]
    for size in (head_width, CLASS_PAD, width, width, WIDTH_OUT, WIDTH_IN, SQUEEZE, SQUEEZE, EXPERTS):
        cuts.append(cuts[-1] + size)
    parts = [every[:, cuts[k] : cuts[k + 1]] for k in range(len(cuts) - 1)]
    features_all, logits_all, pooled_all, dz_gate_all, head_pool_all, pooled_in_all, grad_sq_all, sq_all, dz_head_all = parts

    def shard(x, size):
        return lax.dynamic_slice_in_dim(x, z * size, size, 1)

    grad_classifier = dot(shard(features_all, own_head), logits_all[:, :CLASSES], TN, highest)
    dz_own = shard(dz_gate_all, own)
    grad_reduce = dot(grad_sq_all, shard(pooled_all, own), TN, highest)
    grad_excite = dot(sq_all, dz_own, TN, highest)
    grad_route_head = dot(head_pool_all, dz_head_all, TN, highest)

    def channel_rows(stats, count):
        return stats[: 2 * count].reshape(2, count * LANES)

    chunks = width // LANES
    head_chunks = head_width // LANES
    sums_one = shard(channel_rows(sums_one, chunks), own)
    sums_two = shard(channel_rows(sums_two, chunks), own)
    loss_sum = sums_four[2 * head_chunks, 0]
    sums_four = shard(channel_rows(sums_four, head_chunks), own_head)
    grad_side = jnp.concatenate(
        [
            grad_reduce,
            grad_excite,
            sums_one[1:2],
            sums_one[0:1],
            sums_two[1:2],
            sums_two[0:1],
            jnp.sum(dz_own, axis=0, keepdims=True),
        ],
        axis=0,
    )
    grad_hside = jnp.concatenate([sums_four[1][:, None], sums_four[0][:, None], grad_classifier], axis=1)

    def out_rows(stats):
        return stats[: 2 * OUT_CHUNKS].reshape(2, OUT_CHUNKS * LANES)[:, :WIDTH_OUT]

    sums_three = out_rows(sums_three)

    grad_block = jnp.concatenate([grad_a[:first_rows], grad_b[:WIDTH_OUT]], axis=0)
    grad_head = grad_h[:WIDTH_OUT]
    weights = (block_w, chan_side, head_w, head_side)
    grads = (grad_block, grad_side, grad_head, grad_hside)
    squares = jnp.stack([square_sum(g) for g in grads] + [square_sum(w) for w in weights])
    me = lax.axis_index("dp") * nz + z
    images_all = nd * nz * nb
    slots = images_all * EXPERTS // LANES
    dz_flat = lax.dynamic_update_slice(
        jnp.zeros((images_all, EXPERTS), f32), dz_in[:nb], (me * nb, 0)
    ).reshape(slots, LANES)
    square_row = jnp.pad(squares / nd, (0, LANES - 8))[None]
    last = all_sum(grow(jnp.concatenate([dz_flat, square_row], axis=0), slots + 8), nd, nz, 14)
    dz_in_all = last[:slots].reshape(images_all, EXPERTS)
    squares = last[slots, :8]
    grad_route_in = dot(pooled_in_all, dz_in_all, TN, highest)
    grad_shared = jnp.concatenate(
        [
            grad_route_in.reshape(-1),
            grad_route_head.reshape(-1),
            sums_three[1],
            sums_three[0],
            jnp.sum(grad_sq_all, axis=0),
            jnp.sum(logits_all[:, :CLASSES], axis=0),
        ]
    )
    factors = [jnp.sqrt(squares[4 + k]) * lax.rsqrt(squares[k] + 1e-12) for k in range(4)]
    moments = (block_mom, side_mom, head_mom, hside_mom)
    averages = (block_ema, side_ema, head_ema, hside_ema)
    results = [
        update(weights[k], grads[k].astype(f32), moments[k], averages[k], factors[k]) for k in range(4)
    ]
    results.append(
        update(
            shared,
            grad_shared,
            shared_mom,
            shared_ema,
            jnp.sqrt(jnp.sum(shared * shared)) * lax.rsqrt(jnp.sum(grad_shared * grad_shared) + 1e-12),
        )
    )
    total = totals[2 * chunks, 0]
    loss = loss_sum / totals[2 * chunks + 1, 0]

    def moving(old, sums):
        mean = sums[0] / total
        var = sums[1] / total - mean * mean
        return 0.5 * old + 0.5 * jnp.stack([mean, var * (total / (total - 1.0))])

    new_chan = jnp.concatenate(
        [
            moving(chan_stats[0:2], shard(channel_rows(stats_one, chunks), own)),
            moving(chan_stats[2:4], shard(channel_rows(stats_two, chunks), own)),
        ]
    )
    new_head = moving(head_stats, shard(channel_rows(stats_four, head_chunks), own_head))
    new_proj = moving(proj_stats, shard(out_rows(stats_three), proj_stats.shape[1]))
    return (
        (loss,)
        + tuple(results[k][0] for k in range(5))
        + tuple(results[k][1] for k in range(5))
        + tuple(results[k][2] for k in range(5))
        + (new_chan, new_head, new_proj)
    )


def solution(mesh):
    nd, nz = mesh.shape["dp"], mesh.shape["chan"]
    cols = P(None, "chan")
    state = (cols, cols, cols, P("chan", None), P())
    return jax.shard_map(
        functools.partial(body, nd, nz),
        mesh=mesh,
        in_specs=(P("dp", None, None), P("dp", None), P("dp"), P("dp"))
        + state * 3
        + (cols, cols, cols),
        out_specs=(P(),) + state * 3 + (cols, cols, cols),
        check_vma=False,
    )
```

```python
import functools

import jax
import jax.numpy as jnp
from jax import lax
from jax.experimental import pallas as pl
from jax.experimental.pallas import tpu as pltpu
from jax.sharding import PartitionSpec as P

WIDTH_IN = 192
WIDTH_OUT = 320
SQUEEZE = 48
CLASSES = 1000
EXPERTS = 8
KERNEL = 5
MAP_SIDE = 16
TAPS = KERNEL * KERNEL
PIXELS = MAP_SIDE * MAP_SIDE
LANES = 128
CLASS_PAD = 1024
TOTAL_ROW = 18
eps_norm = 0.001
highest = lax.Precision.HIGHEST
MESH = pl.DeviceIdType.MESH
f32 = jnp.float32
bf16 = jnp.bfloat16
VMEM = pltpu.VMEM
VLIMIT = 60 * 1024 * 1024


def dot(a, b, dims=((1,), (0,)), precision=None):
    return lax.dot_general(a, b, (dims, ((), ())), precision=precision, preferred_element_type=f32)


NN = ((1,), (0,))
NT = ((1,), (1,))
TN = ((0,), (0,))


def sig(x):
    return 0.5 * jnp.tanh(0.5 * x) + 0.5


def dsilu(n):
    s = sig(n)
    return s * (1.0 + n * (1.0 - s))


def rsum(x):
    return jnp.sum(x, axis=0, keepdims=True)


def split(x):
    high = x.astype(bf16)
    return jnp.concatenate([high, (x - high.astype(f32)).astype(bf16)], axis=0)


def sum_peers(nd, nz):
    d = lax.axis_index("dp")
    z = lax.axis_index("chan")
    in_plane = [(lax.rem(d + k, nd), z) for k in range(1, nd)]
    along = [(d, lax.rem(z + k, nz)) for k in range(1, nz)]
    return in_plane, along


def signal(peers):
    barrier = pltpu.get_barrier_semaphore()
    for peer in peers:
        pl.semaphore_signal(barrier, inc=1, device_id=peer, device_id_type=MESH)


def sum_start(nd, nz):
    in_plane, along = sum_peers(nd, nz)
    signal(in_plane + along)


def met(nd, nz):
    pl.semaphore_wait(pltpu.get_barrier_semaphore(), nd + nz - 2)


def sum_finish(nd, nz, x_ref, o_ref, plane, depth, s1, r1, s2, r2):
    d = lax.axis_index("dp")
    z = lax.axis_index("chan")
    in_plane, along = sum_peers(nd, nz)
    first = []
    for k, peer in enumerate(in_plane):
        first.append(
            pltpu.make_async_remote_copy(
                src_ref=x_ref,
                dst_ref=plane.at[d],
                send_sem=s1.at[k],
                recv_sem=r1.at[k],
                device_id=peer,
                device_id_type=MESH,
            )
        )
        first[-1].start()
    plane[d] = x_ref[...]
    for copy in first:
        copy.wait_recv()
    total = plane[0]
    for k in range(1, nd):
        total = total + plane[k]
    depth[z] = total
    second = []
    for k, peer in enumerate(along):
        second.append(
            pltpu.make_async_remote_copy(
                src_ref=depth.at[z],
                dst_ref=depth.at[z],
                send_sem=s2.at[k],
                recv_sem=r2.at[k],
                device_id=peer,
                device_id_type=MESH,
            )
        )
        second[-1].start()
    for copy in second:
        copy.wait_recv()
    total = depth[0]
    for k in range(1, nz):
        total = total + depth[k]
    o_ref[...] = total
    for copy in first + second:
        copy.wait_send()


def sum_scratch(rows, nd, nz):
    return [
        VMEM((rows, LANES), f32),
        VMEM((nd, rows, LANES), f32),
        VMEM((nz, rows, LANES), f32),
        pltpu.SemaphoreType.DMA((nd,)),
        pltpu.SemaphoreType.DMA((nd,)),
        pltpu.SemaphoreType.DMA((nz,)),
        pltpu.SemaphoreType.DMA((nz,)),
    ]


def params(ident=None):
    if ident is None:
        return pltpu.CompilerParams(vmem_limit_bytes=VLIMIT)
    return pltpu.CompilerParams(vmem_limit_bytes=VLIMIT, collective_id=ident, has_side_effects=True)


def sum_kernel(nd, nz, x_ref, o_ref, *comm):
    sum_start(nd, nz)
    met(nd, nz)
    sum_finish(nd, nz, x_ref, o_ref, *comm)


def all_sum(x, nd, nz, ident):
    return pl.pallas_call(
        functools.partial(sum_kernel, nd, nz),
        out_shape=jax.ShapeDtypeStruct(x.shape, x.dtype),
        in_specs=[pl.BlockSpec(memory_space=VMEM)],
        out_specs=pl.BlockSpec(memory_space=VMEM),
        scratch_shapes=sum_scratch(x.shape[0], nd, nz)[1:],
        compiler_params=params(ident),
        name="all_sum",
    )(x)


def by_column(width):
    return (width // 2) % LANES == 0


def pad_rows(rows, width, nd):
    unit = 16 * (nd // 2 if by_column(width) else nd)
    return -(-rows // unit) * unit


def core_block(rows, width, core):
    if by_column(width):
        return 0, rows, pl.multiple_of(core * (width // 2), LANES), width // 2
    return pl.multiple_of(core * (rows // 2), 16), rows // 2, 0, width


def part(rows, width, nd, core, place):
    row, count, col, cols = core_block(rows, width, core)
    unit = count // (nd // 2)
    return pl.multiple_of(row + place * unit, 16), unit, col, cols


class Net:
    def __init__(self, nd, nz):
        self.nd, self.nz, self.nxy = nd, nz, nd // 2
        self.d = lax.axis_index("dp")
        self.z = lax.axis_index("chan")
        self.core = lax.rem(self.d, 2)
        self.place = self.d // 2
        self.far = [lax.rem(self.z + k, nz) for k in range(1, nz)]
        self.others = [lax.rem(self.place + k, self.nxy) for k in range(1, self.nxy)]
        self.along = [(self.d, zz) for zz in self.far]
        self.plane = [(2 * o + self.core, self.z) for o in self.others]
        self.twin = (2 * self.place + 1 - self.core, self.z)

    def copy(self, src, dst, sems, k, peer):
        return pltpu.make_async_remote_copy(
            src_ref=src,
            dst_ref=dst,
            send_sem=sems[0].at[k],
            recv_sem=sems[1].at[k],
            device_id=peer,
            device_id_type=MESH,
        )


def start(copies):
    for copy in copies:
        copy.start()


def arrived(copies):
    for copy in copies:
        copy.wait_recv()


def sent(copies):
    for copy in copies:
        copy.wait_send()


def pair(n):
    return [pltpu.SemaphoreType.DMA((n,)), pltpu.SemaphoreType.DMA((n,))]


def lanes(first, count):
    return pl.ds(pl.multiple_of(first, LANES), count)


def tall(first, count):
    return pl.ds(pl.multiple_of(first, 16), count)


def spot(ref, shape, zz, row, unit, col, cols):
    if len(ref.shape) == 3:
        return ref.at[zz, tall(row, unit), lanes(col, cols)]
    return ref.at[tall(row, unit), lanes(zz * shape[1] + col, cols)]


def shard_shape(full, nz):
    if len(full.shape) == 3:
        return full.shape[1:]
    return (full.shape[0], full.shape[1] // nz)


def own_copy(net, shape, src, dst, sem):
    return pltpu.make_async_copy(src, spot(dst, shape, net.z, 0, shape[0], 0, shape[1]), sem)


def gather_far(net, shape, src, dst, sems):
    rows, width = shape
    row, unit, col, cols = part(rows, width, net.nd, net.core, net.place)
    block = src.at[tall(row, unit), lanes(col, cols)]
    return [
        net.copy(block, spot(dst, shape, net.z, row, unit, col, cols), sems, k, peer)
        for k, peer in enumerate(net.along)
    ]


def gather_plane(net, shape, ref, sems, k):
    rows, width = shape
    row, unit, col, cols = part(rows, width, net.nd, net.core, net.place)
    block = spot(ref, shape, net.far[k], row, unit, col, cols)
    n = net.nxy - 1
    return [net.copy(block, block, sems, k * n + q, peer) for q, peer in enumerate(net.plane)]


def gather_twin(net, shape, ref, sems, k):
    rows, width = shape
    row, unit, col, cols = core_block(rows, width, net.core)
    block = spot(ref, shape, net.far[k], row, unit, col, cols)
    return [net.copy(block, block, sems, k, net.twin)]


def every(stage, net, shape, ref, sems):
    return [copy for k in range(net.nz - 1) for copy in stage(net, shape, ref, sems, k)]


def squares_of(ref, rows):
    step_rows = 16 if ref.dtype == bf16 else 8
    whole_rows = rows // step_rows * step_rows

    def step(i, total):
        value = ref[pl.ds(pl.multiple_of(i * step_rows, step_rows), step_rows), :].astype(f32)
        return total + value * value

    total = jnp.sum(lax.fori_loop(0, whole_rows // step_rows, step, jnp.zeros((step_rows, ref.shape[1]), f32)))
    if whole_rows < rows:
        last = ref[whole_rows:rows, :].astype(f32)
        total = total + jnp.sum(last * last)
    return total


def row_of(total):
    lane = lax.broadcasted_iota(jnp.int32, (1, LANES), 1)
    return jnp.where(lane == 0, total, 0.0)


def first_kernel(nd, nz, shape, shape_b, block_ref, head_ref, hside_ref, side_ref, full, full_b, side, gain, kb, kh, kc, squares, wide, tall_h, tall_s, low, side_buf, gain_buf, far_s, far_r, plane_s, plane_r, twin_s, twin_r, side_s, side_r, gain_s, gain_r, later_s, later_r, local):
    net = Net(nd, nz)
    signal(net.along + net.plane + [net.twin])
    rows = shape[0]
    total_rows = block_ref.shape[0]
    fetch = [
        pltpu.make_async_copy(block_ref.at[pl.ds(0, rows)], wide.at[pl.ds(0, rows)], local.at[0]),
        pltpu.make_async_copy(
            block_ref.at[pl.ds(rows, total_rows - rows)], wide.at[pl.ds(rows, total_rows - rows)], local.at[1]
        ),
        pltpu.make_async_copy(hside_ref, tall_s, local.at[2]),
        pltpu.make_async_copy(head_ref, tall_h, local.at[3]),
    ]
    fetch[0].start()
    fetch[0].wait()
    start(fetch[1:])

    @pl.loop(0, rows // 16)
    def _(i):
        at = tall(i * 16, 16)
        low[at, :] = wide[at, :].astype(bf16)

    own = own_copy(net, shape, low, full, local.at[4])
    own.start()
    pl.semaphore_wait(pltpu.get_barrier_semaphore(), nz - 1 + nd // 2)
    far = gather_far(net, shape, low, full, (far_s, far_r))
    start(far)
    side_buf[net.z] = jnp.transpose(side_ref[...])
    sides = [
        net.copy(side_buf.at[net.z], side_buf.at[net.z], (side_s, side_r), k, peer)
        for k, peer in enumerate(net.along)
    ]
    start(sides)
    fetch[2].wait()
    gain_buf[net.z] = jnp.transpose(tall_s[:, 0:LANES])[0:8]
    gains = [
        net.copy(gain_buf.at[net.z], gain_buf.at[net.z], (gain_s, gain_r), k, peer)
        for k, peer in enumerate(net.along)
    ]
    start(gains)
    fetch[1].wait()
    first = WIDTH_IN + TAPS
    for i in range(WIDTH_OUT // 16):
        kb[16 * i : 16 * (i + 1), :] = wide[first + 16 * i : first + 16 * (i + 1), :].astype(bf16)
    own_b = own_copy(net, shape_b, kb, full_b, local.at[5])
    own_b.start()
    planes = []
    for k in range(nz - 1):
        arrived([far[nz - 2 - k]])
        planes.append(gather_plane(net, shape, full, (plane_s, plane_r), k))
        start(planes[k])
    later = gather_far(net, shape_b, kb, full_b, (later_s, later_r))
    start(later)
    fetch[3].wait()

    @pl.loop(0, WIDTH_OUT // 16)
    def _(i):
        at = tall(i * 16, 16)
        kh[at, :] = tall_h[at, :].astype(bf16)

    for i in range(tall_s.shape[0] // 16):
        value = tall_s[16 * i : 16 * (i + 1), 2 : 2 + CLASSES]
        kc[16 * i : 16 * (i + 1), :] = jnp.concatenate(
            [value, jnp.zeros((16, CLASS_PAD - CLASSES), f32)], axis=1
        ).astype(bf16)
    squares[...] = jnp.zeros_like(squares)
    for k, (ref, count) in enumerate(
        ((wide, total_rows), (side_ref, side_ref.shape[0]), (tall_h, WIDTH_OUT), (tall_s, tall_s.shape[0]))
    ):
        squares[k : k + 1, :] = row_of(squares_of(ref, count))
    twins = []
    for k in range(nz - 1):
        arrived(planes[k])
        twins.append(gather_twin(net, shape, full, (twin_s, twin_r), k))
        start(twins[k])
    arrived(sides + gains)
    side[...] = jnp.zeros_like(side)
    side[0 : side_ref.shape[1], :] = jnp.concatenate([side_buf[k] for k in range(nz)], axis=1)
    gain[...] = jnp.concatenate([gain_buf[k] for k in range(nz)], axis=1)
    for k in range(nz - 1):
        arrived(twins[k])
    arrived(later)
    sent(far + sides + gains + later)
    for k in range(nz - 1):
        sent(planes[k] + twins[k])
    own.wait()
    own_b.wait()


def first_gather(block, head_w, head_side, side, nd, nz, ident):
    shape = (pad_rows(WIDTH_IN + TAPS, block.shape[1], nd), block.shape[1])
    shape_b = (pad_rows(WIDTH_OUT, block.shape[1], nd), block.shape[1])
    shape_h = (pad_rows(WIDTH_OUT, head_w.shape[1], nd), head_w.shape[1])
    shape_c = (pad_rows(head_side.shape[0], CLASS_PAD, nd), CLASS_PAD)
    hbm = pl.BlockSpec(memory_space=pltpu.HBM)
    vmem = pl.BlockSpec(memory_space=VMEM)
    own_head = head_side.shape[0]
    return pl.pallas_call(
        functools.partial(first_kernel, nd, nz, shape, shape_b),
        out_shape=[
            jax.ShapeDtypeStruct((shape[0], nz * shape[1]), bf16),
            jax.ShapeDtypeStruct((shape_b[0], nz * shape_b[1]), bf16),
            jax.ShapeDtypeStruct((104, nz * side.shape[0]), f32),
            jax.ShapeDtypeStruct((8, nz * own_head), f32),
            jax.ShapeDtypeStruct(shape_b, bf16),
            jax.ShapeDtypeStruct(shape_h, bf16),
            jax.ShapeDtypeStruct(shape_c, bf16),
            jax.ShapeDtypeStruct((8, LANES), f32),
        ],
        in_specs=[hbm, hbm, hbm, vmem],
        out_specs=[hbm, hbm] + [vmem] * 6,
        scratch_shapes=[
            VMEM(block.shape, f32),
            VMEM(head_w.shape, f32),
            VMEM(head_side.shape, f32),
            VMEM(shape, bf16),
            VMEM((nz, side.shape[1], side.shape[0]), f32),
            VMEM((nz, 8, own_head), f32),
        ]
        + pair(nz - 1)
        + pair((nz - 1) * (nd // 2 - 1))
        + pair(nz - 1)
        + pair(nz - 1) * 3
        + [pltpu.SemaphoreType.DMA((6,))],
        compiler_params=params(ident),
        name="first_gather",
    )(block, head_w, head_side, side)


def reduce_sizes(rows, width, nd):
    unit, cols = (rows, width // 2) if by_column(width) else (rows // 2, width)
    return unit, cols, unit // (nd // 2)


def reduce_twin(net, shape, g_ref, twin_buf, sems, k):
    row, unit, col, cols = core_block(shape[0], shape[1], 1 - net.core)
    return net.copy(
        g_ref.at[tall(row, unit), lanes(k * shape[1] + col, cols)], twin_buf.at[k], sems, k, net.twin
    )


def reduce_add(net, shape, g_ref, half, twin_buf, k):
    row, unit, col, cols = core_block(shape[0], shape[1], net.core)

    @pl.loop(0, unit // 16)
    def _(i):
        at = tall(i * 16, 16)
        mine = g_ref[tall(row + i * 16, 16), lanes(k * shape[1] + col, cols)]
        half[k, at, :] = (mine.astype(f32) + twin_buf[k, at, :].astype(f32)).astype(bf16)


def reduce_plane(net, shape, half, plane_buf, sems, k, base):
    size = reduce_sizes(*shape, net.nd)[2]
    n = net.nxy - 1
    return [
        net.copy(half.at[k, tall(o * size, size)], plane_buf.at[q, k - base], sems, (k - base) * n + q, net.plane[q])
        for q, o in enumerate(net.others)
    ]


def reduce_plane_sum(net, shape, half, plane_buf, out, k, base):
    size = reduce_sizes(*shape, net.nd)[2]

    @pl.loop(0, size // 16)
    def _(i):
        at = tall(i * 16, 16)
        total = half[k, tall(net.place * size + i * 16, 16), :].astype(f32)
        for q in range(net.nxy - 1):
            total = total + plane_buf[q, k - base, at, :].astype(f32)
        out[k, at, :] = total.astype(bf16)


def reduce_far(net, sums, depth_buf, sems):
    return [net.copy(sums.at[zz], depth_buf.at[k], sems, k, net.along[k]) for k, zz in enumerate(net.far)]


def reduce_far_sum(net, shape, sums, depth_buf, piece):
    @pl.loop(0, reduce_sizes(*shape, net.nd)[2] // 16)
    def _(i):
        at = tall(i * 16, 16)
        total = sums[net.z, at, :].astype(f32)
        for q in range(net.nz - 1):
            total = total + depth_buf[q, at, :].astype(f32)
        piece[at, :] = total.astype(bf16)


def spread_block(net, shape, out):
    row, unit, col, cols = part(shape[0], shape[1], net.nd, net.core, net.place)
    return out.at[tall(row, unit), lanes(col, cols)]


def spread_plane(net, shape, piece, out, sems):
    block = spread_block(net, shape, out)
    return [net.copy(piece, block, sems, q, peer) for q, peer in enumerate(net.plane)]


def spread_twin(net, shape, out, sems):
    row, unit, col, cols = core_block(shape[0], shape[1], net.core)
    block = out.at[tall(row, unit), lanes(col, cols)]
    return [net.copy(block, block, sems, 0, net.twin)]


def twin_scratch(shape, nd, nz):
    unit, cols, size = reduce_sizes(*shape, nd)
    return [VMEM((shape[0], nz * shape[1]), bf16), VMEM((nz, unit, cols), bf16)] + pair(nz)


def plane_scratch(shape, nd, count):
    unit, cols, size = reduce_sizes(*shape, nd)
    return [VMEM((nd // 2 - 1, count, size, cols), bf16)] + pair(count * (nd // 2 - 1))


def half_shape(shape, nd, nz):
    unit, cols, size = reduce_sizes(*shape, nd)
    return (nz, unit, cols)


def part_shape(shape, nd, nz):
    unit, cols, size = reduce_sizes(*shape, nd)
    return (nz, size, cols)


def ready(shape, k):
    return max(2, -(-(k + 1) * shape[1] // (LANES * EXPERTS)))


class Steps:
    def __init__(self):
        self.steps = {}

    def at(self, step, action):
        self.steps.setdefault(step, []).append(action)

    def emit(self, now, last):
        for step in sorted(self.steps):
            if step < last:

                @pl.when(now == step)
                def _(step=step):
                    for action in self.steps[step]:
                        action()

    def end(self, last):
        for step in sorted(self.steps):
            if step >= last:
                for action in self.steps[step]:
                    action()


def spread_scratch(shape, nd, nz):
    unit, cols, size = reduce_sizes(*shape, nd)
    return (
        [VMEM((nz - 1, size, cols), bf16), VMEM((size, cols), bf16), pltpu.SemaphoreType.DMA((1,))]
        + pair(nz - 1)
        + pair(nd // 2 - 1)
        + pair(1)
    )


class Twin:
    def __init__(self, net, shape, half, g_ref, twin_buf, ts, tr):
        self.net, self.shape, self.half, self.g, self.buf, self.sems = net, shape, half, g_ref, twin_buf, (ts, tr)

    def copy(self, k):
        return reduce_twin(self.net, self.shape, self.g, self.buf, self.sems, k)

    def begin(self, k):
        self.copy(k).start()

    def add(self, k):
        self.copy(k).wait_recv()
        reduce_add(self.net, self.shape, self.g, self.half, self.buf, k)

    def finish(self):
        for k in range(self.net.nz):
            self.copy(k).wait_send()


class Plane:
    def __init__(self, net, shape, half, out, base, count, buf, ps, pr):
        self.net, self.shape, self.half, self.out = net, shape, half, out
        self.shards, self.base, self.buf, self.sems = range(base, base + count), base, buf, (ps, pr)

    def copies(self, k):
        return reduce_plane(self.net, self.shape, self.half, self.buf, self.sems, k, self.base)

    def begin(self, k):
        start(self.copies(k))

    def add(self, then=None):
        for k in self.shards:
            arrived(self.copies(k))
            reduce_plane_sum(self.net, self.shape, self.half, self.buf, self.out, k, self.base)
            if then is not None:
                then(k)

    def finish(self):
        for k in self.shards:
            sent(self.copies(k))


class Spread:
    def __init__(self, net, shape, sums, out, depth_buf, piece, local, fs, fr, ps, pr, ts, tr):
        self.net, self.shape, self.sums, self.out = net, shape, sums, out
        self.depth_buf, self.piece, self.local = depth_buf, piece, local
        self.far_sems, self.plane_sems, self.twin_sems = (fs, fr), (ps, pr), (ts, tr)

    def far(self):
        return reduce_far(self.net, self.sums, self.depth_buf, self.far_sems)

    def own(self):
        return pltpu.make_async_copy(self.piece, spread_block(self.net, self.shape, self.out), self.local.at[0])

    def plane(self):
        return spread_plane(self.net, self.shape, self.piece, self.out, self.plane_sems)

    def twin(self):
        return spread_twin(self.net, self.shape, self.out, self.twin_sems)

    def send(self, k):
        net = self.net
        slot = lax.rem(k - net.z - 1 + net.nz, net.nz)

        @pl.when(net.z != k)
        def _():
            net.copy(self.sums.at[k], self.depth_buf.at[slot], self.far_sems, slot, (net.d, k)).start()

    def share(self):
        arrived(self.far())
        reduce_far_sum(self.net, self.shape, self.sums, self.depth_buf, self.piece)
        self.own().start()
        start(self.plane())

    def cross(self):
        arrived(self.plane())
        self.own().wait()
        start(self.twin())

    def finish(self):
        arrived(self.twin())
        sent(self.far() + self.plane() + self.twin())


def up_to(size):
    return -(-size // LANES) * LANES


def share_width(lines, nz):
    one = [0]
    for x in lines[0], lines[2], lines[3]:
        one.append(one[-1] + up_to(x.shape[1] // nz))
    for _ in range(3):
        one.append(one[-1] + LANES)
    two = [0]
    for x in lines[1], lines[4], lines[5]:
        two.append(two[-1] + up_to(x.shape[1]))
    return one, two, max(one[-1], two[-1])


def share_scratch(width, nd, nz):
    return (
        [VMEM((nz, 8, width), f32), pltpu.SemaphoreType.DMA((1,))]
        + pair(nz - 1)
        + pair(nd // 2 - 1)
        + pair(nd // 2)
    )


def fit(x, width):
    if x.shape[1] == width:
        return x
    return jnp.concatenate([x, jnp.zeros((x.shape[0], width - x.shape[1]), f32)], axis=1)


class Share:
    def __init__(self, net, rows_all, lines, local, fs, fr, ps, pr, ts, tr):
        self.net, self.rows, self.lines, self.local = net, rows_all, lines, local
        self.far_sems, self.plane_sems, self.twin_sems = (fs, fr), (ps, pr), (ts, tr)
        self.me = net.d * net.nz + net.z

    def fill(self, nb, cut, narrow, wide):
        width = self.lines.shape[2]
        self.lines[...] = jnp.zeros_like(self.lines)
        two = fit(jnp.concatenate([fit(x, up_to(x.shape[1])) for x in wide], axis=1), width)[:nb]
        last = [fit(x, LANES) for x in narrow]
        for k in range(self.net.nz):
            parts = []
            for x in cut:
                own = x.shape[1] // self.net.nz
                parts.append(fit(x[:, k * own : (k + 1) * own], up_to(own)))
            one = fit(jnp.concatenate(parts + last, axis=1), width)[:nb]
            self.lines[k, 0 : 2 * nb, :] = jnp.concatenate([one, two], axis=0)

    def far_copies(self):
        net = self.net
        return [
            net.copy(self.lines.at[zz], self.rows.at[self.me], self.far_sems, k, net.along[k])
            for k, zz in enumerate(net.far)
        ]

    def plane_copies(self):
        net = self.net
        block = self.rows.at[pl.ds(net.d * net.nz, net.nz)]
        return [net.copy(block, block, self.plane_sems, q, peer) for q, peer in enumerate(net.plane)]

    def twin_copies(self):
        net = self.net
        out = []
        for o in range(net.nxy):
            block = self.rows.at[pl.ds((2 * o + net.core) * net.nz, net.nz)]
            out.append(net.copy(block, block, self.twin_sems, o, net.twin))
        return out

    def far(self):
        start(self.far_copies())
        self.own().start()

    def own(self):
        return pltpu.make_async_copy(self.lines.at[self.net.z], self.rows.at[self.me], self.local.at[0])

    def plane(self):
        arrived(self.far_copies())
        self.own().wait()
        start(self.plane_copies())

    def twin(self):
        arrived(self.plane_copies())
        start(self.twin_copies())

    def finish(self):
        arrived(self.twin_copies())
        sent(self.far_copies() + self.plane_copies() + self.twin_copies())


def build_mix(gates, nb, ref):
    deep = LANES * EXPERTS
    row = lax.broadcasted_iota(jnp.int32, (deep, EXPERTS), 0)
    col = lax.broadcasted_iota(jnp.int32, (deep, EXPERTS), 1)
    pick = jnp.where((row & (EXPERTS - 1)) == col, 1.0, 0.0).astype(f32)
    row = lax.broadcasted_iota(jnp.int32, (deep, LANES), 0)
    col = lax.broadcasted_iota(jnp.int32, (deep, LANES), 1)
    same = (row >> 3) == col
    for b in range(nb):
        spread = jnp.broadcast_to(gates[b : b + 1, :], (LANES, EXPERTS))
        value = jnp.where(same, dot(pick, spread, NT, highest), 0.0)
        high = value.astype(bf16)
        ref[:, b * LANES : (b + 1) * LANES] = high
        ref[:, (nb + b) * LANES : (nb + b + 1) * LANES] = (value - high.astype(f32)).astype(bf16)


def mix_kernels(kernels, mix):
    both = dot(kernels, mix)
    half = both.shape[1] // 2
    return both[:, :half] + both[:, half:]


def gate_sums(rows):
    deep = LANES * EXPERTS
    row = lax.broadcasted_iota(jnp.int32, (deep, EXPERTS), 0)
    col = lax.broadcasted_iota(jnp.int32, (deep, EXPERTS), 1)
    pick = jnp.where((row & (EXPERTS - 1)) == col, 1.0, 0.0).astype(f32)
    return dot(rows, pick, NN, highest)


def gate_rows(grad, kernel_block):
    both = dot(grad, kernel_block, TN)
    row = lax.broadcasted_iota(jnp.int32, both.shape, 0)
    col = lax.broadcasted_iota(jnp.int32, both.shape, 1)
    return rsum(jnp.where(row == (col >> 3), both, 0.0))


def norm_rows(stats, chunk, chunks, total):
    mean = stats[pl.ds(chunk, 1), :] / total
    var = stats[pl.ds(chunks + chunk, 1), :] / total - mean * mean
    return mean, lax.rsqrt(var + eps_norm)


def whole(shape):
    return pl.BlockSpec(shape, lambda *_: (0,) * len(shape), pipeline_mode=pl.Buffered(1))


def image(b):
    return pl.ds(pl.multiple_of(b * PIXELS, PIXELS), PIXELS)


def expand_kernel(nd, nz, nb, chunks, shapes, kern_ref, images, mask, mask_rows, counts, route, in_b, kh, pre, taps, stats_all, mix, gates, pooled, full_b, full_h, stats, *comm):
    j = pl.program_id(0)
    sems = comm[6:]
    comm = comm[:6]
    net = Net(nd, nz)
    local = sems[4]

    def copies():
        return every(gather_plane, net, shapes[0], full_b, sems[0:2]) + gather_far(
            net, shapes[1], kh, full_h, sems[2:4]
        )

    def own():
        return [own_copy(net, shapes[1], kh, full_h, local.at[0])]

    @pl.when(j == 1)
    def _():
        met(nd, nz)
        start(copies() + own())

    @pl.when(j == 0)
    def _():
        sum_start(nd, nz)
        stats[...] = jnp.zeros_like(stats)
        stats[2 * chunks : 2 * chunks + 1, :] = rsum(counts[...])
        stats[2 * chunks + 1 : 2 * chunks + 2, :] = rsum(jnp.where(counts[...] > 0.0, 1.0, 0.0))
        pool = dot(mask_rows[...], images[...]) / jnp.maximum(counts[:, 0:1], 1.0)
        pooled[...] = pool
        gate = sig(dot(pool, route[...], NN, highest))
        gates[...] = gate
        build_mix(gate, nb, mix)

    mixed = mix_kernels(kern_ref[...], mix[...])
    one = jnp.zeros((1, LANES), f32)
    two = jnp.zeros((1, LANES), f32)
    for b in range(nb):
        at = slice(b * PIXELS, (b + 1) * PIXELS)
        lane = slice(b * LANES, (b + 1) * LANES)
        taps[b] = mixed[WIDTH_IN : WIDTH_IN + 32, lane]
        value = dot(images[at, :], mixed[:WIDTH_IN, lane].astype(bf16))
        pre[at, :] = value
        masked = mask[at, :] * value
        one = one + rsum(masked)
        two = two + rsum(masked * value)
    stats[pl.ds(j, 1), :] = one
    stats[pl.ds(chunks + j, 1), :] = two

    @pl.when(j == chunks - 1)
    def _():
        sum_finish(nd, nz, stats, stats_all, *comm)
        arrived(copies())
        sent(copies())
        for copy in own():
            copy.wait()


def expand(kern, images, mask, mask_rows, counts, route, full_b, kh, nb, width, nd, nz, ident):
    chunks = width // LANES
    rows = nb * PIXELS
    deep = LANES * EXPERTS
    shapes = ((full_b.shape[0], full_b.shape[1] // nz), kh.shape)
    hbm = pl.BlockSpec(memory_space=pltpu.HBM)
    return pl.pallas_call(
        functools.partial(expand_kernel, nd, nz, nb, chunks, shapes),
        grid=(chunks,),
        out_shape=[
            jax.ShapeDtypeStruct((rows, width), f32),
            jax.ShapeDtypeStruct((nb, 32, width), f32),
            jax.ShapeDtypeStruct((24, LANES), f32),
            jax.ShapeDtypeStruct((deep, 2 * nb * LANES), bf16),
            jax.ShapeDtypeStruct((8, EXPERTS), f32),
            jax.ShapeDtypeStruct((8, WIDTH_IN), f32),
        ]
        + [
            jax.ShapeDtypeStruct(full_b.shape, bf16),
            jax.ShapeDtypeStruct((kh.shape[0], nz * kh.shape[1]), bf16),
        ],
        in_specs=[
            pl.BlockSpec((kern.shape[0], deep), lambda j: (0, j)),
            whole(images.shape),
            whole(mask.shape),
            whole(mask_rows.shape),
            whole(counts.shape),
            whole(route.shape),
        ]
        + [hbm, whole(kh.shape)],
        out_specs=[
            pl.BlockSpec((rows, LANES), lambda j: (0, j)),
            pl.BlockSpec((nb, 32, LANES), lambda j: (0, 0, j)),
            whole((24, LANES)),
            whole((deep, 2 * nb * LANES)),
            whole((8, EXPERTS)),
            whole((8, WIDTH_IN)),
        ]
        + [hbm] * 2,
        scratch_shapes=sum_scratch(24, nd, nz)
        + pair((nz - 1) * (nd // 2 - 1))
        + pair(nz - 1)
        + [pltpu.SemaphoreType.DMA((1,))],
        input_output_aliases={6: 6},
        compiler_params=params(ident),
        name="expand",
    )(kern, images, mask, mask_rows, counts, route, full_b, kh)


def shifted(value, step):
    if step == 0:
        return value
    col = lax.broadcasted_iota(jnp.int32, value.shape, 0) & (MAP_SIDE - 1)
    moved = pltpu.roll(value, (-step) % PIXELS, 0)
    keep = (col + step >= 0) & (col + step < MAP_SIDE)
    return jnp.where(keep, moved, 0.0)


def depth_kernel(nd, nz, nb, chunks, shapes, pre, taps, mask, side, stats, in_b, in_h, kc, out, sums_all, full_b, full_h, full_c, buf, held, sums, *comm):
    j = pl.program_id(0)
    sems = comm[6:]
    comm = comm[:6]
    net = Net(nd, nz)

    def copies():
        return (
            every(gather_twin, net, shapes[0], full_b, sems[0:2])
            + every(gather_plane, net, shapes[1], full_h, sems[2:4])
            + gather_far(net, shapes[2], kc, full_c, sems[4:6])
        )

    def own():
        return own_copy(net, shapes[2], kc, full_c, sems[6].at[0])


    @pl.when(j == 0)
    def _():
        sum_start(nd, nz)

    @pl.when(j == 1)
    def _():
        met(nd, nz)
        start(copies())
        own().start()

    @pl.when(j == 0)
    def _():
        sums[...] = jnp.zeros_like(sums)

    mean, rstd = norm_rows(stats, j, chunks, stats[2 * chunks : 2 * chunks + 1, :])
    scale = rstd * side[2 * SQUEEZE : 2 * SQUEEZE + 1, :]
    bias = side[2 * SQUEEZE + 1 : 2 * SQUEEZE + 2, :]
    held[...] = jnp.zeros_like(held)

    @pl.loop(0, nb)
    def _(b):
        at = image(b)
        normed = (pre[at, :] - mean) * scale + bias
        act = normed * sig(normed) * mask[at, :]
        for s in range(KERNEL):
            buf[s] = shifted(act, s - KERNEL // 2)
        taps_now = [jnp.broadcast_to(taps[b, t : t + 1, :], (MAP_SIDE, LANES)) for t in range(TAPS)]
        acc = [None] * MAP_SIDE
        for y in range(MAP_SIDE):
            for s in range(KERNEL):
                x = buf[s, y * MAP_SIDE : (y + 1) * MAP_SIDE, :]
                for r in range(KERNEL):
                    i = y - r + KERNEL // 2
                    if 0 <= i < MAP_SIDE:
                        term = taps_now[r * KERNEL + s] * x
                        acc[i] = term if acc[i] is None else acc[i] + term
            done = [y - 2] if y < MAP_SIDE - 1 else [y - 2, y - 1, y]
            for i in done:
                if i >= 0:
                    out[pl.ds(pl.multiple_of(b * PIXELS + i * MAP_SIDE, MAP_SIDE), MAP_SIDE), :] = acc[i]
        value = out[at, :]
        masked = mask[at, :] * value
        held[0:1, :] += rsum(masked)
        held[1:2, :] += rsum(masked * value)

    sums[pl.ds(j, 1), :] = held[0:1, :]
    sums[pl.ds(chunks + j, 1), :] = held[1:2, :]

    @pl.when(j == chunks - 1)
    def _():
        sum_finish(nd, nz, sums, sums_all, *comm)
        arrived(copies())
        sent(copies())
        own().wait()


def depthwise(pre, taps, mask, side, stats, full_b, full_h, kc, nb, nd, nz, ident):
    rows, width = pre.shape
    chunks = width // LANES
    wide = lambda j: (0, j)
    later = (full_b, full_h)
    shapes = tuple(shard_shape(k, nz) for k in later) + (kc.shape,)
    hbm = pl.BlockSpec(memory_space=pltpu.HBM)
    planes = (nz - 1) * (nd // 2 - 1)
    return pl.pallas_call(
        functools.partial(depth_kernel, nd, nz, nb, chunks, shapes),
        grid=(chunks,),
        out_shape=[
            jax.ShapeDtypeStruct((rows, width), f32),
            jax.ShapeDtypeStruct((24, LANES), f32),
        ]
        + [jax.ShapeDtypeStruct(k.shape, bf16) for k in later]
        + [jax.ShapeDtypeStruct((nz,) + kc.shape, bf16)],
        in_specs=[
            pl.BlockSpec((rows, LANES), wide),
            pl.BlockSpec((nb, 32, LANES), lambda j: (0, 0, j)),
            whole(mask.shape),
            pl.BlockSpec((side.shape[0], LANES), wide),
            whole(stats.shape),
        ]
        + [hbm, hbm, whole(kc.shape)],
        out_specs=[pl.BlockSpec((rows, LANES), wide), whole((24, LANES))] + [hbm] * 3,
        scratch_shapes=[VMEM((KERNEL, PIXELS, LANES), f32), VMEM((8, LANES), f32)]
        + sum_scratch(24, nd, nz)
        + pair(nz - 1)
        + pair(planes)
        + pair(nz - 1)
        + [pltpu.SemaphoreType.DMA((1,))],
        input_output_aliases={5: 2, 6: 3},
        compiler_params=params(ident),
        name="depthwise",
    )(pre, taps, mask, side, stats, *later, kc)


def store_wide(ref, row, value):
    width = value.shape[1]
    for k in range(-(-width // LANES)):
        lanes = min(LANES, width - k * LANES)
        ref[row + k : row + k + 1, :lanes] = value[:, k * LANES : k * LANES + lanes]


def load_wide(ref, row, width):
    parts = []
    for k in range(-(-width // LANES)):
        lanes = min(LANES, width - k * LANES)
        parts.append(ref[row + k : row + k + 1, :lanes])
    return jnp.concatenate(parts, axis=1)


OUT_CHUNKS = -(-WIDTH_OUT // LANES)


def project_kernel(nd, nz, nb, chunks, shapes, dpre, mask, side, stats, totals, counts, sq_bias, kern, mix, in_h, in_c, excited, proj, pooled, gate_out, squeezed, sums_all, mixed, full_h, full_c, act, exc, sums, *comm):
    phase = pl.program_id(0)
    sems = comm[6:]
    comm = comm[:6]
    net = Net(nd, nz)

    def copies():
        return every(gather_twin, net, shapes[0], full_h, sems[0:2]) + every(
            gather_plane, net, shapes[1], full_c, sems[2:4]
        )

    j = pl.program_id(1)

    @pl.when((phase == 0) & (j == 0))
    def _():
        sum_start(nd, nz)

    @pl.when((phase == 0) & (j == 1))
    def _():
        met(nd, nz)
        start(copies())
    total = totals[2 * chunks : 2 * chunks + 1, :]

    @pl.when((phase == 0) & (j == 0))
    def _():
        squeezed[...] = jnp.zeros_like(squeezed)
        pooled[...] = jnp.zeros_like(pooled)
        sums[...] = jnp.zeros_like(sums)

    lane = pl.ds(pl.multiple_of(j * LANES, LANES), LANES)

    @pl.when(phase == 0)
    def _():
        both = mix_kernels(kern[...], mix[...])
        for b in range(nb):
            mixed[b, :, lane] = both[:, b * LANES : (b + 1) * LANES].astype(bf16)
        mean, rstd = norm_rows(stats, j, chunks, total)
        scale = rstd * side[2 * SQUEEZE + 2 : 2 * SQUEEZE + 3, :]
        bias = side[2 * SQUEEZE + 3 : 2 * SQUEEZE + 4, :]
        for b in range(nb):
            at = slice(b * PIXELS, (b + 1) * PIXELS)
            normed = (dpre[at, :] - mean) * scale + bias
            value = normed * sig(normed) * mask[at, :]
            act[j, at, :] = value
            pooled[b : b + 1, lane] = rsum(value) / jnp.maximum(counts[b : b + 1, :], 1.0)
        squeezed[...] += dot(pooled[:, lane], side[0:SQUEEZE, :], NT, highest)

    @pl.when(phase == 1)
    def _():
        before = squeezed[...] + sq_bias[...]
        gate = sig(
            dot(before * sig(before), side[SQUEEZE : 2 * SQUEEZE, :], NN, highest)
            + side[2 * SQUEEZE + 4 : 2 * SQUEEZE + 5, :]
        )
        gate_out[:, lane] = gate
        for b in range(nb):
            at = slice(b * PIXELS, (b + 1) * PIXELS)
            value = (act[j, at, :] * gate[b : b + 1, :]).astype(bf16)
            excited[at, :] = value
            exc[at, lane] = value

    @pl.when((phase == 1) & (j == chunks - 1))
    def _():
        one = jnp.zeros((1, WIDTH_OUT), f32)
        two = jnp.zeros((1, WIDTH_OUT), f32)
        for b in range(nb):
            at = slice(b * PIXELS, (b + 1) * PIXELS)
            value = dot(exc[at, :], mixed[b], NT)
            proj[at, :] = value
            masked = mask[at, 0:1] * value
            one = one + rsum(masked)
            two = two + rsum(masked * value)
        store_wide(sums, 0, one)
        store_wide(sums, OUT_CHUNKS, two)

    @pl.when((phase == 1) & (j == chunks - 1))
    def _():
        sum_finish(nd, nz, sums, sums_all, *comm)
        arrived(copies())
        sent(copies())


def project(dpre, mask, side, stats, totals, counts, sq_bias, full_b, mix, full_h, full_c, nb, nd, nz, ident):
    rows, width = dpre.shape
    chunks = width // LANES
    deep = LANES * EXPERTS
    later = (full_h, full_c)
    shapes = tuple(shard_shape(k, nz) for k in later)
    hbm = pl.BlockSpec(memory_space=pltpu.HBM)
    return pl.pallas_call(
        functools.partial(project_kernel, nd, nz, nb, chunks, shapes),
        grid=(2, chunks),
        out_shape=[
            jax.ShapeDtypeStruct((rows, width), bf16),
            jax.ShapeDtypeStruct((rows, WIDTH_OUT), f32),
            jax.ShapeDtypeStruct((8, width), f32),
            jax.ShapeDtypeStruct((8, width), f32),
            jax.ShapeDtypeStruct((8, SQUEEZE), f32),
            jax.ShapeDtypeStruct((8, LANES), f32),
            jax.ShapeDtypeStruct((nb, WIDTH_OUT, width), bf16),
        ]
        + [jax.ShapeDtypeStruct(k.shape, bf16) for k in later],
        in_specs=[
            pl.BlockSpec((rows, LANES), lambda p, j: (0, jnp.where(p == 0, j, chunks - 1))),
            whole(mask.shape),
            pl.BlockSpec((side.shape[0], LANES), lambda p, j: (0, j)),
            whole(stats.shape),
            whole(totals.shape),
            whole(counts.shape),
            whole(sq_bias.shape),
            pl.BlockSpec((WIDTH_OUT, deep), lambda p, j: (0, jnp.where(p == 0, j, chunks - 1))),
            whole(mix.shape),
        ]
        + [hbm] * 2,
        out_specs=[
            pl.BlockSpec((rows, LANES), lambda p, j: (0, jnp.where(p == 0, 0, j))),
            whole((rows, WIDTH_OUT)),
            whole((8, width)),
            whole((8, width)),
            whole((8, SQUEEZE)),
            whole((8, LANES)),
            whole((nb, WIDTH_OUT, width)),
        ]
        + [hbm] * 2,
        scratch_shapes=[VMEM((chunks, rows, LANES), f32), VMEM((rows, width), bf16)]
        + sum_scratch(8, nd, nz)
        + pair(nz - 1)
        + pair((nz - 1) * (nd // 2 - 1)),
        input_output_aliases={9: 7, 10: 8},
        compiler_params=params(ident),
        name="project",
    )(dpre, mask, side, stats, totals, counts, sq_bias, full_b, mix, *later)


def out_norm(sums, total):
    mean = load_wide(sums, 0, WIDTH_OUT) / total
    var = load_wide(sums, OUT_CHUNKS, WIDTH_OUT) / total - mean * mean
    return mean, lax.rsqrt(var + eps_norm)


def head_kernel(nd, nz, nb, chunks, shape, kern, proj, mask, mask_rows, counts, gain, route, stats, totals, in_c, low, pre, mixed_out, sums_all, mix_out, gates, pooled, full_c, sums, *comm):
    j = pl.program_id(0)
    sems = comm[6:]
    comm = comm[:6]
    net = Net(nd, nz)

    def copies():
        return every(gather_twin, net, shape, full_c, sems)


    @pl.when(j == 0)
    def _():
        sum_start(nd, nz)

    @pl.when(j == 1)
    def _():
        met(nd, nz)
        start(copies())

    @pl.when(j == 0)
    def _():
        sums[...] = jnp.zeros_like(sums)
        mean, rstd = out_norm(stats, totals[TOTAL_ROW : TOTAL_ROW + 1, 0:1])
        scale = rstd * gain[0:1, :]
        for b in range(nb):
            at = slice(b * PIXELS, (b + 1) * PIXELS)
            low[at, :] = (((proj[at, :] - mean) * scale + gain[1:2, :]) * mask[at, 0:1]).astype(bf16)
        pool = dot(mask_rows[...], low[...]) / jnp.maximum(counts[:, 0:1], 1.0)
        pooled[...] = pool
        gate = sig(dot(pool, route[...], NN, highest))
        gates[...] = gate
        build_mix(gate, nb, mix_out)

    mixed = mix_kernels(kern[...], mix_out[...])
    one = jnp.zeros((1, LANES), f32)
    two = jnp.zeros((1, LANES), f32)
    for b in range(nb):
        at = slice(b * PIXELS, (b + 1) * PIXELS)
        weight = mixed[:, b * LANES : (b + 1) * LANES].astype(bf16)
        mixed_out[b] = weight
        value = dot(low[at, :], weight)
        pre[at, :] = value
        masked = mask[at, :] * value
        one = one + rsum(masked)
        two = two + rsum(masked * value)
    sums[pl.ds(j, 1), :] = one
    sums[pl.ds(chunks + j, 1), :] = two


    @pl.when(j == chunks - 1)
    def _():
        sum_finish(nd, nz, sums, sums_all, *comm)
        arrived(copies())
        sent(copies())


def head(kern, proj, mask, mask_rows, counts, gain, route, stats, totals, full_c, nb, nd, nz, ident):
    rows = proj.shape[0]
    width = kern.shape[1] // EXPERTS
    chunks = width // LANES
    deep = LANES * EXPERTS
    wide = lambda j: (0, j)
    return pl.pallas_call(
        functools.partial(head_kernel, nd, nz, nb, chunks, shard_shape(full_c, nz)),
        grid=(chunks,),
        out_shape=[
            jax.ShapeDtypeStruct((rows, WIDTH_OUT), bf16),
            jax.ShapeDtypeStruct((rows, width), f32),
            jax.ShapeDtypeStruct((nb, WIDTH_OUT, width), bf16),
            jax.ShapeDtypeStruct((24, LANES), f32),
            jax.ShapeDtypeStruct((deep, 2 * nb * LANES), bf16),
            jax.ShapeDtypeStruct((8, EXPERTS), f32),
            jax.ShapeDtypeStruct((8, WIDTH_OUT), f32),
            jax.ShapeDtypeStruct(full_c.shape, bf16),
        ],
        in_specs=[
            pl.BlockSpec((WIDTH_OUT, deep), wide),
            whole(proj.shape),
            whole(mask.shape),
            whole(mask_rows.shape),
            whole(counts.shape),
            whole(gain.shape),
            whole(route.shape),
            whole(stats.shape),
            whole(totals.shape),
            pl.BlockSpec(memory_space=pltpu.HBM),
        ],
        out_specs=[
            whole((rows, WIDTH_OUT)),
            pl.BlockSpec((rows, LANES), wide),
            pl.BlockSpec((nb, WIDTH_OUT, LANES), lambda j: (0, 0, j)),
            whole((24, LANES)),
            whole((deep, 2 * nb * LANES)),
            whole((8, EXPERTS)),
            whole((8, WIDTH_OUT)),
            pl.BlockSpec(memory_space=pltpu.HBM),
        ],
        scratch_shapes=sum_scratch(24, nd, nz) + pair(nz - 1),
        input_output_aliases={9: 7},
        compiler_params=params(ident),
        name="head",
    )(kern, proj, mask, mask_rows, counts, gain, route, stats, totals, full_c)


def loss_kernel(nd, nz, nb, chunks, pre, mask, counts, labels, bias, cls, gain, stats, totals, features, grad_logits, grad_features, sums_all, logits, sums, *comm):
    phase = pl.program_id(0)
    j = pl.program_id(1)

    @pl.when((phase == 0) & (j == 0))
    def _():
        sum_start(nd, nz)

    @pl.when((phase == 0) & (j == 1))
    def _():
        met(nd, nz)
    lane = pl.ds(pl.multiple_of(j * LANES, LANES), LANES)

    @pl.when((phase == 0) & (j == 0))
    def _():
        sums[...] = jnp.zeros_like(sums)
        features[...] = jnp.zeros_like(features)
        logits[...] = jnp.zeros_like(logits)

    mean, rstd = norm_rows(stats, j, chunks, totals[TOTAL_ROW : TOTAL_ROW + 1, :])
    scale = rstd * gain[0:1, :]

    @pl.when(phase == 0)
    def _():
        for b in range(nb):
            at = slice(b * PIXELS, (b + 1) * PIXELS)
            normed = (pre[at, :] - mean) * scale + gain[1:2, :]
            features[b : b + 1, lane] = rsum(normed * sig(normed) * mask[at, :]) / jnp.maximum(
                counts[b : b + 1, :], 1.0
            )
        both = dot(split(features[:, lane]), cls[lane, :])
        logits[...] += both[:8] + both[8:]

    @pl.when((phase == 1) & (j == 0))
    def _():
        col = lax.broadcasted_iota(jnp.int32, (8, CLASS_PAD), 1)
        inside = col < CLASSES
        scores = jnp.where(inside, logits[...] + bias[...], -1e30)
        top = jnp.max(scores, axis=1, keepdims=True)
        spread = jnp.where(inside, jnp.exp(scores - top), 0.0)
        mass = jnp.sum(spread, axis=1, keepdims=True)
        hot = jnp.where(col == labels[:, 0:1], 1.0, 0.0)
        shifted_scores = jnp.where(inside, scores - top - jnp.log(mass), 0.0)
        per_image = -(
            0.9 * jnp.sum(shifted_scores * hot, axis=1, keepdims=True)
            + (0.1 / CLASSES) * jnp.sum(shifted_scores, axis=1, keepdims=True)
        )
        valid = jnp.where(counts[:, 0:1] > 0.0, 1.0, 0.0)
        sums[2 * chunks : 2 * chunks + 1, :] = jnp.broadcast_to(rsum(per_image * valid), (1, LANES))
        weight = valid / totals[TOTAL_ROW + 1 : TOTAL_ROW + 2, 0:1]
        grad_logits[...] = weight * jnp.where(inside, spread / mass - 0.9 * hot - 0.1 / CLASSES, 0.0)

    @pl.when(phase == 1)
    def _():
        both = dot(split(grad_logits[...]), cls[lane, :], NT)
        grads = (both[:8] + both[8:]) / jnp.maximum(counts[...], 1.0)
        grad_features[:, lane] = grads
        one = jnp.zeros((1, LANES), f32)
        two = jnp.zeros((1, LANES), f32)
        for b in range(nb):
            at = slice(b * PIXELS, (b + 1) * PIXELS)
            hat = (pre[at, :] - mean) * rstd
            grad = mask[at, :] * dsilu(hat * gain[0:1, :] + gain[1:2, :]) * grads[b : b + 1, :]
            one = one + rsum(grad)
            two = two + rsum(grad * hat)
        sums[pl.ds(j, 1), :] = one
        sums[pl.ds(chunks + j, 1), :] = two

    @pl.when((phase == 1) & (j == chunks - 1))
    def _():
        sum_finish(nd, nz, sums, sums_all, *comm)


def loss_stage(pre, mask, counts, labels, bias, cls, gain, stats, totals, nb, nd, nz, ident):
    rows, width = pre.shape
    chunks = width // LANES
    return pl.pallas_call(
        functools.partial(loss_kernel, nd, nz, nb, chunks),
        grid=(2, chunks),
        out_shape=[
            jax.ShapeDtypeStruct((8, width), f32),
            jax.ShapeDtypeStruct((8, CLASS_PAD), f32),
            jax.ShapeDtypeStruct((8, width), f32),
            jax.ShapeDtypeStruct((24, LANES), f32),
        ],
        in_specs=[
            pl.BlockSpec((rows, LANES), lambda p, j: (0, j)),
            whole(mask.shape),
            whole(counts.shape),
            whole(labels.shape),
            whole(bias.shape),
            whole(cls.shape),
            pl.BlockSpec((8, LANES), lambda p, j: (0, j)),
            whole(stats.shape),
            whole(totals.shape),
        ],
        out_specs=[whole((8, width)), whole((8, CLASS_PAD)), whole((8, width)), whole((24, LANES))],
        scratch_shapes=[VMEM((8, CLASS_PAD), f32)]
        + sum_scratch(24, nd, nz),
        compiler_params=params(ident),
        name="loss_stage",
    )(pre, mask, counts, labels, bias, cls, gain, stats, totals)


def head_back_kernel(nd, nz, nb, chunks, shape, pre, grad_features, mask, counts, gain, stats, sums_in, totals, low, kern, mixed, mix, gates, route, proj, proj_stats, grad_out, sums_all, dz_out, half, part, held, grads, gate_acc, sums, *comm):
    j = pl.program_id(0)
    net = Net(nd, nz)
    twin = Twin(net, shape, half, *comm[6:10])
    plane = Plane(net, shape, half, part, 0, nz // 2, *comm[10:13])
    made = comm[6]
    comm = comm[:6]
    steps = Steps()
    for k in range(nz):
        first = ready(shape, k)
        steps.at(first, functools.partial(twin.begin, k))
        steps.at(first + 2, functools.partial(twin.add, k))
        if k < nz // 2:
            steps.at(first + 2, functools.partial(plane.begin, k))

    @pl.when(j == 0)
    def _():
        sum_start(nd, nz)

    @pl.when(j == 1)
    def _():
        met(nd, nz)

    steps.emit(j, chunks)
    lane = pl.ds(pl.multiple_of(j * LANES, LANES), LANES)
    total = totals[TOTAL_ROW : TOTAL_ROW + 1, :]

    @pl.when(j == 0)
    def _():
        gate_acc[...] = jnp.zeros_like(gate_acc)
        sums[...] = jnp.zeros_like(sums)

    mean, rstd = norm_rows(stats, j, chunks, total)
    scale = rstd * gain[0:1, :]
    one = sums_in[pl.ds(j, 1), :] / total
    two = sums_in[pl.ds(chunks + j, 1), :] / total
    for b in range(nb):
        at = slice(b * PIXELS, (b + 1) * PIXELS)
        hat = (pre[at, :] - mean) * rstd
        grad = dsilu(hat * gain[0:1, :] + gain[1:2, :]) * grad_features[b : b + 1, :]
        value = (scale * mask[at, :] * (grad - one - hat * two)).astype(bf16)
        held[at, lane] = value
        grad_mixed = dot(low[at, :], value, TN).astype(bf16)
        grads[:, b * LANES : (b + 1) * LANES] = grad_mixed
        gate_acc[b : b + 1, :] += gate_rows(grad_mixed, kern[...])
    made[:WIDTH_OUT, lanes(j * LANES * EXPERTS, LANES * EXPERTS)] = dot(grads[...], mix[:, : nb * LANES], NT).astype(bf16)

    @pl.when(j == chunks - 1)
    def _():
        dz = gate_sums(gate_acc[...]) * gates[...] * (1.0 - gates[...])
        dz_out[...] = dz
        pool_grad = dot(dz, route[...], NT, highest) / jnp.maximum(counts[:, 0:1], 1.0)
        mean, rstd = out_norm(proj_stats, total[:, 0:1])
        one = jnp.zeros((1, WIDTH_OUT), f32)
        two = jnp.zeros((1, WIDTH_OUT), f32)
        for b in range(nb):
            at = slice(b * PIXELS, (b + 1) * PIXELS)
            value = (dot(held[at, :], mixed[b], NT) + pool_grad[b : b + 1, :]) * mask[at, 0:1]
            grad_out[at, :] = value
            one = one + rsum(value)
            two = two + rsum(value * ((proj[at, :] - mean) * rstd))
        store_wide(sums, 0, one)
        store_wide(sums, OUT_CHUNKS, two)

    @pl.when(j == chunks - 1)
    def _():
        late = [k for k in range(nz) if ready(shape, k) >= chunks]
        for k in late:
            twin.begin(k)
        sum_finish(nd, nz, sums, sums_all, *comm)
        for k in range(nz):
            if ready(shape, k) + 2 >= chunks:
                twin.add(k)
                if k < nz // 2:
                    plane.begin(k)
        plane.add()
        twin.finish()
        plane.finish()


def head_back(pre, grad_features, mask, counts, gain, stats, sums_in, totals, low, kern, mixed, mix, gates, route, proj, proj_stats, nb, nd, nz, ident):
    rows, width = pre.shape
    chunks = width // LANES
    deep = LANES * EXPERTS
    shape = (kern.shape[0], kern.shape[1] // nz)
    wide = lambda j: (0, j)
    return pl.pallas_call(
        functools.partial(head_back_kernel, nd, nz, nb, chunks, shape),
        grid=(chunks,),
        out_shape=[
            jax.ShapeDtypeStruct((rows, WIDTH_OUT), f32),
            jax.ShapeDtypeStruct((8, LANES), f32),
            jax.ShapeDtypeStruct((8, EXPERTS), f32),
            jax.ShapeDtypeStruct(half_shape(shape, nd, nz), bf16),
            jax.ShapeDtypeStruct(part_shape(shape, nd, nz // 2), bf16),
        ],
        in_specs=[
            pl.BlockSpec((rows, LANES), wide),
            pl.BlockSpec((8, LANES), wide),
            whole(mask.shape),
            whole(counts.shape),
            pl.BlockSpec((8, LANES), wide),
            whole(stats.shape),
            whole(sums_in.shape),
            whole(totals.shape),
            whole(low.shape),
            pl.BlockSpec((WIDTH_OUT, deep), wide),
            whole(mixed.shape),
            whole(mix.shape),
            whole(gates.shape),
            whole(route.shape),
            whole(proj.shape),
            whole(proj_stats.shape),
        ],
        out_specs=[
            whole((rows, WIDTH_OUT)),
            whole((8, LANES)),
            whole((8, EXPERTS)),
            whole(half_shape(shape, nd, nz)),
            whole(part_shape(shape, nd, nz // 2)),
        ],
        scratch_shapes=[
            VMEM((rows, width), bf16),
            VMEM((WIDTH_OUT, nb * LANES), bf16),
            VMEM((8, deep), f32),
        ]
        + sum_scratch(8, nd, nz)
        + twin_scratch(shape, nd, nz)
        + plane_scratch(shape, nd, nz // 2),
        compiler_params=params(ident),
        name="head_back",
    )(pre, grad_features, mask, counts, gain, stats, sums_in, totals, low, kern, mixed, mix, gates, route, proj, proj_stats)


def project_back_kernel(nd, nz, nb, chunks, shape_h, shape, half_h, part_h, grad_in, proj, proj_stats, proj_sums, gain, mask, counts, totals, stats, side, dpre, excited, mixed, kern, mix, gate, pooled, squeezed, sq_bias, grad_norm, sums_all, grad_squeeze, gate_grad, dz_gate, done_h, half, part, low, held, grads, gate_acc, sums_h, sums, *comm):
    phase = pl.program_id(0)
    net = Net(nd, nz)
    few = nz // 2
    cut_one = 9 + len(spread_scratch(shape_h, nd, nz))
    plane_h = Plane(net, shape_h, half_h, sums_h, few, nz - few, *comm[6:9])
    up = Spread(net, shape_h, sums_h, done_h, *comm[9:cut_one])
    twin = Twin(net, shape, half, *comm[cut_one : cut_one + 4])
    plane = Plane(net, shape, half, part, 0, few, *comm[cut_one + 4 : cut_one + 7])
    made = comm[cut_one]
    comm = comm[:6]
    steps = Steps()

    def begin():
        met(nd, nz)
        for k in plane_h.shards:
            plane_h.begin(k)
        sums_h[0:few] = part_h[...]
        for k in range(few):
            up.send(k)

    steps.at(1, begin)
    steps.at(chunks - 1, functools.partial(plane_h.add, up.send))
    steps.at(chunks + 3, up.share)
    steps.at(2 * chunks - 2, up.cross)
    for k in range(nz):
        first = ready(shape, k)
        steps.at(first, functools.partial(twin.begin, k))
        steps.at(first + 2, functools.partial(twin.add, k))
        if k < few:
            steps.at(first + 2, functools.partial(plane.begin, k))
    j = pl.program_id(1)

    @pl.when((phase == 0) & (j == 0))
    def _():
        sum_start(nd, nz)

    steps.emit(phase * chunks + j, 2 * chunks)
    lane = pl.ds(pl.multiple_of(j * LANES, LANES), LANES)
    total = totals[TOTAL_ROW : TOTAL_ROW + 1, :]

    @pl.when((phase == 0) & (j == 0))
    def _():
        gate_acc[...] = jnp.zeros_like(gate_acc)
        sums[...] = jnp.zeros_like(sums)
        grad_squeeze[...] = jnp.zeros_like(grad_squeeze)
        dz_gate[...] = jnp.zeros_like(dz_gate)
        mean, rstd = out_norm(proj_stats, total[:, 0:1])
        scale = rstd * gain[0:1, :]
        one = load_wide(proj_sums, 0, WIDTH_OUT) / total[:, 0:1]
        two = load_wide(proj_sums, OUT_CHUNKS, WIDTH_OUT) / total[:, 0:1]
        for b in range(nb):
            at = slice(b * PIXELS, (b + 1) * PIXELS)
            hat = (proj[at, :] - mean) * rstd
            low[at, :] = (scale * (grad_in[at, :] - mask[at, 0:1] * (one + hat * two))).astype(bf16)

    mean, rstd = norm_rows(stats, j, chunks, total)
    gain_now = side[2 * SQUEEZE + 2 : 2 * SQUEEZE + 3, :]
    bias_now = side[2 * SQUEEZE + 3 : 2 * SQUEEZE + 4, :]

    @pl.when(phase == 0)
    def _():
        for b in range(nb):
            at = slice(b * PIXELS, (b + 1) * PIXELS)
            grad_mixed = dot(low[at, :], excited[at, :], TN).astype(bf16)
            grads[:, b * LANES : (b + 1) * LANES] = grad_mixed
            gate_acc[b : b + 1, :] += gate_rows(grad_mixed, kern[...])
            value = dot(low[at, :], mixed[b])
            held[j, at, :] = value
            normed = (dpre[at, :] - mean) * (rstd * gain_now) + bias_now
            act = normed * sig(normed) * mask[at, :]
            now = gate[b : b + 1, :]
            dz_gate[b : b + 1, lane] = rsum(value * act) * now * (1.0 - now)
        made[:WIDTH_OUT, lanes(j * LANES * EXPERTS, LANES * EXPERTS)] = dot(grads[...], mix[:, : nb * LANES], NT).astype(bf16)
        grad_squeeze[...] += dot(dz_gate[:, lane], side[SQUEEZE : 2 * SQUEEZE, :], NT, highest)

    @pl.when((phase == 1) & (j == 0))
    def _():
        grad_squeeze[...] = grad_squeeze[...] * dsilu(squeezed[...] + sq_bias[...])
        gate_grad[...] = gate_sums(gate_acc[...])

    @pl.when(phase == 1)
    def _():
        pool_grad = dot(grad_squeeze[...], side[0:SQUEEZE, :], NN, highest) / jnp.maximum(counts[...], 1.0)
        one = jnp.zeros((1, LANES), f32)
        two = jnp.zeros((1, LANES), f32)
        for b in range(nb):
            at = slice(b * PIXELS, (b + 1) * PIXELS)
            hat = (dpre[at, :] - mean) * rstd
            grad = held[j, at, :] * gate[b : b + 1, :] + pool_grad[b : b + 1, :]
            value = mask[at, :] * grad * dsilu(hat * gain_now + bias_now)
            grad_norm[at, :] = value
            one = one + rsum(value)
            two = two + rsum(value * hat)
        sums[pl.ds(j, 1), :] = one
        sums[pl.ds(chunks + j, 1), :] = two

    @pl.when((phase == 1) & (j == chunks - 1))
    def _():
        sum_finish(nd, nz, sums, sums_all, *comm)
        plane.add()
        up.finish()
        twin.finish()
        plane.finish()
        plane_h.finish()


def project_back(half_h, part_h, shape_h, grad_in, proj, proj_stats, proj_sums, gain, mask, counts, totals, stats, side, dpre, excited, mixed, kern, mix, gate, pooled, squeezed, sq_bias, nb, nd, nz, ident):
    rows, width = dpre.shape
    shape = (kern.shape[0], kern.shape[1] // nz)
    few = nz // 2
    chunks = width // LANES
    deep = LANES * EXPERTS
    wide = lambda p, j: (0, j)
    early = lambda p, j: (0, jnp.where(p == 0, j, chunks - 1))
    late = lambda p, j: (0, jnp.where(p == 0, 0, j))
    return pl.pallas_call(
        functools.partial(project_back_kernel, nd, nz, nb, chunks, shape_h, shape),
        grid=(2, chunks),
        out_shape=[
            jax.ShapeDtypeStruct((rows, width), f32),
            jax.ShapeDtypeStruct((24, LANES), f32),
            jax.ShapeDtypeStruct((8, SQUEEZE), f32),
            jax.ShapeDtypeStruct((8, EXPERTS), f32),
            jax.ShapeDtypeStruct((8, width), f32),
            jax.ShapeDtypeStruct(shape_h, bf16),
            jax.ShapeDtypeStruct(half_shape(shape, nd, nz), bf16),
            jax.ShapeDtypeStruct(part_shape(shape, nd, few), bf16),
        ],
        in_specs=[
            whole(half_h.shape),
            whole(part_h.shape),
            whole(grad_in.shape),
            whole(proj.shape),
            whole(proj_stats.shape),
            whole(proj_sums.shape),
            whole(gain.shape),
            whole(mask.shape),
            whole(counts.shape),
            whole(totals.shape),
            whole(stats.shape),
            pl.BlockSpec((side.shape[0], LANES), wide),
            pl.BlockSpec((rows, LANES), wide),
            pl.BlockSpec((rows, LANES), early),
            pl.BlockSpec((nb, WIDTH_OUT, LANES), lambda p, j: (0, 0, jnp.where(p == 0, j, chunks - 1))),
            pl.BlockSpec((WIDTH_OUT, deep), early),
            whole(mix.shape),
            pl.BlockSpec((8, LANES), wide),
            pl.BlockSpec((8, LANES), wide),
            whole(squeezed.shape),
            whole(sq_bias.shape),
        ],
        out_specs=[
            pl.BlockSpec((rows, LANES), late),
            whole((24, LANES)),
            whole((8, SQUEEZE)),
            whole((8, EXPERTS)),
            whole((8, width)),
            pl.BlockSpec(memory_space=pltpu.HBM),
            whole(half_shape(shape, nd, nz)),
            whole(part_shape(shape, nd, few)),
        ],
        scratch_shapes=[
            VMEM((rows, WIDTH_OUT), bf16),
            VMEM((chunks, rows, LANES), f32),
            VMEM((WIDTH_OUT, nb * LANES), bf16),
            VMEM((8, deep), f32),
            VMEM(part_shape(shape_h, nd, nz), bf16),
        ]
        + sum_scratch(24, nd, nz)
        + plane_scratch(shape_h, nd, nz - few)
        + spread_scratch(shape_h, nd, nz)
        + twin_scratch(shape, nd, nz)
        + plane_scratch(shape, nd, few),
        compiler_params=params(ident),
        name="project_back",
    )(half_h, part_h, grad_in, proj, proj_stats, proj_sums, gain, mask, counts, totals, stats, side, dpre, excited, mixed, kern, mix, gate, pooled, squeezed, sq_bias)


def depth_back_kernel(nd, nz, nb, chunks, shape, half, part, grad_in, dpre, pre, taps, mask, side, stats_one, stats_two, sums_two, totals, features, logits, pooled, dz_gate, head_pool, pooled_in, grad_sq, before, sq_bias, dz_head, grad_out, tap_grads, sums_all, done, rows_all, buf, acts, held, sums_b, sums, *comm):
    j = pl.program_id(0)
    net = Net(nd, nz)
    few = nz // 2
    plane = Plane(net, shape, half, sums_b, few, nz - few, *comm[6:9])
    up = Spread(net, shape, sums_b, done, *comm[9 : 9 + len(spread_scratch(shape, nd, nz))])
    share = Share(net, rows_all, *comm[9 + len(spread_scratch(shape, nd, nz)) :])
    comm = comm[:6]
    steps = Steps()

    def begin():
        met(nd, nz)
        for k in plane.shards:
            plane.begin(k)
        sums_b[0:few] = part[...]
        for k in range(few):
            up.send(k)

    steps.at(1, begin)
    steps.at(2, share.far)
    steps.at(4, functools.partial(plane.add, up.send))
    steps.at(4, share.plane)
    steps.at(chunks - 3, up.share)
    steps.at(chunks - 3, share.twin)
    steps.at(chunks - 1, up.cross)

    @pl.when(j == 0)
    def _():
        sum_start(nd, nz)

    steps.emit(j, chunks)

    @pl.when(j == 0)
    def _():
        total_before = before[...] + sq_bias[...]
        squeezed = total_before * sig(total_before)
        share.fill(
            nb,
            [features, pooled, dz_gate],
            [grad_sq[...], squeezed, dz_head[...]],
            [logits[...], head_pool[...], pooled_in[...]],
        )

    total = totals[TOTAL_ROW : TOTAL_ROW + 1, :]

    @pl.when(j == 0)
    def _():
        sums[...] = jnp.zeros_like(sums)

    mean_two, rstd_two = norm_rows(stats_two, j, chunks, total)
    scale_two = rstd_two * side[2 * SQUEEZE + 2 : 2 * SQUEEZE + 3, :]
    one_two = sums_two[pl.ds(j, 1), :] / total
    two_two = sums_two[pl.ds(chunks + j, 1), :] / total
    mean, rstd = norm_rows(stats_one, j, chunks, total)
    gain = side[2 * SQUEEZE : 2 * SQUEEZE + 1, :]
    bias = side[2 * SQUEEZE + 1 : 2 * SQUEEZE + 2, :]
    held[...] = jnp.zeros_like(held)
    reach = KERNEL // 2

    @pl.loop(0, nb)
    def _(b):
        at = image(b)
        hat = (dpre[at, :] - mean_two) * rstd_two
        grad = scale_two * (grad_in[at, :] - mask[at, :] * (one_two + hat * two_two))
        for s in range(KERNEL):
            buf[s] = shifted(grad, reach - s)
        hat = (pre[at, :] - mean) * rstd
        normed = hat * gain + bias
        acts[...] = normed * sig(normed) * mask[at, :]
        taps_now = [jnp.broadcast_to(taps[b, t : t + 1, :], (MAP_SIDE, LANES)) for t in range(TAPS)]
        acc = [None] * MAP_SIDE
        for q in range(MAP_SIDE):
            for s in range(KERNEL):
                x = buf[s, q * MAP_SIDE : (q + 1) * MAP_SIDE, :]
                for r in range(KERNEL):
                    y = q + r - reach
                    if 0 <= y < MAP_SIDE:
                        term = taps_now[r * KERNEL + s] * x
                        acc[y] = term if acc[y] is None else acc[y] + term
            done = [q - 2] if q < MAP_SIDE - 1 else [q - 2, q - 1, q]
            for i in done:
                if i >= 0:
                    grad_out[pl.ds(pl.multiple_of(b * PIXELS + i * MAP_SIDE, MAP_SIDE), MAP_SIDE), :] = acc[i]
        tap_acc = [None] * TAPS
        for q in range(MAP_SIDE):
            for s in range(KERNEL):
                x = buf[s, q * MAP_SIDE : (q + 1) * MAP_SIDE, :]
                for r in range(KERNEL):
                    y = q + r - reach
                    if 0 <= y < MAP_SIDE:
                        both = acts[y * MAP_SIDE : (y + 1) * MAP_SIDE, :] * x
                        term = both[:8] + both[8:]
                        t = r * KERNEL + s
                        tap_acc[t] = term if tap_acc[t] is None else tap_acc[t] + term
        tap_grads[b] = jnp.zeros((32, LANES), f32)
        for t in range(TAPS):
            tap_grads[b, t : t + 1, :] = rsum(tap_acc[t])
        hat = (pre[at, :] - mean) * rstd
        value = grad_out[at, :] * mask[at, :] * dsilu(hat * gain + bias)
        grad_out[at, :] = value
        held[0:1, :] += rsum(value)
        held[1:2, :] += rsum(value * hat)

    sums[pl.ds(j, 1), :] = held[0:1, :]
    sums[pl.ds(chunks + j, 1), :] = held[1:2, :]

    @pl.when(j == chunks - 1)
    def _():
        sum_finish(nd, nz, sums, sums_all, *comm)
        share.finish()
        up.finish()
        plane.finish()


def depth_back(half, part, shape, grad_in, dpre, pre, taps, mask, side, stats_one, stats_two, sums_two, totals, lines, nb, nd, nz, ident):
    rows, width = pre.shape
    chunks = width // LANES
    wide = lambda j: (0, j)
    tall = pl.BlockSpec((rows, LANES), wide)
    hbm = pl.BlockSpec(memory_space=pltpu.HBM)
    return pl.pallas_call(
        functools.partial(depth_back_kernel, nd, nz, nb, chunks, shape),
        grid=(chunks,),
        out_shape=[
            jax.ShapeDtypeStruct((rows, width), f32),
            jax.ShapeDtypeStruct((nb, 32, width), f32),
            jax.ShapeDtypeStruct((24, LANES), f32),
            jax.ShapeDtypeStruct(shape, bf16),
            jax.ShapeDtypeStruct((nd * nz, 8, share_width(lines, nz)[-1]), f32),
        ],
        in_specs=[
            whole(half.shape),
            whole(part.shape),
            tall,
            tall,
            tall,
            pl.BlockSpec((nb, 32, LANES), lambda j: (0, 0, j)),
            whole(mask.shape),
            pl.BlockSpec((side.shape[0], LANES), wide),
            whole(stats_one.shape),
            whole(stats_two.shape),
            whole(sums_two.shape),
            whole(totals.shape),
        ]
        + [whole(x.shape) for x in lines],
        out_specs=[tall, pl.BlockSpec((nb, 32, LANES), lambda j: (0, 0, j)), whole((24, LANES)), hbm, hbm],
        scratch_shapes=[
            VMEM((KERNEL, PIXELS, LANES), f32),
            VMEM((PIXELS, LANES), f32),
            VMEM((8, LANES), f32),
            VMEM(part_shape(shape, nd, nz), bf16),
        ]
        + sum_scratch(24, nd, nz)
        + plane_scratch(shape, nd, nz - nz // 2)
        + spread_scratch(shape, nd, nz)
        + share_scratch(share_width(lines, nz)[-1], nd, nz),
        compiler_params=params(ident),
        name="depth_back",
    )(half, part, grad_in, dpre, pre, taps, mask, side, stats_one, stats_two, sums_two, totals, *lines)


def expand_back_kernel(nd, nz, nb, chunks, shape, cuts_one, cuts_two, grad_in, pre, images, tap_grads, mask, side, stats, sums_in, totals, kern, mix, gates, gate_grad, rows_all, grad_b, grad_h, squares_w, stats_two, stats_three, stats_four, sums_two, sums_four, chan_old, head_old, proj_old, done, grad_cls, grad_side_out, factors, route_in, route_head, sq_bias, class_bias, chan_new, head_new, proj_new, loss, grads, gate_acc, grad_side, every_sum, half, sums, *comm):
    j = pl.program_id(0)
    net = Net(nd, nz)
    low = comm[0]
    sum_comm = comm[1:7]
    comm = comm[7:]
    twin = Twin(net, shape, half, *comm[0:4])
    plane = Plane(net, shape, half, sums, 0, nz, *comm[4:7])
    up = Spread(net, shape, sums, done, *comm[7:])
    made = comm[0]
    steps = Steps()
    for k in range(nz):
        first = ready(shape, k)
        steps.at(first, functools.partial(twin.begin, k))
        steps.at(first + 1, functools.partial(twin.add, k))
        steps.at(first + 1, functools.partial(plane.begin, k))

    @pl.when(j == 0)
    def _():
        sum_start(nd, nz)

    @pl.when(j == 1)
    def _():
        met(nd, nz)

    steps.emit(j, chunks)

    total = totals[TOTAL_ROW : TOTAL_ROW + 1, :]

    @pl.when(j == 0)
    def _():
        gate_acc[...] = jnp.zeros_like(gate_acc)
        grads[...] = jnp.zeros_like(grads)

    mean, rstd = norm_rows(stats, j, chunks, total)
    scale = rstd * side[2 * SQUEEZE : 2 * SQUEEZE + 1, :]
    one = sums_in[pl.ds(j, 1), :] / total
    two = sums_in[pl.ds(chunks + j, 1), :] / total
    for b in range(nb):
        at = slice(b * PIXELS, (b + 1) * PIXELS)
        lane = slice(b * LANES, (b + 1) * LANES)
        hat = (pre[at, :] - mean) * rstd
        value = (scale * (grad_in[at, :] - mask[at, :] * (one + hat * two))).astype(bf16)
        grads[0:WIDTH_IN, lane] = dot(images[at, :], value, TN).astype(bf16)
        grads[WIDTH_IN : WIDTH_IN + 32, lane] = tap_grads[b].astype(bf16)
        gate_acc[b : b + 1, :] += gate_rows(grads[:, lane], kern[...])
    made[:, lanes(j * LANES * EXPERTS, LANES * EXPERTS)] = dot(grads[...], mix[:, : nb * LANES], NT).astype(bf16)

    @pl.when(j == chunks - 1)
    def _():
        dz = (gate_sums(gate_acc[...]) + gate_grad[...]) * gates[...] * (1.0 - gates[...])
        steps.end(chunks)
        z = net.z
        me = net.d * nz + z
        devices = nd * nz
        own = chan_old.shape[1]
        own_head = head_old.shape[1]
        own_proj = proj_old.shape[1]
        width = own * nz
        head_width = own_head * nz
        head_chunks = head_width // LANES
        count = devices * 8
        row = lax.broadcasted_iota(jnp.int32, (count, 1), 0)
        keep = jnp.where((row & 7) < nb, 1.0, 0.0)

        def one(k, size):
            return rows_all[:, :, cuts_one[k] : cuts_one[k] + size].reshape(count, size) * keep

        def two(k, size):
            return pltpu.roll(rows_all[:, :, cuts_two[k] : cuts_two[k] + size].reshape(count, size), count - nb, 0)

        features = one(0, own_head)
        logits = two(0, CLASS_PAD)
        pooled = one(1, own)
        dz_gate = one(2, own)
        grad_sq = one(3, SQUEEZE)
        grad_cls[...] = dot(features, logits, TN, highest)
        grad_side[...] = jnp.zeros_like(grad_side)
        grad_side[0:SQUEEZE, :own] = dot(grad_sq, pooled, TN, highest)
        grad_side[SQUEEZE : 2 * SQUEEZE, :own] = dot(one(4, SQUEEZE), dz_gate, TN, highest)

        def channel(ref, at, n, size, own_size):
            return turn(load_wide(ref, at, size), z * own_size)[:, :own_size]

        at = 2 * SQUEEZE
        grad_side[at : at + 1, :own] = channel(sums_in, chunks, chunks, width, own)
        grad_side[at + 1 : at + 2, :own] = channel(sums_in, 0, chunks, width, own)
        grad_side[at + 2 : at + 3, :own] = channel(sums_two, chunks, chunks, width, own)
        grad_side[at + 3 : at + 4, :own] = channel(sums_two, 0, chunks, width, own)
        grad_side[at + 4 : at + 5, :own] = rsum(dz_gate)
        route_head[...] = dot(two(1, WIDTH_OUT), one(5, EXPERTS), TN, highest)
        sq_bias[...] = rsum(grad_sq)
        class_bias[...] = rsum(logits * keep)
        head_gain = channel(sums_four, head_chunks, head_chunks, head_width, own_head)
        head_bias = channel(sums_four, 0, head_chunks, head_width, own_head)
        totals = stats[TOTAL_ROW : TOTAL_ROW + 1, 0:1]
        loss[...] = jnp.broadcast_to(
            sums_four[2 * head_chunks : 2 * head_chunks + 1, :] / stats[TOTAL_ROW + 1 : TOTAL_ROW + 2, :], (8, LANES)
        )

        def moving(new, old, ref, at, n, size, own_size):
            mean = load_wide(ref, 0, size) / totals
            var = (load_wide(ref, n, size) / totals - mean * mean) * (totals / (totals - 1.0))
            new[at : at + 1, :] = 0.5 * old[at : at + 1, :] + 0.5 * turn(mean, z * own_size)[:, :own_size]
            new[at + 1 : at + 2, :] = 0.5 * old[at + 1 : at + 2, :] + 0.5 * turn(var, z * own_size)[:, :own_size]

        moving(chan_new, chan_old, stats, 0, chunks, width, own)
        moving(chan_new, chan_old, stats_two, 2, chunks, width, own)
        moving(head_new, head_old, stats_four, 0, head_chunks, head_width, own_head)
        moving(proj_new, proj_old, stats_three, 0, OUT_CHUNKS, WIDTH_OUT, own_proj)
        low[...] = jnp.zeros_like(low)
        low[pl.ds(me, 1), 0 : nb * EXPERTS] = jnp.concatenate([dz[b : b + 1, :] for b in range(nb)], axis=1)
        share = 1.0 / nd
        g_hside = jnp.sum(grad_cls[...] * grad_cls[...]) + jnp.sum(head_gain * head_gain) + jnp.sum(head_bias * head_bias)
        sums = (
            squares_of(grad_b, WIDTH_OUT),
            squares_of(grad_side, 104),
            squares_of(grad_h, WIDTH_OUT),
            g_hside,
        )
        for k in range(4):
            low[devices + k : devices + k + 1, :] = row_of(sums[k] * share)
            low[devices + 4 + k : devices + 5 + k, :] = squares_w[k : k + 1, :] * share
        plane.add(up.send)
        up.share()
        low[devices : devices + 1, :] += row_of(squares_of(up.piece, up.piece.shape[0]))
        sum_finish(nd, nz, low, every_sum, *sum_comm)
        up.cross()
        for k in range(4):
            grad_sq_sum = jnp.sum(every_sum[devices + k : devices + k + 1, :], axis=1, keepdims=True)
            weight_sq = jnp.sum(every_sum[devices + 4 + k : devices + 5 + k, :], axis=1, keepdims=True)
            factors[k : k + 1, :] = jnp.broadcast_to(
                jnp.sqrt(weight_sq) * lax.rsqrt(grad_sq_sum + 1e-12), (1, LANES)
            )
        row = lax.broadcasted_iota(jnp.int32, (count, devices), 0)
        col = lax.broadcasted_iota(jnp.int32, (count, devices), 1)
        spread = dot(jnp.where((row >> 3) == col, 1.0, 0.0), every_sum[0:devices, :], NN, highest)
        row = lax.broadcasted_iota(jnp.int32, (count, LANES), 0)
        col = lax.broadcasted_iota(jnp.int32, (count, LANES), 1)
        spread = jnp.where((col >> 3) == (row & 7) - nb, spread, 0.0)
        row = lax.broadcasted_iota(jnp.int32, (LANES, EXPERTS), 0)
        col = lax.broadcasted_iota(jnp.int32, (LANES, EXPERTS), 1)
        dz_rows = dot(spread, jnp.where((row & (EXPERTS - 1)) == col, 1.0, 0.0), NN, highest)
        pooled_in = rows_all[:, :, cuts_two[2] : cuts_two[2] + 256].reshape(count, 256)
        route_in[...] = dot(pooled_in, dz_rows, TN, highest)[:WIDTH_IN]
        grad_side_out[...] = jnp.transpose(grad_side[...])[:own]
        values = grad_cls[:, :CLASSES]
        both = jnp.concatenate([head_gain, head_bias] + [jnp.zeros((6, own_head), f32)], axis=0)
        grad_cls[...] = jnp.concatenate(
            [jnp.transpose(both)[:, 0:2], values, jnp.zeros((own_head, CLASS_PAD - CLASSES - 2), f32)], axis=1
        )
        up.finish()
        twin.finish()
        plane.finish()


def expand_back(grad_in, pre, images, tap_grads, mask, side, stats, sums_in, totals, kern, mix, gates, gate_grad, small, cuts, nb, nd, nz, ident):
    rows, width = pre.shape
    chunks = width // LANES
    deep = LANES * EXPERTS
    wide = lambda j: (0, j)
    tall = pl.BlockSpec((rows, LANES), wide)
    shape = (kern.shape[0], kern.shape[1] // nz)
    devices = nd * nz
    chan_old, head_old, proj_old = small[-3:]
    own, own_head = chan_old.shape[1], head_old.shape[1]
    outs = [(own_head, CLASS_PAD), (own, 104), (8, LANES)]
    outs += [(WIDTH_IN, EXPERTS), (WIDTH_OUT, EXPERTS), (1, SQUEEZE), (1, CLASS_PAD)]
    outs += [chan_old.shape, head_old.shape, proj_old.shape, (8, LANES)]
    return pl.pallas_call(
        functools.partial(expand_back_kernel, nd, nz, nb, chunks, shape, *cuts),
        grid=(chunks,),
        out_shape=[
            jax.ShapeDtypeStruct(shape, bf16),
        ]
        + [jax.ShapeDtypeStruct(x, f32) for x in outs],
        in_specs=[
            tall,
            tall,
            whole(images.shape),
            pl.BlockSpec((nb, 32, LANES), lambda j: (0, 0, j)),
            whole(mask.shape),
            pl.BlockSpec((side.shape[0], LANES), wide),
            whole(stats.shape),
            whole(sums_in.shape),
            whole(totals.shape),
            pl.BlockSpec((kern.shape[0], deep), wide),
            whole(mix.shape),
            whole(gates.shape),
            whole(gate_grad.shape),
        ]
        + [whole(x.shape) for x in small],
        out_specs=[pl.BlockSpec(memory_space=pltpu.HBM)] + [whole(x) for x in outs],
        scratch_shapes=[VMEM((kern.shape[0], nb * LANES), bf16), VMEM((8, deep), f32)]
        + [VMEM((104, up_to(own)), f32)]
        + sum_scratch(devices + 8, nd, nz)[:1]
        + [VMEM(half_shape(shape, nd, nz), bf16), VMEM(part_shape(shape, nd, nz), bf16)]
        + sum_scratch(devices + 8, nd, nz)
        + twin_scratch(shape, nd, nz)
        + plane_scratch(shape, nd, nz)
        + spread_scratch(shape, nd, nz),
        compiler_params=params(ident),
        name="expand_back",
    )(grad_in, pre, images, tap_grads, mask, side, stats, sums_in, totals, kern, mix, gates, gate_grad, *small)


def update(weight, grad, moment, average, factor):
    scaled = grad * factor
    moment_new = 0.5 * moment + scaled
    weight_new = weight - 0.2 * (scaled + 0.5 * moment_new)
    average_new = 0.5 * average + 0.5 * weight_new
    return (weight_new, moment_new, average_new)


BLOCK_STEP = 64
HEAD_STEP = 32


def turn(x, shift):
    width = x.shape[1]
    return pltpu.roll(x, lax.rem(width - shift, width), 1)


def apply_kernel(
    factors,
    grad_side,
    side_w,
    side_m,
    side_e,
    grad_a,
    grad_b,
    block_w,
    block_m,
    block_e,
    grad_h,
    head_w,
    head_m,
    head_e,
    grad_cls,
    hside_w,
    hside_m,
    hside_e,
    side_wo,
    side_mo,
    side_eo,
    block_wo,
    block_mo,
    block_eo,
    head_wo,
    head_mo,
    head_eo,
    hside_wo,
    hside_mo,
    hside_eo,
    grad_block,
):
    @pl.when(pl.program_id(0) == 0)
    def _():
        fresh = update(side_w[...], grad_side[:, : side_w.shape[1]], side_m[...], side_e[...], factors[1:2, 0:1])
        side_wo[...], side_mo[...], side_eo[...] = fresh
        first = WIDTH_IN + TAPS
        whole_rows = first // 16 * 16

        @pl.loop(0, whole_rows // 16)
        def _(i):
            here = tall(i * 16, 16)
            grad_block[here, :] = grad_a[here, :].astype(f32)

        grad_block[whole_rows:first, :] = grad_a[whole_rows : whole_rows + 16, :].astype(f32)[: first - whole_rows]
        for i in range(WIDTH_OUT // 16):
            grad_block[first + 16 * i : first + 16 * (i + 1), :] = grad_b[16 * i : 16 * (i + 1), :].astype(f32)
        grad_block[first + WIDTH_OUT :, :] = jnp.zeros(
            (grad_block.shape[0] - first - WIDTH_OUT, grad_block.shape[1]), f32
        )

    here = pl.multiple_of(jnp.minimum(pl.program_id(0), grad_block.shape[0] // BLOCK_STEP - 1) * BLOCK_STEP, BLOCK_STEP)

    for k in range(0, BLOCK_STEP, 16):
        rows = slice(k, k + 16)
        fresh = update(
            block_w[rows, :], grad_block[pl.ds(here + k, 16), :], block_m[rows, :], block_e[rows, :], factors[0:1, 0:1]
        )
        block_wo[rows, :], block_mo[rows, :], block_eo[rows, :] = fresh
    for k in range(0, HEAD_STEP, 16):
        rows = slice(k, k + 16)
        fresh = update(
            head_w[rows, :], grad_h[rows, :].astype(f32), head_m[rows, :], head_e[rows, :], factors[2:3, 0:1]
        )
        head_wo[rows, :], head_mo[rows, :], head_eo[rows, :] = fresh
    fresh = update(hside_w[...], grad_cls[:, : hside_w.shape[1]], hside_m[...], hside_e[...], factors[3:4, 0:1])
    hside_wo[...], hside_mo[...], hside_eo[...] = fresh


def apply(factors, side, grads, block, head_arrays, hside):
    def stepped(array, size):
        last = -(-array.shape[0] // size) - 1
        return pl.BlockSpec((size, array.shape[1]), lambda j: (jnp.minimum(j, last), 0))

    steps = max(-(-block[0].shape[0] // BLOCK_STEP), -(-WIDTH_OUT // HEAD_STEP))
    blocks = (
        [whole(x.shape) for x in side]
        + [whole(x.shape) for x in grads]
        + [stepped(x, BLOCK_STEP) for x in block]
        + [stepped(x, HEAD_STEP) for x in head_arrays]
        + [stepped(x, HEAD_STEP) for x in hside]
    )
    arrays = side + grads + block + head_arrays + hside
    keep = [k for k in range(17) if k not in (0, 4, 5, 9, 13)]
    return pl.pallas_call(
        apply_kernel,
        grid=(steps,),
        out_shape=[jax.ShapeDtypeStruct(arrays[k].shape, f32) for k in keep],
        in_specs=[whole(factors.shape)] + blocks,
        out_specs=[blocks[k] for k in keep],
        scratch_shapes=[VMEM((-(-block[0].shape[0] // BLOCK_STEP) * BLOCK_STEP, block[0].shape[1]), f32)],
        compiler_params=params(),
        name="apply",
    )(factors, *arrays)


def body(
    nd,
    nz,
    images,
    pixel_mask,
    counts,
    labels,
    block_w,
    chan_side,
    head_w,
    head_side,
    shared,
    block_mom,
    side_mom,
    head_mom,
    hside_mom,
    shared_mom,
    block_ema,
    side_ema,
    head_ema,
    hside_ema,
    shared_ema,
    chan_stats,
    head_stats,
    proj_stats,
):
    z = lax.axis_index("chan")
    nb = images.shape[0] // nz
    own = chan_side.shape[1]
    own_head = head_side.shape[0]
    width = own * nz
    head_width = own_head * nz
    end_route = WIDTH_IN * EXPERTS
    end_head = end_route + WIDTH_OUT * EXPERTS
    end_norm = end_head + 2 * WIDTH_OUT
    end_squeeze = end_norm + SQUEEZE
    route_in = shared[:end_route].reshape(WIDTH_IN, EXPERTS)
    route_head = shared[end_route:end_head].reshape(WIDTH_OUT, EXPERTS)
    gain_out = shared[end_head:end_norm].reshape(2, WIDTH_OUT)
    sq_bias = shared[None, end_norm:end_squeeze]
    class_bias = jnp.pad(shared[end_squeeze:], (0, CLASS_PAD - CLASSES))[None, :]

    def mine(x):
        return lax.dynamic_slice_in_dim(x, z * nb, nb, 0)

    image_rows = mine(images).reshape(nb * PIXELS, WIDTH_IN)
    mask_now = mine(pixel_mask).astype(f32)
    mask = jnp.broadcast_to(mask_now.reshape(-1, 1), (nb * PIXELS, LANES))
    mask_rows = jnp.pad(
        (jnp.eye(nb, dtype=f32)[:, :, None] * mask_now[None]).reshape(nb, nb * PIXELS).astype(bf16),
        ((0, 8 - nb), (0, 0)),
    )
    count_rows = jnp.broadcast_to(jnp.pad(mine(counts).astype(f32), (0, 8 - nb))[:, None], (8, LANES))
    label_rows = jnp.broadcast_to(jnp.pad(mine(labels), (0, 8 - nb))[:, None], (8, LANES))

    full_a, full_b, side, gain_head, kern_b, kern_h, kern_c, squares = first_gather(
        block_w, head_w, head_side, chan_side.T, nd, nz, 1
    )
    pre, taps, stats_one, mix, gates, pooled_in, full_b, full_h = expand(
        full_a, image_rows, mask, mask_rows, count_rows, route_in, full_b, kern_h, nb, width, nd, nz, 3
    )
    totals = stats_one
    dpre, stats_two, full_b, full_h, full_c = depthwise(
        pre, taps, mask, side, stats_one, full_b, full_h, kern_c, nb, nd, nz, 4
    )
    excited, proj, pooled, gate, squeezed, stats_three, mixed_proj, full_h, full_c = project(
        dpre, mask, side, stats_two, totals, count_rows, sq_bias, full_b, mix, full_h, full_c, nb, nd, nz, 5
    )
    low, head_pre, mixed_head, stats_four, mix_head, gates_head, head_pool, full_c = head(
        full_h, proj, mask, mask_rows, count_rows, gain_out, route_head, stats_three, totals, full_c, nb, nd, nz, 6
    )
    cls_full = full_c[:, :own_head].reshape(head_width, CLASS_PAD)
    features, grad_logits, grad_features, sums_four = loss_stage(
        head_pre, mask, count_rows, label_rows, class_bias, cls_full, gain_head, stats_four, totals, nb, nd, nz, 7
    )
    grad_proj, sums_three, dz_head, half_h, part_h = head_back(
        head_pre,
        grad_features,
        mask,
        count_rows,
        gain_head,
        stats_four,
        sums_four,
        totals,
        low,
        full_h,
        mixed_head,
        mix_head,
        gates_head,
        route_head,
        proj,
        stats_three,
        nb,
        nd,
        nz,
        8,
    )
    shape_h, shape_b = kern_h.shape, kern_b.shape
    grad_norm, sums_two, grad_squeeze, gate_grad, dz_gate, grad_h, half_b, part_b = project_back(
        half_h,
        part_h,
        shape_h,
        grad_proj,
        proj,
        stats_three,
        sums_three,
        gain_out,
        mask,
        count_rows,
        totals,
        stats_two,
        side,
        dpre,
        excited,
        mixed_proj,
        full_b,
        mix,
        gate,
        pooled,
        squeezed,
        sq_bias,
        nb,
        nd,
        nz,
        9,
    )
    lines = [features, grad_logits, pooled, dz_gate, head_pool, pooled_in, grad_squeeze, squeezed, sq_bias, dz_head]
    grad_pre, tap_grads, sums_one, grad_b, rows_all = depth_back(
        half_b, part_b, shape_b, grad_norm, dpre, pre, taps, mask, side, stats_one, stats_two, sums_two, totals, lines, nb, nd, nz, 10
    )
    small = [rows_all, grad_b, grad_h, squares, stats_two, stats_three, stats_four, sums_two, sums_four]
    small += [chan_stats, head_stats, proj_stats]
    grad_a, grad_cls, grad_side, factors, *rest = expand_back(
        grad_pre,
        pre,
        image_rows,
        tap_grads,
        mask,
        side,
        stats_one,
        sums_one,
        totals,
        full_a,
        mix,
        gates,
        gate_grad,
        small,
        share_width(lines, nz)[:2],
        nb,
        nd,
        nz,
        11,
    )
    grad_route_in, grad_route_head, grad_sq_bias, grad_class_bias, new_chan, new_head_stats, new_proj, loss = rest
    results = apply(
        factors,
        [grad_side, chan_side.T, side_mom.T, side_ema.T],
        [grad_a, grad_b],
        [block_w, block_mom, block_ema],
        [grad_h, head_w, head_mom, head_ema],
        [grad_cls, head_side, hside_mom, hside_ema],
    )
    new_side, new_block, new_head, new_hside = (results[3 * k : 3 * k + 3] for k in range(4))
    new_side = [x.T for x in new_side]

    def out_row(first):
        return sums_three[first : first + OUT_CHUNKS].reshape(-1)[:WIDTH_OUT]

    grad_shared = jnp.concatenate(
        [
            grad_route_in.reshape(-1),
            grad_route_head.reshape(-1),
            out_row(OUT_CHUNKS),
            out_row(0),
            grad_sq_bias[0],
            grad_class_bias[0, :CLASSES],
        ]
    )
    new_shared = update(
        shared,
        grad_shared,
        shared_mom,
        shared_ema,
        jnp.sqrt(jnp.sum(shared * shared)) * lax.rsqrt(jnp.sum(grad_shared * grad_shared) + 1e-12),
    )
    groups = (new_block, new_side, new_head, new_hside, new_shared)
    return (
        (loss[0, 0],)
        + tuple(group[k] for k in range(3) for group in groups)
        + (new_chan, new_head_stats, new_proj)
    )


def solution(mesh):
    nd, nz = mesh.shape["dp"], mesh.shape["chan"]
    cols = P(None, "chan")
    state = (cols, cols, cols, P("chan", None), P())
    return jax.shard_map(
        functools.partial(body, nd, nz),
        mesh=mesh,
        in_specs=(P("dp", None, None), P("dp", None), P("dp"), P("dp"))
        + state * 3
        + (cols, cols, cols),
        out_specs=(P(),) + state * 3 + (cols, cols, cols),
        check_vma=False,
    )
```

```python
import functools

import jax
import jax.numpy as jnp
from jax import lax
from jax.experimental import pallas as pl
from jax.experimental.pallas import tpu as pltpu
from jax.sharding import PartitionSpec as P

WIDTH_IN = 192
WIDTH_OUT = 320
SQUEEZE = 48
CLASSES = 1000
EXPERTS = 8
KERNEL = 5
MAP_SIDE = 16
TAPS = KERNEL * KERNEL
PIXELS = MAP_SIDE * MAP_SIDE
LANES = 128
CLASS_PAD = 1024
TOTAL_ROW = 18
eps_norm = 0.001
highest = lax.Precision.HIGHEST
MESH = pl.DeviceIdType.MESH
f32 = jnp.float32
bf16 = jnp.bfloat16
VMEM = pltpu.VMEM
VLIMIT = 60 * 1024 * 1024


def dot(a, b, dims=((1,), (0,)), precision=None):
    return lax.dot_general(a, b, (dims, ((), ())), precision=precision, preferred_element_type=f32)


NN = ((1,), (0,))
NT = ((1,), (1,))
TN = ((0,), (0,))


def sig(x):
    return 0.5 * jnp.tanh(0.5 * x) + 0.5


def dsilu(n):
    s = sig(n)
    return s * (1.0 + n * (1.0 - s))


def rsum(x):
    return jnp.sum(x, axis=0, keepdims=True)


def split(x):
    high = x.astype(bf16)
    return jnp.concatenate([high, (x - high.astype(f32)).astype(bf16)], axis=0)


def sum_peers(nd, nz):
    d = lax.axis_index("dp")
    z = lax.axis_index("chan")
    in_plane = [(lax.rem(d + k, nd), z) for k in range(1, nd)]
    along = [(d, lax.rem(z + k, nz)) for k in range(1, nz)]
    return in_plane, along


def signal(peers):
    barrier = pltpu.get_barrier_semaphore()
    for peer in peers:
        pl.semaphore_signal(barrier, inc=1, device_id=peer, device_id_type=MESH)


def sum_start(nd, nz):
    in_plane, along = sum_peers(nd, nz)
    signal(in_plane + along)


def met(nd, nz):
    pl.semaphore_wait(pltpu.get_barrier_semaphore(), nd + nz - 2)


def sum_copies(nd, nz, x_ref, plane, depth, s1, r1, s2, r2):
    d = lax.axis_index("dp")
    z = lax.axis_index("chan")
    in_plane, along = sum_peers(nd, nz)

    def copy(src, dst, send, recv, peer):
        return pltpu.make_async_remote_copy(
            src_ref=src, dst_ref=dst, send_sem=send, recv_sem=recv, device_id=peer, device_id_type=MESH
        )

    first = [copy(x_ref, plane.at[d], s1.at[k], r1.at[k], peer) for k, peer in enumerate(in_plane)]
    second = [copy(depth.at[z], depth.at[z], s2.at[k], r2.at[k], peer) for k, peer in enumerate(along)]
    return first, second


def sum_first(nd, nz, x_ref, plane, *comm):
    start(sum_copies(nd, nz, x_ref, plane, *comm)[0])
    plane[lax.axis_index("dp")] = x_ref[...]


def sum_second(nd, nz, x_ref, plane, depth, *sems):
    first, second = sum_copies(nd, nz, x_ref, plane, depth, *sems)
    arrived(first)
    total = plane[0]
    for k in range(1, nd):
        total = total + plane[k]
    depth[lax.axis_index("chan")] = total
    start(second)


def sum_third(nd, nz, x_ref, plane, depth, *sems):
    first, second = sum_copies(nd, nz, x_ref, plane, depth, *sems)
    arrived(second)
    total = depth[0]
    for k in range(1, nz):
        total = total + depth[k]
    sent(first + second)
    return total


def sum_finish(nd, nz, x_ref, o_ref, *comm):
    sum_first(nd, nz, x_ref, *comm)
    sum_second(nd, nz, x_ref, *comm)
    o_ref[...] = sum_third(nd, nz, x_ref, *comm)


def sum_scratch(rows, nd, nz):
    return [
        VMEM((rows, LANES), f32),
        VMEM((nd, rows, LANES), f32),
        VMEM((nz, rows, LANES), f32),
        pltpu.SemaphoreType.DMA((nd,)),
        pltpu.SemaphoreType.DMA((nd,)),
        pltpu.SemaphoreType.DMA((nz,)),
        pltpu.SemaphoreType.DMA((nz,)),
    ]


def params(ident=None, limit=VLIMIT):
    if ident is None:
        return pltpu.CompilerParams(vmem_limit_bytes=VLIMIT)
    return pltpu.CompilerParams(vmem_limit_bytes=limit, collective_id=ident, has_side_effects=True)


def sum_kernel(nd, nz, x_ref, o_ref, *comm):
    sum_start(nd, nz)
    met(nd, nz)
    sum_finish(nd, nz, x_ref, o_ref, *comm)


def all_sum(x, nd, nz, ident):
    return pl.pallas_call(
        functools.partial(sum_kernel, nd, nz),
        out_shape=jax.ShapeDtypeStruct(x.shape, x.dtype),
        in_specs=[pl.BlockSpec(memory_space=VMEM)],
        out_specs=pl.BlockSpec(memory_space=VMEM),
        scratch_shapes=sum_scratch(x.shape[0], nd, nz)[1:],
        compiler_params=params(ident),
        name="all_sum",
    )(x)


def by_column(width):
    return (width // 2) % LANES == 0


def pad_rows(rows, width, nd):
    unit = 16 * (nd // 2 if by_column(width) else nd)
    return -(-rows // unit) * unit


def core_block(rows, width, core):
    if by_column(width):
        return 0, rows, pl.multiple_of(core * (width // 2), LANES), width // 2
    return pl.multiple_of(core * (rows // 2), 16), rows // 2, 0, width


def part(rows, width, nd, core, place):
    row, count, col, cols = core_block(rows, width, core)
    unit = count // (nd // 2)
    return pl.multiple_of(row + place * unit, 16), unit, col, cols


class Net:
    def __init__(self, nd, nz):
        self.nd, self.nz, self.nxy = nd, nz, nd // 2
        self.d = lax.axis_index("dp")
        self.z = lax.axis_index("chan")
        self.core = lax.rem(self.d, 2)
        self.place = self.d // 2
        self.far = [lax.rem(self.z + k, nz) for k in range(1, nz)]
        self.others = [lax.rem(self.place + k, self.nxy) for k in range(1, self.nxy)]
        self.along = [(self.d, zz) for zz in self.far]
        self.plane = [(2 * o + self.core, self.z) for o in self.others]
        self.twin = (2 * self.place + 1 - self.core, self.z)

    def copy(self, src, dst, sems, k, peer):
        return pltpu.make_async_remote_copy(
            src_ref=src,
            dst_ref=dst,
            send_sem=sems[0].at[k],
            recv_sem=sems[1].at[k],
            device_id=peer,
            device_id_type=MESH,
        )


def start(copies):
    for copy in copies:
        copy.start()


def arrived(copies):
    for copy in copies:
        copy.wait_recv()


def sent(copies):
    for copy in copies:
        copy.wait_send()


def pair(n):
    return [pltpu.SemaphoreType.DMA((n,)), pltpu.SemaphoreType.DMA((n,))]


def lanes(first, count):
    return pl.ds(pl.multiple_of(first, LANES), count)


def tall(first, count):
    return pl.ds(pl.multiple_of(first, 16), count)


def spot(ref, shape, zz, row, unit, col, cols):
    if len(ref.shape) == 3:
        return ref.at[zz, tall(row, unit), lanes(col, cols)]
    return ref.at[tall(row, unit), lanes(zz * shape[1] + col, cols)]


def shard_shape(full, nz):
    if len(full.shape) == 3:
        return full.shape[1:]
    return (full.shape[0], full.shape[1] // nz)


def own_copy(net, shape, src, dst, sem):
    return pltpu.make_async_copy(src, spot(dst, shape, net.z, 0, shape[0], 0, shape[1]), sem)


def gather_far(net, shape, src, dst, sems):
    rows, width = shape
    row, unit, col, cols = part(rows, width, net.nd, net.core, net.place)
    block = src.at[tall(row, unit), lanes(col, cols)]
    return [
        net.copy(block, spot(dst, shape, net.z, row, unit, col, cols), sems, k, peer)
        for k, peer in enumerate(net.along)
    ]


def gather_plane(net, shape, ref, sems, k):
    rows, width = shape
    row, unit, col, cols = part(rows, width, net.nd, net.core, net.place)
    block = spot(ref, shape, net.far[k], row, unit, col, cols)
    n = net.nxy - 1
    return [net.copy(block, block, sems, k * n + q, peer) for q, peer in enumerate(net.plane)]


def gather_twin(net, shape, ref, sems, k):
    rows, width = shape
    row, unit, col, cols = core_block(rows, width, net.core)
    block = spot(ref, shape, net.far[k], row, unit, col, cols)
    return [net.copy(block, block, sems, k, net.twin)]


def late_count(nz):
    return max(1, (nz - 1) // 3)


def some(stage, net, shape, ref, sems, shards):
    return [copy for k in shards for copy in stage(net, shape, ref, sems, k)]


def every(stage, net, shape, ref, sems):
    return [copy for k in range(net.nz - 1) for copy in stage(net, shape, ref, sems, k)]


def squares_of(ref, rows):
    step_rows = 16 if ref.dtype == bf16 else 8
    whole_rows = rows // step_rows * step_rows

    def step(i, total):
        value = ref[pl.ds(pl.multiple_of(i * step_rows, step_rows), step_rows), :].astype(f32)
        return total + value * value

    total = jnp.sum(lax.fori_loop(0, whole_rows // step_rows, step, jnp.zeros((step_rows, ref.shape[1]), f32)))
    if whole_rows < rows:
        last = ref[whole_rows:rows, :].astype(f32)
        total = total + jnp.sum(last * last)
    return total


def row_of(total):
    lane = lax.broadcasted_iota(jnp.int32, (1, LANES), 1)
    return jnp.where(lane == 0, total, 0.0)


def first_kernel(nd, nz, shape, shape_b, block_ref, head_ref, hside_ref, side_ref, full, full_b, side, gain, kh, kc, squares, wide, tall_h, tall_s, kb, low, side_buf, gain_buf, far_s, far_r, plane_s, plane_r, twin_s, twin_r, side_s, side_r, gain_s, gain_r, later_s, later_r, local):
    net = Net(nd, nz)
    signal(net.along + net.plane + [net.twin])
    rows = shape[0]
    total_rows = block_ref.shape[0]
    fetch = [
        pltpu.make_async_copy(block_ref.at[pl.ds(0, rows)], wide.at[pl.ds(0, rows)], local.at[0]),
        pltpu.make_async_copy(
            block_ref.at[pl.ds(rows, total_rows - rows)], wide.at[pl.ds(rows, total_rows - rows)], local.at[1]
        ),
        pltpu.make_async_copy(hside_ref, tall_s, local.at[2]),
        pltpu.make_async_copy(head_ref, tall_h, local.at[3]),
    ]
    fetch[0].start()
    fetch[0].wait()
    start(fetch[1:])

    @pl.loop(0, rows // 16)
    def _(i):
        at = tall(i * 16, 16)
        low[at, :] = wide[at, :].astype(bf16)

    own = own_copy(net, shape, low, full, local.at[4])
    own.start()
    pl.semaphore_wait(pltpu.get_barrier_semaphore(), nz - 1 + nd // 2)
    far = gather_far(net, shape, low, full, (far_s, far_r))
    start(far)
    side_buf[net.z] = jnp.transpose(side_ref[...])
    sides = [
        net.copy(side_buf.at[net.z], side_buf.at[net.z], (side_s, side_r), k, peer)
        for k, peer in enumerate(net.along)
    ]
    start(sides)
    fetch[2].wait()
    gain_buf[net.z] = jnp.transpose(tall_s[:, 0:LANES])[0:8]
    gains = [
        net.copy(gain_buf.at[net.z], gain_buf.at[net.z], (gain_s, gain_r), k, peer)
        for k, peer in enumerate(net.along)
    ]
    start(gains)
    fetch[1].wait()
    first = WIDTH_IN + TAPS
    for i in range(WIDTH_OUT // 16):
        kb[16 * i : 16 * (i + 1), :] = wide[first + 16 * i : first + 16 * (i + 1), :].astype(bf16)
    own_b = own_copy(net, shape_b, kb, full_b, local.at[5])
    own_b.start()
    planes = []
    for k in range(nz - 1):
        arrived([far[nz - 2 - k]])
        planes.append(gather_plane(net, shape, full, (plane_s, plane_r), k))
        start(planes[k])
    later = gather_far(net, shape_b, kb, full_b, (later_s, later_r))
    start(later)
    fetch[3].wait()

    @pl.loop(0, WIDTH_OUT // 16)
    def _(i):
        at = tall(i * 16, 16)
        kh[at, :] = tall_h[at, :].astype(bf16)

    for i in range(tall_s.shape[0] // 16):
        value = tall_s[16 * i : 16 * (i + 1), 2 : 2 + CLASSES]
        kc[16 * i : 16 * (i + 1), :] = jnp.concatenate(
            [value, jnp.zeros((16, CLASS_PAD - CLASSES), f32)], axis=1
        ).astype(bf16)
    squares[...] = jnp.zeros_like(squares)
    for k, (ref, count) in enumerate(
        ((wide, total_rows), (side_ref, side_ref.shape[0]), (tall_h, WIDTH_OUT), (tall_s, tall_s.shape[0]))
    ):
        squares[k : k + 1, :] = row_of(squares_of(ref, count))
    twins = []
    for k in range(nz - 1):
        arrived(planes[k])
        twins.append(gather_twin(net, shape, full, (twin_s, twin_r), k))
        start(twins[k])
    arrived(sides + gains)
    side[...] = jnp.zeros_like(side)
    side[0 : side_ref.shape[1], :] = jnp.concatenate([side_buf[k] for k in range(nz)], axis=1)
    gain[...] = jnp.concatenate([gain_buf[k] for k in range(nz)], axis=1)
    for k in range(nz - 1):
        arrived(twins[k])
    arrived(later)
    sent(far + sides + gains + later)
    for k in range(nz - 1):
        sent(planes[k] + twins[k])
    own.wait()
    own_b.wait()


def first_gather(block, head_w, head_side, side, nd, nz, ident):
    shape = (pad_rows(WIDTH_IN + TAPS, block.shape[1], nd), block.shape[1])
    shape_b = (pad_rows(WIDTH_OUT, block.shape[1], nd), block.shape[1])
    shape_h = (pad_rows(WIDTH_OUT, head_w.shape[1], nd), head_w.shape[1])
    shape_c = (pad_rows(head_side.shape[0], CLASS_PAD, nd), CLASS_PAD)
    hbm = pl.BlockSpec(memory_space=pltpu.HBM)
    vmem = pl.BlockSpec(memory_space=VMEM)
    own_head = head_side.shape[0]
    return pl.pallas_call(
        functools.partial(first_kernel, nd, nz, shape, shape_b),
        out_shape=[
            jax.ShapeDtypeStruct((shape[0], nz * shape[1]), bf16),
            jax.ShapeDtypeStruct((shape_b[0], nz * shape_b[1]), bf16),
            jax.ShapeDtypeStruct((104, nz * side.shape[0]), f32),
            jax.ShapeDtypeStruct((8, nz * own_head), f32),
            jax.ShapeDtypeStruct(shape_h, bf16),
            jax.ShapeDtypeStruct(shape_c, bf16),
            jax.ShapeDtypeStruct((8, LANES), f32),
        ],
        in_specs=[hbm, hbm, hbm, vmem],
        out_specs=[hbm] * 2 + [vmem] * 5,
        scratch_shapes=[
            VMEM(block.shape, f32),
            VMEM(head_w.shape, f32),
            VMEM(head_side.shape, f32),
            VMEM(shape_b, bf16),
            VMEM(shape, bf16),
            VMEM((nz, side.shape[1], side.shape[0]), f32),
            VMEM((nz, 8, own_head), f32),
        ]
        + pair(nz - 1)
        + pair((nz - 1) * (nd // 2 - 1))
        + pair(nz - 1)
        + pair(nz - 1) * 3
        + [pltpu.SemaphoreType.DMA((6,))],
        compiler_params=params(ident),
        name="first_gather",
    )(block, head_w, head_side, side)


def reduce_sizes(rows, width, nd):
    unit, cols = (rows, width // 2) if by_column(width) else (rows // 2, width)
    return unit, cols, unit // (nd // 2)


def reduce_twin(net, shape, g_ref, twin_buf, sems, k):
    row, unit, col, cols = core_block(shape[0], shape[1], 1 - net.core)
    return net.copy(
        g_ref.at[tall(row, unit), lanes(k * shape[1] + col, cols)], twin_buf.at[k], sems, k, net.twin
    )


def reduce_add(net, shape, g_ref, half, twin_buf, k):
    row, unit, col, cols = core_block(shape[0], shape[1], net.core)

    @pl.loop(0, unit // 16)
    def _(i):
        at = tall(i * 16, 16)
        mine = g_ref[tall(row + i * 16, 16), lanes(k * shape[1] + col, cols)]
        half[k, at, :] = (mine.astype(f32) + twin_buf[k, at, :].astype(f32)).astype(bf16)


def reduce_plane(net, shape, half, plane_buf, sems, k, base, shift):
    size = reduce_sizes(*shape, net.nd)[2]
    n = net.nxy - 1
    return [
        net.copy(half.at[k - shift, tall(o * size, size)], plane_buf.at[q, k - base], sems, (k - base) * n + q, net.plane[q])
        for q, o in enumerate(net.others)
    ]


def reduce_plane_sum(net, shape, half, plane_buf, out, k, base, shift):
    size = reduce_sizes(*shape, net.nd)[2]

    @pl.loop(0, size // 16)
    def _(i):
        at = tall(i * 16, 16)
        total = half[k - shift, tall(net.place * size + i * 16, 16), :].astype(f32)
        for q in range(net.nxy - 1):
            total = total + plane_buf[q, k - base, at, :].astype(f32)
        out[k, at, :] = total.astype(bf16)


def reduce_far(net, sums, depth_buf, sems):
    return [net.copy(sums.at[zz], depth_buf.at[k], sems, k, net.along[k]) for k, zz in enumerate(net.far)]


def reduce_far_sum(net, shape, sums, depth_buf, piece):
    @pl.loop(0, reduce_sizes(*shape, net.nd)[2] // 16)
    def _(i):
        at = tall(i * 16, 16)
        total = sums[net.z, at, :].astype(f32)
        for q in range(net.nz - 1):
            total = total + depth_buf[q, at, :].astype(f32)
        piece[at, :] = total.astype(bf16)


def spread_block(net, shape, out):
    row, unit, col, cols = part(shape[0], shape[1], net.nd, net.core, net.place)
    return out.at[tall(row, unit), lanes(col, cols)]


def spread_plane(net, shape, piece, out, sems):
    block = spread_block(net, shape, out)
    return [net.copy(piece, block, sems, q, peer) for q, peer in enumerate(net.plane)]


def spread_twin(net, shape, out, sems):
    row, unit, col, cols = core_block(shape[0], shape[1], net.core)
    block = out.at[tall(row, unit), lanes(col, cols)]
    return [net.copy(block, block, sems, 0, net.twin)]


def twin_scratch(shape, nd, nz):
    unit, cols, size = reduce_sizes(*shape, nd)
    return [VMEM((shape[0], nz * shape[1]), bf16), VMEM((nz, unit, cols), bf16)] + pair(nz)


def plane_scratch(shape, nd, count):
    unit, cols, size = reduce_sizes(*shape, nd)
    return [VMEM((nd // 2 - 1, count, size, cols), bf16)] + pair(count * (nd // 2 - 1))


def half_shape(shape, nd, nz):
    unit, cols, size = reduce_sizes(*shape, nd)
    return (nz, unit, cols)


def part_shape(shape, nd, nz):
    unit, cols, size = reduce_sizes(*shape, nd)
    return (nz, size, cols)


def ready(shape, k):
    return max(2, -(-(k + 1) * shape[1] // (LANES * EXPERTS)))


class Steps:
    def __init__(self):
        self.steps = {}

    def at(self, step, action):
        self.steps.setdefault(step, []).append(action)

    def emit(self, now, last):
        for step in sorted(self.steps):
            if step < last:

                @pl.when(now == step)
                def _(step=step):
                    for action in self.steps[step]:
                        action()

    def end(self, last):
        for step in sorted(self.steps):
            if step >= last:
                for action in self.steps[step]:
                    action()


def far_scratch(shape, nd, nz):
    unit, cols, size = reduce_sizes(*shape, nd)
    return [VMEM((nz - 1, size, cols), bf16)] + pair(nz - 1)


def spread_scratch(shape, nd, nz):
    return [pltpu.SemaphoreType.DMA((1,))] + pair(nd // 2 - 1) + pair(1)


def piece_shape(shape, nd):
    unit, cols, size = reduce_sizes(*shape, nd)
    return (size, cols)


class Twin:
    def __init__(self, net, shape, half, g_ref, twin_buf, ts, tr):
        self.net, self.shape, self.half, self.g, self.buf, self.sems = net, shape, half, g_ref, twin_buf, (ts, tr)

    def copy(self, k):
        return reduce_twin(self.net, self.shape, self.g, self.buf, self.sems, k)

    def begin(self, k):
        self.copy(k).start()

    def add(self, k):
        self.copy(k).wait_recv()
        reduce_add(self.net, self.shape, self.g, self.half, self.buf, k)

    def finish(self):
        for k in range(self.net.nz):
            self.copy(k).wait_send()


class Plane:
    def __init__(self, net, shape, half, out, base, count, buf, ps, pr, shift=0):
        self.net, self.shape, self.half, self.out = net, shape, half, out
        self.shards, self.base, self.buf, self.sems = range(base, base + count), base, buf, (ps, pr)
        self.shift = shift

    def copies(self, k):
        return reduce_plane(self.net, self.shape, self.half, self.buf, self.sems, k, self.base, self.shift)

    def begin(self, k):
        start(self.copies(k))

    def add(self, then=None):
        for k in self.shards:
            arrived(self.copies(k))
            reduce_plane_sum(self.net, self.shape, self.half, self.buf, self.out, k, self.base, self.shift)
            if then is not None:
                then(k)

    def finish(self):
        for k in self.shards:
            sent(self.copies(k))


class Far:
    def __init__(self, net, shape, sums, piece, buf, fs, fr):
        self.net, self.shape, self.sums, self.piece, self.buf, self.sems = net, shape, sums, piece, buf, (fs, fr)

    def copies(self):
        return reduce_far(self.net, self.sums, self.buf, self.sems)

    def send(self, k):
        net = self.net
        slot = lax.rem(k - net.z - 1 + net.nz, net.nz)

        @pl.when(net.z != k)
        def _():
            net.copy(self.sums.at[k], self.buf.at[slot], self.sems, slot, (net.d, k)).start()

    def add(self):
        arrived(self.copies())
        reduce_far_sum(self.net, self.shape, self.sums, self.buf, self.piece)

    def finish(self):
        sent(self.copies())


class Spread:
    def __init__(self, net, shape, piece, out, local, ps, pr, ts, tr):
        self.net, self.shape, self.piece, self.out, self.local = net, shape, piece, out, local
        self.plane_sems, self.twin_sems = (ps, pr), (ts, tr)

    def own(self):
        return pltpu.make_async_copy(self.piece, spread_block(self.net, self.shape, self.out), self.local.at[0])

    def plane(self):
        return spread_plane(self.net, self.shape, self.piece, self.out, self.plane_sems)

    def twin(self):
        return spread_twin(self.net, self.shape, self.out, self.twin_sems)

    def begin(self):
        self.own().start()
        start(self.plane())

    def cross(self):
        arrived(self.plane())
        self.own().wait()
        start(self.twin())

    def finish(self):
        arrived(self.twin())
        sent(self.plane() + self.twin())


def up_to(size):
    return -(-size // LANES) * LANES


def share_width(lines, nz):
    one = [0]
    for x in lines[0], lines[2], lines[3]:
        one.append(one[-1] + up_to(x.shape[1] // nz))
    for _ in range(3):
        one.append(one[-1] + LANES)
    two = [0]
    for x in lines[1], lines[4], lines[5]:
        two.append(two[-1] + up_to(x.shape[1]))
    return one, two, max(one[-1], two[-1])


def share_scratch(width, nd, nz):
    return (
        [VMEM((nz, 8, width), f32), pltpu.SemaphoreType.DMA((1,))]
        + pair(nz - 1)
        + pair(nd // 2 - 1)
        + pair(nd // 2)
    )


def fit(x, width):
    if x.shape[1] == width:
        return x
    return jnp.concatenate([x, jnp.zeros((x.shape[0], width - x.shape[1]), f32)], axis=1)


class Share:
    def __init__(self, net, rows_all, lines, local, fs, fr, ps, pr, ts, tr):
        self.net, self.rows, self.lines, self.local = net, rows_all, lines, local
        self.far_sems, self.plane_sems, self.twin_sems = (fs, fr), (ps, pr), (ts, tr)
        self.me = net.d * net.nz + net.z

    def fill(self, nb, cut, narrow, wide):
        width = self.lines.shape[2]
        self.lines[...] = jnp.zeros_like(self.lines)
        two = fit(jnp.concatenate([fit(x, up_to(x.shape[1])) for x in wide], axis=1), width)[:nb]
        last = [fit(x, LANES) for x in narrow]
        for k in range(self.net.nz):
            parts = []
            for x in cut:
                own = x.shape[1] // self.net.nz
                parts.append(fit(x[:, k * own : (k + 1) * own], up_to(own)))
            one = fit(jnp.concatenate(parts + last, axis=1), width)[:nb]
            self.lines[k, 0 : 2 * nb, :] = jnp.concatenate([one, two], axis=0)

    def far_copies(self):
        net = self.net
        return [
            net.copy(self.lines.at[zz], self.rows.at[self.me], self.far_sems, k, net.along[k])
            for k, zz in enumerate(net.far)
        ]

    def plane_copies(self):
        net = self.net
        block = self.rows.at[pl.ds(net.d * net.nz, net.nz)]
        return [net.copy(block, block, self.plane_sems, q, peer) for q, peer in enumerate(net.plane)]

    def twin_copies(self):
        net = self.net
        out = []
        for o in range(net.nxy):
            block = self.rows.at[pl.ds((2 * o + net.core) * net.nz, net.nz)]
            out.append(net.copy(block, block, self.twin_sems, o, net.twin))
        return out

    def far(self):
        start(self.far_copies())
        self.own().start()

    def own(self):
        return pltpu.make_async_copy(self.lines.at[self.net.z], self.rows.at[self.me], self.local.at[0])

    def plane(self):
        arrived(self.far_copies())
        self.own().wait()
        start(self.plane_copies())

    def twin(self):
        arrived(self.plane_copies())
        start(self.twin_copies())

    def finish(self):
        arrived(self.twin_copies())
        sent(self.far_copies() + self.plane_copies() + self.twin_copies())


def build_mix(gates, nb, ref):
    deep = LANES * EXPERTS
    row = lax.broadcasted_iota(jnp.int32, (deep, EXPERTS), 0)
    col = lax.broadcasted_iota(jnp.int32, (deep, EXPERTS), 1)
    pick = jnp.where((row & (EXPERTS - 1)) == col, 1.0, 0.0).astype(f32)
    row = lax.broadcasted_iota(jnp.int32, (deep, LANES), 0)
    col = lax.broadcasted_iota(jnp.int32, (deep, LANES), 1)
    same = (row >> 3) == col
    for b in range(nb):
        spread = jnp.broadcast_to(gates[b : b + 1, :], (LANES, EXPERTS))
        value = jnp.where(same, dot(pick, spread, NT, highest), 0.0)
        high = value.astype(bf16)
        ref[:, b * LANES : (b + 1) * LANES] = high
        ref[:, (nb + b) * LANES : (nb + b + 1) * LANES] = (value - high.astype(f32)).astype(bf16)


def mix_kernels(kernels, mix):
    both = dot(kernels, mix)
    half = both.shape[1] // 2
    return both[:, :half] + both[:, half:]


def gate_sums(rows):
    deep = LANES * EXPERTS
    row = lax.broadcasted_iota(jnp.int32, (deep, EXPERTS), 0)
    col = lax.broadcasted_iota(jnp.int32, (deep, EXPERTS), 1)
    pick = jnp.where((row & (EXPERTS - 1)) == col, 1.0, 0.0).astype(f32)
    return dot(rows, pick, NN, highest)


def gate_rows(grad, kernel_block):
    both = dot(grad, kernel_block, TN)
    row = lax.broadcasted_iota(jnp.int32, both.shape, 0)
    col = lax.broadcasted_iota(jnp.int32, both.shape, 1)
    return rsum(jnp.where(row == (col >> 3), both, 0.0))


def norm_rows(stats, chunk, chunks, total):
    mean = stats[pl.ds(chunk, 1), :] / total
    var = stats[pl.ds(chunks + chunk, 1), :] / total - mean * mean
    return mean, lax.rsqrt(var + eps_norm)


def whole(shape):
    return pl.BlockSpec(shape, lambda *_: (0,) * len(shape), pipeline_mode=pl.Buffered(1))


def image(b):
    return pl.ds(pl.multiple_of(b * PIXELS, PIXELS), PIXELS)


def shifted(value, step):
    if step == 0:
        return value
    col = lax.broadcasted_iota(jnp.int32, value.shape, 0) & (MAP_SIDE - 1)
    moved = pltpu.roll(value, (-step) % PIXELS, 0)
    keep = (col + step >= 0) & (col + step < MAP_SIDE)
    return jnp.where(keep, moved, 0.0)


def stage_kernel(
    nd,
    nz,
    nb,
    chunks,
    shapes,
    kern_ref,
    images,
    mask,
    mask_rows,
    counts,
    route,
    side,
    in_b,
    kh,
    kc,
    pre_out,
    taps_out,
    out,
    stats_all,
    sums_all,
    mix,
    gates,
    pooled,
    full_b,
    full_h,
    full_c,
    pre,
    taps,
    buf,
    held,
    early,
    late,
    sums,
    *comm,
):
    step = pl.program_id(0)
    comm_early, comm_late, comm_two, sems = comm[0:6], comm[6:12], comm[12:18], comm[18:]
    net = Net(nd, nz)
    few = late_count(nz)
    cut = chunks // 2
    groups = [[k for k in range(nz - 1) if 3 * k // (nz - 1) == g] for g in range(3)]

    def far_h():
        return gather_far(net, shapes[1], kh, full_h, sems[0:2])

    def far_c():
        return gather_far(net, shapes[2], kc, full_c, sems[2:4])

    def planes_b(k):
        return gather_plane(net, shapes[0], full_b, sems[4:6], k)

    def planes_h():
        return some(gather_plane, net, shapes[1], full_h, sems[6:8], range(few))

    def twins_b(k):
        return gather_twin(net, shapes[0], full_b, sems[8:10], k)

    def own():
        return [
            own_copy(net, shapes[1], kh, full_h, sems[10].at[0]),
            own_copy(net, shapes[2], kc, full_c, sems[10].at[1]),
        ]

    def b_planes(group):
        for k in groups[group]:
            start(planes_b(k))

    def begin():
        met(nd, nz)
        b_planes(0)
        start(far_h() + own())

    def early_sum():
        sum_first(nd, nz, early, *comm_early)

    def early_second():
        sum_second(nd, nz, early, *comm_early)

    def early_third():
        stats_all[...] = sum_third(nd, nz, early, *comm_early)
        sum_first(nd, nz, late, *comm_late)

    def late_second():
        sum_second(nd, nz, late, *comm_late)

    def late_third():
        stats_all[...] += sum_third(nd, nz, late, *comm_late)

    def h_planes():
        arrived(far_h())
        start(planes_h() + far_c())

    def b_twins():
        for k in range(nz - 1):
            arrived(planes_b(k))
            start(twins_b(k))

    @pl.when(step == 0)
    def _():
        sum_start(nd, nz)
        early[...] = jnp.zeros_like(early)
        late[...] = jnp.zeros_like(late)
        sums[...] = jnp.zeros_like(sums)
        early[2 * chunks : 2 * chunks + 1, :] = rsum(counts[...])
        early[2 * chunks + 1 : 2 * chunks + 2, :] = rsum(jnp.where(counts[...] > 0.0, 1.0, 0.0))
        pool = dot(mask_rows[...], images[...]) / jnp.maximum(counts[:, 0:1], 1.0)
        pooled[...] = pool
        gate = sig(dot(pool, route[...], NN, highest))
        gates[...] = gate
        build_mix(gate, nb, mix)

    steps = Steps()
    steps.at(1, begin)
    steps.at(cut, early_sum)
    steps.at(cut + 2, early_second)
    steps.at(cut + 3, functools.partial(b_planes, 1))
    steps.at(chunks, early_third)
    steps.at(chunks + 2, late_second)
    steps.at(chunks + 2, functools.partial(b_planes, 2))
    steps.at(chunks + cut, late_third)
    steps.at(chunks + cut, h_planes)
    steps.at(2 * chunks - 2, b_twins)
    steps.emit(step, 2 * chunks)

    @pl.when(step < chunks)
    def _():
        j = step
        mixed = mix_kernels(kern_ref[...], mix[...])
        one = jnp.zeros((1, LANES), f32)
        two = jnp.zeros((1, LANES), f32)
        for b in range(nb):
            at = slice(b * PIXELS, (b + 1) * PIXELS)
            lane = slice(b * LANES, (b + 1) * LANES)
            taps[j, b] = mixed[WIDTH_IN : WIDTH_IN + 32, lane]
            taps_out[b] = mixed[WIDTH_IN : WIDTH_IN + 32, lane]
            value = dot(images[at, :], mixed[:WIDTH_IN, lane].astype(bf16))
            pre[j, at, :] = value
            pre_out[at, :] = value
            masked = mask[at, :] * value
            one = one + rsum(masked)
            two = two + rsum(masked * value)

        @pl.when(j < cut)
        def _():
            early[pl.ds(j, 1), :] = one
            early[pl.ds(chunks + j, 1), :] = two

        @pl.when(j >= cut)
        def _():
            late[pl.ds(j, 1), :] = one
            late[pl.ds(chunks + j, 1), :] = two

    @pl.when(step >= chunks)
    def _():
        j = step - chunks
        mean, rstd = norm_rows(stats_all, j, chunks, stats_all[2 * chunks : 2 * chunks + 1, :])
        scale = rstd * side[2 * SQUEEZE : 2 * SQUEEZE + 1, :]
        bias = side[2 * SQUEEZE + 1 : 2 * SQUEEZE + 2, :]
        held[...] = jnp.zeros_like(held)

        @pl.loop(0, nb)
        def _(b):
            at = image(b)
            normed = (pre[j, at, :] - mean) * scale + bias
            act = normed * sig(normed) * mask[at, :]
            for s in range(KERNEL):
                buf[s] = shifted(act, s - KERNEL // 2)
            taps_now = [jnp.broadcast_to(taps[j, b, t : t + 1, :], (MAP_SIDE, LANES)) for t in range(TAPS)]
            acc = [None] * MAP_SIDE
            for y in range(MAP_SIDE):
                for s in range(KERNEL):
                    x = buf[s, y * MAP_SIDE : (y + 1) * MAP_SIDE, :]
                    for r in range(KERNEL):
                        i = y - r + KERNEL // 2
                        if 0 <= i < MAP_SIDE:
                            term = taps_now[r * KERNEL + s] * x
                            acc[i] = term if acc[i] is None else acc[i] + term
                done = [y - 2] if y < MAP_SIDE - 1 else [y - 2, y - 1, y]
                for i in done:
                    if i >= 0:
                        out[pl.ds(pl.multiple_of(b * PIXELS + i * MAP_SIDE, MAP_SIDE), MAP_SIDE), :] = acc[i]
            value = out[at, :]
            masked = mask[at, :] * value
            held[0:1, :] += rsum(masked)
            held[1:2, :] += rsum(masked * value)

        sums[pl.ds(j, 1), :] = held[0:1, :]
        sums[pl.ds(chunks + j, 1), :] = held[1:2, :]

    @pl.when(step == 2 * chunks - 1)
    def _():
        sum_finish(nd, nz, sums, sums_all, *comm_two)
        for k in range(nz - 1):
            arrived(twins_b(k))
            sent(planes_b(k) + twins_b(k))
        arrived(planes_h() + far_c())
        sent(far_h() + planes_h() + far_c())
        for copy in own():
            copy.wait()


def first_stage(kern, images, mask, mask_rows, counts, route, side, full_b, kh, kc, nb, width, nd, nz, ident):
    chunks = width // LANES
    rows = nb * PIXELS
    deep = LANES * EXPERTS
    planes = (nz - 1) * (nd // 2 - 1)
    shapes = (shard_shape(full_b, nz), kh.shape, kc.shape)
    hbm = pl.BlockSpec(memory_space=pltpu.HBM)
    before = lambda t: jnp.minimum(t, chunks - 1)
    after = lambda t: jnp.maximum(t - chunks, 0)
    return pl.pallas_call(
        functools.partial(stage_kernel, nd, nz, nb, chunks, shapes),
        grid=(2 * chunks,),
        out_shape=[
            jax.ShapeDtypeStruct((rows, width), f32),
            jax.ShapeDtypeStruct((nb, 32, width), f32),
            jax.ShapeDtypeStruct((rows, width), f32),
            jax.ShapeDtypeStruct((24, LANES), f32),
            jax.ShapeDtypeStruct((24, LANES), f32),
            jax.ShapeDtypeStruct((deep, 2 * nb * LANES), bf16),
            jax.ShapeDtypeStruct((8, EXPERTS), f32),
            jax.ShapeDtypeStruct((8, WIDTH_IN), f32),
            jax.ShapeDtypeStruct(full_b.shape, bf16),
            jax.ShapeDtypeStruct((kh.shape[0], nz * kh.shape[1]), bf16),
            jax.ShapeDtypeStruct((nz,) + kc.shape, bf16),
        ],
        in_specs=[
            pl.BlockSpec((kern.shape[0], deep), lambda t: (0, before(t))),
            whole(images.shape),
            whole(mask.shape),
            whole(mask_rows.shape),
            whole(counts.shape),
            whole(route.shape),
            pl.BlockSpec((side.shape[0], LANES), lambda t: (0, after(t))),
            hbm,
            whole(kh.shape),
            whole(kc.shape),
        ],
        out_specs=[
            pl.BlockSpec((rows, LANES), lambda t: (0, before(t))),
            pl.BlockSpec((nb, 32, LANES), lambda t: (0, 0, before(t))),
            pl.BlockSpec((rows, LANES), lambda t: (0, after(t))),
            whole((24, LANES)),
            whole((24, LANES)),
            whole((deep, 2 * nb * LANES)),
            whole((8, EXPERTS)),
            whole((8, WIDTH_IN)),
            hbm,
            hbm,
            hbm,
        ],
        scratch_shapes=[
            VMEM((chunks, rows, LANES), f32),
            VMEM((chunks, nb, 32, LANES), f32),
            VMEM((KERNEL, PIXELS, LANES), f32),
            VMEM((8, LANES), f32),
            VMEM((24, LANES), f32),
            VMEM((24, LANES), f32),
            VMEM((24, LANES), f32),
        ]
        + sum_scratch(24, nd, nz)[1:] * 3
        + pair(nz - 1) * 2
        + pair(planes) * 2
        + pair(nz - 1)
        + [pltpu.SemaphoreType.DMA((2,))],
        input_output_aliases={7: 8},
        compiler_params=params(ident),
        name="first_stage",
    )(kern, images, mask, mask_rows, counts, route, side, full_b, kh, kc)


def store_wide(ref, row, value):
    width = value.shape[1]
    for k in range(-(-width // LANES)):
        lanes = min(LANES, width - k * LANES)
        ref[row + k : row + k + 1, :lanes] = value[:, k * LANES : k * LANES + lanes]


def load_wide(ref, row, width):
    parts = []
    for k in range(-(-width // LANES)):
        lanes = min(LANES, width - k * LANES)
        parts.append(ref[row + k : row + k + 1, :lanes])
    return jnp.concatenate(parts, axis=1)


OUT_CHUNKS = -(-WIDTH_OUT // LANES)


def project_kernel(nd, nz, nb, chunks, shapes, dpre, mask, side, stats, totals, counts, sq_bias, kern, mix, in_h, excited, proj, pooled, gate_out, squeezed, sums_all, mixed, full_h, act, exc, sums, *comm):
    phase = pl.program_id(0)
    j = pl.program_id(1)
    sems = comm[6:]
    comm = comm[:6]
    net = Net(nd, nz)

    few = late_count(nz)

    def twins(shards):
        return some(gather_twin, net, shapes[0], full_h, sems[0:2], shards)

    def planes():
        return some(gather_plane, net, shapes[0], full_h, sems[2:4], range(few, nz - 1))


    @pl.when((phase == 0) & (j == 0))
    def _():
        sum_start(nd, nz)

    @pl.when((phase == 0) & (j == 1))
    def _():
        met(nd, nz)
        start(planes() + twins(range(few)))

    @pl.when((phase == 1) & (j == chunks - 2))
    def _():
        arrived(planes())
        start(twins(range(few, nz - 1)))
    total = totals[2 * chunks : 2 * chunks + 1, :]

    @pl.when((phase == 0) & (j == 0))
    def _():
        squeezed[...] = jnp.zeros_like(squeezed)
        pooled[...] = jnp.zeros_like(pooled)
        sums[...] = jnp.zeros_like(sums)

    lane = pl.ds(pl.multiple_of(j * LANES, LANES), LANES)

    @pl.when(phase == 0)
    def _():
        both = mix_kernels(kern[...], mix[...])
        for b in range(nb):
            mixed[b, :, lane] = both[:, b * LANES : (b + 1) * LANES].astype(bf16)
        mean, rstd = norm_rows(stats, j, chunks, total)
        scale = rstd * side[2 * SQUEEZE + 2 : 2 * SQUEEZE + 3, :]
        bias = side[2 * SQUEEZE + 3 : 2 * SQUEEZE + 4, :]
        for b in range(nb):
            at = slice(b * PIXELS, (b + 1) * PIXELS)
            normed = (dpre[at, :] - mean) * scale + bias
            value = normed * sig(normed) * mask[at, :]
            act[j, at, :] = value
            pooled[b : b + 1, lane] = rsum(value) / jnp.maximum(counts[b : b + 1, :], 1.0)
        squeezed[...] += dot(pooled[:, lane], side[0:SQUEEZE, :], NT, highest)

    @pl.when(phase == 1)
    def _():
        before = squeezed[...] + sq_bias[...]
        gate = sig(
            dot(before * sig(before), side[SQUEEZE : 2 * SQUEEZE, :], NN, highest)
            + side[2 * SQUEEZE + 4 : 2 * SQUEEZE + 5, :]
        )
        gate_out[:, lane] = gate
        for b in range(nb):
            at = slice(b * PIXELS, (b + 1) * PIXELS)
            value = (act[j, at, :] * gate[b : b + 1, :]).astype(bf16)
            excited[at, :] = value
            exc[at, lane] = value

    @pl.when((phase == 1) & (j == chunks - 1))
    def _():
        one = jnp.zeros((1, WIDTH_OUT), f32)
        two = jnp.zeros((1, WIDTH_OUT), f32)
        for b in range(nb):
            at = slice(b * PIXELS, (b + 1) * PIXELS)
            value = dot(exc[at, :], mixed[b], NT)
            proj[at, :] = value
            masked = mask[at, 0:1] * value
            one = one + rsum(masked)
            two = two + rsum(masked * value)
        store_wide(sums, 0, one)
        store_wide(sums, OUT_CHUNKS, two)

    @pl.when((phase == 1) & (j == chunks - 1))
    def _():
        sum_finish(nd, nz, sums, sums_all, *comm)
        arrived(twins(range(nz - 1)))
        sent(planes() + twins(range(nz - 1)))


def project(dpre, mask, side, stats, totals, counts, sq_bias, full_b, mix, full_h, nb, nd, nz, ident):
    rows, width = dpre.shape
    chunks = width // LANES
    deep = LANES * EXPERTS
    later = (full_h,)
    shapes = tuple(shard_shape(k, nz) for k in later)
    hbm = pl.BlockSpec(memory_space=pltpu.HBM)
    return pl.pallas_call(
        functools.partial(project_kernel, nd, nz, nb, chunks, shapes),
        grid=(2, chunks),
        out_shape=[
            jax.ShapeDtypeStruct((rows, width), bf16),
            jax.ShapeDtypeStruct((rows, WIDTH_OUT), f32),
            jax.ShapeDtypeStruct((8, width), f32),
            jax.ShapeDtypeStruct((8, width), f32),
            jax.ShapeDtypeStruct((8, SQUEEZE), f32),
            jax.ShapeDtypeStruct((8, LANES), f32),
            jax.ShapeDtypeStruct((nb, WIDTH_OUT, width), bf16),
        ]
        + [jax.ShapeDtypeStruct(k.shape, bf16) for k in later],
        in_specs=[
            pl.BlockSpec((rows, LANES), lambda p, j: (0, jnp.where(p == 0, j, chunks - 1))),
            whole(mask.shape),
            pl.BlockSpec((side.shape[0], LANES), lambda p, j: (0, j)),
            whole(stats.shape),
            whole(totals.shape),
            whole(counts.shape),
            whole(sq_bias.shape),
            pl.BlockSpec((WIDTH_OUT, deep), lambda p, j: (0, jnp.where(p == 0, j, chunks - 1))),
            whole(mix.shape),
        ]
        + [hbm],
        out_specs=[
            pl.BlockSpec((rows, LANES), lambda p, j: (0, jnp.where(p == 0, 0, j))),
            whole((rows, WIDTH_OUT)),
            whole((8, width)),
            whole((8, width)),
            whole((8, SQUEEZE)),
            whole((8, LANES)),
            whole((nb, WIDTH_OUT, width)),
        ]
        + [hbm],
        scratch_shapes=[VMEM((chunks, rows, LANES), f32), VMEM((rows, width), bf16)]
        + sum_scratch(8, nd, nz)
        + pair(nz - 1)
        + pair((nz - 1) * (nd // 2 - 1)),
        input_output_aliases={9: 7},
        compiler_params=params(ident),
        name="project",
    )(dpre, mask, side, stats, totals, counts, sq_bias, full_b, mix, *later)


def out_norm(sums, total):
    mean = load_wide(sums, 0, WIDTH_OUT) / total
    var = load_wide(sums, OUT_CHUNKS, WIDTH_OUT) / total - mean * mean
    return mean, lax.rsqrt(var + eps_norm)


def head_kernel(nd, nz, nb, chunks, shape, kern, proj, mask, mask_rows, counts, gain, route, stats, totals, in_c, low, pre, mixed_out, sums_all, mix_out, gates, pooled, full_c, sums, *comm):
    j = pl.program_id(0)
    sems = comm[6:]
    comm = comm[:6]
    net = Net(nd, nz)

    def planes():
        return every(gather_plane, net, shape, full_c, sems[0:2])

    def twins():
        return every(gather_twin, net, shape, full_c, sems[2:4])


    @pl.when(j == 0)
    def _():
        sum_start(nd, nz)

    @pl.when(j == 1)
    def _():
        met(nd, nz)
        start(planes())

    @pl.when(j == chunks - 2)
    def _():
        arrived(planes())
        start(twins())

    @pl.when(j == 0)
    def _():
        sums[...] = jnp.zeros_like(sums)
        mean, rstd = out_norm(stats, totals[TOTAL_ROW : TOTAL_ROW + 1, 0:1])
        scale = rstd * gain[0:1, :]
        for b in range(nb):
            at = slice(b * PIXELS, (b + 1) * PIXELS)
            low[at, :] = (((proj[at, :] - mean) * scale + gain[1:2, :]) * mask[at, 0:1]).astype(bf16)
        pool = dot(mask_rows[...], low[...]) / jnp.maximum(counts[:, 0:1], 1.0)
        pooled[...] = pool
        gate = sig(dot(pool, route[...], NN, highest))
        gates[...] = gate
        build_mix(gate, nb, mix_out)

    mixed = mix_kernels(kern[...], mix_out[...])
    one = jnp.zeros((1, LANES), f32)
    two = jnp.zeros((1, LANES), f32)
    for b in range(nb):
        at = slice(b * PIXELS, (b + 1) * PIXELS)
        weight = mixed[:, b * LANES : (b + 1) * LANES].astype(bf16)
        mixed_out[b] = weight
        value = dot(low[at, :], weight)
        pre[at, :] = value
        masked = mask[at, :] * value
        one = one + rsum(masked)
        two = two + rsum(masked * value)
    sums[pl.ds(j, 1), :] = one
    sums[pl.ds(chunks + j, 1), :] = two


    @pl.when(j == chunks - 1)
    def _():
        sum_finish(nd, nz, sums, sums_all, *comm)
        arrived(twins())
        sent(planes() + twins())


def head(kern, proj, mask, mask_rows, counts, gain, route, stats, totals, full_c, nb, nd, nz, ident):
    rows = proj.shape[0]
    width = kern.shape[1] // EXPERTS
    chunks = width // LANES
    deep = LANES * EXPERTS
    wide = lambda j: (0, j)
    return pl.pallas_call(
        functools.partial(head_kernel, nd, nz, nb, chunks, shard_shape(full_c, nz)),
        grid=(chunks,),
        out_shape=[
            jax.ShapeDtypeStruct((rows, WIDTH_OUT), bf16),
            jax.ShapeDtypeStruct((rows, width), f32),
            jax.ShapeDtypeStruct((nb, WIDTH_OUT, width), bf16),
            jax.ShapeDtypeStruct((24, LANES), f32),
            jax.ShapeDtypeStruct((deep, 2 * nb * LANES), bf16),
            jax.ShapeDtypeStruct((8, EXPERTS), f32),
            jax.ShapeDtypeStruct((8, WIDTH_OUT), f32),
            jax.ShapeDtypeStruct(full_c.shape, bf16),
        ],
        in_specs=[
            pl.BlockSpec((WIDTH_OUT, deep), wide),
            whole(proj.shape),
            whole(mask.shape),
            whole(mask_rows.shape),
            whole(counts.shape),
            whole(gain.shape),
            whole(route.shape),
            whole(stats.shape),
            whole(totals.shape),
            pl.BlockSpec(memory_space=pltpu.HBM),
        ],
        out_specs=[
            whole((rows, WIDTH_OUT)),
            pl.BlockSpec((rows, LANES), wide),
            pl.BlockSpec((nb, WIDTH_OUT, LANES), lambda j: (0, 0, j)),
            whole((24, LANES)),
            whole((deep, 2 * nb * LANES)),
            whole((8, EXPERTS)),
            whole((8, WIDTH_OUT)),
            pl.BlockSpec(memory_space=pltpu.HBM),
        ],
        scratch_shapes=sum_scratch(24, nd, nz)
        + pair((nz - 1) * (nd // 2 - 1))
        + pair(nz - 1),
        input_output_aliases={9: 7},
        compiler_params=params(ident),
        name="head",
    )(kern, proj, mask, mask_rows, counts, gain, route, stats, totals, full_c)


def store_sums(early, late, cut, chunks, j, one, two):
    @pl.when(j < cut)
    def _():
        early[pl.ds(j, 1), :] = one
        early[pl.ds(chunks + j, 1), :] = two

    @pl.when(j >= cut)
    def _():
        late[pl.ds(j, 1), :] = one
        late[pl.ds(chunks + j, 1), :] = two


def split_sum(nd, nz, steps, at, early, late, out, comm_early, comm_late):
    def early_third():
        out[...] = sum_third(nd, nz, early, *comm_early)

    def late_third():
        out[...] += sum_third(nd, nz, late, *comm_late)

    steps.at(at[0], lambda: sum_first(nd, nz, early, *comm_early))
    steps.at(at[1], lambda: sum_second(nd, nz, early, *comm_early))
    steps.at(at[2], early_third)
    steps.at(at[3], lambda: sum_first(nd, nz, late, *comm_late))
    steps.at(at[4], lambda: sum_second(nd, nz, late, *comm_late))
    steps.at(at[5], late_third)


def head_back_kernel(
    nd,
    nz,
    nb,
    chunks,
    shape,
    pre,
    mask,
    counts,
    labels,
    bias,
    cls,
    gain,
    stats,
    totals,
    low,
    kern,
    mixed,
    mix,
    gates,
    route,
    proj,
    proj_stats,
    features,
    grad_logits,
    sums_four,
    grad_out,
    sums_all,
    dz_out,
    half,
    part,
    logits,
    grad_features,
    held,
    grads,
    gate_acc,
    early,
    late,
    sums,
    *comm,
):
    step = pl.program_id(0)
    phase = step // chunks
    j = lax.rem(step, chunks)
    net = Net(nd, nz)
    comm_early, comm_late, comm_two, comm = comm[0:6], comm[6:12], comm[12:18], comm[18:]
    twin = Twin(net, shape, half, *comm[0:4])
    plane = Plane(net, shape, half, part, 0, nz // 2, *comm[4:7])
    made = comm[0]
    cut = chunks // 3
    base = 2 * chunks
    steps = Steps()
    steps.at(1, lambda: met(nd, nz))
    places = (chunks + cut, chunks + cut + 3, base, base, base + 1, base + cut)
    split_sum(nd, nz, steps, places, early, late, sums_four, comm_early, comm_late)
    for k in range(nz):
        first = base + ready(shape, k)
        steps.at(first, functools.partial(twin.begin, k))
        steps.at(first + 2, functools.partial(twin.add, k))
        if k < nz // 2:
            steps.at(first + 2, functools.partial(plane.begin, k))

    @pl.when(step == 0)
    def _():
        sum_start(nd, nz)
        for ref in (sums, early, late, features, logits, gate_acc):
            ref[...] = jnp.zeros_like(ref)
        if shape[0] > WIDTH_OUT:
            made[WIDTH_OUT:, :] = jnp.zeros((shape[0] - WIDTH_OUT, made.shape[1]), bf16)

    steps.emit(step, 3 * chunks)
    lane = pl.ds(pl.multiple_of(j * LANES, LANES), LANES)
    total = totals[TOTAL_ROW : TOTAL_ROW + 1, :]
    mean, rstd = norm_rows(stats, j, chunks, total)
    scale = rstd * gain[0:1, :]

    @pl.when(phase == 0)
    def _():
        for b in range(nb):
            at = slice(b * PIXELS, (b + 1) * PIXELS)
            normed = (pre[at, :] - mean) * scale + gain[1:2, :]
            features[b : b + 1, lane] = rsum(normed * sig(normed) * mask[at, :]) / jnp.maximum(
                counts[b : b + 1, :], 1.0
            )
        both = dot(split(features[:, lane]), cls[lane, :])
        logits[...] += both[:8] + both[8:]

    @pl.when((phase == 1) & (j == 0))
    def _():
        col = lax.broadcasted_iota(jnp.int32, (8, CLASS_PAD), 1)
        inside = col < CLASSES
        scores = jnp.where(inside, logits[...] + bias[...], -1e30)
        top = jnp.max(scores, axis=1, keepdims=True)
        spread = jnp.where(inside, jnp.exp(scores - top), 0.0)
        mass = jnp.sum(spread, axis=1, keepdims=True)
        hot = jnp.where(col == labels[:, 0:1], 1.0, 0.0)
        shifted_scores = jnp.where(inside, scores - top - jnp.log(mass), 0.0)
        per_image = -(
            0.9 * jnp.sum(shifted_scores * hot, axis=1, keepdims=True)
            + (0.1 / CLASSES) * jnp.sum(shifted_scores, axis=1, keepdims=True)
        )
        valid = jnp.where(counts[:, 0:1] > 0.0, 1.0, 0.0)
        early[2 * chunks : 2 * chunks + 1, :] = jnp.broadcast_to(rsum(per_image * valid), (1, LANES))
        weight = valid / totals[TOTAL_ROW + 1 : TOTAL_ROW + 2, 0:1]
        grad_logits[...] = weight * jnp.where(inside, spread / mass - 0.9 * hot - 0.1 / CLASSES, 0.0)

    @pl.when(phase == 1)
    def _():
        both = dot(split(grad_logits[...]), cls[lane, :], NT)
        grads = (both[:8] + both[8:]) / jnp.maximum(counts[...], 1.0)
        grad_features[:, lane] = grads
        one = jnp.zeros((1, LANES), f32)
        two = jnp.zeros((1, LANES), f32)
        for b in range(nb):
            at = slice(b * PIXELS, (b + 1) * PIXELS)
            hat = (pre[at, :] - mean) * rstd
            grad = mask[at, :] * dsilu(hat * gain[0:1, :] + gain[1:2, :]) * grads[b : b + 1, :]
            one = one + rsum(grad)
            two = two + rsum(grad * hat)
        store_sums(early, late, cut, chunks, j, one, two)

    @pl.when(phase == 2)
    def _():
        one = sums_four[pl.ds(j, 1), :] / total
        two = sums_four[pl.ds(chunks + j, 1), :] / total
        for b in range(nb):
            at = slice(b * PIXELS, (b + 1) * PIXELS)
            hat = (pre[at, :] - mean) * rstd
            grad = dsilu(hat * gain[0:1, :] + gain[1:2, :]) * grad_features[b : b + 1, lane]
            value = (scale * mask[at, :] * (grad - one - hat * two)).astype(bf16)
            held[at, lane] = value
            grad_mixed = dot(low[at, :], value, TN).astype(bf16)
            grads[:, b * LANES : (b + 1) * LANES] = grad_mixed
            gate_acc[b : b + 1, :] += gate_rows(grad_mixed, kern[...])
        made[:WIDTH_OUT, lanes(j * LANES * EXPERTS, LANES * EXPERTS)] = dot(grads[...], mix[:, : nb * LANES], NT).astype(bf16)

    @pl.when(step == 3 * chunks - 1)
    def _():
        dz = gate_sums(gate_acc[...]) * gates[...] * (1.0 - gates[...])
        dz_out[...] = dz
        pool_grad = dot(dz, route[...], NT, highest) / jnp.maximum(counts[:, 0:1], 1.0)
        mean, rstd = out_norm(proj_stats, total[:, 0:1])
        one = jnp.zeros((1, WIDTH_OUT), f32)
        two = jnp.zeros((1, WIDTH_OUT), f32)
        for b in range(nb):
            at = slice(b * PIXELS, (b + 1) * PIXELS)
            value = (dot(held[at, :], mixed[b], NT) + pool_grad[b : b + 1, :]) * mask[at, 0:1]
            grad_out[at, :] = value
            one = one + rsum(value)
            two = two + rsum(value * ((proj[at, :] - mean) * rstd))
        store_wide(sums, 0, one)
        store_wide(sums, OUT_CHUNKS, two)
        last = [k for k in range(nz) if ready(shape, k) >= chunks]
        for k in last:
            twin.begin(k)
        sum_finish(nd, nz, sums, sums_all, *comm_two)
        for k in range(nz):
            if ready(shape, k) + 2 >= chunks:
                twin.add(k)
                if k < nz // 2:
                    plane.begin(k)
        plane.add()
        twin.finish()
        plane.finish()


def head_back(pre, mask, counts, labels, bias, cls, gain, stats, totals, low, kern, mixed, mix, gates, route, proj, proj_stats, nb, nd, nz, ident):
    rows, width = pre.shape
    chunks = width // LANES
    deep = LANES * EXPERTS
    shape = (kern.shape[0], kern.shape[1] // nz)
    wide = lambda t: (0, lax.rem(t, chunks))
    return pl.pallas_call(
        functools.partial(head_back_kernel, nd, nz, nb, chunks, shape),
        grid=(3 * chunks,),
        out_shape=[
            jax.ShapeDtypeStruct((8, width), f32),
            jax.ShapeDtypeStruct((8, CLASS_PAD), f32),
            jax.ShapeDtypeStruct((24, LANES), f32),
            jax.ShapeDtypeStruct((rows, WIDTH_OUT), f32),
            jax.ShapeDtypeStruct((8, LANES), f32),
            jax.ShapeDtypeStruct((8, EXPERTS), f32),
            jax.ShapeDtypeStruct(half_shape(shape, nd, nz), bf16),
            jax.ShapeDtypeStruct(part_shape(shape, nd, nz // 2), bf16),
        ],
        in_specs=[
            pl.BlockSpec((rows, LANES), wide),
            whole(mask.shape),
            whole(counts.shape),
            whole(labels.shape),
            whole(bias.shape),
            whole(cls.shape),
            pl.BlockSpec((8, LANES), wide),
            whole(stats.shape),
            whole(totals.shape),
            whole(low.shape),
            pl.BlockSpec((WIDTH_OUT, deep), lambda t: (0, jnp.maximum(t - 2 * chunks, 0))),
            whole(mixed.shape),
            whole(mix.shape),
            whole(gates.shape),
            whole(route.shape),
            whole(proj.shape),
            whole(proj_stats.shape),
        ],
        out_specs=[
            whole((8, width)),
            whole((8, CLASS_PAD)),
            whole((24, LANES)),
            whole((rows, WIDTH_OUT)),
            whole((8, LANES)),
            whole((8, EXPERTS)),
            whole(half_shape(shape, nd, nz)),
            whole(part_shape(shape, nd, nz // 2)),
        ],
        scratch_shapes=[
            VMEM((8, CLASS_PAD), f32),
            VMEM((8, width), f32),
            VMEM((rows, width), bf16),
            VMEM((WIDTH_OUT, nb * LANES), bf16),
            VMEM((8, deep), f32),
            VMEM((24, LANES), f32),
            VMEM((24, LANES), f32),
            VMEM((8, LANES), f32),
        ]
        + sum_scratch(24, nd, nz)[1:] * 2
        + sum_scratch(8, nd, nz)[1:]
        + twin_scratch(shape, nd, nz)
        + plane_scratch(shape, nd, nz // 2),
        compiler_params=params(ident),
        name="head_back",
    )(pre, mask, counts, labels, bias, cls, gain, stats, totals, low, kern, mixed, mix, gates, route, proj, proj_stats)


def project_back_kernel(nd, nz, nb, chunks, shape_h, shape, half_h, part_h, grad_in, proj, proj_stats, proj_sums, gain, mask, counts, totals, stats, side, dpre, excited, mixed, kern, mix, gate, pooled, squeezed, sq_bias, grad_norm, sums_all, grad_squeeze, gate_grad, dz_gate, piece_h, half, part, low, held, grads, gate_acc, sums_h, sums, *comm):
    phase = pl.program_id(0)
    net = Net(nd, nz)
    few = nz // 2
    cut_one = 12
    plane_h = Plane(net, shape_h, half_h, sums_h, few, nz - few, *comm[6:9])
    far = Far(net, shape_h, sums_h, piece_h, *comm[9:cut_one])
    twin = Twin(net, shape, half, *comm[cut_one : cut_one + 4])
    plane = Plane(net, shape, half, part, 0, few, *comm[cut_one + 4 : cut_one + 7])
    made = comm[cut_one]
    comm = comm[:6]
    steps = Steps()

    def begin():
        met(nd, nz)
        for k in plane_h.shards:
            plane_h.begin(k)
        sums_h[0:few] = part_h[...]
        for k in range(few):
            far.send(k)

    steps.at(1, begin)
    steps.at(chunks + 3, functools.partial(plane_h.add, far.send))
    for k in range(nz):
        first = ready(shape, k)
        steps.at(first, functools.partial(twin.begin, k))
        steps.at(first + 3, functools.partial(twin.add, k))
        if k < few:
            steps.at(first + 3, functools.partial(plane.begin, k))
    j = pl.program_id(1)

    @pl.when((phase == 0) & (j == 0))
    def _():
        sum_start(nd, nz)

    steps.emit(phase * chunks + j, 2 * chunks)
    lane = pl.ds(pl.multiple_of(j * LANES, LANES), LANES)
    total = totals[TOTAL_ROW : TOTAL_ROW + 1, :]

    @pl.when((phase == 0) & (j == 0))
    def _():
        gate_acc[...] = jnp.zeros_like(gate_acc)
        if shape[0] > WIDTH_OUT:
            made[WIDTH_OUT:, :] = jnp.zeros((shape[0] - WIDTH_OUT, made.shape[1]), bf16)
        sums[...] = jnp.zeros_like(sums)
        grad_squeeze[...] = jnp.zeros_like(grad_squeeze)
        dz_gate[...] = jnp.zeros_like(dz_gate)
        mean, rstd = out_norm(proj_stats, total[:, 0:1])
        scale = rstd * gain[0:1, :]
        one = load_wide(proj_sums, 0, WIDTH_OUT) / total[:, 0:1]
        two = load_wide(proj_sums, OUT_CHUNKS, WIDTH_OUT) / total[:, 0:1]
        for b in range(nb):
            at = slice(b * PIXELS, (b + 1) * PIXELS)
            hat = (proj[at, :] - mean) * rstd
            low[at, :] = (scale * (grad_in[at, :] - mask[at, 0:1] * (one + hat * two))).astype(bf16)

    mean, rstd = norm_rows(stats, j, chunks, total)
    gain_now = side[2 * SQUEEZE + 2 : 2 * SQUEEZE + 3, :]
    bias_now = side[2 * SQUEEZE + 3 : 2 * SQUEEZE + 4, :]

    @pl.when(phase == 0)
    def _():
        for b in range(nb):
            at = slice(b * PIXELS, (b + 1) * PIXELS)
            grad_mixed = dot(low[at, :], excited[at, :], TN).astype(bf16)
            grads[:, b * LANES : (b + 1) * LANES] = grad_mixed
            gate_acc[b : b + 1, :] += gate_rows(grad_mixed, kern[...])
            value = dot(low[at, :], mixed[b])
            held[j, at, :] = value
            normed = (dpre[at, :] - mean) * (rstd * gain_now) + bias_now
            act = normed * sig(normed) * mask[at, :]
            now = gate[b : b + 1, :]
            dz_gate[b : b + 1, lane] = rsum(value * act) * now * (1.0 - now)
        made[:WIDTH_OUT, lanes(j * LANES * EXPERTS, LANES * EXPERTS)] = dot(grads[...], mix[:, : nb * LANES], NT).astype(bf16)
        grad_squeeze[...] += dot(dz_gate[:, lane], side[SQUEEZE : 2 * SQUEEZE, :], NT, highest)

    @pl.when((phase == 1) & (j == 0))
    def _():
        grad_squeeze[...] = grad_squeeze[...] * dsilu(squeezed[...] + sq_bias[...])
        gate_grad[...] = gate_sums(gate_acc[...])

    @pl.when(phase == 1)
    def _():
        pool_grad = dot(grad_squeeze[...], side[0:SQUEEZE, :], NN, highest) / jnp.maximum(counts[...], 1.0)
        one = jnp.zeros((1, LANES), f32)
        two = jnp.zeros((1, LANES), f32)
        for b in range(nb):
            at = slice(b * PIXELS, (b + 1) * PIXELS)
            hat = (dpre[at, :] - mean) * rstd
            grad = held[j, at, :] * gate[b : b + 1, :] + pool_grad[b : b + 1, :]
            value = mask[at, :] * grad * dsilu(hat * gain_now + bias_now)
            grad_norm[at, :] = value
            one = one + rsum(value)
            two = two + rsum(value * hat)
        sums[pl.ds(j, 1), :] = one
        sums[pl.ds(chunks + j, 1), :] = two

    @pl.when((phase == 1) & (j == chunks - 1))
    def _():
        sum_finish(nd, nz, sums, sums_all, *comm)
        far.add()
        plane.add()
        far.finish()
        twin.finish()
        plane.finish()
        plane_h.finish()


def project_back(half_h, part_h, shape_h, grad_in, proj, proj_stats, proj_sums, gain, mask, counts, totals, stats, side, dpre, excited, mixed, kern, mix, gate, pooled, squeezed, sq_bias, nb, nd, nz, ident):
    rows, width = dpre.shape
    shape = (kern.shape[0], kern.shape[1] // nz)
    few = nz // 2
    chunks = width // LANES
    deep = LANES * EXPERTS
    wide = lambda p, j: (0, j)
    early = lambda p, j: (0, jnp.where(p == 0, j, chunks - 1))
    late = lambda p, j: (0, jnp.where(p == 0, 0, j))
    return pl.pallas_call(
        functools.partial(project_back_kernel, nd, nz, nb, chunks, shape_h, shape),
        grid=(2, chunks),
        out_shape=[
            jax.ShapeDtypeStruct((rows, width), f32),
            jax.ShapeDtypeStruct((24, LANES), f32),
            jax.ShapeDtypeStruct((8, SQUEEZE), f32),
            jax.ShapeDtypeStruct((8, EXPERTS), f32),
            jax.ShapeDtypeStruct((8, width), f32),
            jax.ShapeDtypeStruct(piece_shape(shape_h, nd), bf16),
            jax.ShapeDtypeStruct(half_shape(shape, nd, nz), bf16),
            jax.ShapeDtypeStruct(part_shape(shape, nd, few), bf16),
        ],
        in_specs=[
            whole(half_h.shape),
            whole(part_h.shape),
            whole(grad_in.shape),
            whole(proj.shape),
            whole(proj_stats.shape),
            whole(proj_sums.shape),
            whole(gain.shape),
            whole(mask.shape),
            whole(counts.shape),
            whole(totals.shape),
            whole(stats.shape),
            pl.BlockSpec((side.shape[0], LANES), wide),
            pl.BlockSpec((rows, LANES), wide),
            pl.BlockSpec((rows, LANES), early),
            pl.BlockSpec((nb, WIDTH_OUT, LANES), lambda p, j: (0, 0, jnp.where(p == 0, j, chunks - 1))),
            pl.BlockSpec((WIDTH_OUT, deep), early),
            whole(mix.shape),
            pl.BlockSpec((8, LANES), wide),
            pl.BlockSpec((8, LANES), wide),
            whole(squeezed.shape),
            whole(sq_bias.shape),
        ],
        out_specs=[
            pl.BlockSpec((rows, LANES), late),
            whole((24, LANES)),
            whole((8, SQUEEZE)),
            whole((8, EXPERTS)),
            whole((8, width)),
            whole(piece_shape(shape_h, nd)),
            whole(half_shape(shape, nd, nz)),
            whole(part_shape(shape, nd, few)),
        ],
        scratch_shapes=[
            VMEM((rows, WIDTH_OUT), bf16),
            VMEM((chunks, rows, LANES), f32),
            VMEM((WIDTH_OUT, nb * LANES), bf16),
            VMEM((8, deep), f32),
            VMEM(part_shape(shape_h, nd, nz), bf16),
        ]
        + sum_scratch(24, nd, nz)
        + plane_scratch(shape_h, nd, nz - few)
        + far_scratch(shape_h, nd, nz)
        + twin_scratch(shape, nd, nz)
        + plane_scratch(shape, nd, few),
        compiler_params=params(ident),
        name="project_back",
    )(half_h, part_h, grad_in, proj, proj_stats, proj_sums, gain, mask, counts, totals, stats, side, dpre, excited, mixed, kern, mix, gate, pooled, squeezed, sq_bias)


def dz_slots(nb, devices):
    per = max(1, min(devices, LANES // (nb * EXPERTS)))
    return per, -(-devices // (per * 8)) * 8


def stage_back_kernel(
    nd,
    nz,
    nb,
    chunks,
    shape,
    shape_b,
    shape_h,
    cuts_one,
    cuts_two,
    half_b,
    part_b,
    piece_h,
    grad_in,
    dpre,
    pre,
    taps,
    mask,
    side,
    stats_one,
    stats_two,
    sums_two,
    totals,
    features,
    logits,
    pooled,
    dz_gate,
    head_pool,
    pooled_in,
    grad_sq,
    before,
    sq_bias_in,
    dz_head,
    images,
    kern,
    mix,
    gates,
    gate_grad,
    squares_w,
    stats_three,
    stats_four,
    sums_four,
    chan_old,
    head_old,
    proj_old,
    done,
    done_b,
    done_h,
    grad_cls,
    grad_side_out,
    factors,
    route_in,
    route_head,
    sq_bias,
    class_bias,
    chan_new,
    head_new,
    proj_new,
    loss,
    made_norm,
    tap_grads,
    buf,
    acts,
    held,
    early,
    late,
    sums_one,
    sums_b,
    piece_b,
    rows_all,
    grads,
    gate_acc,
    grad_side,
    every_sum,
    low,
    half,
    sums,
    piece,
    *comm,
):
    step = pl.program_id(0)
    net = Net(nd, nz)
    few = nz // 2
    cut = 2 * chunks // 3
    comm_early, comm_late, comm_two, comm = comm[0:6], comm[6:12], comm[12:18], comm[18:]
    plane_b = Plane(net, shape_b, half_b, sums_b, few, nz - few, *comm[0:3], shift=few)
    far_b = Far(net, shape_b, sums_b, piece_b, *comm[3:6])
    up_b = Spread(net, shape_b, piece_b, done_b, *comm[6:11])
    up_h = Spread(net, shape_h, piece_h, done_h, *comm[11:16])
    share = Share(net, rows_all, *comm[16:24])
    comm = comm[24:]
    twin = Twin(net, shape, half, *comm[0:4])
    made = comm[0]
    plane = Plane(net, shape, half, sums, 0, nz, *comm[4:7])
    far = Far(net, shape, sums, piece, *comm[7:10])
    up = Spread(net, shape, piece, done, *comm[10:15])
    steps = Steps()
    first_planes = range(few, few + (nz - few + 1) // 2)
    last_planes = range(first_planes.stop, nz)

    def begin():
        met(nd, nz)
        up_h.begin()
        for k in first_planes:
            plane_b.begin(k)
        sums_b[0:few] = part_b[...]
        for k in range(few):
            far_b.send(k)
        share.far()

    def more_planes():
        for k in last_planes:
            plane_b.begin(k)

    def far_end():
        far_b.add()
        up_b.begin()

    steps.at(1, begin)
    steps.at(4, up_h.cross)
    split_sum(
        nd,
        nz,
        steps,
        (cut, cut + 2, chunks, chunks, chunks + 2, chunks + cut - 1),
        early,
        late,
        sums_one,
        comm_early,
        comm_late,
    )
    steps.at(cut + 1, more_planes)
    steps.at(cut + 2, share.plane)
    steps.at(chunks + 1, functools.partial(plane_b.add, far_b.send))
    steps.at(chunks + 2, share.twin)
    steps.at(chunks + 3, far_end)
    for k in range(nz):
        first = chunks + ready(shape, k)
        steps.at(first, functools.partial(twin.begin, k))
        steps.at(first + 1, functools.partial(twin.add, k))
        steps.at(first + 1, functools.partial(plane.begin, k))
    steps.at(2 * chunks - 2, up_b.cross)

    @pl.when(step == 0)
    def _():
        sum_start(nd, nz)
        total_before = before[...] + sq_bias_in[...]
        squeezed = total_before * sig(total_before)
        share.fill(
            nb,
            [features, pooled, dz_gate],
            [grad_sq[...], squeezed, dz_head[...]],
            [logits[...], head_pool[...], pooled_in[...]],
        )
        for ref in (early, late, gate_acc, grads):
            ref[...] = jnp.zeros_like(ref)

    steps.emit(step, 2 * chunks)
    total = totals[TOTAL_ROW : TOTAL_ROW + 1, :]

    @pl.when(step < chunks)
    def _():
        j = step
        mean_two, rstd_two = norm_rows(stats_two, j, chunks, total)
        scale_two = rstd_two * side[2 * SQUEEZE + 2 : 2 * SQUEEZE + 3, :]
        one_two = sums_two[pl.ds(j, 1), :] / total
        two_two = sums_two[pl.ds(chunks + j, 1), :] / total
        mean, rstd = norm_rows(stats_one, j, chunks, total)
        gain = side[2 * SQUEEZE : 2 * SQUEEZE + 1, :]
        bias = side[2 * SQUEEZE + 1 : 2 * SQUEEZE + 2, :]
        held[...] = jnp.zeros_like(held)
        reach = KERNEL // 2

        @pl.loop(0, nb)
        def _(b):
            at = image(b)
            hat = (dpre[at, :] - mean_two) * rstd_two
            grad = scale_two * (grad_in[at, :] - mask[at, :] * (one_two + hat * two_two))
            for s in range(KERNEL):
                buf[s] = shifted(grad, reach - s)
            hat = (pre[at, :] - mean) * rstd
            normed = hat * gain + bias
            acts[...] = normed * sig(normed) * mask[at, :]
            taps_now = [jnp.broadcast_to(taps[b, t : t + 1, :], (MAP_SIDE, LANES)) for t in range(TAPS)]
            acc = [None] * MAP_SIDE
            for q in range(MAP_SIDE):
                for s in range(KERNEL):
                    x = buf[s, q * MAP_SIDE : (q + 1) * MAP_SIDE, :]
                    for r in range(KERNEL):
                        y = q + r - reach
                        if 0 <= y < MAP_SIDE:
                            term = taps_now[r * KERNEL + s] * x
                            acc[y] = term if acc[y] is None else acc[y] + term
                done = [q - 2] if q < MAP_SIDE - 1 else [q - 2, q - 1, q]
                for i in done:
                    if i >= 0:
                        made_norm[j, pl.ds(pl.multiple_of(b * PIXELS + i * MAP_SIDE, MAP_SIDE), MAP_SIDE), :] = acc[i]
            tap_acc = [None] * TAPS
            for q in range(MAP_SIDE):
                for s in range(KERNEL):
                    x = buf[s, q * MAP_SIDE : (q + 1) * MAP_SIDE, :]
                    for r in range(KERNEL):
                        y = q + r - reach
                        if 0 <= y < MAP_SIDE:
                            both = acts[y * MAP_SIDE : (y + 1) * MAP_SIDE, :] * x
                            term = both[:8] + both[8:]
                            t = r * KERNEL + s
                            tap_acc[t] = term if tap_acc[t] is None else tap_acc[t] + term
            tap_grads[j, b] = jnp.zeros((32, LANES), f32)
            for t in range(TAPS):
                tap_grads[j, b, t : t + 1, :] = rsum(tap_acc[t])
            hat = (pre[at, :] - mean) * rstd
            value = made_norm[j, at, :] * mask[at, :] * dsilu(hat * gain + bias)
            made_norm[j, at, :] = value
            held[0:1, :] += rsum(value)
            held[1:2, :] += rsum(value * hat)

        store_sums(early, late, cut, chunks, j, held[0:1, :], held[1:2, :])

    @pl.when(step >= chunks)
    def _():
        j = step - chunks
        mean, rstd = norm_rows(stats_one, j, chunks, total)
        scale = rstd * side[2 * SQUEEZE : 2 * SQUEEZE + 1, :]
        one = sums_one[pl.ds(j, 1), :] / total
        two = sums_one[pl.ds(chunks + j, 1), :] / total
        for b in range(nb):
            at = slice(b * PIXELS, (b + 1) * PIXELS)
            lane = slice(b * LANES, (b + 1) * LANES)
            hat = (pre[at, :] - mean) * rstd
            value = (scale * (made_norm[j, at, :] - mask[at, :] * (one + hat * two))).astype(bf16)
            grads[0:WIDTH_IN, lane] = dot(images[at, :], value, TN).astype(bf16)
            grads[WIDTH_IN : WIDTH_IN + 32, lane] = tap_grads[j, b].astype(bf16)
            gate_acc[b : b + 1, :] += gate_rows(grads[:, lane], kern[...])
        made[:, lanes(j * LANES * EXPERTS, LANES * EXPERTS)] = dot(grads[...], mix[:, : nb * LANES], NT).astype(bf16)

    @pl.when(step == 2 * chunks - 1)
    def _():
        dz = (gate_sums(gate_acc[...]) + gate_grad[...]) * gates[...] * (1.0 - gates[...])
        steps.end(2 * chunks)
        z = net.z
        me = net.d * nz + z
        devices = nd * nz
        own = chan_old.shape[1]
        own_head = head_old.shape[1]
        own_proj = proj_old.shape[1]
        width = own * nz
        head_width = own_head * nz
        head_chunks = head_width // LANES
        share.finish()
        count = devices * 8
        per, slots = dz_slots(nb, devices)
        row = lax.broadcasted_iota(jnp.int32, (count, 1), 0)
        keep = jnp.where((row & 7) < nb, 1.0, 0.0)

        def one(k, size):
            return rows_all[:, :, cuts_one[k] : cuts_one[k] + size].reshape(count, size) * keep

        def two(k, size):
            return pltpu.roll(rows_all[:, :, cuts_two[k] : cuts_two[k] + size].reshape(count, size), count - nb, 0)

        features = one(0, own_head)
        logits = two(0, CLASS_PAD)
        pooled = one(1, own)
        dz_gate = one(2, own)
        grad_sq = one(3, SQUEEZE)
        grad_cls[...] = dot(features, logits, TN, highest)
        grad_side[...] = jnp.zeros_like(grad_side)
        grad_side[0:SQUEEZE, :own] = dot(grad_sq, pooled, TN, highest)
        grad_side[SQUEEZE : 2 * SQUEEZE, :own] = dot(one(4, SQUEEZE), dz_gate, TN, highest)

        def channel(ref, at, n, size, own_size):
            return turn(load_wide(ref, at, size), z * own_size)[:, :own_size]

        at = 2 * SQUEEZE
        grad_side[at : at + 1, :own] = channel(sums_one, chunks, chunks, width, own)
        grad_side[at + 1 : at + 2, :own] = channel(sums_one, 0, chunks, width, own)
        grad_side[at + 2 : at + 3, :own] = channel(sums_two, chunks, chunks, width, own)
        grad_side[at + 3 : at + 4, :own] = channel(sums_two, 0, chunks, width, own)
        grad_side[at + 4 : at + 5, :own] = rsum(dz_gate)
        route_head[...] = dot(two(1, WIDTH_OUT), one(5, EXPERTS), TN, highest)
        sq_bias[...] = rsum(grad_sq)
        class_bias[...] = rsum(logits * keep)
        head_gain = channel(sums_four, head_chunks, head_chunks, head_width, own_head)
        head_bias = channel(sums_four, 0, head_chunks, head_width, own_head)
        totals = stats_one[TOTAL_ROW : TOTAL_ROW + 1, 0:1]
        loss[...] = jnp.broadcast_to(
            sums_four[2 * head_chunks : 2 * head_chunks + 1, :] / stats_one[TOTAL_ROW + 1 : TOTAL_ROW + 2, :], (8, LANES)
        )

        def moving(new, old, ref, at, n, size, own_size):
            mean = load_wide(ref, 0, size) / totals
            var = (load_wide(ref, n, size) / totals - mean * mean) * (totals / (totals - 1.0))
            new[at : at + 1, :] = 0.5 * old[at : at + 1, :] + 0.5 * turn(mean, z * own_size)[:, :own_size]
            new[at + 1 : at + 2, :] = 0.5 * old[at + 1 : at + 2, :] + 0.5 * turn(var, z * own_size)[:, :own_size]

        moving(chan_new, chan_old, stats_one, 0, chunks, width, own)
        moving(chan_new, chan_old, stats_two, 2, chunks, width, own)
        moving(head_new, head_old, stats_four, 0, head_chunks, head_width, own_head)
        moving(proj_new, proj_old, stats_three, 0, OUT_CHUNKS, WIDTH_OUT, own_proj)
        low[...] = jnp.zeros_like(low)
        own_dz = fit(jnp.concatenate([dz[b : b + 1, :] for b in range(nb)], axis=1), LANES)
        low[pl.ds(me // per, 1), :] = pltpu.roll(own_dz, lax.rem(me, per) * (nb * EXPERTS), 1)
        fraction = 1.0 / nd
        g_hside = jnp.sum(grad_cls[...] * grad_cls[...]) + jnp.sum(head_gain * head_gain) + jnp.sum(head_bias * head_bias)
        sums = (
            0.0,
            squares_of(grad_side, 104),
            squares_of(piece_h, piece_h.shape[0]) * nd,
            g_hside,
        )
        for k in range(4):
            low[slots + k : slots + k + 1, :] = row_of(sums[k] * fraction)
            low[slots + 4 + k : slots + 5 + k, :] = squares_w[k : k + 1, :] * fraction
        plane.add(far.send)
        far.add()
        up.begin()
        low[slots : slots + 1, :] = row_of(
            squares_of(piece, piece.shape[0]) + squares_of(piece_b, piece_b.shape[0])
        )
        sum_finish(nd, nz, low, every_sum, *comm_two)
        up.cross()
        for k in range(4):
            grad_sq_sum = jnp.sum(every_sum[slots + k : slots + k + 1, :], axis=1, keepdims=True)
            weight_sq = jnp.sum(every_sum[slots + 4 + k : slots + 5 + k, :], axis=1, keepdims=True)
            factors[k : k + 1, :] = jnp.broadcast_to(
                jnp.sqrt(weight_sq) * lax.rsqrt(grad_sq_sum + 1e-12), (1, LANES)
            )
        row = lax.broadcasted_iota(jnp.int32, (count, slots), 0)
        col = lax.broadcasted_iota(jnp.int32, (count, slots), 1)
        spread = dot(jnp.where((row >> 3) // per == col, 1.0, 0.0), every_sum[0:slots, :], NN, highest)
        row = lax.broadcasted_iota(jnp.int32, (count, LANES), 0)
        col = lax.broadcasted_iota(jnp.int32, (count, LANES), 1)
        place = lax.rem(row >> 3, per) * nb + (row & 7) - nb
        spread = jnp.where(((col >> 3) == place) & ((row & 7) >= nb), spread, 0.0)
        row = lax.broadcasted_iota(jnp.int32, (LANES, EXPERTS), 0)
        col = lax.broadcasted_iota(jnp.int32, (LANES, EXPERTS), 1)
        dz_rows = dot(spread, jnp.where((row & (EXPERTS - 1)) == col, 1.0, 0.0), NN, highest)
        pooled_in = rows_all[:, :, cuts_two[2] : cuts_two[2] + 256].reshape(count, 256)
        route_in[...] = dot(pooled_in, dz_rows, TN, highest)[:WIDTH_IN]
        grad_side_out[...] = jnp.transpose(grad_side[...])[:own]
        values = grad_cls[:, :CLASSES]
        both = jnp.concatenate([head_gain, head_bias] + [jnp.zeros((6, own_head), f32)], axis=0)
        grad_cls[...] = jnp.concatenate(
            [jnp.transpose(both)[:, 0:2], values, jnp.zeros((own_head, CLASS_PAD - CLASSES - 2), f32)], axis=1
        )
        up.finish()
        up_b.finish()
        up_h.finish()
        plane_b.finish()
        far_b.finish()
        far.finish()
        twin.finish()
        plane.finish()


def stage_back(half_b, part_b, piece_h, grad_in, dpre, pre, taps, mask, side, stats_one, stats_two, sums_two, totals, lines, images, kern, mix, gates, gate_grad, small, shape_b, shape_h, nb, nd, nz, ident):
    rows, width = pre.shape
    chunks = width // LANES
    deep = LANES * EXPERTS
    before = lambda t: jnp.minimum(t, chunks - 1)
    after = lambda t: jnp.maximum(t - chunks, 0)
    shape = (kern.shape[0], kern.shape[1] // nz)
    devices = nd * nz
    slots = dz_slots(nb, devices)[1]
    few = nz // 2
    chan_old, head_old, proj_old = small[-3:]
    own, own_head = chan_old.shape[1], head_old.shape[1]
    outs = [(own_head, CLASS_PAD), (own, 104), (8, LANES)]
    outs += [(WIDTH_IN, EXPERTS), (WIDTH_OUT, EXPERTS), (1, SQUEEZE), (1, CLASS_PAD)]
    outs += [chan_old.shape, head_old.shape, proj_old.shape, (8, LANES)]
    cuts_one, cuts_two, wide = share_width(lines, nz)
    hbm = pl.BlockSpec(memory_space=pltpu.HBM)
    tall_before = pl.BlockSpec((rows, LANES), lambda t: (0, before(t)))
    return pl.pallas_call(
        functools.partial(stage_back_kernel, nd, nz, nb, chunks, shape, shape_b, shape_h, cuts_one, cuts_two),
        grid=(2 * chunks,),
        out_shape=[jax.ShapeDtypeStruct(x, bf16) for x in (shape, shape_b, shape_h)]
        + [jax.ShapeDtypeStruct(x, f32) for x in outs],
        in_specs=[
            pl.BlockSpec(
                (nz - few,) + half_b.shape[1:], lambda t: (1, 0, 0), pipeline_mode=pl.Buffered(1)
            ),
            whole(part_b.shape),
            whole(piece_h.shape),
            tall_before,
            tall_before,
            pl.BlockSpec((rows, LANES), lambda t: (0, lax.rem(t, chunks))),
            pl.BlockSpec((nb, 32, LANES), lambda t: (0, 0, before(t))),
            whole(mask.shape),
            pl.BlockSpec((side.shape[0], LANES), lambda t: (0, lax.rem(t, chunks))),
            whole(stats_one.shape),
            whole(stats_two.shape),
            whole(sums_two.shape),
            whole(totals.shape),
        ]
        + [whole(x.shape) for x in lines]
        + [
            whole(images.shape),
            pl.BlockSpec((kern.shape[0], deep), lambda t: (0, after(t))),
            whole(mix.shape),
            whole(gates.shape),
            whole(gate_grad.shape),
        ]
        + [whole(x.shape) for x in small],
        out_specs=[hbm] * 3 + [whole(x) for x in outs],
        scratch_shapes=[
            VMEM((chunks, rows, LANES), f32),
            VMEM((chunks, nb, 32, LANES), f32),
            VMEM((KERNEL, PIXELS, LANES), f32),
            VMEM((PIXELS, LANES), f32),
            VMEM((8, LANES), f32),
            VMEM((24, LANES), f32),
            VMEM((24, LANES), f32),
            VMEM((24, LANES), f32),
            VMEM(part_shape(shape_b, nd, nz), bf16),
            VMEM(piece_shape(shape_b, nd), bf16),
            VMEM((devices, 8, wide), f32),
            VMEM((kern.shape[0], nb * LANES), bf16),
            VMEM((8, deep), f32),
            VMEM((104, up_to(own)), f32),
            VMEM((slots + 8, LANES), f32),
            VMEM((slots + 8, LANES), f32),
            VMEM(half_shape(shape, nd, nz), bf16),
            VMEM(part_shape(shape, nd, nz), bf16),
            VMEM(piece_shape(shape, nd), bf16),
        ]
        + sum_scratch(24, nd, nz)[1:] * 2
        + sum_scratch(slots + 8, nd, nz)[1:]
        + plane_scratch(shape_b, nd, nz - nz // 2)
        + far_scratch(shape_b, nd, nz)
        + spread_scratch(shape_b, nd, nz)
        + spread_scratch(shape_h, nd, nz)
        + share_scratch(wide, nd, nz)
        + twin_scratch(shape, nd, nz)
        + plane_scratch(shape, nd, nz)
        + far_scratch(shape, nd, nz)
        + spread_scratch(shape, nd, nz),
        compiler_params=params(ident, 62 * 1024 * 1024),
        name="stage_back",
    )(half_b, part_b, piece_h, grad_in, dpre, pre, taps, mask, side, stats_one, stats_two, sums_two, totals, *lines, images, kern, mix, gates, gate_grad, *small)


def update(weight, grad, moment, average, factor):
    scaled = grad * factor
    moment_new = 0.5 * moment + scaled
    weight_new = weight - 0.2 * (scaled + 0.5 * moment_new)
    average_new = 0.5 * average + 0.5 * weight_new
    return (weight_new, moment_new, average_new)


BLOCK_STEP = 64
HEAD_STEP = 32


def turn(x, shift):
    width = x.shape[1]
    return pltpu.roll(x, lax.rem(width - shift, width), 1)


def apply_kernel(
    factors,
    grad_side,
    side_w,
    side_m,
    side_e,
    grad_a,
    grad_b,
    block_w,
    block_m,
    block_e,
    grad_h,
    head_w,
    head_m,
    head_e,
    grad_cls,
    hside_w,
    hside_m,
    hside_e,
    side_wo,
    side_mo,
    side_eo,
    block_wo,
    block_mo,
    block_eo,
    head_wo,
    head_mo,
    head_eo,
    hside_wo,
    hside_mo,
    hside_eo,
    grad_block,
):
    @pl.when(pl.program_id(0) == 0)
    def _():
        fresh = update(side_w[...], grad_side[:, : side_w.shape[1]], side_m[...], side_e[...], factors[1:2, 0:1])
        side_wo[...], side_mo[...], side_eo[...] = fresh
        first = WIDTH_IN + TAPS
        whole_rows = first // 16 * 16

        @pl.loop(0, whole_rows // 16)
        def _(i):
            here = tall(i * 16, 16)
            grad_block[here, :] = grad_a[here, :].astype(f32)

        grad_block[whole_rows:first, :] = grad_a[whole_rows : whole_rows + 16, :].astype(f32)[: first - whole_rows]
        for i in range(WIDTH_OUT // 16):
            grad_block[first + 16 * i : first + 16 * (i + 1), :] = grad_b[16 * i : 16 * (i + 1), :].astype(f32)
        grad_block[first + WIDTH_OUT :, :] = jnp.zeros(
            (grad_block.shape[0] - first - WIDTH_OUT, grad_block.shape[1]), f32
        )

    here = pl.multiple_of(jnp.minimum(pl.program_id(0), grad_block.shape[0] // BLOCK_STEP - 1) * BLOCK_STEP, BLOCK_STEP)

    for k in range(0, BLOCK_STEP, 16):
        rows = slice(k, k + 16)
        fresh = update(
            block_w[rows, :], grad_block[pl.ds(here + k, 16), :], block_m[rows, :], block_e[rows, :], factors[0:1, 0:1]
        )
        block_wo[rows, :], block_mo[rows, :], block_eo[rows, :] = fresh
    for k in range(0, HEAD_STEP, 16):
        rows = slice(k, k + 16)
        fresh = update(
            head_w[rows, :], grad_h[rows, :].astype(f32), head_m[rows, :], head_e[rows, :], factors[2:3, 0:1]
        )
        head_wo[rows, :], head_mo[rows, :], head_eo[rows, :] = fresh
    fresh = update(hside_w[...], grad_cls[:, : hside_w.shape[1]], hside_m[...], hside_e[...], factors[3:4, 0:1])
    hside_wo[...], hside_mo[...], hside_eo[...] = fresh


def apply(factors, side, grads, block, head_arrays, hside):
    def stepped(array, size):
        last = -(-array.shape[0] // size) - 1
        return pl.BlockSpec((size, array.shape[1]), lambda j: (jnp.minimum(j, last), 0))

    steps = max(-(-block[0].shape[0] // BLOCK_STEP), -(-WIDTH_OUT // HEAD_STEP))
    blocks = (
        [whole(x.shape) for x in side]
        + [whole(x.shape) for x in grads]
        + [stepped(x, BLOCK_STEP) for x in block]
        + [stepped(x, HEAD_STEP) for x in head_arrays]
        + [stepped(x, HEAD_STEP) for x in hside]
    )
    arrays = side + grads + block + head_arrays + hside
    keep = [k for k in range(17) if k not in (0, 4, 5, 9, 13)]
    return pl.pallas_call(
        apply_kernel,
        grid=(steps,),
        out_shape=[jax.ShapeDtypeStruct(arrays[k].shape, f32) for k in keep],
        in_specs=[whole(factors.shape)] + blocks,
        out_specs=[blocks[k] for k in keep],
        scratch_shapes=[VMEM((-(-block[0].shape[0] // BLOCK_STEP) * BLOCK_STEP, block[0].shape[1]), f32)],
        compiler_params=params(),
        name="apply",
    )(factors, *arrays)


def body(
    nd,
    nz,
    images,
    pixel_mask,
    counts,
    labels,
    block_w,
    chan_side,
    head_w,
    head_side,
    shared,
    block_mom,
    side_mom,
    head_mom,
    hside_mom,
    shared_mom,
    block_ema,
    side_ema,
    head_ema,
    hside_ema,
    shared_ema,
    chan_stats,
    head_stats,
    proj_stats,
):
    z = lax.axis_index("chan")
    nb = images.shape[0] // nz
    own = chan_side.shape[1]
    own_head = head_side.shape[0]
    width = own * nz
    head_width = own_head * nz
    end_route = WIDTH_IN * EXPERTS
    end_head = end_route + WIDTH_OUT * EXPERTS
    end_norm = end_head + 2 * WIDTH_OUT
    end_squeeze = end_norm + SQUEEZE
    route_in = shared[:end_route].reshape(WIDTH_IN, EXPERTS)
    route_head = shared[end_route:end_head].reshape(WIDTH_OUT, EXPERTS)
    gain_out = shared[end_head:end_norm].reshape(2, WIDTH_OUT)
    sq_bias = shared[None, end_norm:end_squeeze]
    class_bias = jnp.pad(shared[end_squeeze:], (0, CLASS_PAD - CLASSES))[None, :]

    def mine(x):
        return lax.dynamic_slice_in_dim(x, z * nb, nb, 0)

    image_rows = mine(images).reshape(nb * PIXELS, WIDTH_IN)
    mask_now = mine(pixel_mask).astype(f32)
    mask = jnp.broadcast_to(mask_now.reshape(-1, 1), (nb * PIXELS, LANES))
    mask_rows = jnp.pad(
        (jnp.eye(nb, dtype=f32)[:, :, None] * mask_now[None]).reshape(nb, nb * PIXELS).astype(bf16),
        ((0, 8 - nb), (0, 0)),
    )
    count_rows = jnp.broadcast_to(jnp.pad(mine(counts).astype(f32), (0, 8 - nb))[:, None], (8, LANES))
    label_rows = jnp.broadcast_to(jnp.pad(mine(labels), (0, 8 - nb))[:, None], (8, LANES))

    full_a, full_b, side, gain_head, kern_h, kern_c, squares = first_gather(
        block_w, head_w, head_side, chan_side.T, nd, nz, 1
    )
    pre, taps, dpre, stats_one, stats_two, mix, gates, pooled_in, full_b, full_h, full_c = first_stage(
        full_a,
        image_rows,
        mask,
        mask_rows,
        count_rows,
        route_in,
        side,
        full_b,
        kern_h,
        kern_c,
        nb,
        width,
        nd,
        nz,
        3,
    )
    totals = stats_one
    excited, proj, pooled, gate, squeezed, stats_three, mixed_proj, full_h = project(
        dpre, mask, side, stats_two, totals, count_rows, sq_bias, full_b, mix, full_h, nb, nd, nz, 5
    )
    low, head_pre, mixed_head, stats_four, mix_head, gates_head, head_pool, full_c = head(
        full_h, proj, mask, mask_rows, count_rows, gain_out, route_head, stats_three, totals, full_c, nb, nd, nz, 6
    )
    cls_full = full_c[:, :own_head].reshape(head_width, CLASS_PAD)
    features, grad_logits, sums_four, grad_proj, sums_three, dz_head, half_h, part_h = head_back(
        head_pre,
        mask,
        count_rows,
        label_rows,
        class_bias,
        cls_full,
        gain_head,
        stats_four,
        totals,
        low,
        full_h,
        mixed_head,
        mix_head,
        gates_head,
        route_head,
        proj,
        stats_three,
        nb,
        nd,
        nz,
        8,
    )
    shape_h, shape_b = shard_shape(full_h, nz), shard_shape(full_b, nz)
    grad_norm, sums_two, grad_squeeze, gate_grad, dz_gate, piece_h, half_b, part_b = project_back(
        half_h,
        part_h,
        shape_h,
        grad_proj,
        proj,
        stats_three,
        sums_three,
        gain_out,
        mask,
        count_rows,
        totals,
        stats_two,
        side,
        dpre,
        excited,
        mixed_proj,
        full_b,
        mix,
        gate,
        pooled,
        squeezed,
        sq_bias,
        nb,
        nd,
        nz,
        9,
    )
    lines = [features, grad_logits, pooled, dz_gate, head_pool, pooled_in, grad_squeeze, squeezed, sq_bias, dz_head]
    small = [squares, stats_three, stats_four, sums_four, chan_stats, head_stats, proj_stats]
    grad_a, grad_b, grad_h, grad_cls, grad_side, factors, *rest = stage_back(
        half_b,
        part_b,
        piece_h,
        grad_norm,
        dpre,
        pre,
        taps,
        mask,
        side,
        stats_one,
        stats_two,
        sums_two,
        totals,
        lines,
        image_rows,
        full_a,
        mix,
        gates,
        gate_grad,
        small,
        shape_b,
        shape_h,
        nb,
        nd,
        nz,
        11,
    )
    grad_route_in, grad_route_head, grad_sq_bias, grad_class_bias, new_chan, new_head_stats, new_proj, loss = rest
    results = apply(
        factors,
        [grad_side, chan_side.T, side_mom.T, side_ema.T],
        [grad_a, grad_b],
        [block_w, block_mom, block_ema],
        [grad_h, head_w, head_mom, head_ema],
        [grad_cls, head_side, hside_mom, hside_ema],
    )
    new_side, new_block, new_head, new_hside = (results[3 * k : 3 * k + 3] for k in range(4))
    new_side = [x.T for x in new_side]

    def out_row(first):
        return sums_three[first : first + OUT_CHUNKS].reshape(-1)[:WIDTH_OUT]

    grad_shared = jnp.concatenate(
        [
            grad_route_in.reshape(-1),
            grad_route_head.reshape(-1),
            out_row(OUT_CHUNKS),
            out_row(0),
            grad_sq_bias[0],
            grad_class_bias[0, :CLASSES],
        ]
    )
    new_shared = update(
        shared,
        grad_shared,
        shared_mom,
        shared_ema,
        jnp.sqrt(jnp.sum(shared * shared)) * lax.rsqrt(jnp.sum(grad_shared * grad_shared) + 1e-12),
    )
    groups = (new_block, new_side, new_head, new_hside, new_shared)
    return (
        (loss[0, 0],)
        + tuple(group[k] for k in range(3) for group in groups)
        + (new_chan, new_head_stats, new_proj)
    )


def solution(mesh):
    nd, nz = mesh.shape["dp"], mesh.shape["chan"]
    cols = P(None, "chan")
    state = (cols, cols, cols, P("chan", None), P())
    return jax.shard_map(
        functools.partial(body, nd, nz),
        mesh=mesh,
        in_specs=(P("dp", None, None), P("dp", None), P("dp"), P("dp"))
        + state * 3
        + (cols, cols, cols),
        out_specs=(P(),) + state * 3 + (cols, cols, cols),
        check_vma=False,
    )
```

```python
import functools

import jax
import jax.numpy as jnp
from jax import lax
from jax.experimental import pallas as pl
from jax.experimental.pallas import tpu as pltpu
from jax.sharding import PartitionSpec as P

WIDTH_IN = 192
WIDTH_OUT = 320
SQUEEZE = 48
CLASSES = 1000
EXPERTS = 8
KERNEL = 5
MAP_SIDE = 16
TAPS = KERNEL * KERNEL
PIXELS = MAP_SIDE * MAP_SIDE
LANES = 128
CLASS_PAD = 1024
TOTAL_ROW = 18
eps_norm = 0.001
highest = lax.Precision.HIGHEST
MESH = pl.DeviceIdType.MESH
f32 = jnp.float32
bf16 = jnp.bfloat16
VMEM = pltpu.VMEM
VLIMIT = 60 * 1024 * 1024


def dot(a, b, dims=((1,), (0,)), precision=None):
    return lax.dot_general(a, b, (dims, ((), ())), precision=precision, preferred_element_type=f32)


NN = ((1,), (0,))
NT = ((1,), (1,))
TN = ((0,), (0,))


def sig(x):
    return 0.5 * jnp.tanh(0.5 * x) + 0.5


def dsilu(n):
    s = sig(n)
    return s * (1.0 + n * (1.0 - s))


def rsum(x):
    return jnp.sum(x, axis=0, keepdims=True)


def split(x):
    high = x.astype(bf16)
    return jnp.concatenate([high, (x - high.astype(f32)).astype(bf16)], axis=0)


def sum_peers(nd, nz):
    d = lax.axis_index("dp")
    z = lax.axis_index("chan")
    in_plane = [(lax.rem(d + k, nd), z) for k in range(1, nd)]
    along = [(d, lax.rem(z + k, nz)) for k in range(1, nz)]
    return in_plane, along


def signal(peers):
    barrier = pltpu.get_barrier_semaphore()
    for peer in peers:
        pl.semaphore_signal(barrier, inc=1, device_id=peer, device_id_type=MESH)


def sum_start(nd, nz):
    in_plane, along = sum_peers(nd, nz)
    signal(in_plane + along)


def met(nd, nz):
    pl.semaphore_wait(pltpu.get_barrier_semaphore(), nd + nz - 2)


def sum_copies(nd, nz, x_ref, plane, depth, s1, r1, s2, r2):
    d = lax.axis_index("dp")
    z = lax.axis_index("chan")
    in_plane, along = sum_peers(nd, nz)

    def copy(src, dst, send, recv, peer):
        return pltpu.make_async_remote_copy(
            src_ref=src, dst_ref=dst, send_sem=send, recv_sem=recv, device_id=peer, device_id_type=MESH
        )

    first = [copy(x_ref, plane.at[d], s1.at[k], r1.at[k], peer) for k, peer in enumerate(in_plane)]
    second = [copy(depth.at[z], depth.at[z], s2.at[k], r2.at[k], peer) for k, peer in enumerate(along)]
    return first, second


def sum_first(nd, nz, x_ref, plane, *comm):
    start(sum_copies(nd, nz, x_ref, plane, *comm)[0])
    plane[lax.axis_index("dp")] = x_ref[...]


def sum_second(nd, nz, x_ref, plane, depth, *sems):
    first, second = sum_copies(nd, nz, x_ref, plane, depth, *sems)
    arrived(first)
    total = plane[0]
    for k in range(1, nd):
        total = total + plane[k]
    depth[lax.axis_index("chan")] = total
    start(second)


def sum_third(nd, nz, x_ref, plane, depth, *sems):
    first, second = sum_copies(nd, nz, x_ref, plane, depth, *sems)
    arrived(second)
    total = depth[0]
    for k in range(1, nz):
        total = total + depth[k]
    sent(first + second)
    return total


def sum_finish(nd, nz, x_ref, o_ref, *comm):
    sum_first(nd, nz, x_ref, *comm)
    sum_second(nd, nz, x_ref, *comm)
    o_ref[...] = sum_third(nd, nz, x_ref, *comm)


def sum_scratch(rows, nd, nz):
    return [
        VMEM((rows, LANES), f32),
        VMEM((nd, rows, LANES), f32),
        VMEM((nz, rows, LANES), f32),
        pltpu.SemaphoreType.DMA((nd,)),
        pltpu.SemaphoreType.DMA((nd,)),
        pltpu.SemaphoreType.DMA((nz,)),
        pltpu.SemaphoreType.DMA((nz,)),
    ]


def params(ident=None, limit=VLIMIT):
    if ident is None:
        return pltpu.CompilerParams(vmem_limit_bytes=VLIMIT)
    return pltpu.CompilerParams(vmem_limit_bytes=limit, collective_id=ident, has_side_effects=True)


def sum_kernel(nd, nz, x_ref, o_ref, *comm):
    sum_start(nd, nz)
    met(nd, nz)
    sum_finish(nd, nz, x_ref, o_ref, *comm)


def all_sum(x, nd, nz, ident):
    return pl.pallas_call(
        functools.partial(sum_kernel, nd, nz),
        out_shape=jax.ShapeDtypeStruct(x.shape, x.dtype),
        in_specs=[pl.BlockSpec(memory_space=VMEM)],
        out_specs=pl.BlockSpec(memory_space=VMEM),
        scratch_shapes=sum_scratch(x.shape[0], nd, nz)[1:],
        compiler_params=params(ident),
        name="all_sum",
    )(x)


def by_column(width):
    return (width // 2) % LANES == 0


def pad_rows(rows, width, nd):
    unit = 16 * (nd // 2 if by_column(width) else nd)
    return -(-rows // unit) * unit


def core_block(rows, width, core):
    if by_column(width):
        return 0, rows, pl.multiple_of(core * (width // 2), LANES), width // 2
    return pl.multiple_of(core * (rows // 2), 16), rows // 2, 0, width


def part(rows, width, nd, core, place):
    row, count, col, cols = core_block(rows, width, core)
    unit = count // (nd // 2)
    return pl.multiple_of(row + place * unit, 16), unit, col, cols


class Net:
    def __init__(self, nd, nz):
        self.nd, self.nz, self.nxy = nd, nz, nd // 2
        self.d = lax.axis_index("dp")
        self.z = lax.axis_index("chan")
        self.core = lax.rem(self.d, 2)
        self.place = self.d // 2
        self.far = [lax.rem(self.z + k, nz) for k in range(1, nz)]
        self.others = [lax.rem(self.place + k, self.nxy) for k in range(1, self.nxy)]
        self.along = [(self.d, zz) for zz in self.far]
        self.plane = [(2 * o + self.core, self.z) for o in self.others]
        self.twin = (2 * self.place + 1 - self.core, self.z)

    def copy(self, src, dst, sems, k, peer):
        return pltpu.make_async_remote_copy(
            src_ref=src,
            dst_ref=dst,
            send_sem=sems[0].at[k],
            recv_sem=sems[1].at[k],
            device_id=peer,
            device_id_type=MESH,
        )


def start(copies):
    for copy in copies:
        copy.start()


def arrived(copies):
    for copy in copies:
        copy.wait_recv()


def sent(copies):
    for copy in copies:
        copy.wait_send()


def pair(n):
    return [pltpu.SemaphoreType.DMA((n,)), pltpu.SemaphoreType.DMA((n,))]


def lanes(first, count):
    return pl.ds(pl.multiple_of(first, LANES), count)


def tall(first, count):
    return pl.ds(pl.multiple_of(first, 16), count)


def spot(ref, shape, zz, row, unit, col, cols):
    if len(ref.shape) == 3:
        return ref.at[zz, tall(row, unit), lanes(col, cols)]
    return ref.at[tall(row, unit), lanes(zz * shape[1] + col, cols)]


def shard_shape(full, nz):
    if len(full.shape) == 3:
        return full.shape[1:]
    return (full.shape[0], full.shape[1] // nz)


def own_copy(net, shape, src, dst, sem):
    return pltpu.make_async_copy(src, spot(dst, shape, net.z, 0, shape[0], 0, shape[1]), sem)


def gather_far(net, shape, src, dst, sems):
    rows, width = shape
    row, unit, col, cols = part(rows, width, net.nd, net.core, net.place)
    block = src.at[tall(row, unit), lanes(col, cols)]
    return [
        net.copy(block, spot(dst, shape, net.z, row, unit, col, cols), sems, k, peer)
        for k, peer in enumerate(net.along)
    ]


def gather_plane(net, shape, ref, sems, k):
    rows, width = shape
    row, unit, col, cols = part(rows, width, net.nd, net.core, net.place)
    block = spot(ref, shape, net.far[k], row, unit, col, cols)
    n = net.nxy - 1
    return [net.copy(block, block, sems, k * n + q, peer) for q, peer in enumerate(net.plane)]


def gather_twin(net, shape, ref, sems, k):
    rows, width = shape
    row, unit, col, cols = core_block(rows, width, net.core)
    block = spot(ref, shape, net.far[k], row, unit, col, cols)
    return [net.copy(block, block, sems, k, net.twin)]


def late_count(nz):
    return max(1, (nz - 1) // 3)


def some(stage, net, shape, ref, sems, shards):
    return [copy for k in shards for copy in stage(net, shape, ref, sems, k)]


def every(stage, net, shape, ref, sems):
    return [copy for k in range(net.nz - 1) for copy in stage(net, shape, ref, sems, k)]


def squares_of(ref, rows):
    step_rows = 16 if ref.dtype == bf16 else 8
    whole_rows = rows // step_rows * step_rows

    def step(i, total):
        value = ref[pl.ds(pl.multiple_of(i * step_rows, step_rows), step_rows), :].astype(f32)
        return total + value * value

    total = jnp.sum(lax.fori_loop(0, whole_rows // step_rows, step, jnp.zeros((step_rows, ref.shape[1]), f32)))
    if whole_rows < rows:
        last = ref[whole_rows:rows, :].astype(f32)
        total = total + jnp.sum(last * last)
    return total


def row_of(total):
    lane = lax.broadcasted_iota(jnp.int32, (1, LANES), 1)
    return jnp.where(lane == 0, total, 0.0)


def first_kernel(nd, nz, shape, shape_b, block_ref, head_ref, hside_ref, side_ref, full, full_b, side, gain, kh, kc, squares, wide, tall_h, tall_s, kb, low, side_buf, gain_buf, far_s, far_r, plane_s, plane_r, twin_s, twin_r, side_s, side_r, gain_s, gain_r, later_s, later_r, local):
    net = Net(nd, nz)
    signal(net.along + net.plane + [net.twin])
    rows = shape[0]
    total_rows = block_ref.shape[0]
    fetch = [
        pltpu.make_async_copy(block_ref.at[pl.ds(0, rows)], wide.at[pl.ds(0, rows)], local.at[0]),
        pltpu.make_async_copy(
            block_ref.at[pl.ds(rows, total_rows - rows)], wide.at[pl.ds(rows, total_rows - rows)], local.at[1]
        ),
        pltpu.make_async_copy(hside_ref, tall_s, local.at[2]),
        pltpu.make_async_copy(head_ref, tall_h, local.at[3]),
    ]
    fetch[0].start()
    fetch[0].wait()
    start(fetch[1:])

    @pl.loop(0, rows // 16)
    def _(i):
        at = tall(i * 16, 16)
        low[at, :] = wide[at, :].astype(bf16)

    own = own_copy(net, shape, low, full, local.at[4])
    own.start()
    pl.semaphore_wait(pltpu.get_barrier_semaphore(), nz - 1 + nd // 2)
    far = gather_far(net, shape, low, full, (far_s, far_r))
    start(far)
    side_buf[net.z] = jnp.transpose(side_ref[...])
    sides = [
        net.copy(side_buf.at[net.z], side_buf.at[net.z], (side_s, side_r), k, peer)
        for k, peer in enumerate(net.along)
    ]
    start(sides)
    fetch[2].wait()
    gain_buf[net.z] = jnp.transpose(tall_s[:, 0:LANES])[0:8]
    gains = [
        net.copy(gain_buf.at[net.z], gain_buf.at[net.z], (gain_s, gain_r), k, peer)
        for k, peer in enumerate(net.along)
    ]
    start(gains)
    fetch[1].wait()
    first = WIDTH_IN + TAPS
    for i in range(WIDTH_OUT // 16):
        kb[16 * i : 16 * (i + 1), :] = wide[first + 16 * i : first + 16 * (i + 1), :].astype(bf16)
    own_b = own_copy(net, shape_b, kb, full_b, local.at[5])
    own_b.start()
    planes = []
    for k in range(nz - 1):
        arrived([far[nz - 2 - k]])
        planes.append(gather_plane(net, shape, full, (plane_s, plane_r), k))
        start(planes[k])
    later = gather_far(net, shape_b, kb, full_b, (later_s, later_r))
    start(later)
    fetch[3].wait()

    @pl.loop(0, WIDTH_OUT // 16)
    def _(i):
        at = tall(i * 16, 16)
        kh[at, :] = tall_h[at, :].astype(bf16)

    for i in range(tall_s.shape[0] // 16):
        value = tall_s[16 * i : 16 * (i + 1), 2 : 2 + CLASSES]
        kc[16 * i : 16 * (i + 1), :] = jnp.concatenate(
            [value, jnp.zeros((16, CLASS_PAD - CLASSES), f32)], axis=1
        ).astype(bf16)
    squares[...] = jnp.zeros_like(squares)
    for k, (ref, count) in enumerate(
        ((wide, total_rows), (side_ref, side_ref.shape[0]), (tall_h, WIDTH_OUT), (tall_s, tall_s.shape[0]))
    ):
        squares[k : k + 1, :] = row_of(squares_of(ref, count))
    twins = []
    for k in range(nz - 1):
        arrived(planes[k])
        twins.append(gather_twin(net, shape, full, (twin_s, twin_r), k))
        start(twins[k])
    arrived(sides + gains)
    side[...] = jnp.zeros_like(side)
    side[0 : side_ref.shape[1], :] = jnp.concatenate([side_buf[k] for k in range(nz)], axis=1)
    gain[...] = jnp.concatenate([gain_buf[k] for k in range(nz)], axis=1)
    for k in range(nz - 1):
        arrived(twins[k])
    arrived(later)
    sent(far + sides + gains + later)
    for k in range(nz - 1):
        sent(planes[k] + twins[k])
    own.wait()
    own_b.wait()


def first_gather(block, head_w, head_side, side, nd, nz, ident):
    shape = (pad_rows(WIDTH_IN + TAPS, block.shape[1], nd), block.shape[1])
    shape_b = (pad_rows(WIDTH_OUT, block.shape[1], nd), block.shape[1])
    shape_h = (pad_rows(WIDTH_OUT, head_w.shape[1], nd), head_w.shape[1])
    shape_c = (pad_rows(head_side.shape[0], CLASS_PAD, nd), CLASS_PAD)
    hbm = pl.BlockSpec(memory_space=pltpu.HBM)
    vmem = pl.BlockSpec(memory_space=VMEM)
    own_head = head_side.shape[0]
    return pl.pallas_call(
        functools.partial(first_kernel, nd, nz, shape, shape_b),
        out_shape=[
            jax.ShapeDtypeStruct((shape[0], nz * shape[1]), bf16),
            jax.ShapeDtypeStruct((shape_b[0], nz * shape_b[1]), bf16),
            jax.ShapeDtypeStruct((104, nz * side.shape[0]), f32),
            jax.ShapeDtypeStruct((8, nz * own_head), f32),
            jax.ShapeDtypeStruct(shape_h, bf16),
            jax.ShapeDtypeStruct(shape_c, bf16),
            jax.ShapeDtypeStruct((8, LANES), f32),
        ],
        in_specs=[hbm, hbm, hbm, vmem],
        out_specs=[hbm] * 2 + [vmem] * 5,
        scratch_shapes=[
            VMEM(block.shape, f32),
            VMEM(head_w.shape, f32),
            VMEM(head_side.shape, f32),
            VMEM(shape_b, bf16),
            VMEM(shape, bf16),
            VMEM((nz, side.shape[1], side.shape[0]), f32),
            VMEM((nz, 8, own_head), f32),
        ]
        + pair(nz - 1)
        + pair((nz - 1) * (nd // 2 - 1))
        + pair(nz - 1)
        + pair(nz - 1) * 3
        + [pltpu.SemaphoreType.DMA((6,))],
        compiler_params=params(ident),
        name="first_gather",
    )(block, head_w, head_side, side)


def reduce_sizes(rows, width, nd):
    unit, cols = (rows, width // 2) if by_column(width) else (rows // 2, width)
    return unit, cols, unit // (nd // 2)


def reduce_twin(net, shape, g_ref, twin_buf, sems, k):
    row, unit, col, cols = core_block(shape[0], shape[1], 1 - net.core)
    return net.copy(
        g_ref.at[tall(row, unit), lanes(k * shape[1] + col, cols)], twin_buf.at[k], sems, k, net.twin
    )


def reduce_add(net, shape, g_ref, half, twin_buf, k):
    row, unit, col, cols = core_block(shape[0], shape[1], net.core)

    @pl.loop(0, unit // 16)
    def _(i):
        at = tall(i * 16, 16)
        mine = g_ref[tall(row + i * 16, 16), lanes(k * shape[1] + col, cols)]
        half[k, at, :] = (mine.astype(f32) + twin_buf[k, at, :].astype(f32)).astype(bf16)


def reduce_plane(net, shape, half, plane_buf, sems, k, base, shift):
    size = reduce_sizes(*shape, net.nd)[2]
    n = net.nxy - 1
    return [
        net.copy(half.at[k - shift, tall(o * size, size)], plane_buf.at[q, k - base], sems, (k - base) * n + q, net.plane[q])
        for q, o in enumerate(net.others)
    ]


def reduce_plane_sum(net, shape, half, plane_buf, out, k, base, shift):
    size = reduce_sizes(*shape, net.nd)[2]

    @pl.loop(0, size // 16)
    def _(i):
        at = tall(i * 16, 16)
        total = half[k - shift, tall(net.place * size + i * 16, 16), :].astype(f32)
        for q in range(net.nxy - 1):
            total = total + plane_buf[q, k - base, at, :].astype(f32)
        out[k, at, :] = total.astype(bf16)


def reduce_far(net, sums, depth_buf, sems):
    return [net.copy(sums.at[zz], depth_buf.at[k], sems, k, net.along[k]) for k, zz in enumerate(net.far)]


def reduce_far_sum(net, shape, sums, depth_buf, piece):
    @pl.loop(0, reduce_sizes(*shape, net.nd)[2] // 16)
    def _(i):
        at = tall(i * 16, 16)
        total = sums[net.z, at, :].astype(f32)
        for q in range(net.nz - 1):
            total = total + depth_buf[q, at, :].astype(f32)
        piece[at, :] = total.astype(bf16)


def spread_block(net, shape, out):
    row, unit, col, cols = part(shape[0], shape[1], net.nd, net.core, net.place)
    return out.at[tall(row, unit), lanes(col, cols)]


def spread_plane(net, shape, piece, out, sems):
    block = spread_block(net, shape, out)
    return [net.copy(piece, block, sems, q, peer) for q, peer in enumerate(net.plane)]


def spread_twin(net, shape, out, sems):
    row, unit, col, cols = core_block(shape[0], shape[1], net.core)
    block = out.at[tall(row, unit), lanes(col, cols)]
    return [net.copy(block, block, sems, 0, net.twin)]


def twin_scratch(shape, nd, nz):
    unit, cols, size = reduce_sizes(*shape, nd)
    return [VMEM((shape[0], nz * shape[1]), bf16), VMEM((nz, unit, cols), bf16)] + pair(nz)


def plane_scratch(shape, nd, count):
    unit, cols, size = reduce_sizes(*shape, nd)
    return [VMEM((nd // 2 - 1, count, size, cols), bf16)] + pair(count * (nd // 2 - 1))


def half_shape(shape, nd, nz):
    unit, cols, size = reduce_sizes(*shape, nd)
    return (nz, unit, cols)


def part_shape(shape, nd, nz):
    unit, cols, size = reduce_sizes(*shape, nd)
    return (nz, size, cols)


def ready(shape, k):
    return max(2, -(-(k + 1) * shape[1] // (LANES * EXPERTS)))


class Steps:
    def __init__(self):
        self.steps = {}

    def at(self, step, action):
        self.steps.setdefault(step, []).append(action)

    def emit(self, now, last):
        for step in sorted(self.steps):
            if step < last:

                @pl.when(now == step)
                def _(step=step):
                    for action in self.steps[step]:
                        action()

    def end(self, last):
        for step in sorted(self.steps):
            if step >= last:
                for action in self.steps[step]:
                    action()


def far_scratch(shape, nd, nz):
    unit, cols, size = reduce_sizes(*shape, nd)
    return [VMEM((nz - 1, size, cols), bf16)] + pair(nz - 1)


def spread_scratch(shape, nd, nz):
    return [pltpu.SemaphoreType.DMA((1,))] + pair(nd // 2 - 1) + pair(1)


def piece_shape(shape, nd):
    unit, cols, size = reduce_sizes(*shape, nd)
    return (size, cols)


class Twin:
    def __init__(self, net, shape, half, g_ref, twin_buf, ts, tr):
        self.net, self.shape, self.half, self.g, self.buf, self.sems = net, shape, half, g_ref, twin_buf, (ts, tr)

    def copy(self, k):
        return reduce_twin(self.net, self.shape, self.g, self.buf, self.sems, k)

    def begin(self, k):
        self.copy(k).start()

    def add(self, k):
        self.copy(k).wait_recv()
        reduce_add(self.net, self.shape, self.g, self.half, self.buf, k)

    def finish(self):
        for k in range(self.net.nz):
            self.copy(k).wait_send()


class Plane:
    def __init__(self, net, shape, half, out, base, count, buf, ps, pr, shift=0):
        self.net, self.shape, self.half, self.out = net, shape, half, out
        self.shards, self.base, self.buf, self.sems = range(base, base + count), base, buf, (ps, pr)
        self.shift = shift

    def copies(self, k):
        return reduce_plane(self.net, self.shape, self.half, self.buf, self.sems, k, self.base, self.shift)

    def begin(self, k):
        start(self.copies(k))

    def add(self, then=None):
        for k in self.shards:
            self.add_one(k, then)

    def add_one(self, k, then=None):
        arrived(self.copies(k))
        reduce_plane_sum(self.net, self.shape, self.half, self.buf, self.out, k, self.base, self.shift)
        if then is not None:
            then(k)

    def finish(self):
        for k in self.shards:
            sent(self.copies(k))


class Far:
    def __init__(self, net, shape, sums, piece, buf, fs, fr):
        self.net, self.shape, self.sums, self.piece, self.buf, self.sems = net, shape, sums, piece, buf, (fs, fr)

    def copies(self):
        return reduce_far(self.net, self.sums, self.buf, self.sems)

    def send(self, k):
        net = self.net
        slot = lax.rem(k - net.z - 1 + net.nz, net.nz)

        @pl.when(net.z != k)
        def _():
            net.copy(self.sums.at[k], self.buf.at[slot], self.sems, slot, (net.d, k)).start()

    def add(self):
        arrived(self.copies())
        reduce_far_sum(self.net, self.shape, self.sums, self.buf, self.piece)

    def finish(self):
        sent(self.copies())


class Spread:
    def __init__(self, net, shape, piece, out, local, ps, pr, ts, tr):
        self.net, self.shape, self.piece, self.out, self.local = net, shape, piece, out, local
        self.plane_sems, self.twin_sems = (ps, pr), (ts, tr)

    def own(self):
        return pltpu.make_async_copy(self.piece, spread_block(self.net, self.shape, self.out), self.local.at[0])

    def plane(self):
        return spread_plane(self.net, self.shape, self.piece, self.out, self.plane_sems)

    def twin(self):
        return spread_twin(self.net, self.shape, self.out, self.twin_sems)

    def begin(self):
        self.own().start()
        start(self.plane())

    def cross(self):
        arrived(self.plane())
        self.own().wait()
        start(self.twin())

    def finish(self):
        arrived(self.twin())
        sent(self.plane() + self.twin())


def up_to(size):
    return -(-size // LANES) * LANES


def share_width(lines, nz):
    one = [0]
    for x in lines[0], lines[2], lines[3]:
        one.append(one[-1] + up_to(x.shape[1] // nz))
    for _ in range(3):
        one.append(one[-1] + LANES)
    two = [0]
    for x in lines[1], lines[4], lines[5]:
        two.append(two[-1] + up_to(x.shape[1]))
    return one, two, max(one[-1], two[-1])


def share_scratch(width, nd, nz):
    return (
        [VMEM((nz, 8, width), f32), pltpu.SemaphoreType.DMA((1,))]
        + pair(nz - 1)
        + pair(nd // 2 - 1)
        + pair(nd // 2)
    )


def fit(x, width):
    if x.shape[1] == width:
        return x
    return jnp.concatenate([x, jnp.zeros((x.shape[0], width - x.shape[1]), f32)], axis=1)


class Share:
    def __init__(self, net, rows_all, lines, local, fs, fr, ps, pr, ts, tr):
        self.net, self.rows, self.lines, self.local = net, rows_all, lines, local
        self.far_sems, self.plane_sems, self.twin_sems = (fs, fr), (ps, pr), (ts, tr)
        self.me = net.d * net.nz + net.z

    def fill(self, nb, cut, narrow, wide):
        width = self.lines.shape[2]
        self.lines[...] = jnp.zeros_like(self.lines)
        two = fit(jnp.concatenate([fit(x, up_to(x.shape[1])) for x in wide], axis=1), width)[:nb]
        last = [fit(x, LANES) for x in narrow]
        for k in range(self.net.nz):
            parts = []
            for x in cut:
                own = x.shape[1] // self.net.nz
                parts.append(fit(x[:, k * own : (k + 1) * own], up_to(own)))
            one = fit(jnp.concatenate(parts + last, axis=1), width)[:nb]
            self.lines[k, 0 : 2 * nb, :] = jnp.concatenate([one, two], axis=0)

    def far_copies(self):
        net = self.net
        return [
            net.copy(self.lines.at[zz], self.rows.at[self.me], self.far_sems, k, net.along[k])
            for k, zz in enumerate(net.far)
        ]

    def plane_copies(self):
        net = self.net
        block = self.rows.at[pl.ds(net.d * net.nz, net.nz)]
        return [net.copy(block, block, self.plane_sems, q, peer) for q, peer in enumerate(net.plane)]

    def twin_copies(self):
        net = self.net
        out = []
        for o in range(net.nxy):
            block = self.rows.at[pl.ds((2 * o + net.core) * net.nz, net.nz)]
            out.append(net.copy(block, block, self.twin_sems, o, net.twin))
        return out

    def far(self):
        start(self.far_copies())
        self.own().start()

    def own(self):
        return pltpu.make_async_copy(self.lines.at[self.net.z], self.rows.at[self.me], self.local.at[0])

    def plane(self):
        arrived(self.far_copies())
        self.own().wait()
        start(self.plane_copies())

    def twin(self):
        arrived(self.plane_copies())
        start(self.twin_copies())

    def finish(self):
        arrived(self.twin_copies())
        sent(self.far_copies() + self.plane_copies() + self.twin_copies())


def build_mix(gates, nb, ref):
    deep = LANES * EXPERTS
    row = lax.broadcasted_iota(jnp.int32, (deep, EXPERTS), 0)
    col = lax.broadcasted_iota(jnp.int32, (deep, EXPERTS), 1)
    pick = jnp.where((row & (EXPERTS - 1)) == col, 1.0, 0.0).astype(f32)
    row = lax.broadcasted_iota(jnp.int32, (deep, LANES), 0)
    col = lax.broadcasted_iota(jnp.int32, (deep, LANES), 1)
    same = (row >> 3) == col
    for b in range(nb):
        spread = jnp.broadcast_to(gates[b : b + 1, :], (LANES, EXPERTS))
        value = jnp.where(same, dot(pick, spread, NT, highest), 0.0)
        high = value.astype(bf16)
        ref[:, b * LANES : (b + 1) * LANES] = high
        ref[:, (nb + b) * LANES : (nb + b + 1) * LANES] = (value - high.astype(f32)).astype(bf16)


def mix_kernels(kernels, mix):
    both = dot(kernels, mix)
    half = both.shape[1] // 2
    return both[:, :half] + both[:, half:]


def gate_sums(rows):
    deep = LANES * EXPERTS
    row = lax.broadcasted_iota(jnp.int32, (deep, EXPERTS), 0)
    col = lax.broadcasted_iota(jnp.int32, (deep, EXPERTS), 1)
    pick = jnp.where((row & (EXPERTS - 1)) == col, 1.0, 0.0).astype(f32)
    return dot(rows, pick, NN, highest)


def gate_rows(grad, kernel_block):
    both = dot(grad, kernel_block, TN)
    row = lax.broadcasted_iota(jnp.int32, both.shape, 0)
    col = lax.broadcasted_iota(jnp.int32, both.shape, 1)
    return rsum(jnp.where(row == (col >> 3), both, 0.0))


def norm_rows(stats, chunk, chunks, total):
    mean = stats[pl.ds(chunk, 1), :] / total
    var = stats[pl.ds(chunks + chunk, 1), :] / total - mean * mean
    return mean, lax.rsqrt(var + eps_norm)


def whole(shape):
    return pl.BlockSpec(shape, lambda *_: (0,) * len(shape), pipeline_mode=pl.Buffered(1))


def image(b):
    return pl.ds(pl.multiple_of(b * PIXELS, PIXELS), PIXELS)


def shifted(value, step):
    if step == 0:
        return value
    col = lax.broadcasted_iota(jnp.int32, value.shape, 0) & (MAP_SIDE - 1)
    moved = pltpu.roll(value, (-step) % PIXELS, 0)
    keep = (col + step >= 0) & (col + step < MAP_SIDE)
    return jnp.where(keep, moved, 0.0)


def stage_kernel(
    nd,
    nz,
    nb,
    chunks,
    shapes,
    kern_ref,
    images,
    mask,
    mask_rows,
    counts,
    route,
    side,
    sq_bias,
    in_b,
    kh,
    kc,
    pre_out,
    taps_out,
    out,
    stats_all,
    sums_all,
    mix,
    gates,
    pooled,
    excited,
    proj,
    pool_out,
    gate_out,
    squeezed,
    last_all,
    mixed,
    full_b,
    full_h,
    full_c,
    pre,
    taps,
    buf,
    held,
    early,
    late,
    early_two,
    late_two,
    sums_three,
    dpre,
    exc,
    kern_buf,
    *comm,
):
    step = pl.program_id(0)
    comm_early, comm_late, comm_two, sems = comm[0:6], comm[6:12], comm[12:18], comm[18:]
    two_early, two_late, sems = sems[0:6], sems[6:12], sems[12:]
    cut_two = chunks // 2
    net = Net(nd, nz)
    few = late_count(nz)
    cut = chunks // 2
    groups = [[k for k in range(nz - 1) if 3 * k // (nz - 1) == g] for g in range(3)]

    def far_h():
        return gather_far(net, shapes[1], kh, full_h, sems[0:2])

    def far_c():
        return gather_far(net, shapes[2], kc, full_c, sems[2:4])

    def planes_b(k):
        return gather_plane(net, shapes[0], full_b, sems[4:6], k)

    def planes_h():
        return every(gather_plane, net, shapes[1], full_h, sems[6:8])

    def twins_b(k):
        return gather_twin(net, shapes[0], full_b, sems[8:10], k)

    def own():
        return [
            own_copy(net, shapes[1], kh, full_h, sems[10].at[0]),
            own_copy(net, shapes[2], kc, full_c, sems[10].at[1]),
        ]

    def b_planes(group):
        for k in groups[group]:
            start(planes_b(k))

    def begin():
        met(nd, nz)
        b_planes(0)
        start(far_h() + own())

    def early_sum():
        sum_first(nd, nz, early, *comm_early)

    def early_second():
        sum_second(nd, nz, early, *comm_early)

    def early_third():
        stats_all[...] = sum_third(nd, nz, early, *comm_early)
        sum_first(nd, nz, late, *comm_late)

    def late_second():
        sum_second(nd, nz, late, *comm_late)

    def late_third():
        stats_all[...] += sum_third(nd, nz, late, *comm_late)

    def h_planes(k):
        start(gather_plane(net, shapes[1], full_h, sems[6:8], k))

    def twins_h(k):
        return gather_twin(net, shapes[1], full_h, sems[11:13], k)

    def h_twin(k):
        arrived(gather_plane(net, shapes[1], full_h, sems[6:8], k))
        start(twins_h(k))

    def load(k):
        return pltpu.make_async_copy(
            full_b.at[pl.ds(0, WIDTH_OUT), lanes(k * LANES * EXPERTS, LANES * EXPERTS)],
            kern_buf.at[lax.rem(k, 2)],
            sems[13].at[lax.rem(k, 2)],
        )

    def b_whole():
        for k in range(nz - 1):
            arrived(twins_b(k))
        load(0).start()

    def b_twins(group):
        for k in groups[group]:
            arrived(planes_b(k))
            start(twins_b(k))

    @pl.when(step == 0)
    def _():
        sum_start(nd, nz)
        early[...] = jnp.zeros_like(early)
        late[...] = jnp.zeros_like(late)
        for ref in (early_two, late_two, sums_three, squeezed, pool_out):
            ref[...] = jnp.zeros_like(ref)
        early[2 * chunks : 2 * chunks + 1, :] = rsum(counts[...])
        early[2 * chunks + 1 : 2 * chunks + 2, :] = rsum(jnp.where(counts[...] > 0.0, 1.0, 0.0))
        pool = dot(mask_rows[...], images[...]) / jnp.maximum(counts[:, 0:1], 1.0)
        pooled[...] = pool
        gate = sig(dot(pool, route[...], NN, highest))
        gates[...] = gate
        build_mix(gate, nb, mix)

    steps = Steps()
    steps.at(1, begin)
    steps.at(cut, early_sum)
    steps.at(cut + 2, early_second)
    steps.at(cut + 3, functools.partial(b_planes, 1))
    steps.at(chunks, early_third)
    steps.at(chunks + 2, late_second)
    steps.at(chunks + 2, functools.partial(b_planes, 2))
    steps.at(chunks + cut, late_third)
    steps.at(chunks + cut, lambda: arrived(far_h()))
    steps.at(chunks + cut, lambda: start(far_c()))
    places = (chunks + cut_two, chunks + cut_two + 2, 2 * chunks, 2 * chunks, 2 * chunks + 2, 2 * chunks + cut_two)
    split_sum(nd, nz, steps, places, early_two, late_two, sums_all, two_early, two_late)
    later_steps = (chunks + cut_two + 1, 2 * chunks + 1, 2 * chunks + cut_two)
    for k in range(nz - 1):
        group = 3 * k // (nz - 1)
        steps.at(later_steps[group], functools.partial(h_planes, k))
        steps.at((2 * chunks + 2, 3 * chunks, 4 * chunks - 3)[group], functools.partial(h_twin, k))
    steps.at(2 * chunks - 1, b_whole)
    steps.at(chunks - 1, functools.partial(b_twins, 0))
    steps.at(chunks + 3, functools.partial(b_twins, 1))
    steps.at(2 * chunks - 3, functools.partial(b_twins, 2))
    steps.emit(step, 4 * chunks)

    @pl.when(step < chunks)
    def _():
        j = step
        mixed = mix_kernels(kern_ref[...], mix[...])
        one = jnp.zeros((1, LANES), f32)
        two = jnp.zeros((1, LANES), f32)
        for b in range(nb):
            at = slice(b * PIXELS, (b + 1) * PIXELS)
            lane = slice(b * LANES, (b + 1) * LANES)
            taps[j, b] = mixed[WIDTH_IN : WIDTH_IN + 32, lane]
            taps_out[b] = mixed[WIDTH_IN : WIDTH_IN + 32, lane]
            value = dot(images[at, :], mixed[:WIDTH_IN, lane].astype(bf16))
            pre[j, at, :] = value
            pre_out[at, :] = value
            masked = mask[at, :] * value
            one = one + rsum(masked)
            two = two + rsum(masked * value)

        @pl.when(j < cut)
        def _():
            early[pl.ds(j, 1), :] = one
            early[pl.ds(chunks + j, 1), :] = two

        @pl.when(j >= cut)
        def _():
            late[pl.ds(j, 1), :] = one
            late[pl.ds(chunks + j, 1), :] = two

    @pl.when((step >= chunks) & (step < 2 * chunks))
    def _():
        j = step - chunks
        mean, rstd = norm_rows(stats_all, j, chunks, stats_all[2 * chunks : 2 * chunks + 1, :])
        scale = rstd * side[2 * SQUEEZE : 2 * SQUEEZE + 1, :]
        bias = side[2 * SQUEEZE + 1 : 2 * SQUEEZE + 2, :]
        held[...] = jnp.zeros_like(held)

        @pl.loop(0, nb)
        def _(b):
            at = image(b)
            normed = (pre[j, at, :] - mean) * scale + bias
            act = normed * sig(normed) * mask[at, :]
            for s in range(KERNEL):
                buf[s] = shifted(act, s - KERNEL // 2)
            taps_now = [jnp.broadcast_to(taps[j, b, t : t + 1, :], (MAP_SIDE, LANES)) for t in range(TAPS)]
            acc = [None] * MAP_SIDE
            for y in range(MAP_SIDE):
                for s in range(KERNEL):
                    x = buf[s, y * MAP_SIDE : (y + 1) * MAP_SIDE, :]
                    for r in range(KERNEL):
                        i = y - r + KERNEL // 2
                        if 0 <= i < MAP_SIDE:
                            term = taps_now[r * KERNEL + s] * x
                            acc[i] = term if acc[i] is None else acc[i] + term
                done = [y - 2] if y < MAP_SIDE - 1 else [y - 2, y - 1, y]
                for i in done:
                    if i >= 0:
                        out[pl.ds(pl.multiple_of(b * PIXELS + i * MAP_SIDE, MAP_SIDE), MAP_SIDE), :] = acc[i]
            value = out[at, :]
            dpre[j, at, :] = value
            masked = mask[at, :] * value
            held[0:1, :] += rsum(masked)
            held[1:2, :] += rsum(masked * value)

        store_sums(early_two, late_two, cut_two, chunks, j, held[0:1, :], held[1:2, :])

    total = stats_all[2 * chunks : 2 * chunks + 1, :]

    @pl.when((step >= 2 * chunks) & (step < 3 * chunks))
    def _():
        j = step - 2 * chunks
        lane = pl.ds(pl.multiple_of(j * LANES, LANES), LANES)
        load(j).wait()

        @pl.when(j + 1 < chunks)
        def _():
            load(j + 1).start()

        both = mix_kernels(kern_buf[lax.rem(j, 2)], mix[...])
        for b in range(nb):
            mixed[b, :, lane] = both[:, b * LANES : (b + 1) * LANES].astype(bf16)
        mean, rstd = norm_rows(sums_all, j, chunks, total)
        scale = rstd * side[2 * SQUEEZE + 2 : 2 * SQUEEZE + 3, :]
        bias = side[2 * SQUEEZE + 3 : 2 * SQUEEZE + 4, :]
        for b in range(nb):
            at = slice(b * PIXELS, (b + 1) * PIXELS)
            normed = (dpre[j, at, :] - mean) * scale + bias
            value = normed * sig(normed) * mask[at, :]
            dpre[j, at, :] = value
            pool_out[b : b + 1, lane] = rsum(value) / jnp.maximum(counts[b : b + 1, :], 1.0)
        squeezed[...] += dot(pool_out[:, lane], side[0:SQUEEZE, :], NT, highest)

    @pl.when(step >= 3 * chunks)
    def _():
        j = step - 3 * chunks
        lane = pl.ds(pl.multiple_of(j * LANES, LANES), LANES)
        before = squeezed[...] + sq_bias[...]
        gate = sig(
            dot(before * sig(before), side[SQUEEZE : 2 * SQUEEZE, :], NN, highest)
            + side[2 * SQUEEZE + 4 : 2 * SQUEEZE + 5, :]
        )
        gate_out[:, lane] = gate
        for b in range(nb):
            at = slice(b * PIXELS, (b + 1) * PIXELS)
            value = (dpre[j, at, :] * gate[b : b + 1, :]).astype(bf16)
            excited[at, :] = value
            exc[at, lane] = value

    @pl.when(step == 4 * chunks - 1)
    def _():
        one = jnp.zeros((1, WIDTH_OUT), f32)
        two = jnp.zeros((1, WIDTH_OUT), f32)
        for b in range(nb):
            at = slice(b * PIXELS, (b + 1) * PIXELS)
            value = dot(exc[at, :], mixed[b], NT)
            proj[at, :] = value
            masked = mask[at, 0:1] * value
            one = one + rsum(masked)
            two = two + rsum(masked * value)
        store_wide(sums_three, 0, one)
        store_wide(sums_three, OUT_CHUNKS, two)
        sum_finish(nd, nz, sums_three, last_all, *comm_two)
        for k in range(nz - 1):
            arrived(twins_h(k))
            sent(planes_b(k) + twins_b(k) + twins_h(k))
        arrived(far_c())
        sent(far_h() + planes_h() + far_c())
        for copy in own():
            copy.wait()


def first_stage(kern, images, mask, mask_rows, counts, route, side, sq_bias, full_b, kh, kc, nb, width, nd, nz, ident):
    chunks = width // LANES
    rows = nb * PIXELS
    deep = LANES * EXPERTS
    planes = (nz - 1) * (nd // 2 - 1)
    shapes = (shard_shape(full_b, nz), kh.shape, kc.shape)
    hbm = pl.BlockSpec(memory_space=pltpu.HBM)
    before = lambda t: jnp.minimum(t, chunks - 1)
    after = lambda t: jnp.clip(t - chunks, 0, chunks - 1)
    cycled = lambda t: lax.rem(t, chunks)
    return pl.pallas_call(
        functools.partial(stage_kernel, nd, nz, nb, chunks, shapes),
        grid=(4 * chunks,),
        out_shape=[
            jax.ShapeDtypeStruct((rows, width), f32),
            jax.ShapeDtypeStruct((nb, 32, width), f32),
            jax.ShapeDtypeStruct((rows, width), f32),
            jax.ShapeDtypeStruct((24, LANES), f32),
            jax.ShapeDtypeStruct((24, LANES), f32),
            jax.ShapeDtypeStruct((deep, 2 * nb * LANES), bf16),
            jax.ShapeDtypeStruct((8, EXPERTS), f32),
            jax.ShapeDtypeStruct((8, WIDTH_IN), f32),
            jax.ShapeDtypeStruct((rows, width), bf16),
            jax.ShapeDtypeStruct((rows, WIDTH_OUT), f32),
            jax.ShapeDtypeStruct((8, width), f32),
            jax.ShapeDtypeStruct((8, width), f32),
            jax.ShapeDtypeStruct((8, SQUEEZE), f32),
            jax.ShapeDtypeStruct((8, LANES), f32),
            jax.ShapeDtypeStruct((nb, WIDTH_OUT, width), bf16),
            jax.ShapeDtypeStruct(full_b.shape, bf16),
            jax.ShapeDtypeStruct((kh.shape[0], nz * kh.shape[1]), bf16),
            jax.ShapeDtypeStruct((nz,) + kc.shape, bf16),
        ],
        in_specs=[
            pl.BlockSpec((kern.shape[0], deep), lambda t: (0, before(t))),
            whole(images.shape),
            whole(mask.shape),
            whole(mask_rows.shape),
            whole(counts.shape),
            whole(route.shape),
            pl.BlockSpec((side.shape[0], LANES), lambda t: (0, cycled(t))),
            whole(sq_bias.shape),
            hbm,
            whole(kh.shape),
            whole(kc.shape),
        ],
        out_specs=[
            pl.BlockSpec((rows, LANES), lambda t: (0, before(t))),
            pl.BlockSpec((nb, 32, LANES), lambda t: (0, 0, before(t))),
            pl.BlockSpec((rows, LANES), lambda t: (0, after(t))),
            whole((24, LANES)),
            whole((24, LANES)),
            whole((deep, 2 * nb * LANES)),
            whole((8, EXPERTS)),
            whole((8, WIDTH_IN)),
            pl.BlockSpec((rows, LANES), lambda t: (0, jnp.maximum(t - 3 * chunks, 0))),
            whole((rows, WIDTH_OUT)),
            whole((8, width)),
            whole((8, width)),
            whole((8, SQUEEZE)),
            whole((8, LANES)),
            whole((nb, WIDTH_OUT, width)),
            hbm,
            hbm,
            hbm,
        ],
        scratch_shapes=[
            VMEM((chunks, rows, LANES), f32),
            VMEM((chunks, nb, 32, LANES), f32),
            VMEM((KERNEL, PIXELS, LANES), f32),
            VMEM((8, LANES), f32),
            VMEM((24, LANES), f32),
            VMEM((24, LANES), f32),
            VMEM((24, LANES), f32),
            VMEM((24, LANES), f32),
            VMEM((8, LANES), f32),
            VMEM((chunks, rows, LANES), f32),
            VMEM((rows, width), bf16),
            VMEM((2, WIDTH_OUT, deep), bf16),
        ]
        + sum_scratch(24, nd, nz)[1:] * 2
        + sum_scratch(8, nd, nz)[1:]
        + sum_scratch(24, nd, nz)[1:] * 2
        + pair(nz - 1) * 2
        + pair(planes) * 2
        + pair(nz - 1)
        + [pltpu.SemaphoreType.DMA((2,))]
        + pair(nz - 1)
        + [pltpu.SemaphoreType.DMA((2,))],
        input_output_aliases={8: 15},
        compiler_params=params(ident),
        name="first_stage",
    )(kern, images, mask, mask_rows, counts, route, side, sq_bias, full_b, kh, kc)


def store_wide(ref, row, value):
    width = value.shape[1]
    for k in range(-(-width // LANES)):
        lanes = min(LANES, width - k * LANES)
        ref[row + k : row + k + 1, :lanes] = value[:, k * LANES : k * LANES + lanes]


def load_wide(ref, row, width):
    parts = []
    for k in range(-(-width // LANES)):
        lanes = min(LANES, width - k * LANES)
        parts.append(ref[row + k : row + k + 1, :lanes])
    return jnp.concatenate(parts, axis=1)


OUT_CHUNKS = -(-WIDTH_OUT // LANES)


def out_norm(sums, total):
    mean = load_wide(sums, 0, WIDTH_OUT) / total
    var = load_wide(sums, OUT_CHUNKS, WIDTH_OUT) / total - mean * mean
    return mean, lax.rsqrt(var + eps_norm)


def store_sums(early, late, cut, chunks, j, one, two):
    @pl.when(j < cut)
    def _():
        early[pl.ds(j, 1), :] = one
        early[pl.ds(chunks + j, 1), :] = two

    @pl.when(j >= cut)
    def _():
        late[pl.ds(j, 1), :] = one
        late[pl.ds(chunks + j, 1), :] = two


def split_sum(nd, nz, steps, at, early, late, out, comm_early, comm_late):
    def early_third():
        out[...] = sum_third(nd, nz, early, *comm_early)

    def late_third():
        out[...] += sum_third(nd, nz, late, *comm_late)

    steps.at(at[0], lambda: sum_first(nd, nz, early, *comm_early))
    steps.at(at[1], lambda: sum_second(nd, nz, early, *comm_early))
    steps.at(at[2], early_third)
    steps.at(at[3], lambda: sum_first(nd, nz, late, *comm_late))
    steps.at(at[4], lambda: sum_second(nd, nz, late, *comm_late))
    steps.at(at[5], late_third)


def head_back_kernel(
    nd,
    nz,
    nb,
    chunks,
    shape,
    shape_c,
    mask,
    mask_rows,
    counts,
    labels,
    bias,
    gain,
    totals,
    gain_out,
    kern,
    route,
    proj,
    proj_stats,
    in_c,
    head_pool,
    stats,
    features,
    grad_logits,
    sums_four,
    grad_out,
    sums_all,
    dz_out,
    half,
    part,
    full_c,
    pre_all,
    low,
    mixed,
    mix,
    gates,
    cls,
    early_head,
    late_head,
    logits,
    grad_features,
    held,
    grads,
    gate_acc,
    early,
    late,
    sums,
    *comm,
):
    step = pl.program_id(0)
    phase = step // chunks
    j = lax.rem(step, chunks)
    net = Net(nd, nz)
    comm_early, comm_late, comm_two, comm = comm[0:6], comm[6:12], comm[12:18], comm[18:]
    head_early, head_late, sems, comm = comm[0:6], comm[6:12], comm[12:17], comm[17:]
    twin = Twin(net, shape, half, *comm[0:4])
    plane = Plane(net, shape, half, part, 0, nz // 2, *comm[4:7])
    made = comm[0]
    cut = chunks // 3
    head_cut = 2 * chunks // 3
    base = 3 * chunks
    steps = Steps()

    def planes():
        return every(gather_plane, net, shape_c, full_c, sems[0:2])

    def twins():
        return every(gather_twin, net, shape_c, full_c, sems[2:4])

    def load():
        own_rows = cls.shape[0] // nz
        return [
            pltpu.make_async_copy(
                full_c.at[k, pl.ds(0, own_rows)], cls.at[pl.ds(k * own_rows, own_rows)], sems[4].at[k]
            )
            for k in range(nz)
        ]

    def begin():
        met(nd, nz)
        start(planes())

    def cross():
        arrived(planes())
        start(twins())

    def fetch():
        arrived(twins())
        start(load())

    def loaded():
        for copy in load():
            copy.wait()

    steps.at(1, begin)
    steps.at(head_cut - 1, cross)
    steps.at(chunks - 1, fetch)
    steps.at(chunks, loaded)
    places = (head_cut, head_cut + 2, chunks, chunks, chunks + 2, chunks + head_cut)
    split_sum(nd, nz, steps, places, early_head, late_head, stats, head_early, head_late)
    places = (2 * chunks + cut, 2 * chunks + cut + 3, base, base, base + 1, base + cut)
    split_sum(nd, nz, steps, places, early, late, sums_four, comm_early, comm_late)
    for k in range(nz):
        first = base + ready(shape, k)
        steps.at(first, functools.partial(twin.begin, k))
        steps.at(first + 2, functools.partial(twin.add, k))
        if k < nz // 2:
            steps.at(first + 2, functools.partial(plane.begin, k))

    @pl.when(step == 0)
    def _():
        sum_start(nd, nz)
        for ref in (sums, early, late, early_head, late_head, features, logits, gate_acc):
            ref[...] = jnp.zeros_like(ref)
        mean, rstd = out_norm(proj_stats, totals[TOTAL_ROW : TOTAL_ROW + 1, 0:1])
        scale = rstd * gain_out[0:1, :]
        for b in range(nb):
            at = slice(b * PIXELS, (b + 1) * PIXELS)
            low[at, :] = (((proj[at, :] - mean) * scale + gain_out[1:2, :]) * mask[at, 0:1]).astype(bf16)
        pool = dot(mask_rows[...], low[...]) / jnp.maximum(counts[:, 0:1], 1.0)
        head_pool[...] = pool
        gate = sig(dot(pool, route[...], NN, highest))
        gates[...] = gate
        build_mix(gate, nb, mix)
        if shape[0] > WIDTH_OUT:
            made[WIDTH_OUT:, :] = jnp.zeros((shape[0] - WIDTH_OUT, made.shape[1]), bf16)

    steps.emit(step, 4 * chunks)
    pre = pre_all.at[j]

    @pl.when(phase == 0)
    def _():
        lane = pl.ds(pl.multiple_of(j * LANES, LANES), LANES)
        both = mix_kernels(kern[...], mix[...])
        one = jnp.zeros((1, LANES), f32)
        two = jnp.zeros((1, LANES), f32)
        for b in range(nb):
            at = slice(b * PIXELS, (b + 1) * PIXELS)
            weight = both[:, b * LANES : (b + 1) * LANES].astype(bf16)
            mixed[b, :, lane] = weight
            value = dot(low[at, :], weight)
            pre[at, :] = value
            masked = mask[at, :] * value
            one = one + rsum(masked)
            two = two + rsum(masked * value)
        store_sums(early_head, late_head, head_cut, chunks, j, one, two)

    lane = pl.ds(pl.multiple_of(j * LANES, LANES), LANES)
    total = totals[TOTAL_ROW : TOTAL_ROW + 1, :]
    mean, rstd = norm_rows(stats, j, chunks, total)
    scale = rstd * gain[0:1, :]

    @pl.when(phase == 1)
    def _():
        for b in range(nb):
            at = slice(b * PIXELS, (b + 1) * PIXELS)
            normed = (pre[at, :] - mean) * scale + gain[1:2, :]
            features[b : b + 1, lane] = rsum(normed * sig(normed) * mask[at, :]) / jnp.maximum(
                counts[b : b + 1, :], 1.0
            )
        both = dot(split(features[:, lane]), cls[lane, :])
        logits[...] += both[:8] + both[8:]

    @pl.when((phase == 2) & (j == 0))
    def _():
        col = lax.broadcasted_iota(jnp.int32, (8, CLASS_PAD), 1)
        inside = col < CLASSES
        scores = jnp.where(inside, logits[...] + bias[...], -1e30)
        top = jnp.max(scores, axis=1, keepdims=True)
        spread = jnp.where(inside, jnp.exp(scores - top), 0.0)
        mass = jnp.sum(spread, axis=1, keepdims=True)
        hot = jnp.where(col == labels[:, 0:1], 1.0, 0.0)
        shifted_scores = jnp.where(inside, scores - top - jnp.log(mass), 0.0)
        per_image = -(
            0.9 * jnp.sum(shifted_scores * hot, axis=1, keepdims=True)
            + (0.1 / CLASSES) * jnp.sum(shifted_scores, axis=1, keepdims=True)
        )
        valid = jnp.where(counts[:, 0:1] > 0.0, 1.0, 0.0)
        early[2 * chunks : 2 * chunks + 1, :] = jnp.broadcast_to(rsum(per_image * valid), (1, LANES))
        weight = valid / totals[TOTAL_ROW + 1 : TOTAL_ROW + 2, 0:1]
        grad_logits[...] = weight * jnp.where(inside, spread / mass - 0.9 * hot - 0.1 / CLASSES, 0.0)

    @pl.when(phase == 2)
    def _():
        both = dot(split(grad_logits[...]), cls[lane, :], NT)
        grads = (both[:8] + both[8:]) / jnp.maximum(counts[...], 1.0)
        grad_features[:, lane] = grads
        one = jnp.zeros((1, LANES), f32)
        two = jnp.zeros((1, LANES), f32)
        for b in range(nb):
            at = slice(b * PIXELS, (b + 1) * PIXELS)
            hat = (pre[at, :] - mean) * rstd
            grad = mask[at, :] * dsilu(hat * gain[0:1, :] + gain[1:2, :]) * grads[b : b + 1, :]
            one = one + rsum(grad)
            two = two + rsum(grad * hat)
        store_sums(early, late, cut, chunks, j, one, two)

    @pl.when(phase == 3)
    def _():
        one = sums_four[pl.ds(j, 1), :] / total
        two = sums_four[pl.ds(chunks + j, 1), :] / total
        for b in range(nb):
            at = slice(b * PIXELS, (b + 1) * PIXELS)
            hat = (pre[at, :] - mean) * rstd
            grad = dsilu(hat * gain[0:1, :] + gain[1:2, :]) * grad_features[b : b + 1, lane]
            value = (scale * mask[at, :] * (grad - one - hat * two)).astype(bf16)
            held[at, lane] = value
            grad_mixed = dot(low[at, :], value, TN).astype(bf16)
            grads[:, b * LANES : (b + 1) * LANES] = grad_mixed
            gate_acc[b : b + 1, :] += gate_rows(grad_mixed, kern[...])
        made[:WIDTH_OUT, lanes(j * LANES * EXPERTS, LANES * EXPERTS)] = dot(grads[...], mix[:, : nb * LANES], NT).astype(bf16)

    @pl.when(step == 4 * chunks - 1)
    def _():
        dz = gate_sums(gate_acc[...]) * gates[...] * (1.0 - gates[...])
        dz_out[...] = dz
        pool_grad = dot(dz, route[...], NT, highest) / jnp.maximum(counts[:, 0:1], 1.0)
        mean, rstd = out_norm(proj_stats, total[:, 0:1])
        one = jnp.zeros((1, WIDTH_OUT), f32)
        two = jnp.zeros((1, WIDTH_OUT), f32)
        for b in range(nb):
            at = slice(b * PIXELS, (b + 1) * PIXELS)
            value = (dot(held[at, :], mixed[b], NT) + pool_grad[b : b + 1, :]) * mask[at, 0:1]
            grad_out[at, :] = value
            one = one + rsum(value)
            two = two + rsum(value * ((proj[at, :] - mean) * rstd))
        store_wide(sums, 0, one)
        store_wide(sums, OUT_CHUNKS, two)
        last = [k for k in range(nz) if ready(shape, k) >= chunks]
        sum_first(nd, nz, sums, *comm_two)
        for k in last:
            twin.begin(k)
        sum_second(nd, nz, sums, *comm_two)
        sums_all[...] = sum_third(nd, nz, sums, *comm_two)
        for k in range(nz):
            if ready(shape, k) + 2 >= chunks:
                twin.add(k)
                if k < nz // 2:
                    plane.begin(k)
        plane.add()
        twin.finish()
        plane.finish()
        sent(planes() + twins())


def head_stage(mask, mask_rows, counts, labels, bias, gain, totals, gain_out, kern, route, proj, proj_stats, full_c, nb, nd, nz, ident):
    rows = proj.shape[0]
    width = kern.shape[1] // EXPERTS
    chunks = width // LANES
    deep = LANES * EXPERTS
    shape = (kern.shape[0], kern.shape[1] // nz)
    hbm = pl.BlockSpec(memory_space=pltpu.HBM)
    kept = lambda t: (0, jnp.where(t < chunks, t, jnp.maximum(t - 3 * chunks, 0)))
    return pl.pallas_call(
        functools.partial(head_back_kernel, nd, nz, nb, chunks, shape, shard_shape(full_c, nz)),
        grid=(4 * chunks,),
        out_shape=[
            jax.ShapeDtypeStruct((8, WIDTH_OUT), f32),
            jax.ShapeDtypeStruct((24, LANES), f32),
            jax.ShapeDtypeStruct((8, width), f32),
            jax.ShapeDtypeStruct((8, CLASS_PAD), f32),
            jax.ShapeDtypeStruct((24, LANES), f32),
            jax.ShapeDtypeStruct((rows, WIDTH_OUT), f32),
            jax.ShapeDtypeStruct((8, LANES), f32),
            jax.ShapeDtypeStruct((8, EXPERTS), f32),
            jax.ShapeDtypeStruct(half_shape(shape, nd, nz), bf16),
            jax.ShapeDtypeStruct(part_shape(shape, nd, nz // 2), bf16),
            jax.ShapeDtypeStruct(full_c.shape, bf16),
        ],
        in_specs=[
            whole(mask.shape),
            whole(mask_rows.shape),
            whole(counts.shape),
            whole(labels.shape),
            whole(bias.shape),
            pl.BlockSpec((8, LANES), lambda t: (0, lax.rem(t, chunks))),
            whole(totals.shape),
            whole(gain_out.shape),
            pl.BlockSpec((WIDTH_OUT, deep), kept),
            whole(route.shape),
            whole(proj.shape),
            whole(proj_stats.shape),
            hbm,
        ],
        out_specs=[
            whole((8, WIDTH_OUT)),
            whole((24, LANES)),
            whole((8, width)),
            whole((8, CLASS_PAD)),
            whole((24, LANES)),
            whole((rows, WIDTH_OUT)),
            whole((8, LANES)),
            whole((8, EXPERTS)),
            whole(half_shape(shape, nd, nz)),
            whole(part_shape(shape, nd, nz // 2)),
            hbm,
        ],
        scratch_shapes=[
            VMEM((chunks, rows, LANES), f32),
            VMEM((rows, WIDTH_OUT), bf16),
            VMEM((nb, WIDTH_OUT, width), bf16),
            VMEM((deep, 2 * nb * LANES), bf16),
            VMEM((8, EXPERTS), f32),
            VMEM((width, CLASS_PAD), bf16),
            VMEM((24, LANES), f32),
            VMEM((24, LANES), f32),
            VMEM((8, CLASS_PAD), f32),
            VMEM((8, width), f32),
            VMEM((rows, width), bf16),
            VMEM((WIDTH_OUT, nb * LANES), bf16),
            VMEM((8, deep), f32),
            VMEM((24, LANES), f32),
            VMEM((24, LANES), f32),
            VMEM((8, LANES), f32),
        ]
        + sum_scratch(24, nd, nz)[1:] * 2
        + sum_scratch(8, nd, nz)[1:]
        + sum_scratch(24, nd, nz)[1:] * 2
        + pair((nz - 1) * (nd // 2 - 1))
        + pair(nz - 1)
        + [pltpu.SemaphoreType.DMA((nz,))]
        + twin_scratch(shape, nd, nz)
        + plane_scratch(shape, nd, nz // 2),
        input_output_aliases={12: 10},
        compiler_params=params(ident),
        name="head_stage",
    )(mask, mask_rows, counts, labels, bias, gain, totals, gain_out, kern, route, proj, proj_stats, full_c)


def project_back_kernel(nd, nz, nb, chunks, shape_h, shape, half_h, part_h, grad_in, proj, proj_stats, proj_sums, gain, mask, counts, totals, stats, side, dpre, excited, mixed, kern, mix, gate, pooled, squeezed, sq_bias, grad_norm, sums_all, grad_squeeze, gate_grad, dz_gate, piece_h, half, part, low, held, grads, gate_acc, sums_h, sums, *comm):
    phase = pl.program_id(0)
    net = Net(nd, nz)
    few = nz // 2
    cut_one = 12
    plane_h = Plane(net, shape_h, half_h, sums_h, few, nz - few, *comm[6:9])
    far = Far(net, shape_h, sums_h, piece_h, *comm[9:cut_one])
    twin = Twin(net, shape, half, *comm[cut_one : cut_one + 4])
    plane = Plane(net, shape, half, part, 0, few, *comm[cut_one + 4 : cut_one + 7])
    made = comm[cut_one]
    comm = comm[:6]
    steps = Steps()

    def begin():
        met(nd, nz)
        for k in plane_h.shards:
            plane_h.begin(k)
        sums_h[0:few] = part_h[...]
        for k in range(few):
            far.send(k)

    steps.at(1, begin)
    steps.at(chunks + 3, functools.partial(plane_h.add, far.send))
    for k in range(nz):
        first = ready(shape, k)
        steps.at(first, functools.partial(twin.begin, k))
        steps.at(first + 3, functools.partial(twin.add, k))
        if k < few:
            steps.at(first + 3, functools.partial(plane.begin, k))
    j = pl.program_id(1)

    @pl.when((phase == 0) & (j == 0))
    def _():
        sum_start(nd, nz)

    steps.emit(phase * chunks + j, 2 * chunks)
    lane = pl.ds(pl.multiple_of(j * LANES, LANES), LANES)
    total = totals[TOTAL_ROW : TOTAL_ROW + 1, :]

    @pl.when((phase == 0) & (j == 0))
    def _():
        gate_acc[...] = jnp.zeros_like(gate_acc)
        if shape[0] > WIDTH_OUT:
            made[WIDTH_OUT:, :] = jnp.zeros((shape[0] - WIDTH_OUT, made.shape[1]), bf16)
        sums[...] = jnp.zeros_like(sums)
        grad_squeeze[...] = jnp.zeros_like(grad_squeeze)
        dz_gate[...] = jnp.zeros_like(dz_gate)
        mean, rstd = out_norm(proj_stats, total[:, 0:1])
        scale = rstd * gain[0:1, :]
        one = load_wide(proj_sums, 0, WIDTH_OUT) / total[:, 0:1]
        two = load_wide(proj_sums, OUT_CHUNKS, WIDTH_OUT) / total[:, 0:1]
        for b in range(nb):
            at = slice(b * PIXELS, (b + 1) * PIXELS)
            hat = (proj[at, :] - mean) * rstd
            low[at, :] = (scale * (grad_in[at, :] - mask[at, 0:1] * (one + hat * two))).astype(bf16)

    mean, rstd = norm_rows(stats, j, chunks, total)
    gain_now = side[2 * SQUEEZE + 2 : 2 * SQUEEZE + 3, :]
    bias_now = side[2 * SQUEEZE + 3 : 2 * SQUEEZE + 4, :]

    @pl.when(phase == 0)
    def _():
        for b in range(nb):
            at = slice(b * PIXELS, (b + 1) * PIXELS)
            grad_mixed = dot(low[at, :], excited[at, :], TN).astype(bf16)
            grads[:, b * LANES : (b + 1) * LANES] = grad_mixed
            gate_acc[b : b + 1, :] += gate_rows(grad_mixed, kern[...])
            value = dot(low[at, :], mixed[b])
            held[j, at, :] = value
            normed = (dpre[at, :] - mean) * (rstd * gain_now) + bias_now
            act = normed * sig(normed) * mask[at, :]
            now = gate[b : b + 1, :]
            dz_gate[b : b + 1, lane] = rsum(value * act) * now * (1.0 - now)
        made[:WIDTH_OUT, lanes(j * LANES * EXPERTS, LANES * EXPERTS)] = dot(grads[...], mix[:, : nb * LANES], NT).astype(bf16)
        grad_squeeze[...] += dot(dz_gate[:, lane], side[SQUEEZE : 2 * SQUEEZE, :], NT, highest)

    @pl.when((phase == 1) & (j == 0))
    def _():
        grad_squeeze[...] = grad_squeeze[...] * dsilu(squeezed[...] + sq_bias[...])
        gate_grad[...] = gate_sums(gate_acc[...])

    @pl.when(phase == 1)
    def _():
        pool_grad = dot(grad_squeeze[...], side[0:SQUEEZE, :], NN, highest) / jnp.maximum(counts[...], 1.0)
        one = jnp.zeros((1, LANES), f32)
        two = jnp.zeros((1, LANES), f32)
        for b in range(nb):
            at = slice(b * PIXELS, (b + 1) * PIXELS)
            hat = (dpre[at, :] - mean) * rstd
            grad = held[j, at, :] * gate[b : b + 1, :] + pool_grad[b : b + 1, :]
            value = mask[at, :] * grad * dsilu(hat * gain_now + bias_now)
            grad_norm[at, :] = value
            one = one + rsum(value)
            two = two + rsum(value * hat)
        sums[pl.ds(j, 1), :] = one
        sums[pl.ds(chunks + j, 1), :] = two

    @pl.when((phase == 1) & (j == chunks - 1))
    def _():
        sum_finish(nd, nz, sums, sums_all, *comm)
        far.add()
        plane.add()
        far.finish()
        twin.finish()
        plane.finish()
        plane_h.finish()


def project_back(half_h, part_h, shape_h, grad_in, proj, proj_stats, proj_sums, gain, mask, counts, totals, stats, side, dpre, excited, mixed, kern, mix, gate, pooled, squeezed, sq_bias, nb, nd, nz, ident):
    rows, width = dpre.shape
    shape = (kern.shape[0], kern.shape[1] // nz)
    few = nz // 2
    chunks = width // LANES
    deep = LANES * EXPERTS
    wide = lambda p, j: (0, j)
    early = lambda p, j: (0, jnp.where(p == 0, j, chunks - 1))
    late = lambda p, j: (0, jnp.where(p == 0, 0, j))
    return pl.pallas_call(
        functools.partial(project_back_kernel, nd, nz, nb, chunks, shape_h, shape),
        grid=(2, chunks),
        out_shape=[
            jax.ShapeDtypeStruct((rows, width), f32),
            jax.ShapeDtypeStruct((24, LANES), f32),
            jax.ShapeDtypeStruct((8, SQUEEZE), f32),
            jax.ShapeDtypeStruct((8, EXPERTS), f32),
            jax.ShapeDtypeStruct((8, width), f32),
            jax.ShapeDtypeStruct(piece_shape(shape_h, nd), bf16),
            jax.ShapeDtypeStruct(half_shape(shape, nd, nz), bf16),
            jax.ShapeDtypeStruct(part_shape(shape, nd, few), bf16),
        ],
        in_specs=[
            whole(half_h.shape),
            whole(part_h.shape),
            whole(grad_in.shape),
            whole(proj.shape),
            whole(proj_stats.shape),
            whole(proj_sums.shape),
            whole(gain.shape),
            whole(mask.shape),
            whole(counts.shape),
            whole(totals.shape),
            whole(stats.shape),
            pl.BlockSpec((side.shape[0], LANES), wide),
            pl.BlockSpec((rows, LANES), wide),
            pl.BlockSpec((rows, LANES), early),
            pl.BlockSpec((nb, WIDTH_OUT, LANES), lambda p, j: (0, 0, jnp.where(p == 0, j, chunks - 1))),
            pl.BlockSpec((WIDTH_OUT, deep), early),
            whole(mix.shape),
            pl.BlockSpec((8, LANES), wide),
            pl.BlockSpec((8, LANES), wide),
            whole(squeezed.shape),
            whole(sq_bias.shape),
        ],
        out_specs=[
            pl.BlockSpec((rows, LANES), late),
            whole((24, LANES)),
            whole((8, SQUEEZE)),
            whole((8, EXPERTS)),
            whole((8, width)),
            whole(piece_shape(shape_h, nd)),
            whole(half_shape(shape, nd, nz)),
            whole(part_shape(shape, nd, few)),
        ],
        scratch_shapes=[
            VMEM((rows, WIDTH_OUT), bf16),
            VMEM((chunks, rows, LANES), f32),
            VMEM((WIDTH_OUT, nb * LANES), bf16),
            VMEM((8, deep), f32),
            VMEM(part_shape(shape_h, nd, nz), bf16),
        ]
        + sum_scratch(24, nd, nz)
        + plane_scratch(shape_h, nd, nz - few)
        + far_scratch(shape_h, nd, nz)
        + twin_scratch(shape, nd, nz)
        + plane_scratch(shape, nd, few),
        compiler_params=params(ident),
        name="project_back",
    )(half_h, part_h, grad_in, proj, proj_stats, proj_sums, gain, mask, counts, totals, stats, side, dpre, excited, mixed, kern, mix, gate, pooled, squeezed, sq_bias)


def dz_slots(nb, devices):
    per = max(1, min(devices, LANES // (nb * EXPERTS)))
    return per, -(-devices // (per * 8)) * 8


def stage_back_kernel(
    nd,
    nz,
    nb,
    chunks,
    shape,
    shape_b,
    shape_h,
    cuts_one,
    cuts_two,
    half_b,
    part_b,
    piece_h,
    grad_in,
    dpre,
    pre,
    taps,
    mask,
    side,
    stats_one,
    stats_two,
    sums_two,
    totals,
    features,
    logits,
    pooled,
    dz_gate,
    head_pool,
    pooled_in,
    grad_sq,
    before,
    sq_bias_in,
    dz_head,
    images,
    kern,
    mix,
    gates,
    gate_grad,
    squares_w,
    stats_three,
    stats_four,
    sums_four,
    chan_old,
    head_old,
    proj_old,
    done,
    done_b,
    done_h,
    grad_cls,
    grad_side_out,
    factors,
    route_in,
    route_head,
    sq_bias,
    class_bias,
    chan_new,
    head_new,
    proj_new,
    loss,
    made_norm,
    tap_grads,
    buf,
    acts,
    held,
    early,
    late,
    sums_one,
    sums_b,
    piece_b,
    rows_all,
    grads,
    gate_acc,
    grad_side,
    every_sum,
    low,
    half,
    sums,
    piece,
    *comm,
):
    step = pl.program_id(0)
    net = Net(nd, nz)
    few = nz // 2
    cut = 2 * chunks // 3
    comm_early, comm_late, comm_two, comm = comm[0:6], comm[6:12], comm[12:18], comm[18:]
    plane_b = Plane(net, shape_b, half_b, sums_b, few, nz - few, *comm[0:3], shift=few)
    far_b = Far(net, shape_b, sums_b, piece_b, *comm[3:6])
    up_b = Spread(net, shape_b, piece_b, done_b, *comm[6:11])
    up_h = Spread(net, shape_h, piece_h, done_h, *comm[11:16])
    share = Share(net, rows_all, *comm[16:24])
    comm = comm[24:]
    twin = Twin(net, shape, half, *comm[0:4])
    made = comm[0]
    plane = Plane(net, shape, half, sums, 0, nz, *comm[4:7])
    far = Far(net, shape, sums, piece, *comm[7:10])
    up = Spread(net, shape, piece, done, *comm[10:15])
    steps = Steps()
    first_planes = range(few, few + (nz - few + 1) // 2)
    last_planes = range(first_planes.stop, nz)

    def begin():
        met(nd, nz)
        up_h.begin()
        for k in first_planes:
            plane_b.begin(k)
        sums_b[0:few] = part_b[...]
        for k in range(few):
            far_b.send(k)
        share.far()

    def more_planes():
        for k in last_planes:
            plane_b.begin(k)

    def far_end():
        far_b.add()
        up_b.begin()

    steps.at(1, begin)
    steps.at(4, up_h.cross)
    split_sum(
        nd,
        nz,
        steps,
        (cut, cut + 2, chunks, chunks, chunks + 2, chunks + cut - 1),
        early,
        late,
        sums_one,
        comm_early,
        comm_late,
    )
    steps.at(cut + 1, more_planes)
    steps.at(cut + 2, share.plane)
    steps.at(chunks + 1, functools.partial(plane_b.add, far_b.send))
    steps.at(chunks + 2, share.twin)
    steps.at(chunks + 3, far_end)
    for k in range(nz):
        first = chunks + ready(shape, k)
        steps.at(first, functools.partial(twin.begin, k))
        steps.at(first + 1, functools.partial(twin.add, k))
        steps.at(first + 1, functools.partial(plane.begin, k))
        if first + 4 < 2 * chunks:
            steps.at(first + 4, functools.partial(plane.add_one, k, far.send))
    steps.at(2 * chunks - 2, up_b.cross)

    @pl.when(step == 0)
    def _():
        sum_start(nd, nz)
        total_before = before[...] + sq_bias_in[...]
        squeezed = total_before * sig(total_before)
        share.fill(
            nb,
            [features, pooled, dz_gate],
            [grad_sq[...], squeezed, dz_head[...]],
            [logits[...], head_pool[...], pooled_in[...]],
        )
        for ref in (early, late, gate_acc, grads):
            ref[...] = jnp.zeros_like(ref)

    steps.emit(step, 2 * chunks)
    total = totals[TOTAL_ROW : TOTAL_ROW + 1, :]

    @pl.when(step < chunks)
    def _():
        j = step
        mean_two, rstd_two = norm_rows(stats_two, j, chunks, total)
        scale_two = rstd_two * side[2 * SQUEEZE + 2 : 2 * SQUEEZE + 3, :]
        one_two = sums_two[pl.ds(j, 1), :] / total
        two_two = sums_two[pl.ds(chunks + j, 1), :] / total
        mean, rstd = norm_rows(stats_one, j, chunks, total)
        gain = side[2 * SQUEEZE : 2 * SQUEEZE + 1, :]
        bias = side[2 * SQUEEZE + 1 : 2 * SQUEEZE + 2, :]
        held[...] = jnp.zeros_like(held)
        reach = KERNEL // 2

        @pl.loop(0, nb)
        def _(b):
            at = image(b)
            hat = (dpre[at, :] - mean_two) * rstd_two
            grad = scale_two * (grad_in[at, :] - mask[at, :] * (one_two + hat * two_two))
            for s in range(KERNEL):
                buf[s] = shifted(grad, reach - s)
            hat = (pre[at, :] - mean) * rstd
            normed = hat * gain + bias
            acts[...] = normed * sig(normed) * mask[at, :]
            taps_now = [jnp.broadcast_to(taps[b, t : t + 1, :], (MAP_SIDE, LANES)) for t in range(TAPS)]
            acc = [None] * MAP_SIDE
            for q in range(MAP_SIDE):
                for s in range(KERNEL):
                    x = buf[s, q * MAP_SIDE : (q + 1) * MAP_SIDE, :]
                    for r in range(KERNEL):
                        y = q + r - reach
                        if 0 <= y < MAP_SIDE:
                            term = taps_now[r * KERNEL + s] * x
                            acc[y] = term if acc[y] is None else acc[y] + term
                done = [q - 2] if q < MAP_SIDE - 1 else [q - 2, q - 1, q]
                for i in done:
                    if i >= 0:
                        made_norm[j, pl.ds(pl.multiple_of(b * PIXELS + i * MAP_SIDE, MAP_SIDE), MAP_SIDE), :] = acc[i]
            tap_acc = [None] * TAPS
            for q in range(MAP_SIDE):
                for s in range(KERNEL):
                    x = buf[s, q * MAP_SIDE : (q + 1) * MAP_SIDE, :]
                    for r in range(KERNEL):
                        y = q + r - reach
                        if 0 <= y < MAP_SIDE:
                            both = acts[y * MAP_SIDE : (y + 1) * MAP_SIDE, :] * x
                            term = both[:8] + both[8:]
                            t = r * KERNEL + s
                            tap_acc[t] = term if tap_acc[t] is None else tap_acc[t] + term
            tap_grads[j, b] = jnp.zeros((32, LANES), f32)
            for t in range(TAPS):
                tap_grads[j, b, t : t + 1, :] = rsum(tap_acc[t])
            hat = (pre[at, :] - mean) * rstd
            value = made_norm[j, at, :] * mask[at, :] * dsilu(hat * gain + bias)
            made_norm[j, at, :] = value
            held[0:1, :] += rsum(value)
            held[1:2, :] += rsum(value * hat)

        store_sums(early, late, cut, chunks, j, held[0:1, :], held[1:2, :])

    @pl.when(step >= chunks)
    def _():
        j = step - chunks
        mean, rstd = norm_rows(stats_one, j, chunks, total)
        scale = rstd * side[2 * SQUEEZE : 2 * SQUEEZE + 1, :]
        one = sums_one[pl.ds(j, 1), :] / total
        two = sums_one[pl.ds(chunks + j, 1), :] / total
        for b in range(nb):
            at = slice(b * PIXELS, (b + 1) * PIXELS)
            lane = slice(b * LANES, (b + 1) * LANES)
            hat = (pre[at, :] - mean) * rstd
            value = (scale * (made_norm[j, at, :] - mask[at, :] * (one + hat * two))).astype(bf16)
            grads[0:WIDTH_IN, lane] = dot(images[at, :], value, TN).astype(bf16)
            grads[WIDTH_IN : WIDTH_IN + 32, lane] = tap_grads[j, b].astype(bf16)
            gate_acc[b : b + 1, :] += gate_rows(grads[:, lane], kern[...])
        made[:, lanes(j * LANES * EXPERTS, LANES * EXPERTS)] = dot(grads[...], mix[:, : nb * LANES], NT).astype(bf16)

    @pl.when(step == 2 * chunks - 1)
    def _():
        dz = (gate_sums(gate_acc[...]) + gate_grad[...]) * gates[...] * (1.0 - gates[...])
        steps.end(2 * chunks)
        z = net.z
        me = net.d * nz + z
        devices = nd * nz
        own = chan_old.shape[1]
        own_head = head_old.shape[1]
        own_proj = proj_old.shape[1]
        width = own * nz
        head_width = own_head * nz
        head_chunks = head_width // LANES
        share.finish()
        count = devices * 8
        per, slots = dz_slots(nb, devices)
        row = lax.broadcasted_iota(jnp.int32, (count, 1), 0)
        keep = jnp.where((row & 7) < nb, 1.0, 0.0)

        def one(k, size):
            return rows_all[:, :, cuts_one[k] : cuts_one[k] + size].reshape(count, size) * keep

        def two(k, size):
            return pltpu.roll(rows_all[:, :, cuts_two[k] : cuts_two[k] + size].reshape(count, size), count - nb, 0)

        features = one(0, own_head)
        logits = two(0, CLASS_PAD)
        pooled = one(1, own)
        dz_gate = one(2, own)
        grad_sq = one(3, SQUEEZE)
        grad_cls[...] = dot(features, logits, TN, highest)
        grad_side[...] = jnp.zeros_like(grad_side)
        grad_side[0:SQUEEZE, :own] = dot(grad_sq, pooled, TN, highest)
        grad_side[SQUEEZE : 2 * SQUEEZE, :own] = dot(one(4, SQUEEZE), dz_gate, TN, highest)

        def channel(ref, at, n, size, own_size):
            return turn(load_wide(ref, at, size), z * own_size)[:, :own_size]

        at = 2 * SQUEEZE
        grad_side[at : at + 1, :own] = channel(sums_one, chunks, chunks, width, own)
        grad_side[at + 1 : at + 2, :own] = channel(sums_one, 0, chunks, width, own)
        grad_side[at + 2 : at + 3, :own] = channel(sums_two, chunks, chunks, width, own)
        grad_side[at + 3 : at + 4, :own] = channel(sums_two, 0, chunks, width, own)
        grad_side[at + 4 : at + 5, :own] = rsum(dz_gate)
        route_head[...] = dot(two(1, WIDTH_OUT), one(5, EXPERTS), TN, highest)
        sq_bias[...] = rsum(grad_sq)
        class_bias[...] = rsum(logits * keep)
        head_gain = channel(sums_four, head_chunks, head_chunks, head_width, own_head)
        head_bias = channel(sums_four, 0, head_chunks, head_width, own_head)
        totals = stats_one[TOTAL_ROW : TOTAL_ROW + 1, 0:1]
        loss[...] = jnp.broadcast_to(
            sums_four[2 * head_chunks : 2 * head_chunks + 1, :] / stats_one[TOTAL_ROW + 1 : TOTAL_ROW + 2, :], (8, LANES)
        )

        def moving(new, old, ref, at, n, size, own_size):
            mean = load_wide(ref, 0, size) / totals
            var = (load_wide(ref, n, size) / totals - mean * mean) * (totals / (totals - 1.0))
            new[at : at + 1, :] = 0.5 * old[at : at + 1, :] + 0.5 * turn(mean, z * own_size)[:, :own_size]
            new[at + 1 : at + 2, :] = 0.5 * old[at + 1 : at + 2, :] + 0.5 * turn(var, z * own_size)[:, :own_size]

        moving(chan_new, chan_old, stats_one, 0, chunks, width, own)
        moving(chan_new, chan_old, stats_two, 2, chunks, width, own)
        moving(head_new, head_old, stats_four, 0, head_chunks, head_width, own_head)
        moving(proj_new, proj_old, stats_three, 0, OUT_CHUNKS, WIDTH_OUT, own_proj)
        low[...] = jnp.zeros_like(low)
        own_dz = fit(jnp.concatenate([dz[b : b + 1, :] for b in range(nb)], axis=1), LANES)
        low[pl.ds(me // per, 1), :] = pltpu.roll(own_dz, lax.rem(me, per) * (nb * EXPERTS), 1)
        fraction = 1.0 / nd
        g_hside = jnp.sum(grad_cls[...] * grad_cls[...]) + jnp.sum(head_gain * head_gain) + jnp.sum(head_bias * head_bias)
        sums = (
            0.0,
            squares_of(grad_side, 104),
            squares_of(piece_h, piece_h.shape[0]) * nd,
            g_hside,
        )
        for k in range(4):
            low[slots + k : slots + k + 1, :] = row_of(sums[k] * fraction)
            low[slots + 4 + k : slots + 5 + k, :] = squares_w[k : k + 1, :] * fraction
        for k in range(nz):
            if chunks + ready(shape, k) + 4 >= 2 * chunks:
                plane.add_one(k, far.send)
        far.add()
        low[slots : slots + 1, :] = row_of(
            squares_of(piece, piece.shape[0]) + squares_of(piece_b, piece_b.shape[0])
        )
        sum_first(nd, nz, low, *comm_two)
        up.begin()
        sum_second(nd, nz, low, *comm_two)
        up.cross()
        every_sum[...] = sum_third(nd, nz, low, *comm_two)
        for k in range(4):
            grad_sq_sum = jnp.sum(every_sum[slots + k : slots + k + 1, :], axis=1, keepdims=True)
            weight_sq = jnp.sum(every_sum[slots + 4 + k : slots + 5 + k, :], axis=1, keepdims=True)
            factors[k : k + 1, :] = jnp.broadcast_to(
                jnp.sqrt(weight_sq) * lax.rsqrt(grad_sq_sum + 1e-12), (1, LANES)
            )
        row = lax.broadcasted_iota(jnp.int32, (count, slots), 0)
        col = lax.broadcasted_iota(jnp.int32, (count, slots), 1)
        spread = dot(jnp.where((row >> 3) // per == col, 1.0, 0.0), every_sum[0:slots, :], NN, highest)
        row = lax.broadcasted_iota(jnp.int32, (count, LANES), 0)
        col = lax.broadcasted_iota(jnp.int32, (count, LANES), 1)
        place = lax.rem(row >> 3, per) * nb + (row & 7) - nb
        spread = jnp.where(((col >> 3) == place) & ((row & 7) >= nb), spread, 0.0)
        row = lax.broadcasted_iota(jnp.int32, (LANES, EXPERTS), 0)
        col = lax.broadcasted_iota(jnp.int32, (LANES, EXPERTS), 1)
        dz_rows = dot(spread, jnp.where((row & (EXPERTS - 1)) == col, 1.0, 0.0), NN, highest)
        pooled_in = rows_all[:, :, cuts_two[2] : cuts_two[2] + 256].reshape(count, 256)
        route_in[...] = dot(pooled_in, dz_rows, TN, highest)[:WIDTH_IN]
        grad_side_out[...] = jnp.transpose(grad_side[...])[:own]
        values = grad_cls[:, :CLASSES]
        both = jnp.concatenate([head_gain, head_bias] + [jnp.zeros((6, own_head), f32)], axis=0)
        grad_cls[...] = jnp.concatenate(
            [jnp.transpose(both)[:, 0:2], values, jnp.zeros((own_head, CLASS_PAD - CLASSES - 2), f32)], axis=1
        )
        up.finish()
        up_b.finish()
        up_h.finish()
        plane_b.finish()
        far_b.finish()
        far.finish()
        twin.finish()
        plane.finish()


def stage_back(half_b, part_b, piece_h, grad_in, dpre, pre, taps, mask, side, stats_one, stats_two, sums_two, totals, lines, images, kern, mix, gates, gate_grad, small, shape_b, shape_h, nb, nd, nz, ident):
    rows, width = pre.shape
    chunks = width // LANES
    deep = LANES * EXPERTS
    before = lambda t: jnp.minimum(t, chunks - 1)
    after = lambda t: jnp.maximum(t - chunks, 0)
    shape = (kern.shape[0], kern.shape[1] // nz)
    devices = nd * nz
    slots = dz_slots(nb, devices)[1]
    few = nz // 2
    chan_old, head_old, proj_old = small[-3:]
    own, own_head = chan_old.shape[1], head_old.shape[1]
    outs = [(own_head, CLASS_PAD), (own, 104), (8, LANES)]
    outs += [(WIDTH_IN, EXPERTS), (WIDTH_OUT, EXPERTS), (1, SQUEEZE), (1, CLASS_PAD)]
    outs += [chan_old.shape, head_old.shape, proj_old.shape, (8, LANES)]
    cuts_one, cuts_two, wide = share_width(lines, nz)
    hbm = pl.BlockSpec(memory_space=pltpu.HBM)
    tall_before = pl.BlockSpec((rows, LANES), lambda t: (0, before(t)))
    return pl.pallas_call(
        functools.partial(stage_back_kernel, nd, nz, nb, chunks, shape, shape_b, shape_h, cuts_one, cuts_two),
        grid=(2 * chunks,),
        out_shape=[jax.ShapeDtypeStruct(x, bf16) for x in (shape, shape_b, shape_h)]
        + [jax.ShapeDtypeStruct(x, f32) for x in outs],
        in_specs=[
            pl.BlockSpec(
                (nz - few,) + half_b.shape[1:], lambda t: (1, 0, 0), pipeline_mode=pl.Buffered(1)
            ),
            whole(part_b.shape),
            whole(piece_h.shape),
            tall_before,
            tall_before,
            pl.BlockSpec((rows, LANES), lambda t: (0, lax.rem(t, chunks))),
            pl.BlockSpec((nb, 32, LANES), lambda t: (0, 0, before(t))),
            whole(mask.shape),
            pl.BlockSpec((side.shape[0], LANES), lambda t: (0, lax.rem(t, chunks))),
            whole(stats_one.shape),
            whole(stats_two.shape),
            whole(sums_two.shape),
            whole(totals.shape),
        ]
        + [whole(x.shape) for x in lines]
        + [
            whole(images.shape),
            pl.BlockSpec((kern.shape[0], deep), lambda t: (0, after(t))),
            whole(mix.shape),
            whole(gates.shape),
            whole(gate_grad.shape),
        ]
        + [whole(x.shape) for x in small],
        out_specs=[hbm] * 3 + [whole(x) for x in outs],
        scratch_shapes=[
            VMEM((chunks, rows, LANES), f32),
            VMEM((chunks, nb, 32, LANES), f32),
            VMEM((KERNEL, PIXELS, LANES), f32),
            VMEM((PIXELS, LANES), f32),
            VMEM((8, LANES), f32),
            VMEM((24, LANES), f32),
            VMEM((24, LANES), f32),
            VMEM((24, LANES), f32),
            VMEM(part_shape(shape_b, nd, nz), bf16),
            VMEM(piece_shape(shape_b, nd), bf16),
            VMEM((devices, 8, wide), f32),
            VMEM((kern.shape[0], nb * LANES), bf16),
            VMEM((8, deep), f32),
            VMEM((104, up_to(own)), f32),
            VMEM((slots + 8, LANES), f32),
            VMEM((slots + 8, LANES), f32),
            VMEM(half_shape(shape, nd, nz), bf16),
            VMEM(part_shape(shape, nd, nz), bf16),
            VMEM(piece_shape(shape, nd), bf16),
        ]
        + sum_scratch(24, nd, nz)[1:] * 2
        + sum_scratch(slots + 8, nd, nz)[1:]
        + plane_scratch(shape_b, nd, nz - nz // 2)
        + far_scratch(shape_b, nd, nz)
        + spread_scratch(shape_b, nd, nz)
        + spread_scratch(shape_h, nd, nz)
        + share_scratch(wide, nd, nz)
        + twin_scratch(shape, nd, nz)
        + plane_scratch(shape, nd, nz)
        + far_scratch(shape, nd, nz)
        + spread_scratch(shape, nd, nz),
        compiler_params=params(ident, 62 * 1024 * 1024),
        name="stage_back",
    )(half_b, part_b, piece_h, grad_in, dpre, pre, taps, mask, side, stats_one, stats_two, sums_two, totals, *lines, images, kern, mix, gates, gate_grad, *small)


def update(weight, grad, moment, average, factor):
    scaled = grad * factor
    moment_new = 0.5 * moment + scaled
    weight_new = weight - 0.2 * (scaled + 0.5 * moment_new)
    average_new = 0.5 * average + 0.5 * weight_new
    return (weight_new, moment_new, average_new)


BLOCK_STEP = 64
HEAD_STEP = 32


def turn(x, shift):
    width = x.shape[1]
    return pltpu.roll(x, lax.rem(width - shift, width), 1)


def apply_kernel(
    factors,
    grad_side,
    side_w,
    side_m,
    side_e,
    grad_a,
    grad_b,
    block_w,
    block_m,
    block_e,
    grad_h,
    head_w,
    head_m,
    head_e,
    grad_cls,
    hside_w,
    hside_m,
    hside_e,
    side_wo,
    side_mo,
    side_eo,
    block_wo,
    block_mo,
    block_eo,
    head_wo,
    head_mo,
    head_eo,
    hside_wo,
    hside_mo,
    hside_eo,
    grad_block,
):
    @pl.when(pl.program_id(0) == 0)
    def _():
        fresh = update(side_w[...], grad_side[:, : side_w.shape[1]], side_m[...], side_e[...], factors[1:2, 0:1])
        side_wo[...], side_mo[...], side_eo[...] = fresh
        first = WIDTH_IN + TAPS
        whole_rows = first // 16 * 16

        @pl.loop(0, whole_rows // 16)
        def _(i):
            here = tall(i * 16, 16)
            grad_block[here, :] = grad_a[here, :].astype(f32)

        grad_block[whole_rows:first, :] = grad_a[whole_rows : whole_rows + 16, :].astype(f32)[: first - whole_rows]
        for i in range(WIDTH_OUT // 16):
            grad_block[first + 16 * i : first + 16 * (i + 1), :] = grad_b[16 * i : 16 * (i + 1), :].astype(f32)
        grad_block[first + WIDTH_OUT :, :] = jnp.zeros(
            (grad_block.shape[0] - first - WIDTH_OUT, grad_block.shape[1]), f32
        )

    here = pl.multiple_of(jnp.minimum(pl.program_id(0), grad_block.shape[0] // BLOCK_STEP - 1) * BLOCK_STEP, BLOCK_STEP)

    for k in range(0, BLOCK_STEP, 16):
        rows = slice(k, k + 16)
        fresh = update(
            block_w[rows, :], grad_block[pl.ds(here + k, 16), :], block_m[rows, :], block_e[rows, :], factors[0:1, 0:1]
        )
        block_wo[rows, :], block_mo[rows, :], block_eo[rows, :] = fresh
    for k in range(0, HEAD_STEP, 16):
        rows = slice(k, k + 16)
        fresh = update(
            head_w[rows, :], grad_h[rows, :].astype(f32), head_m[rows, :], head_e[rows, :], factors[2:3, 0:1]
        )
        head_wo[rows, :], head_mo[rows, :], head_eo[rows, :] = fresh
    fresh = update(hside_w[...], grad_cls[:, : hside_w.shape[1]], hside_m[...], hside_e[...], factors[3:4, 0:1])
    hside_wo[...], hside_mo[...], hside_eo[...] = fresh


def apply(factors, side, grads, block, head_arrays, hside):
    def stepped(array, size):
        last = -(-array.shape[0] // size) - 1
        return pl.BlockSpec((size, array.shape[1]), lambda j: (jnp.minimum(j, last), 0))

    steps = max(-(-block[0].shape[0] // BLOCK_STEP), -(-WIDTH_OUT // HEAD_STEP))
    blocks = (
        [whole(x.shape) for x in side]
        + [whole(x.shape) for x in grads]
        + [stepped(x, BLOCK_STEP) for x in block]
        + [stepped(x, HEAD_STEP) for x in head_arrays]
        + [stepped(x, HEAD_STEP) for x in hside]
    )
    arrays = side + grads + block + head_arrays + hside
    keep = [k for k in range(17) if k not in (0, 4, 5, 9, 13)]
    return pl.pallas_call(
        apply_kernel,
        grid=(steps,),
        out_shape=[jax.ShapeDtypeStruct(arrays[k].shape, f32) for k in keep],
        in_specs=[whole(factors.shape)] + blocks,
        out_specs=[blocks[k] for k in keep],
        scratch_shapes=[VMEM((-(-block[0].shape[0] // BLOCK_STEP) * BLOCK_STEP, block[0].shape[1]), f32)],
        compiler_params=params(),
        name="apply",
    )(factors, *arrays)


def body(
    nd,
    nz,
    images,
    pixel_mask,
    counts,
    labels,
    block_w,
    chan_side,
    head_w,
    head_side,
    shared,
    block_mom,
    side_mom,
    head_mom,
    hside_mom,
    shared_mom,
    block_ema,
    side_ema,
    head_ema,
    hside_ema,
    shared_ema,
    chan_stats,
    head_stats,
    proj_stats,
):
    z = lax.axis_index("chan")
    nb = images.shape[0] // nz
    own = chan_side.shape[1]
    own_head = head_side.shape[0]
    width = own * nz
    head_width = own_head * nz
    end_route = WIDTH_IN * EXPERTS
    end_head = end_route + WIDTH_OUT * EXPERTS
    end_norm = end_head + 2 * WIDTH_OUT
    end_squeeze = end_norm + SQUEEZE
    route_in = shared[:end_route].reshape(WIDTH_IN, EXPERTS)
    route_head = shared[end_route:end_head].reshape(WIDTH_OUT, EXPERTS)
    gain_out = shared[end_head:end_norm].reshape(2, WIDTH_OUT)
    sq_bias = shared[None, end_norm:end_squeeze]
    class_bias = jnp.pad(shared[end_squeeze:], (0, CLASS_PAD - CLASSES))[None, :]

    def mine(x):
        return lax.dynamic_slice_in_dim(x, z * nb, nb, 0)

    image_rows = mine(images).reshape(nb * PIXELS, WIDTH_IN)
    mask_now = mine(pixel_mask).astype(f32)
    mask = jnp.broadcast_to(mask_now.reshape(-1, 1), (nb * PIXELS, LANES))
    mask_rows = jnp.pad(
        (jnp.eye(nb, dtype=f32)[:, :, None] * mask_now[None]).reshape(nb, nb * PIXELS).astype(bf16),
        ((0, 8 - nb), (0, 0)),
    )
    count_rows = jnp.broadcast_to(jnp.pad(mine(counts).astype(f32), (0, 8 - nb))[:, None], (8, LANES))
    label_rows = jnp.broadcast_to(jnp.pad(mine(labels), (0, 8 - nb))[:, None], (8, LANES))

    full_a, full_b, side, gain_head, kern_h, kern_c, squares = first_gather(
        block_w, head_w, head_side, chan_side.T, nd, nz, 1
    )
    (
        pre,
        taps,
        dpre,
        stats_one,
        stats_two,
        mix,
        gates,
        pooled_in,
        excited,
        proj,
        pooled,
        gate,
        squeezed,
        stats_three,
        mixed_proj,
        full_b,
        full_h,
        full_c,
    ) = first_stage(
        full_a,
        image_rows,
        mask,
        mask_rows,
        count_rows,
        route_in,
        side,
        sq_bias,
        full_b,
        kern_h,
        kern_c,
        nb,
        width,
        nd,
        nz,
        3,
    )
    totals = stats_one
    head_pool, stats_four, features, grad_logits, sums_four, grad_proj, sums_three, dz_head, half_h, part_h, _ = head_stage(
        mask,
        mask_rows,
        count_rows,
        label_rows,
        class_bias,
        gain_head,
        totals,
        gain_out,
        full_h,
        route_head,
        proj,
        stats_three,
        full_c,
        nb,
        nd,
        nz,
        8,
    )
    shape_h, shape_b = shard_shape(full_h, nz), shard_shape(full_b, nz)
    grad_norm, sums_two, grad_squeeze, gate_grad, dz_gate, piece_h, half_b, part_b = project_back(
        half_h,
        part_h,
        shape_h,
        grad_proj,
        proj,
        stats_three,
        sums_three,
        gain_out,
        mask,
        count_rows,
        totals,
        stats_two,
        side,
        dpre,
        excited,
        mixed_proj,
        full_b,
        mix,
        gate,
        pooled,
        squeezed,
        sq_bias,
        nb,
        nd,
        nz,
        9,
    )
    lines = [features, grad_logits, pooled, dz_gate, head_pool, pooled_in, grad_squeeze, squeezed, sq_bias, dz_head]
    small = [squares, stats_three, stats_four, sums_four, chan_stats, head_stats, proj_stats]
    grad_a, grad_b, grad_h, grad_cls, grad_side, factors, *rest = stage_back(
        half_b,
        part_b,
        piece_h,
        grad_norm,
        dpre,
        pre,
        taps,
        mask,
        side,
        stats_one,
        stats_two,
        sums_two,
        totals,
        lines,
        image_rows,
        full_a,
        mix,
        gates,
        gate_grad,
        small,
        shape_b,
        shape_h,
        nb,
        nd,
        nz,
        11,
    )
    grad_route_in, grad_route_head, grad_sq_bias, grad_class_bias, new_chan, new_head_stats, new_proj, loss = rest
    results = apply(
        factors,
        [grad_side, chan_side.T, side_mom.T, side_ema.T],
        [grad_a, grad_b],
        [block_w, block_mom, block_ema],
        [grad_h, head_w, head_mom, head_ema],
        [grad_cls, head_side, hside_mom, hside_ema],
    )
    new_side, new_block, new_head, new_hside = (results[3 * k : 3 * k + 3] for k in range(4))
    new_side = [x.T for x in new_side]

    def out_row(first):
        return sums_three[first : first + OUT_CHUNKS].reshape(-1)[:WIDTH_OUT]

    grad_shared = jnp.concatenate(
        [
            grad_route_in.reshape(-1),
            grad_route_head.reshape(-1),
            out_row(OUT_CHUNKS),
            out_row(0),
            grad_sq_bias[0],
            grad_class_bias[0, :CLASSES],
        ]
    )
    new_shared = update(
        shared,
        grad_shared,
        shared_mom,
        shared_ema,
        jnp.sqrt(jnp.sum(shared * shared)) * lax.rsqrt(jnp.sum(grad_shared * grad_shared) + 1e-12),
    )
    groups = (new_block, new_side, new_head, new_hside, new_shared)
    return (
        (loss[0, 0],)
        + tuple(group[k] for k in range(3) for group in groups)
        + (new_chan, new_head_stats, new_proj)
    )


def solution(mesh):
    nd, nz = mesh.shape["dp"], mesh.shape["chan"]
    cols = P(None, "chan")
    state = (cols, cols, cols, P("chan", None), P())
    return jax.shard_map(
        functools.partial(body, nd, nz),
        mesh=mesh,
        in_specs=(P("dp", None, None), P("dp", None), P("dp"), P("dp"))
        + state * 3
        + (cols, cols, cols),
        out_specs=(P(),) + state * 3 + (cols, cols, cols),
        check_vma=False,
    )
```

```python
import functools

import jax
import jax.numpy as jnp
from jax import lax
from jax.experimental import pallas as pl
from jax.experimental.pallas import tpu as pltpu
from jax.sharding import PartitionSpec as P

WIDTH_IN = 192
WIDTH_OUT = 320
SQUEEZE = 48
CLASSES = 1000
EXPERTS = 8
KERNEL = 5
MAP_SIDE = 16
TAPS = KERNEL * KERNEL
PIXELS = MAP_SIDE * MAP_SIDE
LANES = 128
CLASS_PAD = 1024
TOTAL_ROW = 18
eps_norm = 0.001
highest = lax.Precision.HIGHEST
MESH = pl.DeviceIdType.MESH
f32 = jnp.float32
bf16 = jnp.bfloat16
VMEM = pltpu.VMEM
VLIMIT = 60 * 1024 * 1024


def dot(a, b, dims=((1,), (0,)), precision=None):
    return lax.dot_general(a, b, (dims, ((), ())), precision=precision, preferred_element_type=f32)


NN = ((1,), (0,))
NT = ((1,), (1,))
TN = ((0,), (0,))


def sig(x):
    return 0.5 * jnp.tanh(0.5 * x) + 0.5


def dsilu(n):
    s = sig(n)
    return s * (1.0 + n * (1.0 - s))


def rsum(x):
    return jnp.sum(x, axis=0, keepdims=True)


def split(x):
    high = x.astype(bf16)
    return jnp.concatenate([high, (x - high.astype(f32)).astype(bf16)], axis=0)


def sum_peers(nd, nz):
    d = lax.axis_index("dp")
    z = lax.axis_index("chan")
    in_plane = [(lax.rem(d + k, nd), z) for k in range(1, nd)]
    along = [(d, lax.rem(z + k, nz)) for k in range(1, nz)]
    return in_plane, along


def signal(peers):
    barrier = pltpu.get_barrier_semaphore()
    for peer in peers:
        pl.semaphore_signal(barrier, inc=1, device_id=peer, device_id_type=MESH)


def sum_start(nd, nz):
    in_plane, along = sum_peers(nd, nz)
    signal(in_plane + along)


def met(nd, nz):
    pl.semaphore_wait(pltpu.get_barrier_semaphore(), nd + nz - 2)


def sum_copies(nd, nz, x_ref, plane, depth, s1, r1, s2, r2):
    d = lax.axis_index("dp")
    z = lax.axis_index("chan")
    in_plane, along = sum_peers(nd, nz)

    def copy(src, dst, send, recv, peer):
        return pltpu.make_async_remote_copy(
            src_ref=src, dst_ref=dst, send_sem=send, recv_sem=recv, device_id=peer, device_id_type=MESH
        )

    first = [copy(x_ref, plane.at[d], s1.at[k], r1.at[k], peer) for k, peer in enumerate(in_plane)]
    second = [copy(depth.at[z], depth.at[z], s2.at[k], r2.at[k], peer) for k, peer in enumerate(along)]
    return first, second


def sum_first(nd, nz, x_ref, plane, *comm):
    start(sum_copies(nd, nz, x_ref, plane, *comm)[0])
    plane[lax.axis_index("dp")] = x_ref[...]


def sum_second(nd, nz, x_ref, plane, depth, *sems):
    first, second = sum_copies(nd, nz, x_ref, plane, depth, *sems)
    arrived(first)
    total = plane[0]
    for k in range(1, nd):
        total = total + plane[k]
    depth[lax.axis_index("chan")] = total
    start(second)


def sum_third(nd, nz, x_ref, plane, depth, *sems):
    first, second = sum_copies(nd, nz, x_ref, plane, depth, *sems)
    arrived(second)
    total = depth[0]
    for k in range(1, nz):
        total = total + depth[k]
    sent(first + second)
    return total


def sum_finish(nd, nz, x_ref, o_ref, *comm):
    sum_first(nd, nz, x_ref, *comm)
    sum_second(nd, nz, x_ref, *comm)
    o_ref[...] = sum_third(nd, nz, x_ref, *comm)


def sum_scratch(rows, nd, nz):
    return [
        VMEM((rows, LANES), f32),
        VMEM((nd, rows, LANES), f32),
        VMEM((nz, rows, LANES), f32),
        pltpu.SemaphoreType.DMA((nd,)),
        pltpu.SemaphoreType.DMA((nd,)),
        pltpu.SemaphoreType.DMA((nz,)),
        pltpu.SemaphoreType.DMA((nz,)),
    ]


def params(ident=None, limit=VLIMIT):
    if ident is None:
        return pltpu.CompilerParams(vmem_limit_bytes=VLIMIT)
    return pltpu.CompilerParams(vmem_limit_bytes=limit, collective_id=ident, has_side_effects=True)


def sum_kernel(nd, nz, x_ref, o_ref, *comm):
    sum_start(nd, nz)
    met(nd, nz)
    sum_finish(nd, nz, x_ref, o_ref, *comm)


def all_sum(x, nd, nz, ident):
    return pl.pallas_call(
        functools.partial(sum_kernel, nd, nz),
        out_shape=jax.ShapeDtypeStruct(x.shape, x.dtype),
        in_specs=[pl.BlockSpec(memory_space=VMEM)],
        out_specs=pl.BlockSpec(memory_space=VMEM),
        scratch_shapes=sum_scratch(x.shape[0], nd, nz)[1:],
        compiler_params=params(ident),
        name="all_sum",
    )(x)


def by_column(width):
    return (width // 2) % LANES == 0


def pad_rows(rows, width, nd):
    unit = 16 * (nd // 2 if by_column(width) else nd)
    return -(-rows // unit) * unit


def core_block(rows, width, core):
    if by_column(width):
        return 0, rows, pl.multiple_of(core * (width // 2), LANES), width // 2
    return pl.multiple_of(core * (rows // 2), 16), rows // 2, 0, width


def part(rows, width, nd, core, place):
    row, count, col, cols = core_block(rows, width, core)
    unit = count // (nd // 2)
    return pl.multiple_of(row + place * unit, 16), unit, col, cols


class Net:
    def __init__(self, nd, nz):
        self.nd, self.nz, self.nxy = nd, nz, nd // 2
        self.d = lax.axis_index("dp")
        self.z = lax.axis_index("chan")
        self.core = lax.rem(self.d, 2)
        self.place = self.d // 2
        self.far = [lax.rem(self.z + k, nz) for k in range(1, nz)]
        self.others = [lax.rem(self.place + k, self.nxy) for k in range(1, self.nxy)]
        self.along = [(self.d, zz) for zz in self.far]
        self.plane = [(2 * o + self.core, self.z) for o in self.others]
        self.twin = (2 * self.place + 1 - self.core, self.z)

    def copy(self, src, dst, sems, k, peer):
        return pltpu.make_async_remote_copy(
            src_ref=src,
            dst_ref=dst,
            send_sem=sems[0].at[k],
            recv_sem=sems[1].at[k],
            device_id=peer,
            device_id_type=MESH,
        )


def start(copies):
    for copy in copies:
        copy.start()


def arrived(copies):
    for copy in copies:
        copy.wait_recv()


def sent(copies):
    for copy in copies:
        copy.wait_send()


def pair(n):
    return [pltpu.SemaphoreType.DMA((n,)), pltpu.SemaphoreType.DMA((n,))]


def lanes(first, count):
    return pl.ds(pl.multiple_of(first, LANES), count)


def tall(first, count):
    return pl.ds(pl.multiple_of(first, 16), count)


def spot(ref, shape, zz, row, unit, col, cols):
    if len(ref.shape) == 3:
        return ref.at[zz, tall(row, unit), lanes(col, cols)]
    return ref.at[tall(row, unit), lanes(zz * shape[1] + col, cols)]


def shard_shape(full, nz):
    if len(full.shape) == 3:
        return full.shape[1:]
    return (full.shape[0], full.shape[1] // nz)


def own_copy(net, shape, src, dst, sem):
    return pltpu.make_async_copy(src, spot(dst, shape, net.z, 0, shape[0], 0, shape[1]), sem)


def gather_far(net, shape, src, dst, sems):
    rows, width = shape
    row, unit, col, cols = part(rows, width, net.nd, net.core, net.place)
    block = src.at[tall(row, unit), lanes(col, cols)]
    return [
        net.copy(block, spot(dst, shape, net.z, row, unit, col, cols), sems, k, peer)
        for k, peer in enumerate(net.along)
    ]


def gather_plane(net, shape, ref, sems, k):
    rows, width = shape
    row, unit, col, cols = part(rows, width, net.nd, net.core, net.place)
    block = spot(ref, shape, net.far[k], row, unit, col, cols)
    n = net.nxy - 1
    return [net.copy(block, block, sems, k * n + q, peer) for q, peer in enumerate(net.plane)]


def gather_twin(net, shape, ref, sems, k):
    rows, width = shape
    row, unit, col, cols = core_block(rows, width, net.core)
    block = spot(ref, shape, net.far[k], row, unit, col, cols)
    return [net.copy(block, block, sems, k, net.twin)]


def late_count(nz):
    return max(1, (nz - 1) // 3)


def some(stage, net, shape, ref, sems, shards):
    return [copy for k in shards for copy in stage(net, shape, ref, sems, k)]


def every(stage, net, shape, ref, sems):
    return [copy for k in range(net.nz - 1) for copy in stage(net, shape, ref, sems, k)]


def squares_of(ref, rows):
    step_rows = 16 if ref.dtype == bf16 else 8
    whole_rows = rows // step_rows * step_rows

    def step(i, total):
        value = ref[pl.ds(pl.multiple_of(i * step_rows, step_rows), step_rows), :].astype(f32)
        return total + value * value

    total = jnp.sum(lax.fori_loop(0, whole_rows // step_rows, step, jnp.zeros((step_rows, ref.shape[1]), f32)))
    if whole_rows < rows:
        last = ref[whole_rows:rows, :].astype(f32)
        total = total + jnp.sum(last * last)
    return total


def row_of(total):
    lane = lax.broadcasted_iota(jnp.int32, (1, LANES), 1)
    return jnp.where(lane == 0, total, 0.0)


def first_kernel(nd, nz, shape, shape_b, block_ref, head_ref, hside_ref, side_ref, full, full_b, side, gain, kh, kc, squares, wide, tall_h, tall_s, kb, low, side_buf, gain_buf, far_s, far_r, plane_s, plane_r, twin_s, twin_r, side_s, side_r, gain_s, gain_r, later_s, later_r, local):
    net = Net(nd, nz)
    signal(net.along + net.plane + [net.twin])
    rows = shape[0]
    total_rows = block_ref.shape[0]
    fetch = [
        pltpu.make_async_copy(block_ref.at[pl.ds(0, rows)], wide.at[pl.ds(0, rows)], local.at[0]),
        pltpu.make_async_copy(
            block_ref.at[pl.ds(rows, total_rows - rows)], wide.at[pl.ds(rows, total_rows - rows)], local.at[1]
        ),
        pltpu.make_async_copy(hside_ref, tall_s, local.at[2]),
        pltpu.make_async_copy(head_ref, tall_h, local.at[3]),
    ]
    fetch[0].start()
    fetch[0].wait()
    start(fetch[1:])

    @pl.loop(0, rows // 16)
    def _(i):
        at = tall(i * 16, 16)
        low[at, :] = wide[at, :].astype(bf16)

    own = own_copy(net, shape, low, full, local.at[4])
    own.start()
    pl.semaphore_wait(pltpu.get_barrier_semaphore(), nz - 1 + nd // 2)
    far = gather_far(net, shape, low, full, (far_s, far_r))
    start(far)
    side_buf[net.z] = jnp.transpose(side_ref[...])
    sides = [
        net.copy(side_buf.at[net.z], side_buf.at[net.z], (side_s, side_r), k, peer)
        for k, peer in enumerate(net.along)
    ]
    start(sides)
    fetch[2].wait()
    gain_buf[net.z] = jnp.transpose(tall_s[:, 0:LANES])[0:8]
    gains = [
        net.copy(gain_buf.at[net.z], gain_buf.at[net.z], (gain_s, gain_r), k, peer)
        for k, peer in enumerate(net.along)
    ]
    start(gains)
    fetch[1].wait()
    first = WIDTH_IN + TAPS
    for i in range(WIDTH_OUT // 16):
        kb[16 * i : 16 * (i + 1), :] = wide[first + 16 * i : first + 16 * (i + 1), :].astype(bf16)
    own_b = own_copy(net, shape_b, kb, full_b, local.at[5])
    own_b.start()
    planes = []
    for k in range(nz - 1):
        arrived([far[nz - 2 - k]])
        planes.append(gather_plane(net, shape, full, (plane_s, plane_r), k))
        start(planes[k])
    later = gather_far(net, shape_b, kb, full_b, (later_s, later_r))
    start(later)
    fetch[3].wait()

    @pl.loop(0, WIDTH_OUT // 16)
    def _(i):
        at = tall(i * 16, 16)
        kh[at, :] = tall_h[at, :].astype(bf16)

    for i in range(tall_s.shape[0] // 16):
        value = tall_s[16 * i : 16 * (i + 1), 2 : 2 + CLASSES]
        kc[16 * i : 16 * (i + 1), :] = jnp.concatenate(
            [value, jnp.zeros((16, CLASS_PAD - CLASSES), f32)], axis=1
        ).astype(bf16)
    squares[...] = jnp.zeros_like(squares)
    for k, (ref, count) in enumerate(
        ((wide, total_rows), (side_ref, side_ref.shape[0]), (tall_h, WIDTH_OUT), (tall_s, tall_s.shape[0]))
    ):
        squares[k : k + 1, :] = row_of(squares_of(ref, count))
    twins = []
    for k in range(nz - 1):
        arrived(planes[k])
        twins.append(gather_twin(net, shape, full, (twin_s, twin_r), k))
        start(twins[k])
    arrived(sides + gains)
    side[...] = jnp.zeros_like(side)
    side[0 : side_ref.shape[1], :] = jnp.concatenate([side_buf[k] for k in range(nz)], axis=1)
    gain[...] = jnp.concatenate([gain_buf[k] for k in range(nz)], axis=1)
    for k in range(nz - 1):
        arrived(twins[k])
    arrived(later)
    sent(far + sides + gains + later)
    for k in range(nz - 1):
        sent(planes[k] + twins[k])
    own.wait()
    own_b.wait()


def first_gather(block, head_w, head_side, side, nd, nz, ident):
    shape = (pad_rows(WIDTH_IN + TAPS, block.shape[1], nd), block.shape[1])
    shape_b = (pad_rows(WIDTH_OUT, block.shape[1], nd), block.shape[1])
    shape_h = (pad_rows(WIDTH_OUT, head_w.shape[1], nd), head_w.shape[1])
    shape_c = (pad_rows(head_side.shape[0], CLASS_PAD, nd), CLASS_PAD)
    hbm = pl.BlockSpec(memory_space=pltpu.HBM)
    vmem = pl.BlockSpec(memory_space=VMEM)
    own_head = head_side.shape[0]
    return pl.pallas_call(
        functools.partial(first_kernel, nd, nz, shape, shape_b),
        out_shape=[
            jax.ShapeDtypeStruct((shape[0], nz * shape[1]), bf16),
            jax.ShapeDtypeStruct((shape_b[0], nz * shape_b[1]), bf16),
            jax.ShapeDtypeStruct((104, nz * side.shape[0]), f32),
            jax.ShapeDtypeStruct((8, nz * own_head), f32),
            jax.ShapeDtypeStruct(shape_h, bf16),
            jax.ShapeDtypeStruct(shape_c, bf16),
            jax.ShapeDtypeStruct((8, LANES), f32),
        ],
        in_specs=[hbm, hbm, hbm, vmem],
        out_specs=[hbm] * 2 + [vmem] * 5,
        scratch_shapes=[
            VMEM(block.shape, f32),
            VMEM(head_w.shape, f32),
            VMEM(head_side.shape, f32),
            VMEM(shape_b, bf16),
            VMEM(shape, bf16),
            VMEM((nz, side.shape[1], side.shape[0]), f32),
            VMEM((nz, 8, own_head), f32),
        ]
        + pair(nz - 1)
        + pair((nz - 1) * (nd // 2 - 1))
        + pair(nz - 1)
        + pair(nz - 1) * 3
        + [pltpu.SemaphoreType.DMA((6,))],
        compiler_params=params(ident),
        name="first_gather",
    )(block, head_w, head_side, side)


def reduce_sizes(rows, width, nd):
    unit, cols = (rows, width // 2) if by_column(width) else (rows // 2, width)
    return unit, cols, unit // (nd // 2)


def reduce_twin(net, shape, g_ref, twin_buf, sems, k):
    row, unit, col, cols = core_block(shape[0], shape[1], 1 - net.core)
    return net.copy(
        g_ref.at[tall(row, unit), lanes(k * shape[1] + col, cols)], twin_buf.at[k], sems, k, net.twin
    )


def reduce_add(net, shape, g_ref, half, twin_buf, k):
    row, unit, col, cols = core_block(shape[0], shape[1], net.core)

    @pl.loop(0, unit // 16)
    def _(i):
        at = tall(i * 16, 16)
        mine = g_ref[tall(row + i * 16, 16), lanes(k * shape[1] + col, cols)]
        half[k, at, :] = (mine.astype(f32) + twin_buf[k, at, :].astype(f32)).astype(bf16)


def reduce_plane(net, shape, half, plane_buf, sems, k, base, shift):
    size = reduce_sizes(*shape, net.nd)[2]
    n = net.nxy - 1
    return [
        net.copy(half.at[k - shift, tall(o * size, size)], plane_buf.at[q, k - base], sems, (k - base) * n + q, net.plane[q])
        for q, o in enumerate(net.others)
    ]


def reduce_plane_sum(net, shape, half, plane_buf, out, k, base, shift):
    size = reduce_sizes(*shape, net.nd)[2]

    @pl.loop(0, size // 16)
    def _(i):
        at = tall(i * 16, 16)
        total = half[k - shift, tall(net.place * size + i * 16, 16), :].astype(f32)
        for q in range(net.nxy - 1):
            total = total + plane_buf[q, k - base, at, :].astype(f32)
        out[k, at, :] = total.astype(bf16)


def reduce_far(net, sums, depth_buf, sems):
    return [net.copy(sums.at[zz], depth_buf.at[k], sems, k, net.along[k]) for k, zz in enumerate(net.far)]


def reduce_far_sum(net, shape, sums, depth_buf, piece):
    @pl.loop(0, reduce_sizes(*shape, net.nd)[2] // 16)
    def _(i):
        at = tall(i * 16, 16)
        total = sums[net.z, at, :].astype(f32)
        for q in range(net.nz - 1):
            total = total + depth_buf[q, at, :].astype(f32)
        piece[at, :] = total.astype(bf16)


def spread_block(net, shape, out):
    row, unit, col, cols = part(shape[0], shape[1], net.nd, net.core, net.place)
    return out.at[tall(row, unit), lanes(col, cols)]


def spread_plane(net, shape, piece, out, sems):
    block = spread_block(net, shape, out)
    return [net.copy(piece, block, sems, q, peer) for q, peer in enumerate(net.plane)]


def spread_twin(net, shape, out, sems):
    row, unit, col, cols = core_block(shape[0], shape[1], net.core)
    block = out.at[tall(row, unit), lanes(col, cols)]
    return [net.copy(block, block, sems, 0, net.twin)]


def twin_scratch(shape, nd, nz):
    unit, cols, size = reduce_sizes(*shape, nd)
    return [VMEM((shape[0], nz * shape[1]), bf16), VMEM((nz, unit, cols), bf16)] + pair(nz)


def plane_scratch(shape, nd, count):
    unit, cols, size = reduce_sizes(*shape, nd)
    return [VMEM((nd // 2 - 1, count, size, cols), bf16)] + pair(count * (nd // 2 - 1))


def half_shape(shape, nd, nz):
    unit, cols, size = reduce_sizes(*shape, nd)
    return (nz, unit, cols)


def part_shape(shape, nd, nz):
    unit, cols, size = reduce_sizes(*shape, nd)
    return (nz, size, cols)


def ready(shape, k):
    return max(2, -(-(k + 1) * shape[1] // (LANES * EXPERTS)))


class Steps:
    def __init__(self):
        self.steps = {}

    def at(self, step, action):
        self.steps.setdefault(step, []).append(action)

    def emit(self, now, last):
        for step in sorted(self.steps):
            if step < last:

                @pl.when(now == step)
                def _(step=step):
                    for action in self.steps[step]:
                        action()

    def end(self, last):
        for step in sorted(self.steps):
            if step >= last:
                for action in self.steps[step]:
                    action()


def far_scratch(shape, nd, nz):
    unit, cols, size = reduce_sizes(*shape, nd)
    return [VMEM((nz - 1, size, cols), bf16)] + pair(nz - 1)


def spread_scratch(shape, nd, nz):
    return [pltpu.SemaphoreType.DMA((1,))] + pair(nd // 2 - 1) + pair(1)


def piece_shape(shape, nd):
    unit, cols, size = reduce_sizes(*shape, nd)
    return (size, cols)


class Twin:
    def __init__(self, net, shape, half, g_ref, twin_buf, ts, tr):
        self.net, self.shape, self.half, self.g, self.buf, self.sems = net, shape, half, g_ref, twin_buf, (ts, tr)

    def copy(self, k):
        return reduce_twin(self.net, self.shape, self.g, self.buf, self.sems, k)

    def begin(self, k):
        self.copy(k).start()

    def add(self, k):
        self.copy(k).wait_recv()
        reduce_add(self.net, self.shape, self.g, self.half, self.buf, k)

    def finish(self):
        for k in range(self.net.nz):
            self.copy(k).wait_send()


class Plane:
    def __init__(self, net, shape, half, out, base, count, buf, ps, pr, shift=0):
        self.net, self.shape, self.half, self.out = net, shape, half, out
        self.shards, self.base, self.buf, self.sems = range(base, base + count), base, buf, (ps, pr)
        self.shift = shift

    def copies(self, k):
        return reduce_plane(self.net, self.shape, self.half, self.buf, self.sems, k, self.base, self.shift)

    def begin(self, k):
        start(self.copies(k))

    def add(self, then=None):
        for k in self.shards:
            self.add_one(k, then)

    def add_one(self, k, then=None):
        arrived(self.copies(k))
        reduce_plane_sum(self.net, self.shape, self.half, self.buf, self.out, k, self.base, self.shift)
        if then is not None:
            then(k)

    def finish(self):
        for k in self.shards:
            sent(self.copies(k))


class Far:
    def __init__(self, net, shape, sums, piece, buf, fs, fr):
        self.net, self.shape, self.sums, self.piece, self.buf, self.sems = net, shape, sums, piece, buf, (fs, fr)

    def copies(self):
        return reduce_far(self.net, self.sums, self.buf, self.sems)

    def send(self, k):
        net = self.net
        slot = lax.rem(k - net.z - 1 + net.nz, net.nz)

        @pl.when(net.z != k)
        def _():
            net.copy(self.sums.at[k], self.buf.at[slot], self.sems, slot, (net.d, k)).start()

    def add(self):
        arrived(self.copies())
        reduce_far_sum(self.net, self.shape, self.sums, self.buf, self.piece)

    def finish(self):
        sent(self.copies())


class Spread:
    def __init__(self, net, shape, piece, out, local, ps, pr, ts, tr):
        self.net, self.shape, self.piece, self.out, self.local = net, shape, piece, out, local
        self.plane_sems, self.twin_sems = (ps, pr), (ts, tr)

    def own(self):
        return pltpu.make_async_copy(self.piece, spread_block(self.net, self.shape, self.out), self.local.at[0])

    def plane(self):
        return spread_plane(self.net, self.shape, self.piece, self.out, self.plane_sems)

    def twin(self):
        return spread_twin(self.net, self.shape, self.out, self.twin_sems)

    def begin(self):
        self.own().start()
        start(self.plane())

    def cross(self):
        arrived(self.plane())
        self.own().wait()
        start(self.twin())

    def finish(self):
        arrived(self.twin())
        sent(self.plane() + self.twin())


def up_to(size):
    return -(-size // LANES) * LANES


def share_width(lines, nz):
    one = [0]
    for x in lines[0], lines[2], lines[3]:
        one.append(one[-1] + up_to(x.shape[1] // nz))
    for _ in range(3):
        one.append(one[-1] + LANES)
    two = [0]
    for x in lines[1], lines[4], lines[5]:
        two.append(two[-1] + up_to(x.shape[1]))
    return one, two, max(one[-1], two[-1])


def share_scratch(width, nd, nz):
    return (
        [VMEM((nz, 8, width), f32), pltpu.SemaphoreType.DMA((1,))]
        + pair(nz - 1)
        + pair(nd // 2 - 1)
        + pair(nd // 2)
    )


def fit(x, width):
    if x.shape[1] == width:
        return x
    return jnp.concatenate([x, jnp.zeros((x.shape[0], width - x.shape[1]), f32)], axis=1)


class Share:
    def __init__(self, net, rows_all, lines, local, fs, fr, ps, pr, ts, tr):
        self.net, self.rows, self.lines, self.local = net, rows_all, lines, local
        self.far_sems, self.plane_sems, self.twin_sems = (fs, fr), (ps, pr), (ts, tr)
        self.me = net.d * net.nz + net.z

    def fill(self, nb, cut, narrow, wide):
        width = self.lines.shape[2]
        self.lines[...] = jnp.zeros_like(self.lines)
        two = fit(jnp.concatenate([fit(x, up_to(x.shape[1])) for x in wide], axis=1), width)[:nb]
        last = [fit(x, LANES) for x in narrow]
        for k in range(self.net.nz):
            parts = []
            for x in cut:
                own = x.shape[1] // self.net.nz
                parts.append(fit(x[:, k * own : (k + 1) * own], up_to(own)))
            one = fit(jnp.concatenate(parts + last, axis=1), width)[:nb]
            self.lines[k, 0 : 2 * nb, :] = jnp.concatenate([one, two], axis=0)

    def far_copies(self):
        net = self.net
        return [
            net.copy(self.lines.at[zz], self.rows.at[self.me], self.far_sems, k, net.along[k])
            for k, zz in enumerate(net.far)
        ]

    def plane_copies(self):
        net = self.net
        block = self.rows.at[pl.ds(net.d * net.nz, net.nz)]
        return [net.copy(block, block, self.plane_sems, q, peer) for q, peer in enumerate(net.plane)]

    def twin_copies(self):
        net = self.net
        out = []
        for o in range(net.nxy):
            block = self.rows.at[pl.ds((2 * o + net.core) * net.nz, net.nz)]
            out.append(net.copy(block, block, self.twin_sems, o, net.twin))
        return out

    def far(self):
        start(self.far_copies())
        self.own().start()

    def own(self):
        return pltpu.make_async_copy(self.lines.at[self.net.z], self.rows.at[self.me], self.local.at[0])

    def plane(self):
        arrived(self.far_copies())
        self.own().wait()
        start(self.plane_copies())

    def twin(self):
        arrived(self.plane_copies())
        start(self.twin_copies())

    def finish(self):
        arrived(self.twin_copies())
        sent(self.far_copies() + self.plane_copies() + self.twin_copies())


def build_mix(gates, nb, ref):
    deep = LANES * EXPERTS
    row = lax.broadcasted_iota(jnp.int32, (deep, EXPERTS), 0)
    col = lax.broadcasted_iota(jnp.int32, (deep, EXPERTS), 1)
    pick = jnp.where((row & (EXPERTS - 1)) == col, 1.0, 0.0).astype(f32)
    row = lax.broadcasted_iota(jnp.int32, (deep, LANES), 0)
    col = lax.broadcasted_iota(jnp.int32, (deep, LANES), 1)
    same = (row >> 3) == col
    for b in range(nb):
        spread = jnp.broadcast_to(gates[b : b + 1, :], (LANES, EXPERTS))
        value = jnp.where(same, dot(pick, spread, NT, highest), 0.0)
        high = value.astype(bf16)
        ref[:, b * LANES : (b + 1) * LANES] = high
        ref[:, (nb + b) * LANES : (nb + b + 1) * LANES] = (value - high.astype(f32)).astype(bf16)


def mix_kernels(kernels, mix):
    both = dot(kernels, mix)
    half = both.shape[1] // 2
    return both[:, :half] + both[:, half:]


def gate_sums(rows):
    deep = LANES * EXPERTS
    row = lax.broadcasted_iota(jnp.int32, (deep, EXPERTS), 0)
    col = lax.broadcasted_iota(jnp.int32, (deep, EXPERTS), 1)
    pick = jnp.where((row & (EXPERTS - 1)) == col, 1.0, 0.0).astype(f32)
    return dot(rows, pick, NN, highest)


def gate_rows(grads, kernel_block, nb):
    both = dot(grads, kernel_block, TN)
    channels = LANES // EXPERTS
    row = lax.broadcasted_iota(jnp.int32, (channels, LANES), 0)
    col = lax.broadcasted_iota(jnp.int32, (channels, LANES), 1)
    same = row == (col >> 3)
    out = []
    for b in range(nb):
        parts = []
        for m in range(EXPERTS):
            first = b * LANES + m * channels
            block = both[first : first + channels, m * LANES : (m + 1) * LANES]
            parts.append(rsum(jnp.where(same, block, 0.0)))
        out.append(jnp.concatenate(parts, axis=1))
    return jnp.concatenate(out, axis=0)


def norm_rows(stats, chunk, chunks, total):
    mean = stats[pl.ds(chunk, 1), :] / total
    var = stats[pl.ds(chunks + chunk, 1), :] / total - mean * mean
    return mean, lax.rsqrt(var + eps_norm)


def whole(shape):
    return pl.BlockSpec(shape, lambda *_: (0,) * len(shape), pipeline_mode=pl.Buffered(1))


def image(b):
    return pl.ds(pl.multiple_of(b * PIXELS, PIXELS), PIXELS)


def shifted(value, step):
    if step == 0:
        return value
    col = lax.broadcasted_iota(jnp.int32, value.shape, 0) & (MAP_SIDE - 1)
    moved = pltpu.roll(value, (-step) % PIXELS, 0)
    keep = (col + step >= 0) & (col + step < MAP_SIDE)
    return jnp.where(keep, moved, 0.0)


def stage_kernel(
    nd,
    nz,
    nb,
    chunks,
    shapes,
    kern_ref,
    images,
    mask,
    mask_rows,
    counts,
    route,
    side,
    sq_bias,
    in_b,
    kh,
    kc,
    pre_out,
    taps_out,
    out,
    stats_all,
    sums_all,
    mix,
    gates,
    pooled,
    excited,
    proj,
    pool_out,
    gate_out,
    squeezed,
    last_all,
    mixed,
    full_b,
    full_h,
    full_c,
    pre,
    taps,
    buf,
    held,
    early,
    late,
    early_two,
    late_two,
    sums_three,
    dpre,
    exc,
    kern_buf,
    *comm,
):
    step = pl.program_id(0)
    comm_early, comm_late, comm_two, sems = comm[0:6], comm[6:12], comm[12:18], comm[18:]
    two_early, two_late, sems = sems[0:6], sems[6:12], sems[12:]
    cut_two = chunks // 2
    net = Net(nd, nz)
    few = late_count(nz)
    cut = chunks // 2
    groups = [[k for k in range(nz - 1) if 3 * k // (nz - 1) == g] for g in range(3)]

    def far_h():
        return gather_far(net, shapes[1], kh, full_h, sems[0:2])

    def far_c():
        return gather_far(net, shapes[2], kc, full_c, sems[2:4])

    def planes_b(k):
        return gather_plane(net, shapes[0], full_b, sems[4:6], k)

    def planes_h():
        return every(gather_plane, net, shapes[1], full_h, sems[6:8])

    def twins_b(k):
        return gather_twin(net, shapes[0], full_b, sems[8:10], k)

    def own():
        return [
            own_copy(net, shapes[1], kh, full_h, sems[10].at[0]),
            own_copy(net, shapes[2], kc, full_c, sems[10].at[1]),
        ]

    def b_planes(group):
        for k in groups[group]:
            start(planes_b(k))

    def begin():
        met(nd, nz)
        b_planes(0)
        start(far_h() + own())

    def early_sum():
        sum_first(nd, nz, early, *comm_early)

    def early_second():
        sum_second(nd, nz, early, *comm_early)

    def early_third():
        stats_all[...] = sum_third(nd, nz, early, *comm_early)
        sum_first(nd, nz, late, *comm_late)

    def late_second():
        sum_second(nd, nz, late, *comm_late)

    def late_third():
        stats_all[...] += sum_third(nd, nz, late, *comm_late)

    def h_planes(k):
        start(gather_plane(net, shapes[1], full_h, sems[6:8], k))

    def twins_h(k):
        return gather_twin(net, shapes[1], full_h, sems[11:13], k)

    def h_twin(k):
        arrived(gather_plane(net, shapes[1], full_h, sems[6:8], k))
        start(twins_h(k))

    def load(k):
        return pltpu.make_async_copy(
            full_b.at[pl.ds(0, WIDTH_OUT), lanes(k * LANES * EXPERTS, LANES * EXPERTS)],
            kern_buf.at[lax.rem(k, 2)],
            sems[13].at[lax.rem(k, 2)],
        )

    def b_whole():
        for k in range(nz - 1):
            arrived(twins_b(k))
        load(0).start()

    def b_twins(group):
        for k in groups[group]:
            arrived(planes_b(k))
            start(twins_b(k))

    @pl.when(step == 0)
    def _():
        sum_start(nd, nz)
        early[...] = jnp.zeros_like(early)
        late[...] = jnp.zeros_like(late)
        for ref in (early_two, late_two, sums_three, squeezed, pool_out):
            ref[...] = jnp.zeros_like(ref)
        early[2 * chunks : 2 * chunks + 1, :] = rsum(counts[...])
        early[2 * chunks + 1 : 2 * chunks + 2, :] = rsum(jnp.where(counts[...] > 0.0, 1.0, 0.0))
        pool = dot(mask_rows[...], images[...]) / jnp.maximum(counts[:, 0:1], 1.0)
        pooled[...] = pool
        gate = sig(dot(pool, route[...], NN, highest))
        gates[...] = gate
        build_mix(gate, nb, mix)

    steps = Steps()
    steps.at(1, begin)
    steps.at(cut, early_sum)
    steps.at(cut + 2, early_second)
    steps.at(cut + 3, functools.partial(b_planes, 1))
    steps.at(chunks, early_third)
    steps.at(chunks + 2, late_second)
    steps.at(chunks + 2, functools.partial(b_planes, 2))
    steps.at(chunks + cut, late_third)
    steps.at(chunks + cut, lambda: arrived(far_h()))
    steps.at(chunks + cut, lambda: start(far_c()))
    places = (chunks + cut_two, chunks + cut_two + 2, 2 * chunks, 2 * chunks, 2 * chunks + 2, 2 * chunks + cut_two)
    split_sum(nd, nz, steps, places, early_two, late_two, sums_all, two_early, two_late)
    later_steps = (chunks + cut_two + 1, 2 * chunks + 1, 2 * chunks + cut_two)
    for k in range(nz - 1):
        group = 3 * k // (nz - 1)
        steps.at(later_steps[group], functools.partial(h_planes, k))
        steps.at((2 * chunks + 2, 3 * chunks, 4 * chunks - 3)[group], functools.partial(h_twin, k))
    steps.at(2 * chunks - 1, b_whole)
    steps.at(chunks - 1, functools.partial(b_twins, 0))
    steps.at(chunks + 3, functools.partial(b_twins, 1))
    steps.at(2 * chunks - 3, functools.partial(b_twins, 2))
    steps.emit(step, 4 * chunks)

    @pl.when(step < chunks)
    def _():
        j = step
        mixed = mix_kernels(kern_ref[...], mix[...])
        one = jnp.zeros((1, LANES), f32)
        two = jnp.zeros((1, LANES), f32)
        for b in range(nb):
            at = slice(b * PIXELS, (b + 1) * PIXELS)
            lane = slice(b * LANES, (b + 1) * LANES)
            taps[j, b] = mixed[WIDTH_IN : WIDTH_IN + 32, lane]
            taps_out[b] = mixed[WIDTH_IN : WIDTH_IN + 32, lane]
            value = dot(images[at, :], mixed[:WIDTH_IN, lane].astype(bf16))
            pre[j, at, :] = value
            pre_out[at, :] = value
            masked = mask[at, :] * value
            one = one + rsum(masked)
            two = two + rsum(masked * value)

        @pl.when(j < cut)
        def _():
            early[pl.ds(j, 1), :] = one
            early[pl.ds(chunks + j, 1), :] = two

        @pl.when(j >= cut)
        def _():
            late[pl.ds(j, 1), :] = one
            late[pl.ds(chunks + j, 1), :] = two

    @pl.when((step >= chunks) & (step < 2 * chunks))
    def _():
        j = step - chunks
        mean, rstd = norm_rows(stats_all, j, chunks, stats_all[2 * chunks : 2 * chunks + 1, :])
        scale = rstd * side[2 * SQUEEZE : 2 * SQUEEZE + 1, :]
        bias = side[2 * SQUEEZE + 1 : 2 * SQUEEZE + 2, :]
        held[...] = jnp.zeros_like(held)

        @pl.loop(0, nb)
        def _(b):
            at = image(b)
            normed = (pre[j, at, :] - mean) * scale + bias
            act = normed * sig(normed) * mask[at, :]
            for s in range(KERNEL):
                buf[s] = shifted(act, s - KERNEL // 2)
            taps_now = [jnp.broadcast_to(taps[j, b, t : t + 1, :], (MAP_SIDE, LANES)) for t in range(TAPS)]
            acc = [None] * MAP_SIDE
            for y in range(MAP_SIDE):
                for s in range(KERNEL):
                    x = buf[s, y * MAP_SIDE : (y + 1) * MAP_SIDE, :]
                    for r in range(KERNEL):
                        i = y - r + KERNEL // 2
                        if 0 <= i < MAP_SIDE:
                            term = taps_now[r * KERNEL + s] * x
                            acc[i] = term if acc[i] is None else acc[i] + term
                done = [y - 2] if y < MAP_SIDE - 1 else [y - 2, y - 1, y]
                for i in done:
                    if i >= 0:
                        out[pl.ds(pl.multiple_of(b * PIXELS + i * MAP_SIDE, MAP_SIDE), MAP_SIDE), :] = acc[i]
            value = out[at, :]
            dpre[j, at, :] = value
            masked = mask[at, :] * value
            held[0:1, :] += rsum(masked)
            held[1:2, :] += rsum(masked * value)

        store_sums(early_two, late_two, cut_two, chunks, j, held[0:1, :], held[1:2, :])

    total = stats_all[2 * chunks : 2 * chunks + 1, :]

    @pl.when((step >= 2 * chunks) & (step < 3 * chunks))
    def _():
        j = step - 2 * chunks
        lane = pl.ds(pl.multiple_of(j * LANES, LANES), LANES)
        load(j).wait()

        @pl.when(j + 1 < chunks)
        def _():
            load(j + 1).start()

        both = mix_kernels(kern_buf[lax.rem(j, 2)], mix[...])
        for b in range(nb):
            mixed[b, :, lane] = both[:, b * LANES : (b + 1) * LANES].astype(bf16)
        mean, rstd = norm_rows(sums_all, j, chunks, total)
        scale = rstd * side[2 * SQUEEZE + 2 : 2 * SQUEEZE + 3, :]
        bias = side[2 * SQUEEZE + 3 : 2 * SQUEEZE + 4, :]
        for b in range(nb):
            at = slice(b * PIXELS, (b + 1) * PIXELS)
            normed = (dpre[j, at, :] - mean) * scale + bias
            value = normed * sig(normed) * mask[at, :]
            dpre[j, at, :] = value
            pool_out[b : b + 1, lane] = rsum(value) / jnp.maximum(counts[b : b + 1, :], 1.0)
        squeezed[...] += dot(pool_out[:, lane], side[0:SQUEEZE, :], NT, highest)

    @pl.when(step >= 3 * chunks)
    def _():
        j = step - 3 * chunks
        lane = pl.ds(pl.multiple_of(j * LANES, LANES), LANES)
        before = squeezed[...] + sq_bias[...]
        gate = sig(
            dot(before * sig(before), side[SQUEEZE : 2 * SQUEEZE, :], NN, highest)
            + side[2 * SQUEEZE + 4 : 2 * SQUEEZE + 5, :]
        )
        gate_out[:, lane] = gate
        for b in range(nb):
            at = slice(b * PIXELS, (b + 1) * PIXELS)
            value = (dpre[j, at, :] * gate[b : b + 1, :]).astype(bf16)
            excited[at, :] = value
            exc[at, lane] = value

    @pl.when(step == 4 * chunks - 1)
    def _():
        one = jnp.zeros((1, WIDTH_OUT), f32)
        two = jnp.zeros((1, WIDTH_OUT), f32)
        for b in range(nb):
            at = slice(b * PIXELS, (b + 1) * PIXELS)
            value = dot(exc[at, :], mixed[b], NT)
            proj[at, :] = value
            masked = mask[at, 0:1] * value
            one = one + rsum(masked)
            two = two + rsum(masked * value)
        store_wide(sums_three, 0, one)
        store_wide(sums_three, OUT_CHUNKS, two)
        sum_finish(nd, nz, sums_three, last_all, *comm_two)
        for k in range(nz - 1):
            arrived(twins_h(k))
            sent(planes_b(k) + twins_b(k) + twins_h(k))
        arrived(far_c())
        sent(far_h() + planes_h() + far_c())
        for copy in own():
            copy.wait()


def first_stage(kern, images, mask, mask_rows, counts, route, side, sq_bias, full_b, kh, kc, nb, width, nd, nz, ident):
    chunks = width // LANES
    rows = nb * PIXELS
    deep = LANES * EXPERTS
    planes = (nz - 1) * (nd // 2 - 1)
    shapes = (shard_shape(full_b, nz), kh.shape, kc.shape)
    hbm = pl.BlockSpec(memory_space=pltpu.HBM)
    before = lambda t: jnp.minimum(t, chunks - 1)
    after = lambda t: jnp.clip(t - chunks, 0, chunks - 1)
    cycled = lambda t: lax.rem(t, chunks)
    return pl.pallas_call(
        functools.partial(stage_kernel, nd, nz, nb, chunks, shapes),
        grid=(4 * chunks,),
        out_shape=[
            jax.ShapeDtypeStruct((rows, width), f32),
            jax.ShapeDtypeStruct((nb, 32, width), f32),
            jax.ShapeDtypeStruct((rows, width), f32),
            jax.ShapeDtypeStruct((24, LANES), f32),
            jax.ShapeDtypeStruct((24, LANES), f32),
            jax.ShapeDtypeStruct((deep, 2 * nb * LANES), bf16),
            jax.ShapeDtypeStruct((8, EXPERTS), f32),
            jax.ShapeDtypeStruct((8, WIDTH_IN), f32),
            jax.ShapeDtypeStruct((rows, width), bf16),
            jax.ShapeDtypeStruct((rows, WIDTH_OUT), f32),
            jax.ShapeDtypeStruct((8, width), f32),
            jax.ShapeDtypeStruct((8, width), f32),
            jax.ShapeDtypeStruct((8, SQUEEZE), f32),
            jax.ShapeDtypeStruct((8, LANES), f32),
            jax.ShapeDtypeStruct((nb, WIDTH_OUT, width), bf16),
            jax.ShapeDtypeStruct(full_b.shape, bf16),
            jax.ShapeDtypeStruct((kh.shape[0], nz * kh.shape[1]), bf16),
            jax.ShapeDtypeStruct((nz,) + kc.shape, bf16),
        ],
        in_specs=[
            pl.BlockSpec((kern.shape[0], deep), lambda t: (0, before(t))),
            whole(images.shape),
            whole(mask.shape),
            whole(mask_rows.shape),
            whole(counts.shape),
            whole(route.shape),
            pl.BlockSpec((side.shape[0], LANES), lambda t: (0, cycled(t))),
            whole(sq_bias.shape),
            hbm,
            whole(kh.shape),
            whole(kc.shape),
        ],
        out_specs=[
            pl.BlockSpec((rows, LANES), lambda t: (0, before(t))),
            pl.BlockSpec((nb, 32, LANES), lambda t: (0, 0, before(t))),
            pl.BlockSpec((rows, LANES), lambda t: (0, after(t))),
            whole((24, LANES)),
            whole((24, LANES)),
            whole((deep, 2 * nb * LANES)),
            whole((8, EXPERTS)),
            whole((8, WIDTH_IN)),
            pl.BlockSpec((rows, LANES), lambda t: (0, jnp.maximum(t - 3 * chunks, 0))),
            whole((rows, WIDTH_OUT)),
            whole((8, width)),
            whole((8, width)),
            whole((8, SQUEEZE)),
            whole((8, LANES)),
            whole((nb, WIDTH_OUT, width)),
            hbm,
            hbm,
            hbm,
        ],
        scratch_shapes=[
            VMEM((chunks, rows, LANES), f32),
            VMEM((chunks, nb, 32, LANES), f32),
            VMEM((KERNEL, PIXELS, LANES), f32),
            VMEM((8, LANES), f32),
            VMEM((24, LANES), f32),
            VMEM((24, LANES), f32),
            VMEM((24, LANES), f32),
            VMEM((24, LANES), f32),
            VMEM((8, LANES), f32),
            VMEM((chunks, rows, LANES), f32),
            VMEM((rows, width), bf16),
            VMEM((2, WIDTH_OUT, deep), bf16),
        ]
        + sum_scratch(24, nd, nz)[1:] * 2
        + sum_scratch(8, nd, nz)[1:]
        + sum_scratch(24, nd, nz)[1:] * 2
        + pair(nz - 1) * 2
        + pair(planes) * 2
        + pair(nz - 1)
        + [pltpu.SemaphoreType.DMA((2,))]
        + pair(nz - 1)
        + [pltpu.SemaphoreType.DMA((2,))],
        input_output_aliases={8: 15},
        compiler_params=params(ident),
        name="first_stage",
    )(kern, images, mask, mask_rows, counts, route, side, sq_bias, full_b, kh, kc)


def store_wide(ref, row, value):
    width = value.shape[1]
    for k in range(-(-width // LANES)):
        lanes = min(LANES, width - k * LANES)
        ref[row + k : row + k + 1, :lanes] = value[:, k * LANES : k * LANES + lanes]


def load_wide(ref, row, width):
    parts = []
    for k in range(-(-width // LANES)):
        lanes = min(LANES, width - k * LANES)
        parts.append(ref[row + k : row + k + 1, :lanes])
    return jnp.concatenate(parts, axis=1)


OUT_CHUNKS = -(-WIDTH_OUT // LANES)


def out_norm(sums, total):
    mean = load_wide(sums, 0, WIDTH_OUT) / total
    var = load_wide(sums, OUT_CHUNKS, WIDTH_OUT) / total - mean * mean
    return mean, lax.rsqrt(var + eps_norm)


def store_sums(early, late, cut, chunks, j, one, two):
    @pl.when(j < cut)
    def _():
        early[pl.ds(j, 1), :] = one
        early[pl.ds(chunks + j, 1), :] = two

    @pl.when(j >= cut)
    def _():
        late[pl.ds(j, 1), :] = one
        late[pl.ds(chunks + j, 1), :] = two


def split_sum(nd, nz, steps, at, early, late, out, comm_early, comm_late):
    def early_third():
        out[...] = sum_third(nd, nz, early, *comm_early)

    def late_third():
        out[...] += sum_third(nd, nz, late, *comm_late)

    steps.at(at[0], lambda: sum_first(nd, nz, early, *comm_early))
    steps.at(at[1], lambda: sum_second(nd, nz, early, *comm_early))
    steps.at(at[2], early_third)
    steps.at(at[3], lambda: sum_first(nd, nz, late, *comm_late))
    steps.at(at[4], lambda: sum_second(nd, nz, late, *comm_late))
    steps.at(at[5], late_third)


def head_back_kernel(
    nd,
    nz,
    nb,
    chunks,
    shape,
    shape_c,
    mask,
    mask_rows,
    counts,
    labels,
    bias,
    gain,
    totals,
    gain_out,
    kern,
    route,
    proj,
    proj_stats,
    in_c,
    head_pool,
    stats,
    features,
    grad_logits,
    sums_four,
    grad_out,
    sums_all,
    dz_out,
    half,
    part,
    full_c,
    pre_all,
    low,
    low_t,
    mixed,
    mix,
    gates,
    cls,
    early_head,
    late_head,
    logits,
    grad_features,
    held,
    grads,
    gate_acc,
    early,
    late,
    sums,
    *comm,
):
    step = pl.program_id(0)
    phase = step // chunks
    j = lax.rem(step, chunks)
    net = Net(nd, nz)
    comm_early, comm_late, comm_two, comm = comm[0:6], comm[6:12], comm[12:18], comm[18:]
    head_early, head_late, sems, comm = comm[0:6], comm[6:12], comm[12:17], comm[17:]
    twin = Twin(net, shape, half, *comm[0:4])
    plane = Plane(net, shape, half, part, 0, nz // 2, *comm[4:7])
    made = comm[0]
    cut = chunks // 3
    head_cut = 2 * chunks // 3
    base = 3 * chunks
    steps = Steps()

    def planes():
        return every(gather_plane, net, shape_c, full_c, sems[0:2])

    def twins():
        return every(gather_twin, net, shape_c, full_c, sems[2:4])

    def load():
        own_rows = cls.shape[0] // nz
        return [
            pltpu.make_async_copy(
                full_c.at[k, pl.ds(0, own_rows)], cls.at[pl.ds(k * own_rows, own_rows)], sems[4].at[k]
            )
            for k in range(nz)
        ]

    def begin():
        met(nd, nz)
        start(planes())

    def cross():
        arrived(planes())
        start(twins())

    def fetch():
        arrived(twins())
        start(load())

    def loaded():
        for copy in load():
            copy.wait()

    steps.at(1, begin)
    steps.at(head_cut - 1, cross)
    steps.at(chunks - 1, fetch)
    steps.at(chunks, loaded)
    places = (head_cut, head_cut + 2, chunks, chunks, chunks + 2, chunks + head_cut)
    split_sum(nd, nz, steps, places, early_head, late_head, stats, head_early, head_late)
    places = (2 * chunks + cut, 2 * chunks + cut + 3, base, base, base + 1, base + cut)
    split_sum(nd, nz, steps, places, early, late, sums_four, comm_early, comm_late)
    for k in range(nz):
        first = base + ready(shape, k)
        steps.at(first, functools.partial(twin.begin, k))
        steps.at(first + 2, functools.partial(twin.add, k))
        if k < nz // 2:
            steps.at(first + 2, functools.partial(plane.begin, k))

    @pl.when(step == 0)
    def _():
        sum_start(nd, nz)
        for ref in (sums, early, late, early_head, late_head, features, logits, gate_acc):
            ref[...] = jnp.zeros_like(ref)
        mean, rstd = out_norm(proj_stats, totals[TOTAL_ROW : TOTAL_ROW + 1, 0:1])
        scale = rstd * gain_out[0:1, :]
        for b in range(nb):
            at = slice(b * PIXELS, (b + 1) * PIXELS)
            low[at, :] = (((proj[at, :] - mean) * scale + gain_out[1:2, :]) * mask[at, 0:1]).astype(bf16)
            low_t[b] = jnp.transpose(low[at, :])
        pool = dot(mask_rows[...], low[...]) / jnp.maximum(counts[:, 0:1], 1.0)
        head_pool[...] = pool
        gate = sig(dot(pool, route[...], NN, highest))
        gates[...] = gate
        build_mix(gate, nb, mix)
        if shape[0] > WIDTH_OUT:
            made[WIDTH_OUT:, :] = jnp.zeros((shape[0] - WIDTH_OUT, made.shape[1]), bf16)

    steps.emit(step, 4 * chunks)
    pre = pre_all.at[j]

    @pl.when(phase == 0)
    def _():
        lane = pl.ds(pl.multiple_of(j * LANES, LANES), LANES)
        both = mix_kernels(kern[...], mix[...])
        one = jnp.zeros((1, LANES), f32)
        two = jnp.zeros((1, LANES), f32)
        for b in range(nb):
            at = slice(b * PIXELS, (b + 1) * PIXELS)
            weight = both[:, b * LANES : (b + 1) * LANES].astype(bf16)
            mixed[b, :, lane] = weight
            value = dot(low[at, :], weight)
            pre[at, :] = value
            masked = mask[at, :] * value
            one = one + rsum(masked)
            two = two + rsum(masked * value)
        store_sums(early_head, late_head, head_cut, chunks, j, one, two)

    lane = pl.ds(pl.multiple_of(j * LANES, LANES), LANES)
    total = totals[TOTAL_ROW : TOTAL_ROW + 1, :]
    mean, rstd = norm_rows(stats, j, chunks, total)
    scale = rstd * gain[0:1, :]

    @pl.when(phase == 1)
    def _():
        for b in range(nb):
            at = slice(b * PIXELS, (b + 1) * PIXELS)
            normed = (pre[at, :] - mean) * scale + gain[1:2, :]
            features[b : b + 1, lane] = rsum(normed * sig(normed) * mask[at, :]) / jnp.maximum(
                counts[b : b + 1, :], 1.0
            )
        both = dot(split(features[:, lane]), cls[lane, :])
        logits[...] += both[:8] + both[8:]

    @pl.when((phase == 2) & (j == 0))
    def _():
        col = lax.broadcasted_iota(jnp.int32, (8, CLASS_PAD), 1)
        inside = col < CLASSES
        scores = jnp.where(inside, logits[...] + bias[...], -1e30)
        top = jnp.max(scores, axis=1, keepdims=True)
        spread = jnp.where(inside, jnp.exp(scores - top), 0.0)
        mass = jnp.sum(spread, axis=1, keepdims=True)
        hot = jnp.where(col == labels[:, 0:1], 1.0, 0.0)
        shifted_scores = jnp.where(inside, scores - top - jnp.log(mass), 0.0)
        per_image = -(
            0.9 * jnp.sum(shifted_scores * hot, axis=1, keepdims=True)
            + (0.1 / CLASSES) * jnp.sum(shifted_scores, axis=1, keepdims=True)
        )
        valid = jnp.where(counts[:, 0:1] > 0.0, 1.0, 0.0)
        early[2 * chunks : 2 * chunks + 1, :] = jnp.broadcast_to(rsum(per_image * valid), (1, LANES))
        weight = valid / totals[TOTAL_ROW + 1 : TOTAL_ROW + 2, 0:1]
        grad_logits[...] = weight * jnp.where(inside, spread / mass - 0.9 * hot - 0.1 / CLASSES, 0.0)

    @pl.when(phase == 2)
    def _():
        both = dot(split(grad_logits[...]), cls[lane, :], NT)
        grads = (both[:8] + both[8:]) / jnp.maximum(counts[...], 1.0)
        grad_features[:, lane] = grads
        one = jnp.zeros((1, LANES), f32)
        two = jnp.zeros((1, LANES), f32)
        for b in range(nb):
            at = slice(b * PIXELS, (b + 1) * PIXELS)
            hat = (pre[at, :] - mean) * rstd
            grad = mask[at, :] * dsilu(hat * gain[0:1, :] + gain[1:2, :]) * grads[b : b + 1, :]
            one = one + rsum(grad)
            two = two + rsum(grad * hat)
        store_sums(early, late, cut, chunks, j, one, two)

    @pl.when(phase == 3)
    def _():
        one = sums_four[pl.ds(j, 1), :] / total
        two = sums_four[pl.ds(chunks + j, 1), :] / total
        for b in range(nb):
            at = slice(b * PIXELS, (b + 1) * PIXELS)
            hat = (pre[at, :] - mean) * rstd
            grad = dsilu(hat * gain[0:1, :] + gain[1:2, :]) * grad_features[b : b + 1, lane]
            value = (scale * mask[at, :] * (grad - one - hat * two)).astype(bf16)
            held[at, lane] = value
            grads[:, b * LANES : (b + 1) * LANES] = dot(low_t[b], value).astype(bf16)
        gate_acc[0:nb, :] += gate_rows(grads[...], kern[...], nb)
        made[:WIDTH_OUT, lanes(j * LANES * EXPERTS, LANES * EXPERTS)] = dot(grads[...], mix[:, : nb * LANES], NT).astype(bf16)

    @pl.when(step == 4 * chunks - 1)
    def _():
        dz = gate_sums(gate_acc[...]) * gates[...] * (1.0 - gates[...])
        dz_out[...] = dz
        pool_grad = dot(dz, route[...], NT, highest) / jnp.maximum(counts[:, 0:1], 1.0)
        mean, rstd = out_norm(proj_stats, total[:, 0:1])
        one = jnp.zeros((1, WIDTH_OUT), f32)
        two = jnp.zeros((1, WIDTH_OUT), f32)
        for b in range(nb):
            at = slice(b * PIXELS, (b + 1) * PIXELS)
            value = (dot(held[at, :], mixed[b], NT) + pool_grad[b : b + 1, :]) * mask[at, 0:1]
            grad_out[at, :] = value
            one = one + rsum(value)
            two = two + rsum(value * ((proj[at, :] - mean) * rstd))
        store_wide(sums, 0, one)
        store_wide(sums, OUT_CHUNKS, two)
        last = [k for k in range(nz) if ready(shape, k) >= chunks]
        sum_first(nd, nz, sums, *comm_two)
        for k in last:
            twin.begin(k)
        sum_second(nd, nz, sums, *comm_two)
        sums_all[...] = sum_third(nd, nz, sums, *comm_two)
        for k in range(nz):
            if ready(shape, k) + 2 >= chunks:
                twin.add(k)
                if k < nz // 2:
                    plane.begin(k)
        plane.add()
        twin.finish()
        plane.finish()
        sent(planes() + twins())


def head_stage(mask, mask_rows, counts, labels, bias, gain, totals, gain_out, kern, route, proj, proj_stats, full_c, nb, nd, nz, ident):
    rows = proj.shape[0]
    width = kern.shape[1] // EXPERTS
    chunks = width // LANES
    deep = LANES * EXPERTS
    shape = (kern.shape[0], kern.shape[1] // nz)
    hbm = pl.BlockSpec(memory_space=pltpu.HBM)
    kept = lambda t: (0, jnp.where(t < chunks, t, jnp.maximum(t - 3 * chunks, 0)))
    return pl.pallas_call(
        functools.partial(head_back_kernel, nd, nz, nb, chunks, shape, shard_shape(full_c, nz)),
        grid=(4 * chunks,),
        out_shape=[
            jax.ShapeDtypeStruct((8, WIDTH_OUT), f32),
            jax.ShapeDtypeStruct((24, LANES), f32),
            jax.ShapeDtypeStruct((8, width), f32),
            jax.ShapeDtypeStruct((8, CLASS_PAD), f32),
            jax.ShapeDtypeStruct((24, LANES), f32),
            jax.ShapeDtypeStruct((rows, WIDTH_OUT), f32),
            jax.ShapeDtypeStruct((8, LANES), f32),
            jax.ShapeDtypeStruct((8, EXPERTS), f32),
            jax.ShapeDtypeStruct(half_shape(shape, nd, nz), bf16),
            jax.ShapeDtypeStruct(part_shape(shape, nd, nz // 2), bf16),
            jax.ShapeDtypeStruct(full_c.shape, bf16),
        ],
        in_specs=[
            whole(mask.shape),
            whole(mask_rows.shape),
            whole(counts.shape),
            whole(labels.shape),
            whole(bias.shape),
            pl.BlockSpec((8, LANES), lambda t: (0, lax.rem(t, chunks))),
            whole(totals.shape),
            whole(gain_out.shape),
            pl.BlockSpec((WIDTH_OUT, deep), kept),
            whole(route.shape),
            whole(proj.shape),
            whole(proj_stats.shape),
            hbm,
        ],
        out_specs=[
            whole((8, WIDTH_OUT)),
            whole((24, LANES)),
            whole((8, width)),
            whole((8, CLASS_PAD)),
            whole((24, LANES)),
            whole((rows, WIDTH_OUT)),
            whole((8, LANES)),
            whole((8, EXPERTS)),
            whole(half_shape(shape, nd, nz)),
            whole(part_shape(shape, nd, nz // 2)),
            hbm,
        ],
        scratch_shapes=[
            VMEM((chunks, rows, LANES), f32),
            VMEM((rows, WIDTH_OUT), bf16),
            VMEM((nb, WIDTH_OUT, PIXELS), bf16),
            VMEM((nb, WIDTH_OUT, width), bf16),
            VMEM((deep, 2 * nb * LANES), bf16),
            VMEM((8, EXPERTS), f32),
            VMEM((width, CLASS_PAD), bf16),
            VMEM((24, LANES), f32),
            VMEM((24, LANES), f32),
            VMEM((8, CLASS_PAD), f32),
            VMEM((8, width), f32),
            VMEM((rows, width), bf16),
            VMEM((WIDTH_OUT, nb * LANES), bf16),
            VMEM((8, deep), f32),
            VMEM((24, LANES), f32),
            VMEM((24, LANES), f32),
            VMEM((8, LANES), f32),
        ]
        + sum_scratch(24, nd, nz)[1:] * 2
        + sum_scratch(8, nd, nz)[1:]
        + sum_scratch(24, nd, nz)[1:] * 2
        + pair((nz - 1) * (nd // 2 - 1))
        + pair(nz - 1)
        + [pltpu.SemaphoreType.DMA((nz,))]
        + twin_scratch(shape, nd, nz)
        + plane_scratch(shape, nd, nz // 2),
        input_output_aliases={12: 10},
        compiler_params=params(ident),
        name="head_stage",
    )(mask, mask_rows, counts, labels, bias, gain, totals, gain_out, kern, route, proj, proj_stats, full_c)


def project_back_kernel(nd, nz, nb, chunks, shape_h, shape, half_h, part_h, grad_in, proj, proj_stats, proj_sums, gain, mask, counts, totals, stats, side, dpre, excited, mixed, kern, mix, gate, pooled, squeezed, sq_bias, grad_norm, sums_all, grad_squeeze, gate_grad, dz_gate, piece_h, half, part, low, low_t, held, grads, gate_acc, sums_h, sums, *comm):
    phase = pl.program_id(0)
    net = Net(nd, nz)
    few = nz // 2
    cut_one = 12
    plane_h = Plane(net, shape_h, half_h, sums_h, few, nz - few, *comm[6:9])
    far = Far(net, shape_h, sums_h, piece_h, *comm[9:cut_one])
    twin = Twin(net, shape, half, *comm[cut_one : cut_one + 4])
    plane = Plane(net, shape, half, part, 0, few, *comm[cut_one + 4 : cut_one + 7])
    made = comm[cut_one]
    comm = comm[:6]
    steps = Steps()

    def begin():
        met(nd, nz)
        for k in plane_h.shards:
            plane_h.begin(k)
        sums_h[0:few] = part_h[...]
        for k in range(few):
            far.send(k)

    steps.at(1, begin)
    steps.at(chunks + 3, functools.partial(plane_h.add, far.send))
    for k in range(nz):
        first = ready(shape, k)
        steps.at(first, functools.partial(twin.begin, k))
        steps.at(first + 3, functools.partial(twin.add, k))
        if k < few:
            steps.at(first + 3, functools.partial(plane.begin, k))
    j = pl.program_id(1)

    @pl.when((phase == 0) & (j == 0))
    def _():
        sum_start(nd, nz)

    steps.emit(phase * chunks + j, 2 * chunks)
    lane = pl.ds(pl.multiple_of(j * LANES, LANES), LANES)
    total = totals[TOTAL_ROW : TOTAL_ROW + 1, :]

    @pl.when((phase == 0) & (j == 0))
    def _():
        gate_acc[...] = jnp.zeros_like(gate_acc)
        if shape[0] > WIDTH_OUT:
            made[WIDTH_OUT:, :] = jnp.zeros((shape[0] - WIDTH_OUT, made.shape[1]), bf16)
        sums[...] = jnp.zeros_like(sums)
        grad_squeeze[...] = jnp.zeros_like(grad_squeeze)
        dz_gate[...] = jnp.zeros_like(dz_gate)
        mean, rstd = out_norm(proj_stats, total[:, 0:1])
        scale = rstd * gain[0:1, :]
        one = load_wide(proj_sums, 0, WIDTH_OUT) / total[:, 0:1]
        two = load_wide(proj_sums, OUT_CHUNKS, WIDTH_OUT) / total[:, 0:1]
        for b in range(nb):
            at = slice(b * PIXELS, (b + 1) * PIXELS)
            hat = (proj[at, :] - mean) * rstd
            low[at, :] = (scale * (grad_in[at, :] - mask[at, 0:1] * (one + hat * two))).astype(bf16)
            low_t[b] = jnp.transpose(low[at, :])

    mean, rstd = norm_rows(stats, j, chunks, total)
    gain_now = side[2 * SQUEEZE + 2 : 2 * SQUEEZE + 3, :]
    bias_now = side[2 * SQUEEZE + 3 : 2 * SQUEEZE + 4, :]

    @pl.when(phase == 0)
    def _():
        for b in range(nb):
            at = slice(b * PIXELS, (b + 1) * PIXELS)
            grads[:, b * LANES : (b + 1) * LANES] = dot(low_t[b], excited[at, :]).astype(bf16)
            value = dot(low[at, :], mixed[b])
            held[j, at, :] = value
            normed = (dpre[at, :] - mean) * (rstd * gain_now) + bias_now
            act = normed * sig(normed) * mask[at, :]
            now = gate[b : b + 1, :]
            dz_gate[b : b + 1, lane] = rsum(value * act) * now * (1.0 - now)
        gate_acc[0:nb, :] += gate_rows(grads[...], kern[...], nb)
        made[:WIDTH_OUT, lanes(j * LANES * EXPERTS, LANES * EXPERTS)] = dot(grads[...], mix[:, : nb * LANES], NT).astype(bf16)
        grad_squeeze[...] += dot(dz_gate[:, lane], side[SQUEEZE : 2 * SQUEEZE, :], NT, highest)

    @pl.when((phase == 1) & (j == 0))
    def _():
        grad_squeeze[...] = grad_squeeze[...] * dsilu(squeezed[...] + sq_bias[...])
        gate_grad[...] = gate_sums(gate_acc[...])

    @pl.when(phase == 1)
    def _():
        pool_grad = dot(grad_squeeze[...], side[0:SQUEEZE, :], NN, highest) / jnp.maximum(counts[...], 1.0)
        one = jnp.zeros((1, LANES), f32)
        two = jnp.zeros((1, LANES), f32)
        for b in range(nb):
            at = slice(b * PIXELS, (b + 1) * PIXELS)
            hat = (dpre[at, :] - mean) * rstd
            grad = held[j, at, :] * gate[b : b + 1, :] + pool_grad[b : b + 1, :]
            value = mask[at, :] * grad * dsilu(hat * gain_now + bias_now)
            grad_norm[at, :] = value
            one = one + rsum(value)
            two = two + rsum(value * hat)
        sums[pl.ds(j, 1), :] = one
        sums[pl.ds(chunks + j, 1), :] = two

    @pl.when((phase == 1) & (j == chunks - 1))
    def _():
        sum_finish(nd, nz, sums, sums_all, *comm)
        far.add()
        plane.add()
        far.finish()
        twin.finish()
        plane.finish()
        plane_h.finish()


def project_back(half_h, part_h, shape_h, grad_in, proj, proj_stats, proj_sums, gain, mask, counts, totals, stats, side, dpre, excited, mixed, kern, mix, gate, pooled, squeezed, sq_bias, nb, nd, nz, ident):
    rows, width = dpre.shape
    shape = (kern.shape[0], kern.shape[1] // nz)
    few = nz // 2
    chunks = width // LANES
    deep = LANES * EXPERTS
    wide = lambda p, j: (0, j)
    early = lambda p, j: (0, jnp.where(p == 0, j, chunks - 1))
    late = lambda p, j: (0, jnp.where(p == 0, 0, j))
    return pl.pallas_call(
        functools.partial(project_back_kernel, nd, nz, nb, chunks, shape_h, shape),
        grid=(2, chunks),
        out_shape=[
            jax.ShapeDtypeStruct((rows, width), f32),
            jax.ShapeDtypeStruct((24, LANES), f32),
            jax.ShapeDtypeStruct((8, SQUEEZE), f32),
            jax.ShapeDtypeStruct((8, EXPERTS), f32),
            jax.ShapeDtypeStruct((8, width), f32),
            jax.ShapeDtypeStruct(piece_shape(shape_h, nd), bf16),
            jax.ShapeDtypeStruct(half_shape(shape, nd, nz), bf16),
            jax.ShapeDtypeStruct(part_shape(shape, nd, few), bf16),
        ],
        in_specs=[
            whole(half_h.shape),
            whole(part_h.shape),
            whole(grad_in.shape),
            whole(proj.shape),
            whole(proj_stats.shape),
            whole(proj_sums.shape),
            whole(gain.shape),
            whole(mask.shape),
            whole(counts.shape),
            whole(totals.shape),
            whole(stats.shape),
            pl.BlockSpec((side.shape[0], LANES), wide),
            pl.BlockSpec((rows, LANES), wide),
            pl.BlockSpec((rows, LANES), early),
            pl.BlockSpec((nb, WIDTH_OUT, LANES), lambda p, j: (0, 0, jnp.where(p == 0, j, chunks - 1))),
            pl.BlockSpec((WIDTH_OUT, deep), early),
            whole(mix.shape),
            pl.BlockSpec((8, LANES), wide),
            pl.BlockSpec((8, LANES), wide),
            whole(squeezed.shape),
            whole(sq_bias.shape),
        ],
        out_specs=[
            pl.BlockSpec((rows, LANES), late),
            whole((24, LANES)),
            whole((8, SQUEEZE)),
            whole((8, EXPERTS)),
            whole((8, width)),
            whole(piece_shape(shape_h, nd)),
            whole(half_shape(shape, nd, nz)),
            whole(part_shape(shape, nd, few)),
        ],
        scratch_shapes=[
            VMEM((rows, WIDTH_OUT), bf16),
            VMEM((nb, WIDTH_OUT, PIXELS), bf16),
            VMEM((chunks, rows, LANES), f32),
            VMEM((WIDTH_OUT, nb * LANES), bf16),
            VMEM((8, deep), f32),
            VMEM(part_shape(shape_h, nd, nz), bf16),
        ]
        + sum_scratch(24, nd, nz)
        + plane_scratch(shape_h, nd, nz - few)
        + far_scratch(shape_h, nd, nz)
        + twin_scratch(shape, nd, nz)
        + plane_scratch(shape, nd, few),
        compiler_params=params(ident),
        name="project_back",
    )(half_h, part_h, grad_in, proj, proj_stats, proj_sums, gain, mask, counts, totals, stats, side, dpre, excited, mixed, kern, mix, gate, pooled, squeezed, sq_bias)


def dz_slots(nb, devices):
    per = max(1, min(devices, LANES // (nb * EXPERTS)))
    return per, -(-devices // (per * 8)) * 8


def stage_back_kernel(
    nd,
    nz,
    nb,
    chunks,
    shape,
    shape_b,
    shape_h,
    cuts_one,
    cuts_two,
    half_b,
    part_b,
    piece_h,
    grad_in,
    dpre,
    pre,
    taps,
    mask,
    side,
    stats_one,
    stats_two,
    sums_two,
    totals,
    features,
    logits,
    pooled,
    dz_gate,
    head_pool,
    pooled_in,
    grad_sq,
    before,
    sq_bias_in,
    dz_head,
    images,
    kern,
    mix,
    gates,
    gate_grad,
    squares_w,
    stats_three,
    stats_four,
    sums_four,
    chan_old,
    head_old,
    proj_old,
    done,
    done_b,
    done_h,
    grad_cls,
    grad_side_out,
    factors,
    route_in,
    route_head,
    sq_bias,
    class_bias,
    chan_new,
    head_new,
    proj_new,
    loss,
    made_norm,
    tap_grads,
    buf,
    acts,
    held,
    early,
    late,
    sums_one,
    sums_b,
    piece_b,
    rows_all,
    images_t,
    grads,
    gate_acc,
    grad_side,
    every_sum,
    low,
    half,
    sums,
    piece,
    *comm,
):
    step = pl.program_id(0)
    net = Net(nd, nz)
    few = nz // 2
    cut = 2 * chunks // 3
    comm_early, comm_late, comm_two, comm = comm[0:6], comm[6:12], comm[12:18], comm[18:]
    plane_b = Plane(net, shape_b, half_b, sums_b, few, nz - few, *comm[0:3], shift=few)
    far_b = Far(net, shape_b, sums_b, piece_b, *comm[3:6])
    up_b = Spread(net, shape_b, piece_b, done_b, *comm[6:11])
    up_h = Spread(net, shape_h, piece_h, done_h, *comm[11:16])
    share = Share(net, rows_all, *comm[16:24])
    comm = comm[24:]
    twin = Twin(net, shape, half, *comm[0:4])
    made = comm[0]
    plane = Plane(net, shape, half, sums, 0, nz, *comm[4:7])
    far = Far(net, shape, sums, piece, *comm[7:10])
    up = Spread(net, shape, piece, done, *comm[10:15])
    steps = Steps()
    first_planes = range(few, few + (nz - few + 1) // 2)
    last_planes = range(first_planes.stop, nz)

    def begin():
        met(nd, nz)
        up_h.begin()
        for k in first_planes:
            plane_b.begin(k)
        sums_b[0:few] = part_b[...]
        for k in range(few):
            far_b.send(k)
        share.far()

    def more_planes():
        for k in last_planes:
            plane_b.begin(k)

    def far_end():
        far_b.add()
        up_b.begin()

    steps.at(1, begin)
    steps.at(4, up_h.cross)
    split_sum(
        nd,
        nz,
        steps,
        (cut, cut + 2, chunks, chunks, chunks + 2, chunks + cut - 1),
        early,
        late,
        sums_one,
        comm_early,
        comm_late,
    )
    steps.at(cut + 1, more_planes)
    steps.at(cut + 2, share.plane)
    steps.at(chunks + 1, functools.partial(plane_b.add, far_b.send))
    steps.at(chunks + 2, share.twin)
    steps.at(chunks + 3, far_end)
    for k in range(nz):
        first = chunks + ready(shape, k)
        steps.at(first, functools.partial(twin.begin, k))
        steps.at(first + 1, functools.partial(twin.add, k))
        steps.at(first + 1, functools.partial(plane.begin, k))
        if first + 4 < 2 * chunks:
            steps.at(first + 4, functools.partial(plane.add_one, k, far.send))
    steps.at(2 * chunks - 2, up_b.cross)

    @pl.when(step == 0)
    def _():
        sum_start(nd, nz)
        total_before = before[...] + sq_bias_in[...]
        squeezed = total_before * sig(total_before)
        share.fill(
            nb,
            [features, pooled, dz_gate],
            [grad_sq[...], squeezed, dz_head[...]],
            [logits[...], head_pool[...], pooled_in[...]],
        )
        for b in range(nb):
            images_t[b] = jnp.transpose(images[b * PIXELS : (b + 1) * PIXELS, :])
        for ref in (early, late, gate_acc, grads):
            ref[...] = jnp.zeros_like(ref)

    steps.emit(step, 2 * chunks)
    total = totals[TOTAL_ROW : TOTAL_ROW + 1, :]

    @pl.when(step < chunks)
    def _():
        j = step
        mean_two, rstd_two = norm_rows(stats_two, j, chunks, total)
        scale_two = rstd_two * side[2 * SQUEEZE + 2 : 2 * SQUEEZE + 3, :]
        one_two = sums_two[pl.ds(j, 1), :] / total
        two_two = sums_two[pl.ds(chunks + j, 1), :] / total
        mean, rstd = norm_rows(stats_one, j, chunks, total)
        gain = side[2 * SQUEEZE : 2 * SQUEEZE + 1, :]
        bias = side[2 * SQUEEZE + 1 : 2 * SQUEEZE + 2, :]
        held[...] = jnp.zeros_like(held)
        reach = KERNEL // 2

        @pl.loop(0, nb)
        def _(b):
            at = image(b)
            hat = (dpre[at, :] - mean_two) * rstd_two
            grad = scale_two * (grad_in[at, :] - mask[at, :] * (one_two + hat * two_two))
            for s in range(KERNEL):
                buf[s] = shifted(grad, reach - s)
            hat = (pre[at, :] - mean) * rstd
            normed = hat * gain + bias
            acts[...] = normed * sig(normed) * mask[at, :]
            taps_now = [jnp.broadcast_to(taps[b, t : t + 1, :], (MAP_SIDE, LANES)) for t in range(TAPS)]
            acc = [None] * MAP_SIDE
            for q in range(MAP_SIDE):
                for s in range(KERNEL):
                    x = buf[s, q * MAP_SIDE : (q + 1) * MAP_SIDE, :]
                    for r in range(KERNEL):
                        y = q + r - reach
                        if 0 <= y < MAP_SIDE:
                            term = taps_now[r * KERNEL + s] * x
                            acc[y] = term if acc[y] is None else acc[y] + term
                done = [q - 2] if q < MAP_SIDE - 1 else [q - 2, q - 1, q]
                for i in done:
                    if i >= 0:
                        made_norm[j, pl.ds(pl.multiple_of(b * PIXELS + i * MAP_SIDE, MAP_SIDE), MAP_SIDE), :] = acc[i]
            tap_acc = [None] * TAPS
            for q in range(MAP_SIDE):
                for s in range(KERNEL):
                    x = buf[s, q * MAP_SIDE : (q + 1) * MAP_SIDE, :]
                    for r in range(KERNEL):
                        y = q + r - reach
                        if 0 <= y < MAP_SIDE:
                            both = acts[y * MAP_SIDE : (y + 1) * MAP_SIDE, :] * x
                            term = both[:8] + both[8:]
                            t = r * KERNEL + s
                            tap_acc[t] = term if tap_acc[t] is None else tap_acc[t] + term
            tap_grads[j, b] = jnp.zeros((32, LANES), f32)
            for t in range(TAPS):
                tap_grads[j, b, t : t + 1, :] = rsum(tap_acc[t])
            hat = (pre[at, :] - mean) * rstd
            value = made_norm[j, at, :] * mask[at, :] * dsilu(hat * gain + bias)
            made_norm[j, at, :] = value
            held[0:1, :] += rsum(value)
            held[1:2, :] += rsum(value * hat)

        store_sums(early, late, cut, chunks, j, held[0:1, :], held[1:2, :])

    @pl.when(step >= chunks)
    def _():
        j = step - chunks
        mean, rstd = norm_rows(stats_one, j, chunks, total)
        scale = rstd * side[2 * SQUEEZE : 2 * SQUEEZE + 1, :]
        one = sums_one[pl.ds(j, 1), :] / total
        two = sums_one[pl.ds(chunks + j, 1), :] / total
        for b in range(nb):
            at = slice(b * PIXELS, (b + 1) * PIXELS)
            lane = slice(b * LANES, (b + 1) * LANES)
            hat = (pre[at, :] - mean) * rstd
            value = (scale * (made_norm[j, at, :] - mask[at, :] * (one + hat * two))).astype(bf16)
            grads[0:WIDTH_IN, lane] = dot(images_t[b], value).astype(bf16)
            grads[WIDTH_IN : WIDTH_IN + 32, lane] = tap_grads[j, b].astype(bf16)
        gate_acc[0:nb, :] += gate_rows(grads[...], kern[...], nb)
        made[:, lanes(j * LANES * EXPERTS, LANES * EXPERTS)] = dot(grads[...], mix[:, : nb * LANES], NT).astype(bf16)

    @pl.when(step == 2 * chunks - 1)
    def _():
        dz = (gate_sums(gate_acc[...]) + gate_grad[...]) * gates[...] * (1.0 - gates[...])
        steps.end(2 * chunks)
        z = net.z
        me = net.d * nz + z
        devices = nd * nz
        own = chan_old.shape[1]
        own_head = head_old.shape[1]
        own_proj = proj_old.shape[1]
        width = own * nz
        head_width = own_head * nz
        head_chunks = head_width // LANES
        share.finish()
        count = devices * 8
        per, slots = dz_slots(nb, devices)
        row = lax.broadcasted_iota(jnp.int32, (count, 1), 0)
        keep = jnp.where((row & 7) < nb, 1.0, 0.0)

        def one(k, size):
            return rows_all[:, :, cuts_one[k] : cuts_one[k] + size].reshape(count, size) * keep

        def two(k, size):
            return pltpu.roll(rows_all[:, :, cuts_two[k] : cuts_two[k] + size].reshape(count, size), count - nb, 0)

        features = one(0, own_head)
        logits = two(0, CLASS_PAD)
        pooled = one(1, own)
        dz_gate = one(2, own)
        grad_sq = one(3, SQUEEZE)
        grad_cls[...] = dot(features, logits, TN, highest)
        grad_side[...] = jnp.zeros_like(grad_side)
        grad_side[0:SQUEEZE, :own] = dot(grad_sq, pooled, TN, highest)
        grad_side[SQUEEZE : 2 * SQUEEZE, :own] = dot(one(4, SQUEEZE), dz_gate, TN, highest)

        def channel(ref, at, n, size, own_size):
            return turn(load_wide(ref, at, size), z * own_size)[:, :own_size]

        at = 2 * SQUEEZE
        grad_side[at : at + 1, :own] = channel(sums_one, chunks, chunks, width, own)
        grad_side[at + 1 : at + 2, :own] = channel(sums_one, 0, chunks, width, own)
        grad_side[at + 2 : at + 3, :own] = channel(sums_two, chunks, chunks, width, own)
        grad_side[at + 3 : at + 4, :own] = channel(sums_two, 0, chunks, width, own)
        grad_side[at + 4 : at + 5, :own] = rsum(dz_gate)
        route_head[...] = dot(two(1, WIDTH_OUT), one(5, EXPERTS), TN, highest)
        sq_bias[...] = rsum(grad_sq)
        class_bias[...] = rsum(logits * keep)
        head_gain = channel(sums_four, head_chunks, head_chunks, head_width, own_head)
        head_bias = channel(sums_four, 0, head_chunks, head_width, own_head)
        totals = stats_one[TOTAL_ROW : TOTAL_ROW + 1, 0:1]
        loss[...] = jnp.broadcast_to(
            sums_four[2 * head_chunks : 2 * head_chunks + 1, :] / stats_one[TOTAL_ROW + 1 : TOTAL_ROW + 2, :], (8, LANES)
        )

        def moving(new, old, ref, at, n, size, own_size):
            mean = load_wide(ref, 0, size) / totals
            var = (load_wide(ref, n, size) / totals - mean * mean) * (totals / (totals - 1.0))
            new[at : at + 1, :] = 0.5 * old[at : at + 1, :] + 0.5 * turn(mean, z * own_size)[:, :own_size]
            new[at + 1 : at + 2, :] = 0.5 * old[at + 1 : at + 2, :] + 0.5 * turn(var, z * own_size)[:, :own_size]

        moving(chan_new, chan_old, stats_one, 0, chunks, width, own)
        moving(chan_new, chan_old, stats_two, 2, chunks, width, own)
        moving(head_new, head_old, stats_four, 0, head_chunks, head_width, own_head)
        moving(proj_new, proj_old, stats_three, 0, OUT_CHUNKS, WIDTH_OUT, own_proj)
        low[...] = jnp.zeros_like(low)
        own_dz = fit(jnp.concatenate([dz[b : b + 1, :] for b in range(nb)], axis=1), LANES)
        low[pl.ds(me // per, 1), :] = pltpu.roll(own_dz, lax.rem(me, per) * (nb * EXPERTS), 1)
        fraction = 1.0 / nd
        g_hside = jnp.sum(grad_cls[...] * grad_cls[...]) + jnp.sum(head_gain * head_gain) + jnp.sum(head_bias * head_bias)
        sums = (
            0.0,
            squares_of(grad_side, 104),
            squares_of(piece_h, piece_h.shape[0]) * nd,
            g_hside,
        )
        for k in range(4):
            low[slots + k : slots + k + 1, :] = row_of(sums[k] * fraction)
            low[slots + 4 + k : slots + 5 + k, :] = squares_w[k : k + 1, :] * fraction
        for k in range(nz):
            if chunks + ready(shape, k) + 4 >= 2 * chunks:
                plane.add_one(k, far.send)
        far.add()
        low[slots : slots + 1, :] = row_of(
            squares_of(piece, piece.shape[0]) + squares_of(piece_b, piece_b.shape[0])
        )
        sum_first(nd, nz, low, *comm_two)
        up.begin()
        sum_second(nd, nz, low, *comm_two)
        up.cross()
        every_sum[...] = sum_third(nd, nz, low, *comm_two)
        for k in range(4):
            grad_sq_sum = jnp.sum(every_sum[slots + k : slots + k + 1, :], axis=1, keepdims=True)
            weight_sq = jnp.sum(every_sum[slots + 4 + k : slots + 5 + k, :], axis=1, keepdims=True)
            factors[k : k + 1, :] = jnp.broadcast_to(
                jnp.sqrt(weight_sq) * lax.rsqrt(grad_sq_sum + 1e-12), (1, LANES)
            )
        row = lax.broadcasted_iota(jnp.int32, (count, slots), 0)
        col = lax.broadcasted_iota(jnp.int32, (count, slots), 1)
        spread = dot(jnp.where((row >> 3) // per == col, 1.0, 0.0), every_sum[0:slots, :], NN, highest)
        row = lax.broadcasted_iota(jnp.int32, (count, LANES), 0)
        col = lax.broadcasted_iota(jnp.int32, (count, LANES), 1)
        place = lax.rem(row >> 3, per) * nb + (row & 7) - nb
        spread = jnp.where(((col >> 3) == place) & ((row & 7) >= nb), spread, 0.0)
        row = lax.broadcasted_iota(jnp.int32, (LANES, EXPERTS), 0)
        col = lax.broadcasted_iota(jnp.int32, (LANES, EXPERTS), 1)
        dz_rows = dot(spread, jnp.where((row & (EXPERTS - 1)) == col, 1.0, 0.0), NN, highest)
        pooled_in = rows_all[:, :, cuts_two[2] : cuts_two[2] + 256].reshape(count, 256)
        route_in[...] = dot(pooled_in, dz_rows, TN, highest)[:WIDTH_IN]
        grad_side_out[...] = jnp.transpose(grad_side[...])[:own]
        values = grad_cls[:, :CLASSES]
        both = jnp.concatenate([head_gain, head_bias] + [jnp.zeros((6, own_head), f32)], axis=0)
        grad_cls[...] = jnp.concatenate(
            [jnp.transpose(both)[:, 0:2], values, jnp.zeros((own_head, CLASS_PAD - CLASSES - 2), f32)], axis=1
        )
        up.finish()
        up_b.finish()
        up_h.finish()
        plane_b.finish()
        far_b.finish()
        far.finish()
        twin.finish()
        plane.finish()


def stage_back(half_b, part_b, piece_h, grad_in, dpre, pre, taps, mask, side, stats_one, stats_two, sums_two, totals, lines, images, kern, mix, gates, gate_grad, small, shape_b, shape_h, nb, nd, nz, ident):
    rows, width = pre.shape
    chunks = width // LANES
    deep = LANES * EXPERTS
    before = lambda t: jnp.minimum(t, chunks - 1)
    after = lambda t: jnp.maximum(t - chunks, 0)
    shape = (kern.shape[0], kern.shape[1] // nz)
    devices = nd * nz
    slots = dz_slots(nb, devices)[1]
    few = nz // 2
    chan_old, head_old, proj_old = small[-3:]
    own, own_head = chan_old.shape[1], head_old.shape[1]
    outs = [(own_head, CLASS_PAD), (own, 104), (8, LANES)]
    outs += [(WIDTH_IN, EXPERTS), (WIDTH_OUT, EXPERTS), (1, SQUEEZE), (1, CLASS_PAD)]
    outs += [chan_old.shape, head_old.shape, proj_old.shape, (8, LANES)]
    cuts_one, cuts_two, wide = share_width(lines, nz)
    hbm = pl.BlockSpec(memory_space=pltpu.HBM)
    tall_before = pl.BlockSpec((rows, LANES), lambda t: (0, before(t)))
    return pl.pallas_call(
        functools.partial(stage_back_kernel, nd, nz, nb, chunks, shape, shape_b, shape_h, cuts_one, cuts_two),
        grid=(2 * chunks,),
        out_shape=[jax.ShapeDtypeStruct(x, bf16) for x in (shape, shape_b, shape_h)]
        + [jax.ShapeDtypeStruct(x, f32) for x in outs],
        in_specs=[
            pl.BlockSpec(
                (nz - few,) + half_b.shape[1:], lambda t: (1, 0, 0), pipeline_mode=pl.Buffered(1)
            ),
            whole(part_b.shape),
            whole(piece_h.shape),
            tall_before,
            tall_before,
            pl.BlockSpec((rows, LANES), lambda t: (0, lax.rem(t, chunks))),
            pl.BlockSpec((nb, 32, LANES), lambda t: (0, 0, before(t))),
            whole(mask.shape),
            pl.BlockSpec((side.shape[0], LANES), lambda t: (0, lax.rem(t, chunks))),
            whole(stats_one.shape),
            whole(stats_two.shape),
            whole(sums_two.shape),
            whole(totals.shape),
        ]
        + [whole(x.shape) for x in lines]
        + [
            whole(images.shape),
            pl.BlockSpec((kern.shape[0], deep), lambda t: (0, after(t))),
            whole(mix.shape),
            whole(gates.shape),
            whole(gate_grad.shape),
        ]
        + [whole(x.shape) for x in small],
        out_specs=[hbm] * 3 + [whole(x) for x in outs],
        scratch_shapes=[
            VMEM((chunks, rows, LANES), f32),
            VMEM((chunks, nb, 32, LANES), f32),
            VMEM((KERNEL, PIXELS, LANES), f32),
            VMEM((PIXELS, LANES), f32),
            VMEM((8, LANES), f32),
            VMEM((24, LANES), f32),
            VMEM((24, LANES), f32),
            VMEM((24, LANES), f32),
            VMEM(part_shape(shape_b, nd, nz), bf16),
            VMEM(piece_shape(shape_b, nd), bf16),
            VMEM((devices, 8, wide), f32),
            VMEM((nb, WIDTH_IN, PIXELS), bf16),
            VMEM((kern.shape[0], nb * LANES), bf16),
            VMEM((8, deep), f32),
            VMEM((104, up_to(own)), f32),
            VMEM((slots + 8, LANES), f32),
            VMEM((slots + 8, LANES), f32),
            VMEM(half_shape(shape, nd, nz), bf16),
            VMEM(part_shape(shape, nd, nz), bf16),
            VMEM(piece_shape(shape, nd), bf16),
        ]
        + sum_scratch(24, nd, nz)[1:] * 2
        + sum_scratch(slots + 8, nd, nz)[1:]
        + plane_scratch(shape_b, nd, nz - nz // 2)
        + far_scratch(shape_b, nd, nz)
        + spread_scratch(shape_b, nd, nz)
        + spread_scratch(shape_h, nd, nz)
        + share_scratch(wide, nd, nz)
        + twin_scratch(shape, nd, nz)
        + plane_scratch(shape, nd, nz)
        + far_scratch(shape, nd, nz)
        + spread_scratch(shape, nd, nz),
        compiler_params=params(ident, 62 * 1024 * 1024),
        name="stage_back",
    )(half_b, part_b, piece_h, grad_in, dpre, pre, taps, mask, side, stats_one, stats_two, sums_two, totals, *lines, images, kern, mix, gates, gate_grad, *small)


def update(weight, grad, moment, average, factor):
    scaled = grad * factor
    moment_new = 0.5 * moment + scaled
    weight_new = weight - 0.2 * (scaled + 0.5 * moment_new)
    average_new = 0.5 * average + 0.5 * weight_new
    return (weight_new, moment_new, average_new)


BLOCK_STEP = 64
HEAD_STEP = 32


def turn(x, shift):
    width = x.shape[1]
    return pltpu.roll(x, lax.rem(width - shift, width), 1)


def apply_kernel(
    factors,
    grad_side,
    side_w,
    side_m,
    side_e,
    grad_a,
    grad_b,
    block_w,
    block_m,
    block_e,
    grad_h,
    head_w,
    head_m,
    head_e,
    grad_cls,
    hside_w,
    hside_m,
    hside_e,
    side_wo,
    side_mo,
    side_eo,
    block_wo,
    block_mo,
    block_eo,
    head_wo,
    head_mo,
    head_eo,
    hside_wo,
    hside_mo,
    hside_eo,
    grad_block,
):
    @pl.when(pl.program_id(0) == 0)
    def _():
        fresh = update(side_w[...], grad_side[:, : side_w.shape[1]], side_m[...], side_e[...], factors[1:2, 0:1])
        side_wo[...], side_mo[...], side_eo[...] = fresh
        first = WIDTH_IN + TAPS
        whole_rows = first // 16 * 16

        @pl.loop(0, whole_rows // 16)
        def _(i):
            here = tall(i * 16, 16)
            grad_block[here, :] = grad_a[here, :].astype(f32)

        grad_block[whole_rows:first, :] = grad_a[whole_rows : whole_rows + 16, :].astype(f32)[: first - whole_rows]
        for i in range(WIDTH_OUT // 16):
            grad_block[first + 16 * i : first + 16 * (i + 1), :] = grad_b[16 * i : 16 * (i + 1), :].astype(f32)
        grad_block[first + WIDTH_OUT :, :] = jnp.zeros(
            (grad_block.shape[0] - first - WIDTH_OUT, grad_block.shape[1]), f32
        )

    here = pl.multiple_of(jnp.minimum(pl.program_id(0), grad_block.shape[0] // BLOCK_STEP - 1) * BLOCK_STEP, BLOCK_STEP)

    for k in range(0, BLOCK_STEP, 16):
        rows = slice(k, k + 16)
        fresh = update(
            block_w[rows, :], grad_block[pl.ds(here + k, 16), :], block_m[rows, :], block_e[rows, :], factors[0:1, 0:1]
        )
        block_wo[rows, :], block_mo[rows, :], block_eo[rows, :] = fresh
    for k in range(0, HEAD_STEP, 16):
        rows = slice(k, k + 16)
        fresh = update(
            head_w[rows, :], grad_h[rows, :].astype(f32), head_m[rows, :], head_e[rows, :], factors[2:3, 0:1]
        )
        head_wo[rows, :], head_mo[rows, :], head_eo[rows, :] = fresh
    fresh = update(hside_w[...], grad_cls[:, : hside_w.shape[1]], hside_m[...], hside_e[...], factors[3:4, 0:1])
    hside_wo[...], hside_mo[...], hside_eo[...] = fresh


def apply(factors, side, grads, block, head_arrays, hside):
    def stepped(array, size):
        last = -(-array.shape[0] // size) - 1
        return pl.BlockSpec((size, array.shape[1]), lambda j: (jnp.minimum(j, last), 0))

    steps = max(-(-block[0].shape[0] // BLOCK_STEP), -(-WIDTH_OUT // HEAD_STEP))
    blocks = (
        [whole(x.shape) for x in side]
        + [whole(x.shape) for x in grads]
        + [stepped(x, BLOCK_STEP) for x in block]
        + [stepped(x, HEAD_STEP) for x in head_arrays]
        + [stepped(x, HEAD_STEP) for x in hside]
    )
    arrays = side + grads + block + head_arrays + hside
    keep = [k for k in range(17) if k not in (0, 4, 5, 9, 13)]
    return pl.pallas_call(
        apply_kernel,
        grid=(steps,),
        out_shape=[jax.ShapeDtypeStruct(arrays[k].shape, f32) for k in keep],
        in_specs=[whole(factors.shape)] + blocks,
        out_specs=[blocks[k] for k in keep],
        scratch_shapes=[VMEM((-(-block[0].shape[0] // BLOCK_STEP) * BLOCK_STEP, block[0].shape[1]), f32)],
        compiler_params=params(),
        name="apply",
    )(factors, *arrays)


def body(
    nd,
    nz,
    images,
    pixel_mask,
    counts,
    labels,
    block_w,
    chan_side,
    head_w,
    head_side,
    shared,
    block_mom,
    side_mom,
    head_mom,
    hside_mom,
    shared_mom,
    block_ema,
    side_ema,
    head_ema,
    hside_ema,
    shared_ema,
    chan_stats,
    head_stats,
    proj_stats,
):
    z = lax.axis_index("chan")
    nb = images.shape[0] // nz
    own = chan_side.shape[1]
    own_head = head_side.shape[0]
    width = own * nz
    head_width = own_head * nz
    end_route = WIDTH_IN * EXPERTS
    end_head = end_route + WIDTH_OUT * EXPERTS
    end_norm = end_head + 2 * WIDTH_OUT
    end_squeeze = end_norm + SQUEEZE
    route_in = shared[:end_route].reshape(WIDTH_IN, EXPERTS)
    route_head = shared[end_route:end_head].reshape(WIDTH_OUT, EXPERTS)
    gain_out = shared[end_head:end_norm].reshape(2, WIDTH_OUT)
    sq_bias = shared[None, end_norm:end_squeeze]
    class_bias = jnp.pad(shared[end_squeeze:], (0, CLASS_PAD - CLASSES))[None, :]

    def mine(x):
        return lax.dynamic_slice_in_dim(x, z * nb, nb, 0)

    image_rows = mine(images).reshape(nb * PIXELS, WIDTH_IN)
    mask_now = mine(pixel_mask).astype(f32)
    mask = jnp.broadcast_to(mask_now.reshape(-1, 1), (nb * PIXELS, LANES))
    mask_rows = jnp.pad(
        (jnp.eye(nb, dtype=f32)[:, :, None] * mask_now[None]).reshape(nb, nb * PIXELS).astype(bf16),
        ((0, 8 - nb), (0, 0)),
    )
    count_rows = jnp.broadcast_to(jnp.pad(mine(counts).astype(f32), (0, 8 - nb))[:, None], (8, LANES))
    label_rows = jnp.broadcast_to(jnp.pad(mine(labels), (0, 8 - nb))[:, None], (8, LANES))

    full_a, full_b, side, gain_head, kern_h, kern_c, squares = first_gather(
        block_w, head_w, head_side, chan_side.T, nd, nz, 1
    )
    (
        pre,
        taps,
        dpre,
        stats_one,
        stats_two,
        mix,
        gates,
        pooled_in,
        excited,
        proj,
        pooled,
        gate,
        squeezed,
        stats_three,
        mixed_proj,
        full_b,
        full_h,
        full_c,
    ) = first_stage(
        full_a,
        image_rows,
        mask,
        mask_rows,
        count_rows,
        route_in,
        side,
        sq_bias,
        full_b,
        kern_h,
        kern_c,
        nb,
        width,
        nd,
        nz,
        3,
    )
    totals = stats_one
    head_pool, stats_four, features, grad_logits, sums_four, grad_proj, sums_three, dz_head, half_h, part_h, _ = head_stage(
        mask,
        mask_rows,
        count_rows,
        label_rows,
        class_bias,
        gain_head,
        totals,
        gain_out,
        full_h,
        route_head,
        proj,
        stats_three,
        full_c,
        nb,
        nd,
        nz,
        8,
    )
    shape_h, shape_b = shard_shape(full_h, nz), shard_shape(full_b, nz)
    grad_norm, sums_two, grad_squeeze, gate_grad, dz_gate, piece_h, half_b, part_b = project_back(
        half_h,
        part_h,
        shape_h,
        grad_proj,
        proj,
        stats_three,
        sums_three,
        gain_out,
        mask,
        count_rows,
        totals,
        stats_two,
        side,
        dpre,
        excited,
        mixed_proj,
        full_b,
        mix,
        gate,
        pooled,
        squeezed,
        sq_bias,
        nb,
        nd,
        nz,
        9,
    )
    lines = [features, grad_logits, pooled, dz_gate, head_pool, pooled_in, grad_squeeze, squeezed, sq_bias, dz_head]
    small = [squares, stats_three, stats_four, sums_four, chan_stats, head_stats, proj_stats]
    grad_a, grad_b, grad_h, grad_cls, grad_side, factors, *rest = stage_back(
        half_b,
        part_b,
        piece_h,
        grad_norm,
        dpre,
        pre,
        taps,
        mask,
        side,
        stats_one,
        stats_two,
        sums_two,
        totals,
        lines,
        image_rows,
        full_a,
        mix,
        gates,
        gate_grad,
        small,
        shape_b,
        shape_h,
        nb,
        nd,
        nz,
        11,
    )
    grad_route_in, grad_route_head, grad_sq_bias, grad_class_bias, new_chan, new_head_stats, new_proj, loss = rest
    results = apply(
        factors,
        [grad_side, chan_side.T, side_mom.T, side_ema.T],
        [grad_a, grad_b],
        [block_w, block_mom, block_ema],
        [grad_h, head_w, head_mom, head_ema],
        [grad_cls, head_side, hside_mom, hside_ema],
    )
    new_side, new_block, new_head, new_hside = (results[3 * k : 3 * k + 3] for k in range(4))
    new_side = [x.T for x in new_side]

    def out_row(first):
        return sums_three[first : first + OUT_CHUNKS].reshape(-1)[:WIDTH_OUT]

    grad_shared = jnp.concatenate(
        [
            grad_route_in.reshape(-1),
            grad_route_head.reshape(-1),
            out_row(OUT_CHUNKS),
            out_row(0),
            grad_sq_bias[0],
            grad_class_bias[0, :CLASSES],
        ]
    )
    new_shared = update(
        shared,
        grad_shared,
        shared_mom,
        shared_ema,
        jnp.sqrt(jnp.sum(shared * shared)) * lax.rsqrt(jnp.sum(grad_shared * grad_shared) + 1e-12),
    )
    groups = (new_block, new_side, new_head, new_hside, new_shared)
    return (
        (loss[0, 0],)
        + tuple(group[k] for k in range(3) for group in groups)
        + (new_chan, new_head_stats, new_proj)
    )


def solution(mesh):
    nd, nz = mesh.shape["dp"], mesh.shape["chan"]
    cols = P(None, "chan")
    state = (cols, cols, cols, P("chan", None), P())
    return jax.shard_map(
        functools.partial(body, nd, nz),
        mesh=mesh,
        in_specs=(P("dp", None, None), P("dp", None), P("dp"), P("dp"))
        + state * 3
        + (cols, cols, cols),
        out_specs=(P(),) + state * 3 + (cols, cols, cols),
        check_vma=False,
    )
```

```python
import functools

import jax
import jax.numpy as jnp
from jax import lax
from jax.experimental import pallas as pl
from jax.experimental.pallas import tpu as pltpu
from jax.sharding import PartitionSpec as P

WIDTH_IN = 192
WIDTH_OUT = 320
SQUEEZE = 48
CLASSES = 1000
EXPERTS = 8
KERNEL = 5
MAP_SIDE = 16
TAPS = KERNEL * KERNEL
PIXELS = MAP_SIDE * MAP_SIDE
LANES = 128
CLASS_PAD = 1024
TOTAL_ROW = 18
eps_norm = 0.001
highest = lax.Precision.HIGHEST
MESH = pl.DeviceIdType.MESH
f32 = jnp.float32
bf16 = jnp.bfloat16
VMEM = pltpu.VMEM
VLIMIT = 60 * 1024 * 1024


def dot(a, b, dims=((1,), (0,)), precision=None):
    return lax.dot_general(a, b, (dims, ((), ())), precision=precision, preferred_element_type=f32)


NN = ((1,), (0,))
NT = ((1,), (1,))
TN = ((0,), (0,))


def sig(x):
    return 0.5 * jnp.tanh(0.5 * x) + 0.5


def dsilu(n):
    s = sig(n)
    return s * (1.0 + n * (1.0 - s))


def rsum(x):
    return jnp.sum(x, axis=0, keepdims=True)


def split(x):
    high = x.astype(bf16)
    return jnp.concatenate([high, (x - high.astype(f32)).astype(bf16)], axis=0)


def sum_peers(nd, nz):
    d = lax.axis_index("dp")
    z = lax.axis_index("chan")
    in_plane = [(lax.rem(d + k, nd), z) for k in range(1, nd)]
    along = [(d, lax.rem(z + k, nz)) for k in range(1, nz)]
    return in_plane, along


def signal(peers):
    barrier = pltpu.get_barrier_semaphore()
    for peer in peers:
        pl.semaphore_signal(barrier, inc=1, device_id=peer, device_id_type=MESH)


def sum_start(nd, nz):
    in_plane, along = sum_peers(nd, nz)
    signal(in_plane + along)


def met(nd, nz):
    pl.semaphore_wait(pltpu.get_barrier_semaphore(), nd + nz - 2)


def sum_copies(nd, nz, x_ref, plane, depth, s1, r1, s2, r2):
    d = lax.axis_index("dp")
    z = lax.axis_index("chan")
    in_plane, along = sum_peers(nd, nz)

    def copy(src, dst, send, recv, peer):
        return pltpu.make_async_remote_copy(
            src_ref=src, dst_ref=dst, send_sem=send, recv_sem=recv, device_id=peer, device_id_type=MESH
        )

    first = [copy(x_ref, plane.at[d], s1.at[k], r1.at[k], peer) for k, peer in enumerate(in_plane)]
    second = [copy(depth.at[z], depth.at[z], s2.at[k], r2.at[k], peer) for k, peer in enumerate(along)]
    return first, second


def sum_first(nd, nz, x_ref, plane, *comm):
    start(sum_copies(nd, nz, x_ref, plane, *comm)[0])
    plane[lax.axis_index("dp")] = x_ref[...]


def sum_second(nd, nz, x_ref, plane, depth, *sems):
    first, second = sum_copies(nd, nz, x_ref, plane, depth, *sems)
    arrived(first)
    total = plane[0]
    for k in range(1, nd):
        total = total + plane[k]
    depth[lax.axis_index("chan")] = total
    start(second)


def sum_third(nd, nz, x_ref, plane, depth, *sems):
    first, second = sum_copies(nd, nz, x_ref, plane, depth, *sems)
    arrived(second)
    total = depth[0]
    for k in range(1, nz):
        total = total + depth[k]
    sent(first + second)
    return total


def sum_finish(nd, nz, x_ref, o_ref, *comm):
    sum_first(nd, nz, x_ref, *comm)
    sum_second(nd, nz, x_ref, *comm)
    o_ref[...] = sum_third(nd, nz, x_ref, *comm)


def sum_scratch(rows, nd, nz):
    return [
        VMEM((rows, LANES), f32),
        VMEM((nd, rows, LANES), f32),
        VMEM((nz, rows, LANES), f32),
        pltpu.SemaphoreType.DMA((nd,)),
        pltpu.SemaphoreType.DMA((nd,)),
        pltpu.SemaphoreType.DMA((nz,)),
        pltpu.SemaphoreType.DMA((nz,)),
    ]


def params(ident=None, limit=VLIMIT):
    if ident is None:
        return pltpu.CompilerParams(vmem_limit_bytes=VLIMIT)
    return pltpu.CompilerParams(vmem_limit_bytes=limit, collective_id=ident, has_side_effects=True)


def sum_kernel(nd, nz, x_ref, o_ref, *comm):
    sum_start(nd, nz)
    met(nd, nz)
    sum_finish(nd, nz, x_ref, o_ref, *comm)


def all_sum(x, nd, nz, ident):
    return pl.pallas_call(
        functools.partial(sum_kernel, nd, nz),
        out_shape=jax.ShapeDtypeStruct(x.shape, x.dtype),
        in_specs=[pl.BlockSpec(memory_space=VMEM)],
        out_specs=pl.BlockSpec(memory_space=VMEM),
        scratch_shapes=sum_scratch(x.shape[0], nd, nz)[1:],
        compiler_params=params(ident),
        name="all_sum",
    )(x)


def by_column(width):
    return (width // 2) % LANES == 0


def pad_rows(rows, width, nd):
    unit = 16 * (nd // 2 if by_column(width) else nd)
    return -(-rows // unit) * unit


def core_block(rows, width, core):
    if by_column(width):
        return 0, rows, pl.multiple_of(core * (width // 2), LANES), width // 2
    return pl.multiple_of(core * (rows // 2), 16), rows // 2, 0, width


def part(rows, width, nd, core, place):
    row, count, col, cols = core_block(rows, width, core)
    unit = count // (nd // 2)
    return pl.multiple_of(row + place * unit, 16), unit, col, cols


class Net:
    def __init__(self, nd, nz):
        self.nd, self.nz, self.nxy = nd, nz, nd // 2
        self.d = lax.axis_index("dp")
        self.z = lax.axis_index("chan")
        self.core = lax.rem(self.d, 2)
        self.place = self.d // 2
        self.far = [lax.rem(self.z + k, nz) for k in range(1, nz)]
        self.others = [lax.rem(self.place + k, self.nxy) for k in range(1, self.nxy)]
        self.along = [(self.d, zz) for zz in self.far]
        self.plane = [(2 * o + self.core, self.z) for o in self.others]
        self.twin = (2 * self.place + 1 - self.core, self.z)

    def copy(self, src, dst, sems, k, peer):
        return pltpu.make_async_remote_copy(
            src_ref=src,
            dst_ref=dst,
            send_sem=sems[0].at[k],
            recv_sem=sems[1].at[k],
            device_id=peer,
            device_id_type=MESH,
        )


def start(copies):
    for copy in copies:
        copy.start()


def arrived(copies):
    for copy in copies:
        copy.wait_recv()


def sent(copies):
    for copy in copies:
        copy.wait_send()


def pair(n):
    return [pltpu.SemaphoreType.DMA((n,)), pltpu.SemaphoreType.DMA((n,))]


def lanes(first, count):
    return pl.ds(pl.multiple_of(first, LANES), count)


def tall(first, count):
    return pl.ds(pl.multiple_of(first, 16), count)


def spot(ref, shape, zz, row, unit, col, cols):
    if len(ref.shape) == 3:
        return ref.at[zz, tall(row, unit), lanes(col, cols)]
    return ref.at[tall(row, unit), lanes(zz * shape[1] + col, cols)]


def shard_shape(full, nz):
    if len(full.shape) == 3:
        return full.shape[1:]
    return (full.shape[0], full.shape[1] // nz)


def own_copy(net, shape, src, dst, sem):
    return pltpu.make_async_copy(src, spot(dst, shape, net.z, 0, shape[0], 0, shape[1]), sem)


def gather_far(net, shape, src, dst, sems):
    rows, width = shape
    row, unit, col, cols = part(rows, width, net.nd, net.core, net.place)
    block = src.at[tall(row, unit), lanes(col, cols)]
    return [
        net.copy(block, spot(dst, shape, net.z, row, unit, col, cols), sems, k, peer)
        for k, peer in enumerate(net.along)
    ]


def gather_plane(net, shape, ref, sems, k):
    rows, width = shape
    row, unit, col, cols = part(rows, width, net.nd, net.core, net.place)
    block = spot(ref, shape, net.far[k], row, unit, col, cols)
    n = net.nxy - 1
    return [net.copy(block, block, sems, k * n + q, peer) for q, peer in enumerate(net.plane)]


def gather_twin(net, shape, ref, sems, k):
    rows, width = shape
    row, unit, col, cols = core_block(rows, width, net.core)
    block = spot(ref, shape, net.far[k], row, unit, col, cols)
    return [net.copy(block, block, sems, k, net.twin)]


def late_count(nz):
    return max(1, (nz - 1) // 3)


def some(stage, net, shape, ref, sems, shards):
    return [copy for k in shards for copy in stage(net, shape, ref, sems, k)]


def every(stage, net, shape, ref, sems):
    return [copy for k in range(net.nz - 1) for copy in stage(net, shape, ref, sems, k)]


def squares_of(ref, rows):
    step_rows = 16 if ref.dtype == bf16 else 8
    whole_rows = rows // step_rows * step_rows

    def step(i, total):
        value = ref[pl.ds(pl.multiple_of(i * step_rows, step_rows), step_rows), :].astype(f32)
        return total + value * value

    total = jnp.sum(lax.fori_loop(0, whole_rows // step_rows, step, jnp.zeros((step_rows, ref.shape[1]), f32)))
    if whole_rows < rows:
        last = ref[whole_rows:rows, :].astype(f32)
        total = total + jnp.sum(last * last)
    return total


def row_of(total):
    lane = lax.broadcasted_iota(jnp.int32, (1, LANES), 1)
    return jnp.where(lane == 0, total, 0.0)


def first_kernel(nd, nz, shape, shape_b, block_ref, head_ref, hside_ref, side_ref, full, full_b, side, gain, kh, kc, squares, wide, tall_h, tall_s, kb, low, side_buf, gain_buf, far_s, far_r, plane_s, plane_r, twin_s, twin_r, side_s, side_r, gain_s, gain_r, later_s, later_r, local):
    net = Net(nd, nz)
    signal(net.along + net.plane + [net.twin])
    rows = shape[0]
    total_rows = block_ref.shape[0]
    fetch = [
        pltpu.make_async_copy(block_ref.at[pl.ds(0, rows)], wide.at[pl.ds(0, rows)], local.at[0]),
        pltpu.make_async_copy(
            block_ref.at[pl.ds(rows, total_rows - rows)], wide.at[pl.ds(rows, total_rows - rows)], local.at[1]
        ),
        pltpu.make_async_copy(hside_ref, tall_s, local.at[2]),
        pltpu.make_async_copy(head_ref, tall_h, local.at[3]),
    ]
    fetch[0].start()
    fetch[0].wait()
    start(fetch[1:])

    @pl.loop(0, rows // 16)
    def _(i):
        at = tall(i * 16, 16)
        low[at, :] = wide[at, :].astype(bf16)

    own = own_copy(net, shape, low, full, local.at[4])
    own.start()
    pl.semaphore_wait(pltpu.get_barrier_semaphore(), nz - 1 + nd // 2)
    far = gather_far(net, shape, low, full, (far_s, far_r))
    start(far)
    side_buf[net.z] = jnp.transpose(side_ref[...])
    sides = [
        net.copy(side_buf.at[net.z], side_buf.at[net.z], (side_s, side_r), k, peer)
        for k, peer in enumerate(net.along)
    ]
    start(sides)
    fetch[2].wait()
    gain_buf[net.z] = jnp.transpose(tall_s[:, 0:LANES])[0:8]
    gains = [
        net.copy(gain_buf.at[net.z], gain_buf.at[net.z], (gain_s, gain_r), k, peer)
        for k, peer in enumerate(net.along)
    ]
    start(gains)
    fetch[1].wait()
    first = WIDTH_IN + TAPS
    for i in range(WIDTH_OUT // 16):
        kb[16 * i : 16 * (i + 1), :] = wide[first + 16 * i : first + 16 * (i + 1), :].astype(bf16)
    own_b = own_copy(net, shape_b, kb, full_b, local.at[5])
    own_b.start()
    planes = []
    for k in range(nz - 1):
        arrived([far[nz - 2 - k]])
        planes.append(gather_plane(net, shape, full, (plane_s, plane_r), k))
        start(planes[k])
    later = gather_far(net, shape_b, kb, full_b, (later_s, later_r))
    start(later)
    fetch[3].wait()

    @pl.loop(0, WIDTH_OUT // 16)
    def _(i):
        at = tall(i * 16, 16)
        kh[at, :] = tall_h[at, :].astype(bf16)

    for i in range(tall_s.shape[0] // 16):
        value = tall_s[16 * i : 16 * (i + 1), 2 : 2 + CLASSES]
        kc[16 * i : 16 * (i + 1), :] = jnp.concatenate(
            [value, jnp.zeros((16, CLASS_PAD - CLASSES), f32)], axis=1
        ).astype(bf16)
    squares[...] = jnp.zeros_like(squares)
    for k, (ref, count) in enumerate(
        ((wide, total_rows), (side_ref, side_ref.shape[0]), (tall_h, WIDTH_OUT), (tall_s, tall_s.shape[0]))
    ):
        squares[k : k + 1, :] = row_of(squares_of(ref, count))
    twins = []
    for k in range(nz - 1):
        arrived(planes[k])
        twins.append(gather_twin(net, shape, full, (twin_s, twin_r), k))
        start(twins[k])
    arrived(sides + gains)
    side[...] = jnp.zeros_like(side)
    side[0 : side_ref.shape[1], :] = jnp.concatenate([side_buf[k] for k in range(nz)], axis=1)
    gain[...] = jnp.concatenate([gain_buf[k] for k in range(nz)], axis=1)
    for k in range(nz - 1):
        arrived(twins[k])
    arrived(later)
    sent(far + sides + gains + later)
    for k in range(nz - 1):
        sent(planes[k] + twins[k])
    own.wait()
    own_b.wait()


def first_gather(block, head_w, head_side, side, nd, nz, ident):
    shape = (pad_rows(WIDTH_IN + TAPS, block.shape[1], nd), block.shape[1])
    shape_b = (pad_rows(WIDTH_OUT, block.shape[1], nd), block.shape[1])
    shape_h = (pad_rows(WIDTH_OUT, head_w.shape[1], nd), head_w.shape[1])
    shape_c = (pad_rows(head_side.shape[0], CLASS_PAD, nd), CLASS_PAD)
    hbm = pl.BlockSpec(memory_space=pltpu.HBM)
    vmem = pl.BlockSpec(memory_space=VMEM)
    own_head = head_side.shape[0]
    return pl.pallas_call(
        functools.partial(first_kernel, nd, nz, shape, shape_b),
        out_shape=[
            jax.ShapeDtypeStruct((shape[0], nz * shape[1]), bf16),
            jax.ShapeDtypeStruct((shape_b[0], nz * shape_b[1]), bf16),
            jax.ShapeDtypeStruct((104, nz * side.shape[0]), f32),
            jax.ShapeDtypeStruct((8, nz * own_head), f32),
            jax.ShapeDtypeStruct(shape_h, bf16),
            jax.ShapeDtypeStruct(shape_c, bf16),
            jax.ShapeDtypeStruct((8, LANES), f32),
        ],
        in_specs=[hbm, hbm, hbm, vmem],
        out_specs=[hbm] * 2 + [vmem] * 5,
        scratch_shapes=[
            VMEM(block.shape, f32),
            VMEM(head_w.shape, f32),
            VMEM(head_side.shape, f32),
            VMEM(shape_b, bf16),
            VMEM(shape, bf16),
            VMEM((nz, side.shape[1], side.shape[0]), f32),
            VMEM((nz, 8, own_head), f32),
        ]
        + pair(nz - 1)
        + pair((nz - 1) * (nd // 2 - 1))
        + pair(nz - 1)
        + pair(nz - 1) * 3
        + [pltpu.SemaphoreType.DMA((6,))],
        compiler_params=params(ident),
        name="first_gather",
    )(block, head_w, head_side, side)


def reduce_sizes(rows, width, nd):
    unit, cols = (rows, width // 2) if by_column(width) else (rows // 2, width)
    return unit, cols, unit // (nd // 2)


def reduce_twin(net, shape, g_ref, twin_buf, sems, k):
    row, unit, col, cols = core_block(shape[0], shape[1], 1 - net.core)
    return net.copy(
        g_ref.at[tall(row, unit), lanes(k * shape[1] + col, cols)], twin_buf.at[k], sems, k, net.twin
    )


def reduce_add(net, shape, g_ref, half, twin_buf, k):
    row, unit, col, cols = core_block(shape[0], shape[1], net.core)

    @pl.loop(0, unit // 16)
    def _(i):
        at = tall(i * 16, 16)
        mine = g_ref[tall(row + i * 16, 16), lanes(k * shape[1] + col, cols)]
        half[k, at, :] = (mine.astype(f32) + twin_buf[k, at, :].astype(f32)).astype(bf16)


def reduce_plane(net, shape, half, plane_buf, sems, k, base, shift):
    size = reduce_sizes(*shape, net.nd)[2]
    n = net.nxy - 1
    return [
        net.copy(half.at[k - shift, tall(o * size, size)], plane_buf.at[q, k - base], sems, (k - base) * n + q, net.plane[q])
        for q, o in enumerate(net.others)
    ]


def reduce_plane_sum(net, shape, half, plane_buf, out, k, base, shift):
    size = reduce_sizes(*shape, net.nd)[2]

    @pl.loop(0, size // 16)
    def _(i):
        at = tall(i * 16, 16)
        total = half[k - shift, tall(net.place * size + i * 16, 16), :].astype(f32)
        for q in range(net.nxy - 1):
            total = total + plane_buf[q, k - base, at, :].astype(f32)
        out[k, at, :] = total.astype(bf16)


def reduce_far(net, sums, depth_buf, sems):
    return [net.copy(sums.at[zz], depth_buf.at[k], sems, k, net.along[k]) for k, zz in enumerate(net.far)]


def reduce_far_sum(net, shape, sums, depth_buf, piece):
    @pl.loop(0, reduce_sizes(*shape, net.nd)[2] // 16)
    def _(i):
        at = tall(i * 16, 16)
        total = sums[net.z, at, :].astype(f32)
        for q in range(net.nz - 1):
            total = total + depth_buf[q, at, :].astype(f32)
        piece[at, :] = total.astype(bf16)


def spread_block(net, shape, out):
    row, unit, col, cols = part(shape[0], shape[1], net.nd, net.core, net.place)
    return out.at[tall(row, unit), lanes(col, cols)]


def spread_plane(net, shape, piece, out, sems):
    block = spread_block(net, shape, out)
    return [net.copy(piece, block, sems, q, peer) for q, peer in enumerate(net.plane)]


def spread_twin(net, shape, out, sems):
    row, unit, col, cols = core_block(shape[0], shape[1], net.core)
    block = out.at[tall(row, unit), lanes(col, cols)]
    return [net.copy(block, block, sems, 0, net.twin)]


def twin_scratch(shape, nd, nz):
    unit, cols, size = reduce_sizes(*shape, nd)
    return [VMEM((shape[0], nz * shape[1]), bf16), VMEM((nz, unit, cols), bf16)] + pair(nz)


def plane_scratch(shape, nd, count):
    unit, cols, size = reduce_sizes(*shape, nd)
    return [VMEM((nd // 2 - 1, count, size, cols), bf16)] + pair(count * (nd // 2 - 1))


def half_shape(shape, nd, nz):
    unit, cols, size = reduce_sizes(*shape, nd)
    return (nz, unit, cols)


def part_shape(shape, nd, nz):
    unit, cols, size = reduce_sizes(*shape, nd)
    return (nz, size, cols)


def ready(shape, k):
    return max(2, -(-(k + 1) * shape[1] // (LANES * EXPERTS)))


class Steps:
    def __init__(self):
        self.steps = {}

    def at(self, step, action):
        self.steps.setdefault(step, []).append(action)

    def emit(self, now, last):
        for step in sorted(self.steps):
            if step < last:

                @pl.when(now == step)
                def _(step=step):
                    for action in self.steps[step]:
                        action()

    def end(self, last):
        for step in sorted(self.steps):
            if step >= last:
                for action in self.steps[step]:
                    action()


def far_scratch(shape, nd, nz):
    unit, cols, size = reduce_sizes(*shape, nd)
    return [VMEM((nz - 1, size, cols), bf16)] + pair(nz - 1)


def spread_scratch(shape, nd, nz):
    return [pltpu.SemaphoreType.DMA((1,))] + pair(nd // 2 - 1) + pair(1)


def piece_shape(shape, nd):
    unit, cols, size = reduce_sizes(*shape, nd)
    return (size, cols)


class Twin:
    def __init__(self, net, shape, half, g_ref, twin_buf, ts, tr):
        self.net, self.shape, self.half, self.g, self.buf, self.sems = net, shape, half, g_ref, twin_buf, (ts, tr)

    def copy(self, k):
        return reduce_twin(self.net, self.shape, self.g, self.buf, self.sems, k)

    def begin(self, k):
        self.copy(k).start()

    def add(self, k):
        self.copy(k).wait_recv()
        reduce_add(self.net, self.shape, self.g, self.half, self.buf, k)

    def finish(self):
        for k in range(self.net.nz):
            self.copy(k).wait_send()


class Plane:
    def __init__(self, net, shape, half, out, base, count, buf, ps, pr, shift=0):
        self.net, self.shape, self.half, self.out = net, shape, half, out
        self.shards, self.base, self.buf, self.sems = range(base, base + count), base, buf, (ps, pr)
        self.shift = shift

    def copies(self, k):
        return reduce_plane(self.net, self.shape, self.half, self.buf, self.sems, k, self.base, self.shift)

    def begin(self, k):
        start(self.copies(k))

    def add(self, then=None):
        for k in self.shards:
            self.add_one(k, then)

    def add_one(self, k, then=None):
        arrived(self.copies(k))
        reduce_plane_sum(self.net, self.shape, self.half, self.buf, self.out, k, self.base, self.shift)
        if then is not None:
            then(k)

    def finish(self):
        for k in self.shards:
            sent(self.copies(k))


class Far:
    def __init__(self, net, shape, sums, piece, buf, fs, fr):
        self.net, self.shape, self.sums, self.piece, self.buf, self.sems = net, shape, sums, piece, buf, (fs, fr)

    def copies(self):
        return reduce_far(self.net, self.sums, self.buf, self.sems)

    def send(self, k):
        net = self.net
        slot = lax.rem(k - net.z - 1 + net.nz, net.nz)

        @pl.when(net.z != k)
        def _():
            net.copy(self.sums.at[k], self.buf.at[slot], self.sems, slot, (net.d, k)).start()

    def add(self):
        arrived(self.copies())
        reduce_far_sum(self.net, self.shape, self.sums, self.buf, self.piece)

    def finish(self):
        sent(self.copies())


class Spread:
    def __init__(self, net, shape, piece, out, local, ps, pr, ts, tr):
        self.net, self.shape, self.piece, self.out, self.local = net, shape, piece, out, local
        self.plane_sems, self.twin_sems = (ps, pr), (ts, tr)

    def own(self):
        return pltpu.make_async_copy(self.piece, spread_block(self.net, self.shape, self.out), self.local.at[0])

    def plane(self):
        return spread_plane(self.net, self.shape, self.piece, self.out, self.plane_sems)

    def twin(self):
        return spread_twin(self.net, self.shape, self.out, self.twin_sems)

    def begin(self):
        self.own().start()
        start(self.plane())

    def cross(self):
        arrived(self.plane())
        self.own().wait()
        start(self.twin())

    def finish(self):
        arrived(self.twin())
        sent(self.plane() + self.twin())


def up_to(size):
    return -(-size // LANES) * LANES


def share_width(lines, nz):
    one = [0]
    for x in lines[0], lines[2], lines[3]:
        one.append(one[-1] + up_to(x.shape[1] // nz))
    for _ in range(3):
        one.append(one[-1] + LANES)
    two = [0]
    for x in lines[1], lines[4], lines[5]:
        two.append(two[-1] + up_to(x.shape[1]))
    return one, two, max(one[-1], two[-1])


def share_scratch(width, nd, nz):
    return (
        [VMEM((nz, 8, width), f32), pltpu.SemaphoreType.DMA((1,))]
        + pair(nz - 1)
        + pair(nd // 2 - 1)
        + pair(nd // 2)
    )


def fit(x, width):
    if x.shape[1] == width:
        return x
    return jnp.concatenate([x, jnp.zeros((x.shape[0], width - x.shape[1]), f32)], axis=1)


class Share:
    def __init__(self, net, rows_all, lines, local, fs, fr, ps, pr, ts, tr):
        self.net, self.rows, self.lines, self.local = net, rows_all, lines, local
        self.far_sems, self.plane_sems, self.twin_sems = (fs, fr), (ps, pr), (ts, tr)
        self.me = net.d * net.nz + net.z

    def fill(self, nb, cut, narrow, wide):
        width = self.lines.shape[2]
        self.lines[...] = jnp.zeros_like(self.lines)
        two = fit(jnp.concatenate([fit(x, up_to(x.shape[1])) for x in wide], axis=1), width)[:nb]
        last = [fit(x, LANES) for x in narrow]
        for k in range(self.net.nz):
            parts = []
            for x in cut:
                own = x.shape[1] // self.net.nz
                parts.append(fit(x[:, k * own : (k + 1) * own], up_to(own)))
            one = fit(jnp.concatenate(parts + last, axis=1), width)[:nb]
            self.lines[k, 0 : 2 * nb, :] = jnp.concatenate([one, two], axis=0)

    def far_copies(self):
        net = self.net
        return [
            net.copy(self.lines.at[zz], self.rows.at[self.me], self.far_sems, k, net.along[k])
            for k, zz in enumerate(net.far)
        ]

    def plane_copies(self):
        net = self.net
        block = self.rows.at[pl.ds(net.d * net.nz, net.nz)]
        return [net.copy(block, block, self.plane_sems, q, peer) for q, peer in enumerate(net.plane)]

    def twin_copies(self):
        net = self.net
        out = []
        for o in range(net.nxy):
            block = self.rows.at[pl.ds((2 * o + net.core) * net.nz, net.nz)]
            out.append(net.copy(block, block, self.twin_sems, o, net.twin))
        return out

    def far(self):
        start(self.far_copies())
        self.own().start()

    def own(self):
        return pltpu.make_async_copy(self.lines.at[self.net.z], self.rows.at[self.me], self.local.at[0])

    def plane(self):
        arrived(self.far_copies())
        self.own().wait()
        start(self.plane_copies())

    def twin(self):
        arrived(self.plane_copies())
        start(self.twin_copies())

    def finish(self):
        arrived(self.twin_copies())
        sent(self.far_copies() + self.plane_copies() + self.twin_copies())


def build_mix(gates, nb, ref):
    deep = LANES * EXPERTS
    row = lax.broadcasted_iota(jnp.int32, (deep, EXPERTS), 0)
    col = lax.broadcasted_iota(jnp.int32, (deep, EXPERTS), 1)
    pick = jnp.where((row & (EXPERTS - 1)) == col, 1.0, 0.0).astype(f32)
    row = lax.broadcasted_iota(jnp.int32, (deep, LANES), 0)
    col = lax.broadcasted_iota(jnp.int32, (deep, LANES), 1)
    same = (row >> 3) == col
    for b in range(nb):
        spread = jnp.broadcast_to(gates[b : b + 1, :], (LANES, EXPERTS))
        value = jnp.where(same, dot(pick, spread, NT, highest), 0.0)
        high = value.astype(bf16)
        ref[:, b * LANES : (b + 1) * LANES] = high
        ref[:, (nb + b) * LANES : (nb + b + 1) * LANES] = (value - high.astype(f32)).astype(bf16)


def mix_kernels(kernels, mix):
    both = dot(kernels, mix)
    half = both.shape[1] // 2
    return both[:, :half] + both[:, half:]


def gate_sums(rows):
    deep = LANES * EXPERTS
    row = lax.broadcasted_iota(jnp.int32, (deep, EXPERTS), 0)
    col = lax.broadcasted_iota(jnp.int32, (deep, EXPERTS), 1)
    pick = jnp.where((row & (EXPERTS - 1)) == col, 1.0, 0.0).astype(f32)
    return dot(rows, pick, NN, highest)


def gate_rows(grads, kernel_block, nb):
    both = dot(grads, kernel_block, TN)
    channels = LANES // EXPERTS
    row = lax.broadcasted_iota(jnp.int32, (channels, LANES), 0)
    col = lax.broadcasted_iota(jnp.int32, (channels, LANES), 1)
    same = row == (col >> 3)
    out = []
    for b in range(nb):
        parts = []
        for m in range(EXPERTS):
            first = b * LANES + m * channels
            block = both[first : first + channels, m * LANES : (m + 1) * LANES]
            parts.append(rsum(jnp.where(same, block, 0.0)))
        out.append(jnp.concatenate(parts, axis=1))
    return jnp.concatenate(out, axis=0)


def norm_rows(stats, chunk, chunks, total):
    mean = stats[pl.ds(chunk, 1), :] / total
    var = stats[pl.ds(chunks + chunk, 1), :] / total - mean * mean
    return mean, lax.rsqrt(var + eps_norm)


def whole(shape):
    return pl.BlockSpec(shape, lambda *_: (0,) * len(shape), pipeline_mode=pl.Buffered(1))


def image(b):
    return pl.ds(pl.multiple_of(b * PIXELS, PIXELS), PIXELS)


def shifted(value, step):
    if step == 0:
        return value
    col = lax.broadcasted_iota(jnp.int32, value.shape, 0) & (MAP_SIDE - 1)
    moved = pltpu.roll(value, (-step) % PIXELS, 0)
    keep = (col + step >= 0) & (col + step < MAP_SIDE)
    return jnp.where(keep, moved, 0.0)


def stage_kernel(
    nd,
    nz,
    nb,
    chunks,
    shapes,
    kern_ref,
    images,
    mask,
    mask_rows,
    counts,
    route,
    side,
    sq_bias,
    in_b,
    kh,
    kc,
    pre_out,
    taps_out,
    out,
    stats_all,
    sums_all,
    mix,
    gates,
    pooled,
    excited,
    proj,
    pool_out,
    gate_out,
    squeezed,
    last_all,
    mixed,
    full_b,
    full_h,
    full_c,
    pre,
    taps,
    buf,
    held,
    early,
    late,
    early_two,
    late_two,
    sums_three,
    dpre,
    exc,
    kern_buf,
    *comm,
):
    step = pl.program_id(0)
    comm_early, comm_late, comm_two, sems = comm[0:6], comm[6:12], comm[12:18], comm[18:]
    two_early, two_late, sems = sems[0:6], sems[6:12], sems[12:]
    cut_two = chunks // 2
    net = Net(nd, nz)
    few = late_count(nz)
    cut = chunks // 2
    groups = [[k for k in range(nz - 1) if 3 * k // (nz - 1) == g] for g in range(3)]

    def far_h():
        return gather_far(net, shapes[1], kh, full_h, sems[0:2])

    def far_c():
        return gather_far(net, shapes[2], kc, full_c, sems[2:4])

    def planes_b(k):
        return gather_plane(net, shapes[0], full_b, sems[4:6], k)

    def planes_h():
        return every(gather_plane, net, shapes[1], full_h, sems[6:8])

    def twins_b(k):
        return gather_twin(net, shapes[0], full_b, sems[8:10], k)

    def own():
        return [
            own_copy(net, shapes[1], kh, full_h, sems[10].at[0]),
            own_copy(net, shapes[2], kc, full_c, sems[10].at[1]),
        ]

    def b_planes(group):
        for k in groups[group]:
            start(planes_b(k))

    def begin():
        met(nd, nz)
        b_planes(0)
        start(far_h() + own())

    def early_sum():
        sum_first(nd, nz, early, *comm_early)

    def early_second():
        sum_second(nd, nz, early, *comm_early)

    def early_third():
        stats_all[...] = sum_third(nd, nz, early, *comm_early)
        sum_first(nd, nz, late, *comm_late)

    def late_second():
        sum_second(nd, nz, late, *comm_late)

    def late_third():
        stats_all[...] += sum_third(nd, nz, late, *comm_late)

    def h_planes(k):
        start(gather_plane(net, shapes[1], full_h, sems[6:8], k))

    def twins_h(k):
        return gather_twin(net, shapes[1], full_h, sems[11:13], k)

    def h_twin(k):
        arrived(gather_plane(net, shapes[1], full_h, sems[6:8], k))
        start(twins_h(k))

    def load(k):
        return pltpu.make_async_copy(
            full_b.at[pl.ds(0, WIDTH_OUT), lanes(k * LANES * EXPERTS, LANES * EXPERTS)],
            kern_buf.at[lax.rem(k, 2)],
            sems[13].at[lax.rem(k, 2)],
        )

    def b_whole():
        for k in range(nz - 1):
            arrived(twins_b(k))
        load(0).start()

    def b_twins(group):
        for k in groups[group]:
            arrived(planes_b(k))
            start(twins_b(k))

    @pl.when(step == 0)
    def _():
        sum_start(nd, nz)
        early[...] = jnp.zeros_like(early)
        late[...] = jnp.zeros_like(late)
        for ref in (early_two, late_two, sums_three, squeezed, pool_out):
            ref[...] = jnp.zeros_like(ref)
        early[2 * chunks : 2 * chunks + 1, :] = rsum(counts[...])
        early[2 * chunks + 1 : 2 * chunks + 2, :] = rsum(jnp.where(counts[...] > 0.0, 1.0, 0.0))
        pool = dot(mask_rows[...], images[...]) / jnp.maximum(counts[:, 0:1], 1.0)
        pooled[...] = pool
        gate = sig(dot(pool, route[...], NN, highest))
        gates[...] = gate
        build_mix(gate, nb, mix)

    steps = Steps()
    steps.at(1, begin)
    steps.at(cut, early_sum)
    steps.at(cut + 2, early_second)
    steps.at(cut + 3, functools.partial(b_planes, 1))
    steps.at(chunks, early_third)
    steps.at(chunks + 2, late_second)
    steps.at(chunks + 2, functools.partial(b_planes, 2))
    steps.at(chunks + cut, late_third)
    steps.at(chunks + cut, lambda: arrived(far_h()))
    steps.at(chunks + cut, lambda: start(far_c()))
    places = (chunks + cut_two, chunks + cut_two + 2, 2 * chunks, 2 * chunks, 2 * chunks + 2, 2 * chunks + cut_two)
    split_sum(nd, nz, steps, places, early_two, late_two, sums_all, two_early, two_late)
    later_steps = (chunks + cut_two + 1, 2 * chunks + 1, 2 * chunks + cut_two)
    for k in range(nz - 1):
        group = 3 * k // (nz - 1)
        steps.at(later_steps[group], functools.partial(h_planes, k))
        steps.at((2 * chunks + 2, 3 * chunks, 4 * chunks - 3)[group], functools.partial(h_twin, k))
    steps.at(2 * chunks - 1, b_whole)
    steps.at(chunks - 1, functools.partial(b_twins, 0))
    steps.at(chunks + 3, functools.partial(b_twins, 1))
    steps.at(2 * chunks - 3, functools.partial(b_twins, 2))
    steps.emit(step, 4 * chunks)

    @pl.when(step < chunks)
    def _():
        j = step
        mixed = mix_kernels(kern_ref[...], mix[...])
        one = jnp.zeros((1, LANES), f32)
        two = jnp.zeros((1, LANES), f32)
        for b in range(nb):
            at = slice(b * PIXELS, (b + 1) * PIXELS)
            lane = slice(b * LANES, (b + 1) * LANES)
            taps[j, b] = mixed[WIDTH_IN : WIDTH_IN + 32, lane]
            taps_out[b] = mixed[WIDTH_IN : WIDTH_IN + 32, lane]
            value = dot(images[at, :], mixed[:WIDTH_IN, lane].astype(bf16))
            pre[j, at, :] = value
            pre_out[at, :] = value
            masked = mask[at, :] * value
            one = one + rsum(masked)
            two = two + rsum(masked * value)

        @pl.when(j < cut)
        def _():
            early[pl.ds(j, 1), :] = one
            early[pl.ds(chunks + j, 1), :] = two

        @pl.when(j >= cut)
        def _():
            late[pl.ds(j, 1), :] = one
            late[pl.ds(chunks + j, 1), :] = two

    @pl.when((step >= chunks) & (step < 2 * chunks))
    def _():
        j = step - chunks
        mean, rstd = norm_rows(stats_all, j, chunks, stats_all[2 * chunks : 2 * chunks + 1, :])
        scale = rstd * side[2 * SQUEEZE : 2 * SQUEEZE + 1, :]
        bias = side[2 * SQUEEZE + 1 : 2 * SQUEEZE + 2, :]
        held[...] = jnp.zeros_like(held)

        @pl.loop(0, nb)
        def _(b):
            at = image(b)
            normed = (pre[j, at, :] - mean) * scale + bias
            act = normed * sig(normed) * mask[at, :]
            for s in range(KERNEL):
                buf[s] = shifted(act, s - KERNEL // 2)
            taps_now = [jnp.broadcast_to(taps[j, b, t : t + 1, :], (MAP_SIDE, LANES)) for t in range(TAPS)]
            acc = [None] * MAP_SIDE
            for y in range(MAP_SIDE):
                for s in range(KERNEL):
                    x = buf[s, y * MAP_SIDE : (y + 1) * MAP_SIDE, :]
                    for r in range(KERNEL):
                        i = y - r + KERNEL // 2
                        if 0 <= i < MAP_SIDE:
                            term = taps_now[r * KERNEL + s] * x
                            acc[i] = term if acc[i] is None else acc[i] + term
                done = [y - 2] if y < MAP_SIDE - 1 else [y - 2, y - 1, y]
                for i in done:
                    if i >= 0:
                        out[pl.ds(pl.multiple_of(b * PIXELS + i * MAP_SIDE, MAP_SIDE), MAP_SIDE), :] = acc[i]
            value = out[at, :]
            dpre[j, at, :] = value
            masked = mask[at, :] * value
            held[0:1, :] += rsum(masked)
            held[1:2, :] += rsum(masked * value)

        store_sums(early_two, late_two, cut_two, chunks, j, held[0:1, :], held[1:2, :])

    total = stats_all[2 * chunks : 2 * chunks + 1, :]

    @pl.when((step >= 2 * chunks) & (step < 3 * chunks))
    def _():
        j = step - 2 * chunks
        lane = pl.ds(pl.multiple_of(j * LANES, LANES), LANES)
        load(j).wait()

        @pl.when(j + 1 < chunks)
        def _():
            load(j + 1).start()

        both = mix_kernels(kern_buf[lax.rem(j, 2)], mix[...])
        for b in range(nb):
            mixed[b, :, lane] = both[:, b * LANES : (b + 1) * LANES].astype(bf16)
        mean, rstd = norm_rows(sums_all, j, chunks, total)
        scale = rstd * side[2 * SQUEEZE + 2 : 2 * SQUEEZE + 3, :]
        bias = side[2 * SQUEEZE + 3 : 2 * SQUEEZE + 4, :]
        for b in range(nb):
            at = slice(b * PIXELS, (b + 1) * PIXELS)
            normed = (dpre[j, at, :] - mean) * scale + bias
            value = normed * sig(normed) * mask[at, :]
            dpre[j, at, :] = value
            pool_out[b : b + 1, lane] = rsum(value) / jnp.maximum(counts[b : b + 1, :], 1.0)
        squeezed[...] += dot(pool_out[:, lane], side[0:SQUEEZE, :], NT, highest)

    @pl.when(step >= 3 * chunks)
    def _():
        j = step - 3 * chunks
        lane = pl.ds(pl.multiple_of(j * LANES, LANES), LANES)
        before = squeezed[...] + sq_bias[...]
        gate = sig(
            dot(before * sig(before), side[SQUEEZE : 2 * SQUEEZE, :], NN, highest)
            + side[2 * SQUEEZE + 4 : 2 * SQUEEZE + 5, :]
        )
        gate_out[:, lane] = gate
        for b in range(nb):
            at = slice(b * PIXELS, (b + 1) * PIXELS)
            value = (dpre[j, at, :] * gate[b : b + 1, :]).astype(bf16)
            excited[at, :] = value
            exc[at, lane] = value

    @pl.when(step == 4 * chunks - 1)
    def _():
        one = jnp.zeros((1, WIDTH_OUT), f32)
        two = jnp.zeros((1, WIDTH_OUT), f32)
        for b in range(nb):
            at = slice(b * PIXELS, (b + 1) * PIXELS)
            value = dot(exc[at, :], mixed[b], NT)
            proj[at, :] = value
            masked = mask[at, 0:1] * value
            one = one + rsum(masked)
            two = two + rsum(masked * value)
        store_wide(sums_three, 0, one)
        store_wide(sums_three, OUT_CHUNKS, two)
        sum_finish(nd, nz, sums_three, last_all, *comm_two)
        for k in range(nz - 1):
            arrived(twins_h(k))
            sent(planes_b(k) + twins_b(k) + twins_h(k))
        arrived(far_c())
        sent(far_h() + planes_h() + far_c())
        for copy in own():
            copy.wait()


def first_stage(kern, images, mask, mask_rows, counts, route, side, sq_bias, full_b, kh, kc, nb, width, nd, nz, ident):
    chunks = width // LANES
    rows = nb * PIXELS
    deep = LANES * EXPERTS
    planes = (nz - 1) * (nd // 2 - 1)
    shapes = (shard_shape(full_b, nz), kh.shape, kc.shape)
    hbm = pl.BlockSpec(memory_space=pltpu.HBM)
    before = lambda t: jnp.minimum(t, chunks - 1)
    after = lambda t: jnp.clip(t - chunks, 0, chunks - 1)
    cycled = lambda t: lax.rem(t, chunks)
    return pl.pallas_call(
        functools.partial(stage_kernel, nd, nz, nb, chunks, shapes),
        grid=(4 * chunks,),
        out_shape=[
            jax.ShapeDtypeStruct((rows, width), f32),
            jax.ShapeDtypeStruct((nb, 32, width), f32),
            jax.ShapeDtypeStruct((rows, width), f32),
            jax.ShapeDtypeStruct((24, LANES), f32),
            jax.ShapeDtypeStruct((24, LANES), f32),
            jax.ShapeDtypeStruct((deep, 2 * nb * LANES), bf16),
            jax.ShapeDtypeStruct((8, EXPERTS), f32),
            jax.ShapeDtypeStruct((8, WIDTH_IN), f32),
            jax.ShapeDtypeStruct((rows, width), bf16),
            jax.ShapeDtypeStruct((rows, WIDTH_OUT), f32),
            jax.ShapeDtypeStruct((8, width), f32),
            jax.ShapeDtypeStruct((8, width), f32),
            jax.ShapeDtypeStruct((8, SQUEEZE), f32),
            jax.ShapeDtypeStruct((8, LANES), f32),
            jax.ShapeDtypeStruct((nb, WIDTH_OUT, width), bf16),
            jax.ShapeDtypeStruct(full_b.shape, bf16),
            jax.ShapeDtypeStruct((kh.shape[0], nz * kh.shape[1]), bf16),
            jax.ShapeDtypeStruct((nz,) + kc.shape, bf16),
        ],
        in_specs=[
            pl.BlockSpec((kern.shape[0], deep), lambda t: (0, before(t))),
            whole(images.shape),
            whole(mask.shape),
            whole(mask_rows.shape),
            whole(counts.shape),
            whole(route.shape),
            pl.BlockSpec((side.shape[0], LANES), lambda t: (0, cycled(t))),
            whole(sq_bias.shape),
            hbm,
            whole(kh.shape),
            whole(kc.shape),
        ],
        out_specs=[
            pl.BlockSpec((rows, LANES), lambda t: (0, before(t))),
            pl.BlockSpec((nb, 32, LANES), lambda t: (0, 0, before(t))),
            pl.BlockSpec((rows, LANES), lambda t: (0, after(t))),
            whole((24, LANES)),
            whole((24, LANES)),
            whole((deep, 2 * nb * LANES)),
            whole((8, EXPERTS)),
            whole((8, WIDTH_IN)),
            pl.BlockSpec((rows, LANES), lambda t: (0, jnp.maximum(t - 3 * chunks, 0))),
            whole((rows, WIDTH_OUT)),
            whole((8, width)),
            whole((8, width)),
            whole((8, SQUEEZE)),
            whole((8, LANES)),
            whole((nb, WIDTH_OUT, width)),
            hbm,
            hbm,
            hbm,
        ],
        scratch_shapes=[
            VMEM((chunks, rows, LANES), f32),
            VMEM((chunks, nb, 32, LANES), f32),
            VMEM((KERNEL, PIXELS, LANES), f32),
            VMEM((8, LANES), f32),
            VMEM((24, LANES), f32),
            VMEM((24, LANES), f32),
            VMEM((24, LANES), f32),
            VMEM((24, LANES), f32),
            VMEM((8, LANES), f32),
            VMEM((chunks, rows, LANES), f32),
            VMEM((rows, width), bf16),
            VMEM((2, WIDTH_OUT, deep), bf16),
        ]
        + sum_scratch(24, nd, nz)[1:] * 2
        + sum_scratch(8, nd, nz)[1:]
        + sum_scratch(24, nd, nz)[1:] * 2
        + pair(nz - 1) * 2
        + pair(planes) * 2
        + pair(nz - 1)
        + [pltpu.SemaphoreType.DMA((2,))]
        + pair(nz - 1)
        + [pltpu.SemaphoreType.DMA((2,))],
        input_output_aliases={8: 15},
        compiler_params=params(ident),
        name="first_stage",
    )(kern, images, mask, mask_rows, counts, route, side, sq_bias, full_b, kh, kc)


def store_wide(ref, row, value):
    width = value.shape[1]
    for k in range(-(-width // LANES)):
        lanes = min(LANES, width - k * LANES)
        ref[row + k : row + k + 1, :lanes] = value[:, k * LANES : k * LANES + lanes]


def load_wide(ref, row, width):
    parts = []
    for k in range(-(-width // LANES)):
        lanes = min(LANES, width - k * LANES)
        parts.append(ref[row + k : row + k + 1, :lanes])
    return jnp.concatenate(parts, axis=1)


OUT_CHUNKS = -(-WIDTH_OUT // LANES)


def out_norm(sums, total):
    mean = load_wide(sums, 0, WIDTH_OUT) / total
    var = load_wide(sums, OUT_CHUNKS, WIDTH_OUT) / total - mean * mean
    return mean, lax.rsqrt(var + eps_norm)


def store_sums(early, late, cut, chunks, j, one, two):
    @pl.when(j < cut)
    def _():
        early[pl.ds(j, 1), :] = one
        early[pl.ds(chunks + j, 1), :] = two

    @pl.when(j >= cut)
    def _():
        late[pl.ds(j, 1), :] = one
        late[pl.ds(chunks + j, 1), :] = two


def split_sum(nd, nz, steps, at, early, late, out, comm_early, comm_late):
    def early_third():
        out[...] = sum_third(nd, nz, early, *comm_early)

    def late_third():
        out[...] += sum_third(nd, nz, late, *comm_late)

    steps.at(at[0], lambda: sum_first(nd, nz, early, *comm_early))
    steps.at(at[1], lambda: sum_second(nd, nz, early, *comm_early))
    steps.at(at[2], early_third)
    steps.at(at[3], lambda: sum_first(nd, nz, late, *comm_late))
    steps.at(at[4], lambda: sum_second(nd, nz, late, *comm_late))
    steps.at(at[5], late_third)


def head_back_kernel(
    nd,
    nz,
    nb,
    chunks,
    shape,
    shape_c,
    mask,
    mask_rows,
    counts,
    labels,
    bias,
    gain,
    totals,
    gain_out,
    kern,
    route,
    proj,
    proj_stats,
    in_c,
    head_pool,
    stats,
    features,
    grad_logits,
    sums_four,
    grad_out,
    sums_all,
    dz_out,
    half,
    part,
    full_c,
    pre_all,
    low,
    low_t,
    mixed,
    mix,
    gates,
    cls,
    early_head,
    late_head,
    logits,
    grad_features,
    held,
    grads,
    gate_acc,
    early,
    late,
    sums,
    *comm,
):
    step = pl.program_id(0)
    phase = step // chunks
    j = lax.rem(step, chunks)
    net = Net(nd, nz)
    comm_early, comm_late, comm_two, comm = comm[0:6], comm[6:12], comm[12:18], comm[18:]
    head_early, head_late, sems, comm = comm[0:6], comm[6:12], comm[12:17], comm[17:]
    twin = Twin(net, shape, half, *comm[0:4])
    plane = Plane(net, shape, half, part, 0, nz // 2, *comm[4:7])
    made = comm[0]
    cut = chunks // 3
    head_cut = 2 * chunks // 3
    base = 3 * chunks
    steps = Steps()

    def planes():
        return every(gather_plane, net, shape_c, full_c, sems[0:2])

    def twins():
        return every(gather_twin, net, shape_c, full_c, sems[2:4])

    def load():
        own_rows = cls.shape[0] // nz
        return [
            pltpu.make_async_copy(
                full_c.at[k, pl.ds(0, own_rows)], cls.at[pl.ds(k * own_rows, own_rows)], sems[4].at[k]
            )
            for k in range(nz)
        ]

    def begin():
        met(nd, nz)
        start(planes())

    def cross():
        arrived(planes())
        start(twins())

    def fetch():
        arrived(twins())
        start(load())

    def loaded():
        for copy in load():
            copy.wait()

    steps.at(1, begin)
    steps.at(head_cut - 1, cross)
    steps.at(chunks - 1, fetch)
    steps.at(chunks, loaded)
    places = (head_cut, head_cut + 2, chunks, chunks, chunks + 2, chunks + head_cut)
    split_sum(nd, nz, steps, places, early_head, late_head, stats, head_early, head_late)
    places = (2 * chunks + cut, 2 * chunks + cut + 3, base, base, base + 1, base + cut)
    split_sum(nd, nz, steps, places, early, late, sums_four, comm_early, comm_late)
    for k in range(nz):
        first = base + ready(shape, k)
        steps.at(first, functools.partial(twin.begin, k))
        steps.at(first + 2, functools.partial(twin.add, k))
        if k < nz // 2:
            steps.at(first + 2, functools.partial(plane.begin, k))

    @pl.when(step == 0)
    def _():
        sum_start(nd, nz)
        for ref in (sums, early, late, early_head, late_head, features, logits, gate_acc):
            ref[...] = jnp.zeros_like(ref)
        mean, rstd = out_norm(proj_stats, totals[TOTAL_ROW : TOTAL_ROW + 1, 0:1])
        scale = rstd * gain_out[0:1, :]
        for b in range(nb):
            at = slice(b * PIXELS, (b + 1) * PIXELS)
            low[at, :] = (((proj[at, :] - mean) * scale + gain_out[1:2, :]) * mask[at, 0:1]).astype(bf16)
            low_t[b] = jnp.transpose(low[at, :])
        pool = dot(mask_rows[...], low[...]) / jnp.maximum(counts[:, 0:1], 1.0)
        head_pool[...] = pool
        gate = sig(dot(pool, route[...], NN, highest))
        gates[...] = gate
        build_mix(gate, nb, mix)
        if shape[0] > WIDTH_OUT:
            made[WIDTH_OUT:, :] = jnp.zeros((shape[0] - WIDTH_OUT, made.shape[1]), bf16)

    steps.emit(step, 4 * chunks)
    pre = pre_all.at[j]

    @pl.when(phase == 0)
    def _():
        lane = pl.ds(pl.multiple_of(j * LANES, LANES), LANES)
        both = mix_kernels(kern[...], mix[...])
        one = jnp.zeros((1, LANES), f32)
        two = jnp.zeros((1, LANES), f32)
        for b in range(nb):
            at = slice(b * PIXELS, (b + 1) * PIXELS)
            weight = both[:, b * LANES : (b + 1) * LANES].astype(bf16)
            mixed[b, :, lane] = weight
            value = dot(low[at, :], weight)
            pre[at, :] = value
            masked = mask[at, :] * value
            one = one + rsum(masked)
            two = two + rsum(masked * value)
        store_sums(early_head, late_head, head_cut, chunks, j, one, two)

    lane = pl.ds(pl.multiple_of(j * LANES, LANES), LANES)
    total = totals[TOTAL_ROW : TOTAL_ROW + 1, :]
    mean, rstd = norm_rows(stats, j, chunks, total)
    scale = rstd * gain[0:1, :]

    @pl.when(phase == 1)
    def _():
        for b in range(nb):
            at = slice(b * PIXELS, (b + 1) * PIXELS)
            normed = (pre[at, :] - mean) * scale + gain[1:2, :]
            features[b : b + 1, lane] = rsum(normed * sig(normed) * mask[at, :]) / jnp.maximum(
                counts[b : b + 1, :], 1.0
            )
        both = dot(split(features[:, lane]), cls[lane, :])
        logits[...] += both[:8] + both[8:]

    @pl.when((phase == 2) & (j == 0))
    def _():
        col = lax.broadcasted_iota(jnp.int32, (8, CLASS_PAD), 1)
        inside = col < CLASSES
        scores = jnp.where(inside, logits[...] + bias[...], -1e30)
        top = jnp.max(scores, axis=1, keepdims=True)
        spread = jnp.where(inside, jnp.exp(scores - top), 0.0)
        mass = jnp.sum(spread, axis=1, keepdims=True)
        hot = jnp.where(col == labels[:, 0:1], 1.0, 0.0)
        shifted_scores = jnp.where(inside, scores - top - jnp.log(mass), 0.0)
        per_image = -(
            0.9 * jnp.sum(shifted_scores * hot, axis=1, keepdims=True)
            + (0.1 / CLASSES) * jnp.sum(shifted_scores, axis=1, keepdims=True)
        )
        valid = jnp.where(counts[:, 0:1] > 0.0, 1.0, 0.0)
        early[2 * chunks : 2 * chunks + 1, :] = jnp.broadcast_to(rsum(per_image * valid), (1, LANES))
        weight = valid / totals[TOTAL_ROW + 1 : TOTAL_ROW + 2, 0:1]
        grad_logits[...] = weight * jnp.where(inside, spread / mass - 0.9 * hot - 0.1 / CLASSES, 0.0)

    @pl.when(phase == 2)
    def _():
        both = dot(split(grad_logits[...]), cls[lane, :], NT)
        grads = (both[:8] + both[8:]) / jnp.maximum(counts[...], 1.0)
        grad_features[:, lane] = grads
        one = jnp.zeros((1, LANES), f32)
        two = jnp.zeros((1, LANES), f32)
        for b in range(nb):
            at = slice(b * PIXELS, (b + 1) * PIXELS)
            hat = (pre[at, :] - mean) * rstd
            grad = mask[at, :] * dsilu(hat * gain[0:1, :] + gain[1:2, :]) * grads[b : b + 1, :]
            one = one + rsum(grad)
            two = two + rsum(grad * hat)
        store_sums(early, late, cut, chunks, j, one, two)

    @pl.when(phase == 3)
    def _():
        one = sums_four[pl.ds(j, 1), :] / total
        two = sums_four[pl.ds(chunks + j, 1), :] / total
        for b in range(nb):
            at = slice(b * PIXELS, (b + 1) * PIXELS)
            hat = (pre[at, :] - mean) * rstd
            grad = dsilu(hat * gain[0:1, :] + gain[1:2, :]) * grad_features[b : b + 1, lane]
            value = (scale * mask[at, :] * (grad - one - hat * two)).astype(bf16)
            held[at, lane] = value
            grads[:, b * LANES : (b + 1) * LANES] = dot(low_t[b], value).astype(bf16)
        gate_acc[0:nb, :] += gate_rows(grads[...], kern[...], nb)
        made[:WIDTH_OUT, lanes(j * LANES * EXPERTS, LANES * EXPERTS)] = dot(grads[...], mix[:, : nb * LANES], NT).astype(bf16)

    @pl.when(step == 4 * chunks - 1)
    def _():
        dz = gate_sums(gate_acc[...]) * gates[...] * (1.0 - gates[...])
        dz_out[...] = dz
        pool_grad = dot(dz, route[...], NT, highest) / jnp.maximum(counts[:, 0:1], 1.0)
        mean, rstd = out_norm(proj_stats, total[:, 0:1])
        one = jnp.zeros((1, WIDTH_OUT), f32)
        two = jnp.zeros((1, WIDTH_OUT), f32)
        for b in range(nb):
            at = slice(b * PIXELS, (b + 1) * PIXELS)
            value = (dot(held[at, :], mixed[b], NT) + pool_grad[b : b + 1, :]) * mask[at, 0:1]
            grad_out[at, :] = value
            one = one + rsum(value)
            two = two + rsum(value * ((proj[at, :] - mean) * rstd))
        store_wide(sums, 0, one)
        store_wide(sums, OUT_CHUNKS, two)
        last = [k for k in range(nz) if ready(shape, k) >= chunks]
        sum_first(nd, nz, sums, *comm_two)
        for k in last:
            twin.begin(k)
        sum_second(nd, nz, sums, *comm_two)
        sums_all[...] = sum_third(nd, nz, sums, *comm_two)
        for k in range(nz):
            if ready(shape, k) + 2 >= chunks:
                twin.add(k)
                if k < nz // 2:
                    plane.begin(k)
        plane.add()
        twin.finish()
        plane.finish()
        sent(planes() + twins())


def head_stage(mask, mask_rows, counts, labels, bias, gain, totals, gain_out, kern, route, proj, proj_stats, full_c, nb, nd, nz, ident):
    rows = proj.shape[0]
    width = kern.shape[1] // EXPERTS
    chunks = width // LANES
    deep = LANES * EXPERTS
    shape = (kern.shape[0], kern.shape[1] // nz)
    hbm = pl.BlockSpec(memory_space=pltpu.HBM)
    kept = lambda t: (0, jnp.where(t < chunks, t, jnp.maximum(t - 3 * chunks, 0)))
    return pl.pallas_call(
        functools.partial(head_back_kernel, nd, nz, nb, chunks, shape, shard_shape(full_c, nz)),
        grid=(4 * chunks,),
        out_shape=[
            jax.ShapeDtypeStruct((8, WIDTH_OUT), f32),
            jax.ShapeDtypeStruct((24, LANES), f32),
            jax.ShapeDtypeStruct((8, width), f32),
            jax.ShapeDtypeStruct((8, CLASS_PAD), f32),
            jax.ShapeDtypeStruct((24, LANES), f32),
            jax.ShapeDtypeStruct((rows, WIDTH_OUT), f32),
            jax.ShapeDtypeStruct((8, LANES), f32),
            jax.ShapeDtypeStruct((8, EXPERTS), f32),
            jax.ShapeDtypeStruct(half_shape(shape, nd, nz), bf16),
            jax.ShapeDtypeStruct(part_shape(shape, nd, nz // 2), bf16),
            jax.ShapeDtypeStruct(full_c.shape, bf16),
        ],
        in_specs=[
            whole(mask.shape),
            whole(mask_rows.shape),
            whole(counts.shape),
            whole(labels.shape),
            whole(bias.shape),
            pl.BlockSpec((8, LANES), lambda t: (0, lax.rem(t, chunks))),
            whole(totals.shape),
            whole(gain_out.shape),
            pl.BlockSpec((WIDTH_OUT, deep), kept),
            whole(route.shape),
            whole(proj.shape),
            whole(proj_stats.shape),
            hbm,
        ],
        out_specs=[
            whole((8, WIDTH_OUT)),
            whole((24, LANES)),
            whole((8, width)),
            whole((8, CLASS_PAD)),
            whole((24, LANES)),
            whole((rows, WIDTH_OUT)),
            whole((8, LANES)),
            whole((8, EXPERTS)),
            whole(half_shape(shape, nd, nz)),
            whole(part_shape(shape, nd, nz // 2)),
            hbm,
        ],
        scratch_shapes=[
            VMEM((chunks, rows, LANES), f32),
            VMEM((rows, WIDTH_OUT), bf16),
            VMEM((nb, WIDTH_OUT, PIXELS), bf16),
            VMEM((nb, WIDTH_OUT, width), bf16),
            VMEM((deep, 2 * nb * LANES), bf16),
            VMEM((8, EXPERTS), f32),
            VMEM((width, CLASS_PAD), bf16),
            VMEM((24, LANES), f32),
            VMEM((24, LANES), f32),
            VMEM((8, CLASS_PAD), f32),
            VMEM((8, width), f32),
            VMEM((rows, width), bf16),
            VMEM((WIDTH_OUT, nb * LANES), bf16),
            VMEM((8, deep), f32),
            VMEM((24, LANES), f32),
            VMEM((24, LANES), f32),
            VMEM((8, LANES), f32),
        ]
        + sum_scratch(24, nd, nz)[1:] * 2
        + sum_scratch(8, nd, nz)[1:]
        + sum_scratch(24, nd, nz)[1:] * 2
        + pair((nz - 1) * (nd // 2 - 1))
        + pair(nz - 1)
        + [pltpu.SemaphoreType.DMA((nz,))]
        + twin_scratch(shape, nd, nz)
        + plane_scratch(shape, nd, nz // 2),
        input_output_aliases={12: 10},
        compiler_params=params(ident),
        name="head_stage",
    )(mask, mask_rows, counts, labels, bias, gain, totals, gain_out, kern, route, proj, proj_stats, full_c)


def project_back_kernel(nd, nz, nb, chunks, shape_h, shape, half_h, part_h, grad_in, proj, proj_stats, proj_sums, gain, mask, counts, totals, stats, side, dpre, excited, mixed, kern, mix, gate, pooled, squeezed, sq_bias, grad_norm, sums_all, grad_squeeze, gate_grad, dz_gate, piece_h, half, part, low, low_t, held, grads, gate_acc, sums_h, sums, *comm):
    phase = pl.program_id(0)
    net = Net(nd, nz)
    few = nz // 2
    cut_one = 12
    plane_h = Plane(net, shape_h, half_h, sums_h, few, nz - few, *comm[6:9])
    far = Far(net, shape_h, sums_h, piece_h, *comm[9:cut_one])
    twin = Twin(net, shape, half, *comm[cut_one : cut_one + 4])
    plane = Plane(net, shape, half, part, 0, few, *comm[cut_one + 4 : cut_one + 7])
    made = comm[cut_one]
    comm = comm[:6]
    steps = Steps()

    def begin():
        met(nd, nz)
        for k in plane_h.shards:
            plane_h.begin(k)
        sums_h[0:few] = part_h[...]
        for k in range(few):
            far.send(k)

    steps.at(1, begin)
    steps.at(chunks + 3, functools.partial(plane_h.add, far.send))
    for k in range(nz):
        first = ready(shape, k)
        steps.at(first, functools.partial(twin.begin, k))
        steps.at(first + 3, functools.partial(twin.add, k))
        if k < few:
            steps.at(first + 3, functools.partial(plane.begin, k))
    j = pl.program_id(1)

    @pl.when((phase == 0) & (j == 0))
    def _():
        sum_start(nd, nz)

    steps.emit(phase * chunks + j, 2 * chunks)
    lane = pl.ds(pl.multiple_of(j * LANES, LANES), LANES)
    total = totals[TOTAL_ROW : TOTAL_ROW + 1, :]

    @pl.when((phase == 0) & (j == 0))
    def _():
        gate_acc[...] = jnp.zeros_like(gate_acc)
        if shape[0] > WIDTH_OUT:
            made[WIDTH_OUT:, :] = jnp.zeros((shape[0] - WIDTH_OUT, made.shape[1]), bf16)
        sums[...] = jnp.zeros_like(sums)
        grad_squeeze[...] = jnp.zeros_like(grad_squeeze)
        dz_gate[...] = jnp.zeros_like(dz_gate)
        mean, rstd = out_norm(proj_stats, total[:, 0:1])
        scale = rstd * gain[0:1, :]
        one = load_wide(proj_sums, 0, WIDTH_OUT) / total[:, 0:1]
        two = load_wide(proj_sums, OUT_CHUNKS, WIDTH_OUT) / total[:, 0:1]
        for b in range(nb):
            at = slice(b * PIXELS, (b + 1) * PIXELS)
            hat = (proj[at, :] - mean) * rstd
            low[at, :] = (scale * (grad_in[at, :] - mask[at, 0:1] * (one + hat * two))).astype(bf16)
            low_t[b] = jnp.transpose(low[at, :])

    mean, rstd = norm_rows(stats, j, chunks, total)
    gain_now = side[2 * SQUEEZE + 2 : 2 * SQUEEZE + 3, :]
    bias_now = side[2 * SQUEEZE + 3 : 2 * SQUEEZE + 4, :]

    @pl.when(phase == 0)
    def _():
        for b in range(nb):
            at = slice(b * PIXELS, (b + 1) * PIXELS)
            grads[:, b * LANES : (b + 1) * LANES] = dot(low_t[b], excited[at, :]).astype(bf16)
            value = dot(low[at, :], mixed[b])
            held[j, at, :] = value
            normed = (dpre[at, :] - mean) * (rstd * gain_now) + bias_now
            act = normed * sig(normed) * mask[at, :]
            now = gate[b : b + 1, :]
            dz_gate[b : b + 1, lane] = rsum(value * act) * now * (1.0 - now)
        gate_acc[0:nb, :] += gate_rows(grads[...], kern[...], nb)
        made[:WIDTH_OUT, lanes(j * LANES * EXPERTS, LANES * EXPERTS)] = dot(grads[...], mix[:, : nb * LANES], NT).astype(bf16)
        grad_squeeze[...] += dot(dz_gate[:, lane], side[SQUEEZE : 2 * SQUEEZE, :], NT, highest)

    @pl.when((phase == 1) & (j == 0))
    def _():
        grad_squeeze[...] = grad_squeeze[...] * dsilu(squeezed[...] + sq_bias[...])
        gate_grad[...] = gate_sums(gate_acc[...])

    @pl.when(phase == 1)
    def _():
        pool_grad = dot(grad_squeeze[...], side[0:SQUEEZE, :], NN, highest) / jnp.maximum(counts[...], 1.0)
        one = jnp.zeros((1, LANES), f32)
        two = jnp.zeros((1, LANES), f32)
        for b in range(nb):
            at = slice(b * PIXELS, (b + 1) * PIXELS)
            hat = (dpre[at, :] - mean) * rstd
            grad = held[j, at, :] * gate[b : b + 1, :] + pool_grad[b : b + 1, :]
            value = mask[at, :] * grad * dsilu(hat * gain_now + bias_now)
            grad_norm[at, :] = value
            one = one + rsum(value)
            two = two + rsum(value * hat)
        sums[pl.ds(j, 1), :] = one
        sums[pl.ds(chunks + j, 1), :] = two

    @pl.when((phase == 1) & (j == chunks - 1))
    def _():
        sum_finish(nd, nz, sums, sums_all, *comm)
        far.add()
        plane.add()
        far.finish()
        twin.finish()
        plane.finish()
        plane_h.finish()


def project_back(half_h, part_h, shape_h, grad_in, proj, proj_stats, proj_sums, gain, mask, counts, totals, stats, side, dpre, excited, mixed, kern, mix, gate, pooled, squeezed, sq_bias, nb, nd, nz, ident):
    rows, width = dpre.shape
    shape = (kern.shape[0], kern.shape[1] // nz)
    few = nz // 2
    chunks = width // LANES
    deep = LANES * EXPERTS
    wide = lambda p, j: (0, j)
    early = lambda p, j: (0, jnp.where(p == 0, j, chunks - 1))
    late = lambda p, j: (0, jnp.where(p == 0, 0, j))
    return pl.pallas_call(
        functools.partial(project_back_kernel, nd, nz, nb, chunks, shape_h, shape),
        grid=(2, chunks),
        out_shape=[
            jax.ShapeDtypeStruct((rows, width), f32),
            jax.ShapeDtypeStruct((24, LANES), f32),
            jax.ShapeDtypeStruct((8, SQUEEZE), f32),
            jax.ShapeDtypeStruct((8, EXPERTS), f32),
            jax.ShapeDtypeStruct((8, width), f32),
            jax.ShapeDtypeStruct(piece_shape(shape_h, nd), bf16),
            jax.ShapeDtypeStruct(half_shape(shape, nd, nz), bf16),
            jax.ShapeDtypeStruct(part_shape(shape, nd, few), bf16),
        ],
        in_specs=[
            whole(half_h.shape),
            whole(part_h.shape),
            whole(grad_in.shape),
            whole(proj.shape),
            whole(proj_stats.shape),
            whole(proj_sums.shape),
            whole(gain.shape),
            whole(mask.shape),
            whole(counts.shape),
            whole(totals.shape),
            whole(stats.shape),
            pl.BlockSpec((side.shape[0], LANES), wide),
            pl.BlockSpec((rows, LANES), wide),
            pl.BlockSpec((rows, LANES), early),
            pl.BlockSpec((nb, WIDTH_OUT, LANES), lambda p, j: (0, 0, jnp.where(p == 0, j, chunks - 1))),
            pl.BlockSpec((WIDTH_OUT, deep), early),
            whole(mix.shape),
            pl.BlockSpec((8, LANES), wide),
            pl.BlockSpec((8, LANES), wide),
            whole(squeezed.shape),
            whole(sq_bias.shape),
        ],
        out_specs=[
            pl.BlockSpec((rows, LANES), late),
            whole((24, LANES)),
            whole((8, SQUEEZE)),
            whole((8, EXPERTS)),
            whole((8, width)),
            whole(piece_shape(shape_h, nd)),
            whole(half_shape(shape, nd, nz)),
            whole(part_shape(shape, nd, few)),
        ],
        scratch_shapes=[
            VMEM((rows, WIDTH_OUT), bf16),
            VMEM((nb, WIDTH_OUT, PIXELS), bf16),
            VMEM((chunks, rows, LANES), f32),
            VMEM((WIDTH_OUT, nb * LANES), bf16),
            VMEM((8, deep), f32),
            VMEM(part_shape(shape_h, nd, nz), bf16),
        ]
        + sum_scratch(24, nd, nz)
        + plane_scratch(shape_h, nd, nz - few)
        + far_scratch(shape_h, nd, nz)
        + twin_scratch(shape, nd, nz)
        + plane_scratch(shape, nd, few),
        compiler_params=params(ident),
        name="project_back",
    )(half_h, part_h, grad_in, proj, proj_stats, proj_sums, gain, mask, counts, totals, stats, side, dpre, excited, mixed, kern, mix, gate, pooled, squeezed, sq_bias)


def dz_slots(nb, devices):
    per = max(1, min(devices, LANES // (nb * EXPERTS)))
    return per, -(-devices // (per * 8)) * 8


def stage_back_kernel(
    nd,
    nz,
    nb,
    chunks,
    shape,
    shape_b,
    shape_h,
    cuts_one,
    cuts_two,
    half_b,
    part_b,
    piece_h,
    grad_in,
    dpre,
    pre,
    taps,
    mask,
    side,
    stats_one,
    stats_two,
    sums_two,
    totals,
    features,
    logits,
    pooled,
    dz_gate,
    head_pool,
    pooled_in,
    grad_sq,
    before,
    sq_bias_in,
    dz_head,
    images,
    kern,
    mix,
    gates,
    gate_grad,
    squares_w,
    stats_three,
    stats_four,
    sums_four,
    chan_old,
    head_old,
    proj_old,
    done,
    done_b,
    done_h,
    grad_cls,
    grad_side_out,
    factors,
    route_in,
    route_head,
    sq_bias,
    class_bias,
    chan_new,
    head_new,
    proj_new,
    loss,
    made_norm,
    tap_grads,
    buf,
    acts,
    held,
    early,
    late,
    sums_one,
    sums_b,
    piece_b,
    rows_all,
    images_t,
    grads,
    gate_acc,
    grad_side,
    every_sum,
    low,
    half,
    sums,
    piece,
    *comm,
):
    step = pl.program_id(0)
    net = Net(nd, nz)
    few = nz // 2
    cut = 2 * chunks // 3
    comm_early, comm_late, comm_two, comm = comm[0:6], comm[6:12], comm[12:18], comm[18:]
    plane_b = Plane(net, shape_b, half_b, sums_b, few, nz - few, *comm[0:3], shift=few)
    far_b = Far(net, shape_b, sums_b, piece_b, *comm[3:6])
    up_b = Spread(net, shape_b, piece_b, done_b, *comm[6:11])
    up_h = Spread(net, shape_h, piece_h, done_h, *comm[11:16])
    share = Share(net, rows_all, *comm[16:24])
    comm = comm[24:]
    twin = Twin(net, shape, half, *comm[0:4])
    made = comm[0]
    plane = Plane(net, shape, half, sums, 0, nz, *comm[4:7])
    far = Far(net, shape, sums, piece, *comm[7:10])
    up = Spread(net, shape, piece, done, *comm[10:15])
    steps = Steps()
    first_planes = range(few, few + (nz - few + 1) // 2)
    last_planes = range(first_planes.stop, nz)

    def begin():
        met(nd, nz)
        up_h.begin()
        for k in first_planes:
            plane_b.begin(k)
        sums_b[0:few] = part_b[...]
        for k in range(few):
            far_b.send(k)
        share.far()

    def more_planes():
        for k in last_planes:
            plane_b.begin(k)

    def far_end():
        far_b.add()
        up_b.begin()

    steps.at(1, begin)
    steps.at(4, up_h.cross)
    split_sum(
        nd,
        nz,
        steps,
        (cut, cut + 2, chunks, chunks, chunks + 2, chunks + cut - 1),
        early,
        late,
        sums_one,
        comm_early,
        comm_late,
    )
    steps.at(2, more_planes)
    steps.at(cut + 2, share.plane)
    steps.at(chunks - 2, functools.partial(plane_b.add, far_b.send))
    steps.at(chunks + 2, share.twin)
    steps.at(chunks, far_end)
    for k in range(nz):
        first = chunks + ready(shape, k)
        steps.at(first, functools.partial(twin.begin, k))
        steps.at(first + 1, functools.partial(twin.add, k))
        steps.at(first + 1, functools.partial(plane.begin, k))
        if first + 4 < 2 * chunks:
            steps.at(first + 4, functools.partial(plane.add_one, k, far.send))
    steps.at(2 * chunks - 2, up_b.cross)

    @pl.when(step == 0)
    def _():
        sum_start(nd, nz)
        total_before = before[...] + sq_bias_in[...]
        squeezed = total_before * sig(total_before)
        share.fill(
            nb,
            [features, pooled, dz_gate],
            [grad_sq[...], squeezed, dz_head[...]],
            [logits[...], head_pool[...], pooled_in[...]],
        )
        for b in range(nb):
            images_t[b] = jnp.transpose(images[b * PIXELS : (b + 1) * PIXELS, :])
        for ref in (early, late, gate_acc, grads):
            ref[...] = jnp.zeros_like(ref)

    steps.emit(step, 2 * chunks)
    total = totals[TOTAL_ROW : TOTAL_ROW + 1, :]

    @pl.when(step < chunks)
    def _():
        j = step
        mean_two, rstd_two = norm_rows(stats_two, j, chunks, total)
        scale_two = rstd_two * side[2 * SQUEEZE + 2 : 2 * SQUEEZE + 3, :]
        one_two = sums_two[pl.ds(j, 1), :] / total
        two_two = sums_two[pl.ds(chunks + j, 1), :] / total
        mean, rstd = norm_rows(stats_one, j, chunks, total)
        gain = side[2 * SQUEEZE : 2 * SQUEEZE + 1, :]
        bias = side[2 * SQUEEZE + 1 : 2 * SQUEEZE + 2, :]
        held[...] = jnp.zeros_like(held)
        reach = KERNEL // 2

        @pl.loop(0, nb)
        def _(b):
            at = image(b)
            hat = (dpre[at, :] - mean_two) * rstd_two
            grad = scale_two * (grad_in[at, :] - mask[at, :] * (one_two + hat * two_two))
            for s in range(KERNEL):
                buf[s] = shifted(grad, reach - s)
            hat = (pre[at, :] - mean) * rstd
            normed = hat * gain + bias
            acts[...] = normed * sig(normed) * mask[at, :]
            taps_now = [jnp.broadcast_to(taps[b, t : t + 1, :], (MAP_SIDE, LANES)) for t in range(TAPS)]
            acc = [None] * MAP_SIDE
            for q in range(MAP_SIDE):
                for s in range(KERNEL):
                    x = buf[s, q * MAP_SIDE : (q + 1) * MAP_SIDE, :]
                    for r in range(KERNEL):
                        y = q + r - reach
                        if 0 <= y < MAP_SIDE:
                            term = taps_now[r * KERNEL + s] * x
                            acc[y] = term if acc[y] is None else acc[y] + term
                done = [q - 2] if q < MAP_SIDE - 1 else [q - 2, q - 1, q]
                for i in done:
                    if i >= 0:
                        made_norm[j, pl.ds(pl.multiple_of(b * PIXELS + i * MAP_SIDE, MAP_SIDE), MAP_SIDE), :] = acc[i]
            tap_acc = [None] * TAPS
            for q in range(MAP_SIDE):
                for s in range(KERNEL):
                    x = buf[s, q * MAP_SIDE : (q + 1) * MAP_SIDE, :]
                    for r in range(KERNEL):
                        y = q + r - reach
                        if 0 <= y < MAP_SIDE:
                            both = acts[y * MAP_SIDE : (y + 1) * MAP_SIDE, :] * x
                            term = both[:8] + both[8:]
                            t = r * KERNEL + s
                            tap_acc[t] = term if tap_acc[t] is None else tap_acc[t] + term
            tap_grads[j, b] = jnp.zeros((32, LANES), f32)
            for t in range(TAPS):
                tap_grads[j, b, t : t + 1, :] = rsum(tap_acc[t])
            hat = (pre[at, :] - mean) * rstd
            value = made_norm[j, at, :] * mask[at, :] * dsilu(hat * gain + bias)
            made_norm[j, at, :] = value
            held[0:1, :] += rsum(value)
            held[1:2, :] += rsum(value * hat)

        store_sums(early, late, cut, chunks, j, held[0:1, :], held[1:2, :])

    @pl.when(step >= chunks)
    def _():
        j = step - chunks
        mean, rstd = norm_rows(stats_one, j, chunks, total)
        scale = rstd * side[2 * SQUEEZE : 2 * SQUEEZE + 1, :]
        one = sums_one[pl.ds(j, 1), :] / total
        two = sums_one[pl.ds(chunks + j, 1), :] / total
        for b in range(nb):
            at = slice(b * PIXELS, (b + 1) * PIXELS)
            lane = slice(b * LANES, (b + 1) * LANES)
            hat = (pre[at, :] - mean) * rstd
            value = (scale * (made_norm[j, at, :] - mask[at, :] * (one + hat * two))).astype(bf16)
            grads[0:WIDTH_IN, lane] = dot(images_t[b], value).astype(bf16)
            grads[WIDTH_IN : WIDTH_IN + 32, lane] = tap_grads[j, b].astype(bf16)
        gate_acc[0:nb, :] += gate_rows(grads[...], kern[...], nb)
        made[:, lanes(j * LANES * EXPERTS, LANES * EXPERTS)] = dot(grads[...], mix[:, : nb * LANES], NT).astype(bf16)

    @pl.when(step == 2 * chunks - 1)
    def _():
        dz = (gate_sums(gate_acc[...]) + gate_grad[...]) * gates[...] * (1.0 - gates[...])
        steps.end(2 * chunks)
        z = net.z
        me = net.d * nz + z
        devices = nd * nz
        own = chan_old.shape[1]
        own_head = head_old.shape[1]
        own_proj = proj_old.shape[1]
        width = own * nz
        head_width = own_head * nz
        head_chunks = head_width // LANES
        share.finish()
        count = devices * 8
        per, slots = dz_slots(nb, devices)
        row = lax.broadcasted_iota(jnp.int32, (count, 1), 0)
        keep = jnp.where((row & 7) < nb, 1.0, 0.0)

        def one(k, size):
            return rows_all[:, :, cuts_one[k] : cuts_one[k] + size].reshape(count, size) * keep

        def two(k, size):
            return pltpu.roll(rows_all[:, :, cuts_two[k] : cuts_two[k] + size].reshape(count, size), count - nb, 0)

        features = one(0, own_head)
        logits = two(0, CLASS_PAD)
        pooled = one(1, own)
        dz_gate = one(2, own)
        grad_sq = one(3, SQUEEZE)
        grad_cls[...] = dot(features, logits, TN, highest)
        grad_side[...] = jnp.zeros_like(grad_side)
        grad_side[0:SQUEEZE, :own] = dot(grad_sq, pooled, TN, highest)
        grad_side[SQUEEZE : 2 * SQUEEZE, :own] = dot(one(4, SQUEEZE), dz_gate, TN, highest)

        def channel(ref, at, n, size, own_size):
            return turn(load_wide(ref, at, size), z * own_size)[:, :own_size]

        at = 2 * SQUEEZE
        grad_side[at : at + 1, :own] = channel(sums_one, chunks, chunks, width, own)
        grad_side[at + 1 : at + 2, :own] = channel(sums_one, 0, chunks, width, own)
        grad_side[at + 2 : at + 3, :own] = channel(sums_two, chunks, chunks, width, own)
        grad_side[at + 3 : at + 4, :own] = channel(sums_two, 0, chunks, width, own)
        grad_side[at + 4 : at + 5, :own] = rsum(dz_gate)
        route_head[...] = dot(two(1, WIDTH_OUT), one(5, EXPERTS), TN, highest)
        sq_bias[...] = rsum(grad_sq)
        class_bias[...] = rsum(logits * keep)
        head_gain = channel(sums_four, head_chunks, head_chunks, head_width, own_head)
        head_bias = channel(sums_four, 0, head_chunks, head_width, own_head)
        totals = stats_one[TOTAL_ROW : TOTAL_ROW + 1, 0:1]
        loss[...] = jnp.broadcast_to(
            sums_four[2 * head_chunks : 2 * head_chunks + 1, :] / stats_one[TOTAL_ROW + 1 : TOTAL_ROW + 2, :], (8, LANES)
        )

        def moving(new, old, ref, at, n, size, own_size):
            mean = load_wide(ref, 0, size) / totals
            var = (load_wide(ref, n, size) / totals - mean * mean) * (totals / (totals - 1.0))
            new[at : at + 1, :] = 0.5 * old[at : at + 1, :] + 0.5 * turn(mean, z * own_size)[:, :own_size]
            new[at + 1 : at + 2, :] = 0.5 * old[at + 1 : at + 2, :] + 0.5 * turn(var, z * own_size)[:, :own_size]

        moving(chan_new, chan_old, stats_one, 0, chunks, width, own)
        moving(chan_new, chan_old, stats_two, 2, chunks, width, own)
        moving(head_new, head_old, stats_four, 0, head_chunks, head_width, own_head)
        moving(proj_new, proj_old, stats_three, 0, OUT_CHUNKS, WIDTH_OUT, own_proj)
        low[...] = jnp.zeros_like(low)
        own_dz = fit(jnp.concatenate([dz[b : b + 1, :] for b in range(nb)], axis=1), LANES)
        low[pl.ds(me // per, 1), :] = pltpu.roll(own_dz, lax.rem(me, per) * (nb * EXPERTS), 1)
        fraction = 1.0 / nd
        g_hside = jnp.sum(grad_cls[...] * grad_cls[...]) + jnp.sum(head_gain * head_gain) + jnp.sum(head_bias * head_bias)
        sums = (
            0.0,
            squares_of(grad_side, 104),
            squares_of(piece_h, piece_h.shape[0]) * nd,
            g_hside,
        )
        for k in range(4):
            low[slots + k : slots + k + 1, :] = row_of(sums[k] * fraction)
            low[slots + 4 + k : slots + 5 + k, :] = squares_w[k : k + 1, :] * fraction
        for k in range(nz):
            if chunks + ready(shape, k) + 4 >= 2 * chunks:
                plane.add_one(k, far.send)
        far.add()
        low[slots : slots + 1, :] = row_of(
            squares_of(piece, piece.shape[0]) + squares_of(piece_b, piece_b.shape[0])
        )
        sum_first(nd, nz, low, *comm_two)
        up.begin()
        sum_second(nd, nz, low, *comm_two)
        up.cross()
        every_sum[...] = sum_third(nd, nz, low, *comm_two)
        for k in range(4):
            grad_sq_sum = jnp.sum(every_sum[slots + k : slots + k + 1, :], axis=1, keepdims=True)
            weight_sq = jnp.sum(every_sum[slots + 4 + k : slots + 5 + k, :], axis=1, keepdims=True)
            factors[k : k + 1, :] = jnp.broadcast_to(
                jnp.sqrt(weight_sq) * lax.rsqrt(grad_sq_sum + 1e-12), (1, LANES)
            )
        row = lax.broadcasted_iota(jnp.int32, (count, slots), 0)
        col = lax.broadcasted_iota(jnp.int32, (count, slots), 1)
        spread = dot(jnp.where((row >> 3) // per == col, 1.0, 0.0), every_sum[0:slots, :], NN, highest)
        row = lax.broadcasted_iota(jnp.int32, (count, LANES), 0)
        col = lax.broadcasted_iota(jnp.int32, (count, LANES), 1)
        place = lax.rem(row >> 3, per) * nb + (row & 7) - nb
        spread = jnp.where(((col >> 3) == place) & ((row & 7) >= nb), spread, 0.0)
        row = lax.broadcasted_iota(jnp.int32, (LANES, EXPERTS), 0)
        col = lax.broadcasted_iota(jnp.int32, (LANES, EXPERTS), 1)
        dz_rows = dot(spread, jnp.where((row & (EXPERTS - 1)) == col, 1.0, 0.0), NN, highest)
        pooled_in = rows_all[:, :, cuts_two[2] : cuts_two[2] + 256].reshape(count, 256)
        route_in[...] = dot(pooled_in, dz_rows, TN, highest)[:WIDTH_IN]
        grad_side_out[...] = jnp.transpose(grad_side[...])[:own]
        values = grad_cls[:, :CLASSES]
        both = jnp.concatenate([head_gain, head_bias] + [jnp.zeros((6, own_head), f32)], axis=0)
        grad_cls[...] = jnp.concatenate(
            [jnp.transpose(both)[:, 0:2], values, jnp.zeros((own_head, CLASS_PAD - CLASSES - 2), f32)], axis=1
        )
        up.finish()
        up_b.finish()
        up_h.finish()
        plane_b.finish()
        far_b.finish()
        far.finish()
        twin.finish()
        plane.finish()


def stage_back(half_b, part_b, piece_h, grad_in, dpre, pre, taps, mask, side, stats_one, stats_two, sums_two, totals, lines, images, kern, mix, gates, gate_grad, small, shape_b, shape_h, nb, nd, nz, ident):
    rows, width = pre.shape
    chunks = width // LANES
    deep = LANES * EXPERTS
    before = lambda t: jnp.minimum(t, chunks - 1)
    after = lambda t: jnp.maximum(t - chunks, 0)
    shape = (kern.shape[0], kern.shape[1] // nz)
    devices = nd * nz
    slots = dz_slots(nb, devices)[1]
    few = nz // 2
    chan_old, head_old, proj_old = small[-3:]
    own, own_head = chan_old.shape[1], head_old.shape[1]
    outs = [(own_head, CLASS_PAD), (own, 104), (8, LANES)]
    outs += [(WIDTH_IN, EXPERTS), (WIDTH_OUT, EXPERTS), (1, SQUEEZE), (1, CLASS_PAD)]
    outs += [chan_old.shape, head_old.shape, proj_old.shape, (8, LANES)]
    cuts_one, cuts_two, wide = share_width(lines, nz)
    hbm = pl.BlockSpec(memory_space=pltpu.HBM)
    tall_before = pl.BlockSpec((rows, LANES), lambda t: (0, before(t)))
    return pl.pallas_call(
        functools.partial(stage_back_kernel, nd, nz, nb, chunks, shape, shape_b, shape_h, cuts_one, cuts_two),
        grid=(2 * chunks,),
        out_shape=[jax.ShapeDtypeStruct(x, bf16) for x in (shape, shape_b, shape_h)]
        + [jax.ShapeDtypeStruct(x, f32) for x in outs],
        in_specs=[
            pl.BlockSpec(
                (nz - few,) + half_b.shape[1:], lambda t: (1, 0, 0), pipeline_mode=pl.Buffered(1)
            ),
            whole(part_b.shape),
            whole(piece_h.shape),
            tall_before,
            tall_before,
            pl.BlockSpec((rows, LANES), lambda t: (0, lax.rem(t, chunks))),
            pl.BlockSpec((nb, 32, LANES), lambda t: (0, 0, before(t))),
            whole(mask.shape),
            pl.BlockSpec((side.shape[0], LANES), lambda t: (0, lax.rem(t, chunks))),
            whole(stats_one.shape),
            whole(stats_two.shape),
            whole(sums_two.shape),
            whole(totals.shape),
        ]
        + [whole(x.shape) for x in lines]
        + [
            whole(images.shape),
            pl.BlockSpec((kern.shape[0], deep), lambda t: (0, after(t))),
            whole(mix.shape),
            whole(gates.shape),
            whole(gate_grad.shape),
        ]
        + [whole(x.shape) for x in small],
        out_specs=[hbm] * 3 + [whole(x) for x in outs],
        scratch_shapes=[
            VMEM((chunks, rows, LANES), f32),
            VMEM((chunks, nb, 32, LANES), f32),
            VMEM((KERNEL, PIXELS, LANES), f32),
            VMEM((PIXELS, LANES), f32),
            VMEM((8, LANES), f32),
            VMEM((24, LANES), f32),
            VMEM((24, LANES), f32),
            VMEM((24, LANES), f32),
            VMEM(part_shape(shape_b, nd, nz), bf16),
            VMEM(piece_shape(shape_b, nd), bf16),
            VMEM((devices, 8, wide), f32),
            VMEM((nb, WIDTH_IN, PIXELS), bf16),
            VMEM((kern.shape[0], nb * LANES), bf16),
            VMEM((8, deep), f32),
            VMEM((104, up_to(own)), f32),
            VMEM((slots + 8, LANES), f32),
            VMEM((slots + 8, LANES), f32),
            VMEM(half_shape(shape, nd, nz), bf16),
            VMEM(part_shape(shape, nd, nz), bf16),
            VMEM(piece_shape(shape, nd), bf16),
        ]
        + sum_scratch(24, nd, nz)[1:] * 2
        + sum_scratch(slots + 8, nd, nz)[1:]
        + plane_scratch(shape_b, nd, nz - nz // 2)
        + far_scratch(shape_b, nd, nz)
        + spread_scratch(shape_b, nd, nz)
        + spread_scratch(shape_h, nd, nz)
        + share_scratch(wide, nd, nz)
        + twin_scratch(shape, nd, nz)
        + plane_scratch(shape, nd, nz)
        + far_scratch(shape, nd, nz)
        + spread_scratch(shape, nd, nz),
        compiler_params=params(ident, 62 * 1024 * 1024),
        name="stage_back",
    )(half_b, part_b, piece_h, grad_in, dpre, pre, taps, mask, side, stats_one, stats_two, sums_two, totals, *lines, images, kern, mix, gates, gate_grad, *small)


def update(weight, grad, moment, average, factor):
    scaled = grad * factor
    moment_new = 0.5 * moment + scaled
    weight_new = weight - 0.2 * (scaled + 0.5 * moment_new)
    average_new = 0.5 * average + 0.5 * weight_new
    return (weight_new, moment_new, average_new)


BLOCK_STEP = 64
HEAD_STEP = 32


def turn(x, shift):
    width = x.shape[1]
    return pltpu.roll(x, lax.rem(width - shift, width), 1)


def apply_kernel(
    factors,
    grad_side,
    side_w,
    side_m,
    side_e,
    grad_a,
    grad_b,
    block_w,
    block_m,
    block_e,
    grad_h,
    head_w,
    head_m,
    head_e,
    grad_cls,
    hside_w,
    hside_m,
    hside_e,
    side_wo,
    side_mo,
    side_eo,
    block_wo,
    block_mo,
    block_eo,
    head_wo,
    head_mo,
    head_eo,
    hside_wo,
    hside_mo,
    hside_eo,
    grad_block,
):
    @pl.when(pl.program_id(0) == 0)
    def _():
        fresh = update(side_w[...], grad_side[:, : side_w.shape[1]], side_m[...], side_e[...], factors[1:2, 0:1])
        side_wo[...], side_mo[...], side_eo[...] = fresh
        first = WIDTH_IN + TAPS
        whole_rows = first // 16 * 16

        @pl.loop(0, whole_rows // 16)
        def _(i):
            here = tall(i * 16, 16)
            grad_block[here, :] = grad_a[here, :].astype(f32)

        grad_block[whole_rows:first, :] = grad_a[whole_rows : whole_rows + 16, :].astype(f32)[: first - whole_rows]
        for i in range(WIDTH_OUT // 16):
            grad_block[first + 16 * i : first + 16 * (i + 1), :] = grad_b[16 * i : 16 * (i + 1), :].astype(f32)
        grad_block[first + WIDTH_OUT :, :] = jnp.zeros(
            (grad_block.shape[0] - first - WIDTH_OUT, grad_block.shape[1]), f32
        )

    here = pl.multiple_of(jnp.minimum(pl.program_id(0), grad_block.shape[0] // BLOCK_STEP - 1) * BLOCK_STEP, BLOCK_STEP)

    for k in range(0, BLOCK_STEP, 16):
        rows = slice(k, k + 16)
        fresh = update(
            block_w[rows, :], grad_block[pl.ds(here + k, 16), :], block_m[rows, :], block_e[rows, :], factors[0:1, 0:1]
        )
        block_wo[rows, :], block_mo[rows, :], block_eo[rows, :] = fresh
    for k in range(0, HEAD_STEP, 16):
        rows = slice(k, k + 16)
        fresh = update(
            head_w[rows, :], grad_h[rows, :].astype(f32), head_m[rows, :], head_e[rows, :], factors[2:3, 0:1]
        )
        head_wo[rows, :], head_mo[rows, :], head_eo[rows, :] = fresh
    fresh = update(hside_w[...], grad_cls[:, : hside_w.shape[1]], hside_m[...], hside_e[...], factors[3:4, 0:1])
    hside_wo[...], hside_mo[...], hside_eo[...] = fresh


def apply(factors, side, grads, block, head_arrays, hside):
    def stepped(array, size):
        last = -(-array.shape[0] // size) - 1
        return pl.BlockSpec((size, array.shape[1]), lambda j: (jnp.minimum(j, last), 0))

    steps = max(-(-block[0].shape[0] // BLOCK_STEP), -(-WIDTH_OUT // HEAD_STEP))
    blocks = (
        [whole(x.shape) for x in side]
        + [whole(x.shape) for x in grads]
        + [stepped(x, BLOCK_STEP) for x in block]
        + [stepped(x, HEAD_STEP) for x in head_arrays]
        + [stepped(x, HEAD_STEP) for x in hside]
    )
    arrays = side + grads + block + head_arrays + hside
    keep = [k for k in range(17) if k not in (0, 4, 5, 9, 13)]
    return pl.pallas_call(
        apply_kernel,
        grid=(steps,),
        out_shape=[jax.ShapeDtypeStruct(arrays[k].shape, f32) for k in keep],
        in_specs=[whole(factors.shape)] + blocks,
        out_specs=[blocks[k] for k in keep],
        scratch_shapes=[VMEM((-(-block[0].shape[0] // BLOCK_STEP) * BLOCK_STEP, block[0].shape[1]), f32)],
        compiler_params=params(),
        name="apply",
    )(factors, *arrays)


def body(
    nd,
    nz,
    images,
    pixel_mask,
    counts,
    labels,
    block_w,
    chan_side,
    head_w,
    head_side,
    shared,
    block_mom,
    side_mom,
    head_mom,
    hside_mom,
    shared_mom,
    block_ema,
    side_ema,
    head_ema,
    hside_ema,
    shared_ema,
    chan_stats,
    head_stats,
    proj_stats,
):
    z = lax.axis_index("chan")
    nb = images.shape[0] // nz
    own = chan_side.shape[1]
    own_head = head_side.shape[0]
    width = own * nz
    head_width = own_head * nz
    end_route = WIDTH_IN * EXPERTS
    end_head = end_route + WIDTH_OUT * EXPERTS
    end_norm = end_head + 2 * WIDTH_OUT
    end_squeeze = end_norm + SQUEEZE
    route_in = shared[:end_route].reshape(WIDTH_IN, EXPERTS)
    route_head = shared[end_route:end_head].reshape(WIDTH_OUT, EXPERTS)
    gain_out = shared[end_head:end_norm].reshape(2, WIDTH_OUT)
    sq_bias = shared[None, end_norm:end_squeeze]
    class_bias = jnp.pad(shared[end_squeeze:], (0, CLASS_PAD - CLASSES))[None, :]

    def mine(x):
        return lax.dynamic_slice_in_dim(x, z * nb, nb, 0)

    image_rows = mine(images).reshape(nb * PIXELS, WIDTH_IN)
    mask_now = mine(pixel_mask).astype(f32)
    mask = jnp.broadcast_to(mask_now.reshape(-1, 1), (nb * PIXELS, LANES))
    mask_rows = jnp.pad(
        (jnp.eye(nb, dtype=f32)[:, :, None] * mask_now[None]).reshape(nb, nb * PIXELS).astype(bf16),
        ((0, 8 - nb), (0, 0)),
    )
    count_rows = jnp.broadcast_to(jnp.pad(mine(counts).astype(f32), (0, 8 - nb))[:, None], (8, LANES))
    label_rows = jnp.broadcast_to(jnp.pad(mine(labels), (0, 8 - nb))[:, None], (8, LANES))

    full_a, full_b, side, gain_head, kern_h, kern_c, squares = first_gather(
        block_w, head_w, head_side, chan_side.T, nd, nz, 1
    )
    (
        pre,
        taps,
        dpre,
        stats_one,
        stats_two,
        mix,
        gates,
        pooled_in,
        excited,
        proj,
        pooled,
        gate,
        squeezed,
        stats_three,
        mixed_proj,
        full_b,
        full_h,
        full_c,
    ) = first_stage(
        full_a,
        image_rows,
        mask,
        mask_rows,
        count_rows,
        route_in,
        side,
        sq_bias,
        full_b,
        kern_h,
        kern_c,
        nb,
        width,
        nd,
        nz,
        3,
    )
    totals = stats_one
    head_pool, stats_four, features, grad_logits, sums_four, grad_proj, sums_three, dz_head, half_h, part_h, _ = head_stage(
        mask,
        mask_rows,
        count_rows,
        label_rows,
        class_bias,
        gain_head,
        totals,
        gain_out,
        full_h,
        route_head,
        proj,
        stats_three,
        full_c,
        nb,
        nd,
        nz,
        8,
    )
    shape_h, shape_b = shard_shape(full_h, nz), shard_shape(full_b, nz)
    grad_norm, sums_two, grad_squeeze, gate_grad, dz_gate, piece_h, half_b, part_b = project_back(
        half_h,
        part_h,
        shape_h,
        grad_proj,
        proj,
        stats_three,
        sums_three,
        gain_out,
        mask,
        count_rows,
        totals,
        stats_two,
        side,
        dpre,
        excited,
        mixed_proj,
        full_b,
        mix,
        gate,
        pooled,
        squeezed,
        sq_bias,
        nb,
        nd,
        nz,
        9,
    )
    lines = [features, grad_logits, pooled, dz_gate, head_pool, pooled_in, grad_squeeze, squeezed, sq_bias, dz_head]
    small = [squares, stats_three, stats_four, sums_four, chan_stats, head_stats, proj_stats]
    grad_a, grad_b, grad_h, grad_cls, grad_side, factors, *rest = stage_back(
        half_b,
        part_b,
        piece_h,
        grad_norm,
        dpre,
        pre,
        taps,
        mask,
        side,
        stats_one,
        stats_two,
        sums_two,
        totals,
        lines,
        image_rows,
        full_a,
        mix,
        gates,
        gate_grad,
        small,
        shape_b,
        shape_h,
        nb,
        nd,
        nz,
        11,
    )
    grad_route_in, grad_route_head, grad_sq_bias, grad_class_bias, new_chan, new_head_stats, new_proj, loss = rest
    results = apply(
        factors,
        [grad_side, chan_side.T, side_mom.T, side_ema.T],
        [grad_a, grad_b],
        [block_w, block_mom, block_ema],
        [grad_h, head_w, head_mom, head_ema],
        [grad_cls, head_side, hside_mom, hside_ema],
    )
    new_side, new_block, new_head, new_hside = (results[3 * k : 3 * k + 3] for k in range(4))
    new_side = [x.T for x in new_side]

    def out_row(first):
        return sums_three[first : first + OUT_CHUNKS].reshape(-1)[:WIDTH_OUT]

    grad_shared = jnp.concatenate(
        [
            grad_route_in.reshape(-1),
            grad_route_head.reshape(-1),
            out_row(OUT_CHUNKS),
            out_row(0),
            grad_sq_bias[0],
            grad_class_bias[0, :CLASSES],
        ]
    )
    new_shared = update(
        shared,
        grad_shared,
        shared_mom,
        shared_ema,
        jnp.sqrt(jnp.sum(shared * shared)) * lax.rsqrt(jnp.sum(grad_shared * grad_shared) + 1e-12),
    )
    groups = (new_block, new_side, new_head, new_hside, new_shared)
    return (
        (loss[0, 0],)
        + tuple(group[k] for k in range(3) for group in groups)
        + (new_chan, new_head_stats, new_proj)
    )


def solution(mesh):
    nd, nz = mesh.shape["dp"], mesh.shape["chan"]
    cols = P(None, "chan")
    state = (cols, cols, cols, P("chan", None), P())
    return jax.shard_map(
        functools.partial(body, nd, nz),
        mesh=mesh,
        in_specs=(P("dp", None, None), P("dp", None), P("dp"), P("dp"))
        + state * 3
        + (cols, cols, cols),
        out_specs=(P(),) + state * 3 + (cols, cols, cols),
        check_vma=False,
    )
```
